32 devices in a mesh: dp: 8 (over z, x), tensor: 4 (over y, core).
Axes of the slice: x: 2, y: 2, z: 4, core: 2. Of those that a mesh axis runs over, the one named last changes fastest.
Arguments:
- tokens: bfloat16 [4096, 2048], P('dp'), may hold values from -6 to 6
- norm_attn: float32 [2048], replicated, may hold values from 0.5 to 1.5
- w_query: bfloat16 [2048, 2048], P(None, 'tensor'), may hold values from -0.125 to 0.125
- key_weight: bfloat16 [2048, 1024], P(None, 'tensor'), may hold values from -0.125 to 0.125
- value_weight: bfloat16 [2048, 1024], P(None, 'tensor'), may hold values from -0.125 to 0.125
- query_gain: float32 [128], replicated, may hold values from 0.5 to 1.5
- key_gain: float32 [128], replicated, may hold values from 0.5 to 1.5
- w_out: bfloat16 [2048, 2048], P('tensor'), may hold values from -2 to 2
- norm_mlp: float32 [2048], replicated, may hold values from 0.5 to 1.5
- w_gate: bfloat16 [2048, 6144], P(None, 'tensor'), may hold values from -0.125 to 0.125
- w_up: bfloat16 [2048, 6144], P(None, 'tensor'), may hold values from -0.125 to 0.125
- w_down: bfloat16 [6144, 2048], P('tensor'), may hold values from -0.078125 to 0.078125
- out_grad: bfloat16 [4096, 2048], P('dp'), may hold values from -6 to 6
- prefix_len: int32 [1], replicated, may hold values from 409 to 2048
Outputs:
- block_out: bfloat16 [4096, 2048], P('dp')
- tokens_grad: float32 [4096, 2048], P('dp')
- norm_attn_grad: float32 [2048], P('dp')
- w_query_grad: float32 [2048, 2048], P('dp', 'tensor')
- w_key_grad: float32 [2048, 1024], P('dp', 'tensor')
- w_value_grad: float32 [2048, 1024], P('dp', 'tensor')
- query_gain_grad: float32 [128], replicated
- key_gain_grad: float32 [128], replicated
- w_out_grad: float32 [2048, 2048], P('tensor', 'dp')
- norm_mlp_grad: float32 [2048], P('dp')
- w_gate_grad: float32 [2048, 6144], P('dp', 'tensor')
- w_up_grad: float32 [2048, 6144], P('dp', 'tensor')
- w_down_grad: float32 [6144, 2048], P('tensor', 'dp')
The draws below stay inside these ranges and needn't reach their ends.
Inputs may be any that keep to these rules, and one draw needn't show every extreme that they name: `prefix_len`: leading tokens of each sequence that see one another in both directions.
All inputs are finite; a program needn't handle non-finite values.
Results may differ from the reference program's by a relative error of at most 0.024.
Values may be sent and summed in bfloat16 or wider, within the bound.
A program may use at most 256 MiB of HBM per device.

```python
import math
import jax
import jax.numpy as jnp
from jax import lax

MODEL_WIDTH = 2048
QUERY_HEADS = 16
KEY_VALUE_HEADS = 8
HEAD_SIZE = 128
FF = 6144
SEQLEN = 4096
SEQS = 1
TOKENS = 4096


def spiked(drawn, own_key, source, target, parts, factor):
    def block_of(position):
        return (jnp.arange(drawn.shape[position]) // (drawn.shape[position] // parts)).reshape((-1,) + (1,) * (drawn.ndim - 1 - position))

    one_side = jax.random.permutation(own_key, parts)[block_of(target)]
    second = (block_of(target) + parts // 2) % parts
    return jnp.where((block_of(source) == one_side) | (block_of(source) == second), factor * drawn, drawn)


def steps_of(own_key, shape, shards, low, largest):
    def one(axis_at, blocks):
        heights = jax.random.uniform(jax.random.fold_in(jax.random.fold_in(own_key, 6), axis_at), (blocks,), jnp.float32, low / len(shards), largest / len(shards))
        return jnp.repeat(jnp.exp(heights), shape[axis_at] // blocks).reshape((-1,) + (1,) * (len(shape) - axis_at - 1))

    level = one(*shards[0])
    for cut in shards[1:]:
        level = level * one(*cut)
    return level


def scatter_about(stream_key, shape, spread, limit, pieces=(), kind=jnp.bfloat16):
    loudness = steps_of(stream_key, shape, pieces, -0.22, 0.18) if pieces else 1.0
    entries = jax.random.normal(stream_key, shape, jnp.float32) * spread * loudness
    return jnp.minimum(jnp.maximum(entries, -limit), limit).astype(kind)


def heavy_noise(key, shape, spread, bound, split, heavy, kind=jnp.bfloat16):
    array = spread * jax.random.normal(key, shape, jnp.float32)
    if split:
        array = array * steps_of(key, shape, split, -0.22, 0.18)
    return jnp.clip(spiked(array, jax.random.fold_in(key, 3), *heavy), -bound, bound).astype(kind)


def setup_inputs(seed: int = 0) -> dict:
    key_of = jax.random.split(jax.random.key(seed), 15)
    tokens = heavy_noise(key_of[0], (TOKENS, MODEL_WIDTH), 1.0, 6.0, ((0, 8),), (0, 1, 8, 2.0))
    norm_attn = jnp.clip(1.0 + 0.1 * jax.random.normal(key_of[1], (MODEL_WIDTH,), jnp.float32), 0.5, 1.5)
    w_query = scatter_about(key_of[2], (MODEL_WIDTH, QUERY_HEADS * HEAD_SIZE), MODEL_WIDTH ** -0.5, 0.125, ((1, 4),))
    key_weight = scatter_about(key_of[3], (MODEL_WIDTH, KEY_VALUE_HEADS * HEAD_SIZE), MODEL_WIDTH ** -0.5, 0.125, ((1, 4),))
    value_weight = scatter_about(key_of[4], (MODEL_WIDTH, KEY_VALUE_HEADS * HEAD_SIZE), MODEL_WIDTH ** -0.5, 0.125, ((1, 4),))
    query_gain = jnp.clip(1.0 + 0.1 * jax.random.normal(key_of[5], (HEAD_SIZE,), jnp.float32), 0.5, 1.5)
    key_gain = jnp.clip(1.0 + 0.1 * jax.random.normal(key_of[6], (HEAD_SIZE,), jnp.float32), 0.5, 1.5)
    w_out = scatter_about(key_of[7], (QUERY_HEADS * HEAD_SIZE, MODEL_WIDTH), (max(QUERY_HEADS * HEAD_SIZE // 256, 1)) ** -0.5, 2.0, ((0, 4),))
    norm_mlp = jnp.clip(1.0 + 0.1 * jax.random.normal(key_of[8], (MODEL_WIDTH,), jnp.float32), 0.5, 1.5)
    w_gate = scatter_about(key_of[9], (MODEL_WIDTH, FF), MODEL_WIDTH ** -0.5, 0.125, ((1, 4),))
    w_up = scatter_about(key_of[10], (MODEL_WIDTH, FF), MODEL_WIDTH ** -0.5, 0.125, ((1, 4),))
    w_down = scatter_about(key_of[11], (FF, MODEL_WIDTH), FF ** -0.5, 0.078125, ((0, 4),))
    out_grad = heavy_noise(key_of[12], (TOKENS, MODEL_WIDTH), 1.0, 6.0, ((0, 8),), (0, 1, 8, 2.0))
    prefix_len = jax.random.randint(key_of[13], (SEQS,), SEQLEN // 10, SEQLEN // 2 + 1).astype(jnp.int32)
    return dict(tokens=tokens, norm_attn=norm_attn, w_query=w_query, key_weight=key_weight, value_weight=value_weight, query_gain=query_gain, key_gain=key_gain, w_out=w_out, norm_mlp=norm_mlp, w_gate=w_gate, w_up=w_up, w_down=w_down, out_grad=out_grad, prefix_len=prefix_len)


norm_eps = 1e-06
rope_base = 1000000.0
masked_score = -1e+30

@jax.custom_vjp
def lower_bound(v):
    return lax.optimization_barrier(v.astype(jnp.bfloat16)).astype(jnp.float32)

@jax.custom_vjp
def lower_bound_back(v):
    return v

def low_keep(v):
    return (lower_bound(v), None)

def low_pass(kept, grad):
    return (grad,)

def back_keep(v):
    return (v, None)

def back_low(kept, grad):
    return (lower_bound(grad),)
lower_bound.defvjp(low_keep, low_pass)
lower_bound_back.defvjp(back_keep, back_low)

def rms_scale(value_rows_all, norm_gain):
    return value_rows_all * lax.rsqrt(lax.optimization_barrier(jnp.mean(value_rows_all * value_rows_all, axis=-1, keepdims=True)) + norm_eps) * norm_gain

def rope_tables(positions, head_width):
    counter = jnp.arange(head_width // 2, dtype=jnp.float32)
    frequency = rope_base ** (-2.0 * counter / head_width)
    angles = positions.astype(jnp.float32)[:, None] * frequency[None, :]
    return (jnp.cos(angles)[:, None, :], jnp.sin(angles)[:, None, :])

def rope_apply(value_rows_all, cosine_table, sine_table):
    half_width = value_rows_all.shape[-1] // 2
    first_half = value_rows_all[..., :half_width]
    second_half = value_rows_all[..., half_width:]
    return jnp.concatenate([first_half * cosine_table - second_half * sine_table, second_half * cosine_table + first_half * sine_table], axis=-1)

def matrix_product(left, right):
    return jnp.dot(left, right, precision=lax.Precision.HIGHEST, preferred_element_type=jnp.float32)

def attention(query_rows_all, key_rows_all, value_rows_all, prefix):
    length_total = query_rows_all.shape[0]
    block_row_list = math.gcd(length_total, 512)
    query_per_key_heads = QUERY_HEADS // KEY_VALUE_HEADS
    scores_scale = 1.0 / math.sqrt(HEAD_SIZE)
    grouped_heads = query_rows_all.reshape(length_total // block_row_list, block_row_list, KEY_VALUE_HEADS, query_per_key_heads, HEAD_SIZE)
    starts = (jnp.arange(length_total // block_row_list) * block_row_list).astype(jnp.int32)
    key_pos = jnp.arange(length_total).astype(jnp.int32)

    @jax.checkpoint
    def one_block(scan_item):
        query_block_rows, first_row = scan_item
        attention_scores = jnp.einsum('wluq,clq->luwc', query_block_rows, key_rows_all, precision=lax.Precision.HIGHEST) * scores_scale
        attention_scores = lower_bound_back(attention_scores)
        query_pos = first_row + jnp.arange(block_row_list).astype(jnp.int32)
        allowed = (key_pos[None, :] <= query_pos[:, None]) | (key_pos[None, :] < prefix)
        attention_scores = jnp.where(allowed, attention_scores, masked_score)
        probabilities = lower_bound(jax.nn.softmax(attention_scores, axis=-1))
        attended_rows = jnp.einsum('lxcn,nlp->clxp', probabilities, value_rows_all, precision=lax.Precision.HIGHEST)
        return attended_rows.reshape(block_row_list, QUERY_HEADS * HEAD_SIZE)
    return lax.map(one_block, (grouped_heads, starts)).reshape(length_total, QUERY_HEADS * HEAD_SIZE)

def layer(seq_rows, prefix, norm_attn, w_query, key_weight, value_weight, query_gain, key_gain, w_out, norm_mlp, w_gate, w_up, w_down):
    length_total = seq_rows.shape[0]
    cosine_table, sine_table = rope_tables(jnp.arange(length_total), HEAD_SIZE)
    hidden_first = lower_bound(rms_scale(seq_rows, norm_attn))
    q_proj = lower_bound_back(matrix_product(hidden_first, w_query)).reshape(length_total, QUERY_HEADS, HEAD_SIZE)
    key_projected = lower_bound_back(matrix_product(hidden_first, key_weight)).reshape(length_total, KEY_VALUE_HEADS, HEAD_SIZE)
    value_projected = lower_bound(lower_bound_back(matrix_product(hidden_first, value_weight))).reshape(length_total, KEY_VALUE_HEADS, HEAD_SIZE)
    query_rows_all = lower_bound(rope_apply(rms_scale(q_proj, query_gain), cosine_table, sine_table))
    key_rows_all = lower_bound(rope_apply(rms_scale(key_projected, key_gain), cosine_table, sine_table))
    head_rows = lower_bound(lower_bound_back(attention(query_rows_all, key_rows_all, value_projected, prefix)))
    middle = seq_rows + lower_bound_back(matrix_product(head_rows, w_out))
    h_two = lower_bound(rms_scale(middle, norm_mlp))
    gate_proj = lower_bound_back(matrix_product(h_two, w_gate))
    up_proj = lower_bound_back(matrix_product(h_two, w_up))
    hidden = lower_bound(jax.nn.silu(gate_proj) * up_proj)
    return middle + lower_bound_back(matrix_product(hidden, w_down))

def reference(tokens, norm_attn, w_query, key_weight, value_weight, query_gain, key_gain, w_out, norm_mlp, w_gate, w_up, w_down, out_grad, prefix_len):
    params = (norm_attn.astype(jnp.float32), w_query.astype(jnp.float32), key_weight.astype(jnp.float32), value_weight.astype(jnp.float32), query_gain.astype(jnp.float32), key_gain.astype(jnp.float32), w_out.astype(jnp.float32), norm_mlp.astype(jnp.float32), w_gate.astype(jnp.float32), w_up.astype(jnp.float32), w_down.astype(jnp.float32))
    inputs = tokens.astype(jnp.float32).reshape(SEQS, SEQLEN, MODEL_WIDTH)
    cotangents = out_grad.astype(jnp.float32).reshape(SEQS, SEQLEN, MODEL_WIDTH)

    def per_sequence(totals, scan_item):
        seq_rows, seq_grad, prefix = scan_item
        outputs, pull_back = jax.vjp(lambda seq_in, *weights: layer(seq_in, prefix, *weights), seq_rows, *params)
        grad_list = pull_back(seq_grad)
        totals = jax.tree.map(jnp.add, totals, tuple(grad_list[1:]))
        return (totals, (outputs, grad_list[0]))
    start_totals = tuple((jnp.zeros_like(param_item) for param_item in params))
    totals, (outputs, input_grads) = lax.scan(per_sequence, start_totals, (inputs, cotangents, prefix_len))
    return (outputs.reshape(TOKENS, MODEL_WIDTH).astype(jnp.bfloat16), input_grads.reshape(TOKENS, MODEL_WIDTH), totals[0], totals[1], totals[2], totals[3], totals[4], totals[5], totals[6], totals[7], totals[8], totals[9], totals[10])
```

```python
import functools
import math

import jax
import jax.numpy as jnp
from jax import lax
from jax.experimental import pallas as pl
from jax.experimental.pallas import tpu as pltpu
from jax.sharding import PartitionSpec as P

F32 = jnp.float32
BF16 = jnp.bfloat16
EPS = 1e-06
ROPE_BASE = 1000000.0
MAX_PREFIX = 2048
VMEM_LIMIT = 56 * 2**20

NN = (((1,), (0,)), ((), ()))
NT = (((1,), (1,)), ((), ()))
TN = (((0,), (0,)), ((), ()))


def dot(left, right, dims=NN):
    return lax.dot_general(left, right, dims, preferred_element_type=F32)


def vmem(count):
    return [pl.BlockSpec(memory_space=pltpu.VMEM)] * count


def params():
    return pltpu.CompilerParams(vmem_limit_bytes=VMEM_LIMIT)


def roll_half(value):
    return pltpu.roll(value, value.shape[-1] // 2, 1)


def project_kernel(x_ref, g_ref, *refs, heads, normed, width):
    count = len(heads)
    w_refs = refs[:count]
    gain_refs = refs[count : 2 * count]
    cos_ref, sin_ref = refs[2 * count : 2 * count + 2]
    h_ref, out_ref = refs[2 * count + 2 : 2 * count + 4]
    raw_refs = refs[2 * count + 4 :]
    x = x_ref[...].astype(F32)
    h = (x * lax.rsqrt(jnp.mean(x * x, axis=1, keepdims=True) + EPS) * g_ref[...]).astype(BF16)
    h_ref[...] = h
    cos, sin = cos_ref[...], sin_ref[...]
    column = 0
    raw_at = 0
    for i in range(count):
        product = dot(h, w_refs[i][...])
        if normed[i]:
            raw_refs[raw_at][...] = product
            raw_at += 1
        for j in range(heads[i]):
            u = product[:, j * width : (j + 1) * width]
            if normed[i]:
                u = u * lax.rsqrt(jnp.mean(u * u, axis=1, keepdims=True) + EPS) * gain_refs[i][...]
                u = u * cos + roll_half(u) * sin
            out_ref[:, column : column + width] = u.astype(BF16)
            column += width


def project(x, gain, weights, gains, normed, cos, sin, name):
    rows, model = x.shape
    width = cos.shape[1]
    heads = tuple(w.shape[1] // width for w in weights)
    columns = sum(w.shape[1] for w in weights)
    raws = [w for w, n in zip(weights, normed) if n]
    return pl.pallas_call(
        functools.partial(project_kernel, heads=heads, normed=normed, width=width),
        out_shape=[
            jax.ShapeDtypeStruct((rows, model), BF16),
            jax.ShapeDtypeStruct((rows, columns), BF16),
        ]
        + [jax.ShapeDtypeStruct((rows, w.shape[1]), F32) for w in raws],
        in_specs=vmem(4 + 2 * len(weights)),
        out_specs=vmem(2 + len(raws)),
        compiler_params=params(),
        cost_estimate=pl.CostEstimate(
            flops=2 * rows * model * columns,
            bytes_accessed=4 * rows * model + 2 * model * columns,
            transcendentals=0,
        ),
        name=name,
    )(x, gain, *weights, *gains, cos, sin)


def unproject_kernel(d_ref, raw_ref, gain_ref, cos_ref, sin_ref, out_ref, gain_out_ref, *, width, plain):
    columns = d_ref.shape[1]
    cos, sin = cos_ref[...], sin_ref[...]
    gain = gain_ref[...]
    total = jnp.zeros((1, width), F32)
    for at in range(0, columns - plain, width):
        d = d_ref[:, at : at + width].astype(F32)
        c = d * cos - roll_half(d) * sin
        v = raw_ref[:, at : at + width]
        r = lax.rsqrt(jnp.mean(v * v, axis=1, keepdims=True) + EPS)
        n = v * r
        total = total + jnp.sum(c * n, axis=0, keepdims=True)
        gc = gain * c
        out_ref[:, at : at + width] = (r * (gc - n * jnp.mean(n * gc, axis=1, keepdims=True))).astype(BF16)
    if plain:
        out_ref[:, columns - plain :] = d_ref[:, columns - plain :].astype(BF16)
    gain_out_ref[...] = total


def unproject(d, raw, gain, cos, sin, plain, name):
    rows, columns = d.shape
    width = cos.shape[1]
    return pl.pallas_call(
        functools.partial(unproject_kernel, width=width, plain=plain),
        out_shape=[jax.ShapeDtypeStruct((rows, columns), BF16), jax.ShapeDtypeStruct((1, width), F32)],
        in_specs=vmem(5),
        out_specs=vmem(2),
        compiler_params=params(),
        cost_estimate=pl.CostEstimate(
            flops=20 * rows * columns, bytes_accessed=10 * rows * columns, transcendentals=0
        ),
        name=name,
    )(d, raw, gain, cos, sin)


def block_flags(scalar_ref, slot, rows):
    member, prefix = scalar_ref[0], scalar_ref[1]
    other = scalar_ref[2 + slot]
    key0 = other * rows
    needed = (other >= 0) & ((other <= member) | (key0 < prefix))
    full = (other < member) | (key0 + rows <= prefix)
    return key0, needed, full


def visible(shape, key0, row0, prefix):
    key_pos = key0 + lax.broadcasted_iota(jnp.int32, shape, 1)
    row_pos = row0 + lax.broadcasted_iota(jnp.int32, shape, 0)
    return (key_pos <= row_pos) | (key_pos < prefix)


def attn_fwd_kernel(scalar_ref, q_ref, *refs, slots, kv_heads, repeat, width, tile, coef, first, last):
    kv_refs = refs[:slots]
    rest = refs[slots:]
    if not first:
        acc_in, rest = rest[0], rest[1:]
    if last:
        o_ref, lse_ref, acc = rest
    else:
        (acc,) = rest
    rows = q_ref.shape[0]
    kv_width = kv_heads * width
    if first:
        acc[...] = jnp.zeros_like(acc)
    else:
        acc[...] = acc_in[...]
    ones = jnp.ones((rows, width), BF16)
    row0 = scalar_ref[0] * rows
    prefix = scalar_ref[1]
    for slot in range(slots):
        key0, needed, full = block_flags(scalar_ref, slot, rows)

        def work(masked, slot=slot, key0=key0):
            for h in range(kv_heads):
                k = kv_refs[slot][:, h * width : (h + 1) * width]
                v = kv_refs[slot][:, kv_width + h * width : kv_width + (h + 1) * width]
                v = jnp.concatenate([v, ones], axis=1)
                for g in range(repeat):
                    head = h * repeat + g
                    for at in range(0, rows, tile):
                        q = q_ref[at : at + tile, head * width : (head + 1) * width]
                        p = jnp.exp2(dot(q, k, NT) * coef)
                        if masked:
                            p = jnp.where(visible(p.shape, key0, row0 + at, prefix), p, 0.0)
                        acc[at : at + tile, 2 * head * width : 2 * (head + 1) * width] += dot(
                            p.astype(BF16), v
                        )

        pl.when(needed & full)(functools.partial(work, False))
        pl.when(needed & jnp.logical_not(full))(functools.partial(work, True))
    if last:
        for head in range(kv_heads * repeat):
            total = acc[:, (2 * head + 1) * width : (2 * head + 2) * width]
            o_ref[:, head * width : (head + 1) * width] = (
                acc[:, 2 * head * width : (2 * head + 1) * width] / total
            ).astype(BF16)
            lse_ref[:, head * width : (head + 1) * width] = jnp.log2(total) * (1.0 / coef)


def attn_fwd(scalars, q, blocks, acc, last, dims):
    kv_heads, repeat, width = dims
    rows = q.shape[0]
    columns = kv_heads * repeat * width
    first = acc is None
    acc_shape = jax.ShapeDtypeStruct((rows, 2 * columns), F32)
    if last:
        out_shape = [
            jax.ShapeDtypeStruct((rows, columns), BF16),
            jax.ShapeDtypeStruct((rows, columns), F32),
        ]
        scratch = [pltpu.VMEM(acc_shape.shape, F32)]
    else:
        out_shape = [acc_shape]
        scratch = []
    slots = len(blocks)
    args = [scalars, q, *blocks] + ([] if first else [acc])
    return pl.pallas_call(
        functools.partial(
            attn_fwd_kernel,
            slots=slots,
            kv_heads=kv_heads,
            repeat=repeat,
            width=width,
            tile=min(rows, 256),
            coef=math.log2(math.e) / math.sqrt(width),
            first=first,
            last=last,
        ),
        out_shape=out_shape,
        in_specs=[pl.BlockSpec(memory_space=pltpu.SMEM)] + vmem(len(args) - 1),
        out_specs=vmem(len(out_shape)),
        scratch_shapes=scratch,
        compiler_params=params(),
        cost_estimate=pl.CostEstimate(
            flops=slots * 8 * rows * rows * columns,
            bytes_accessed=12 * rows * columns,
            transcendentals=slots * rows * rows * kv_heads * repeat,
        ),
        name="attn_fwd",
    )(*args)


def split_three(value):
    high = value.astype(BF16)
    left = value - high.astype(F32)
    mid = left.astype(BF16)
    return high.astype(F32), mid.astype(F32), (left - mid.astype(F32)).astype(BF16).astype(F32)


def attn_prep_kernel(q_ref, do_ref, o_ref, lse_ref, qx_ref, dox_ref, *, heads, width):
    rows = q_ref.shape[0]
    lane = lax.broadcasted_iota(jnp.int32, (rows, width), 1)

    def extra(value):
        a, b, c = split_three(value)
        return jnp.where(lane == 0, a, jnp.where(lane == 1, b, jnp.where(lane == 2, c, 0.0))).astype(BF16)

    for head in range(heads):
        at = slice(head * width, (head + 1) * width)
        qx_ref[head, :, :width] = q_ref[:, at]
        qx_ref[head, :, width:] = extra(lse_ref[:, at])
        d = do_ref[:, at]
        delta = jnp.sum(d.astype(F32) * o_ref[:, at].astype(F32), axis=1, keepdims=True)
        dox_ref[head, :, :width] = d
        dox_ref[head, :, width:] = extra(jnp.broadcast_to(delta, (rows, width)))


def attn_prep(q, d_out, out, lse, width):
    rows, columns = q.shape
    heads = columns // width
    return pl.pallas_call(
        functools.partial(attn_prep_kernel, heads=heads, width=width),
        out_shape=[jax.ShapeDtypeStruct((heads, rows, 2 * width), BF16)] * 2,
        in_specs=vmem(4),
        out_specs=vmem(2),
        compiler_params=params(),
        cost_estimate=pl.CostEstimate(
            flops=20 * rows * columns, bytes_accessed=14 * rows * columns, transcendentals=0
        ),
        name="attn_prep",
    )(q, d_out, out, lse)


def attn_bwd_kernel(scalar_ref, qx_ref, dox_ref, *refs, slots, kv_heads, repeat, width, coef, scale, first, last):
    kv_refs = refs[:slots]
    rest = refs[slots:]
    if not first:
        dq_in, rest = rest[0], rest[1:]
    dq_ref = rest[0]
    dkv_refs = rest[1:]
    rows = qx_ref.shape[1]
    kv_width = kv_heads * width
    if first:
        dq_ref[...] = jnp.zeros_like(dq_ref)
    else:
        dq_ref[...] = dq_in[...]
    lane = lax.broadcasted_iota(jnp.int32, (rows, width), 1)
    minus = jnp.where(lane < 3, -1.0, 0.0).astype(BF16)
    row0 = scalar_ref[0] * rows
    prefix = scalar_ref[1]
    for slot in range(slots):
        key0, needed, full = block_flags(scalar_ref, slot, rows)

        def work(masked, slot=slot, key0=key0):
            for h in range(kv_heads):
                k_at = slice(h * width, (h + 1) * width)
                v_at = slice(kv_width + h * width, kv_width + (h + 1) * width)
                k = kv_refs[slot][:, k_at]
                v = kv_refs[slot][:, v_at]
                kx = jnp.concatenate([k, minus], axis=1)
                vx = jnp.concatenate([v, minus], axis=1)
                dk = jnp.zeros((rows, width), F32)
                dv = jnp.zeros((rows, width), F32)
                for g in range(repeat):
                    head = h * repeat + g
                    qx = qx_ref[head]
                    dox = dox_ref[head]
                    p = jnp.exp2(dot(qx, kx, NT) * coef)
                    if masked:
                        p = jnp.where(visible(p.shape, key0, row0, prefix), p, 0.0)
                    ds = (p * dot(dox, vx, NT)).astype(BF16)
                    dv += dot(p.astype(BF16), dox[:, :width], TN)
                    dk += dot(ds, qx[:, :width], TN)
                    dq_ref[:, head * width : (head + 1) * width] += dot(ds, k)
                dkv_refs[slot][:, k_at] = (dk * scale).astype(BF16)
                dkv_refs[slot][:, v_at] = dv.astype(BF16)

        pl.when(needed & full)(functools.partial(work, False))
        pl.when(needed & jnp.logical_not(full))(functools.partial(work, True))

        @pl.when(jnp.logical_not(needed))
        def _(slot=slot):
            dkv_refs[slot][...] = jnp.zeros_like(dkv_refs[slot])

    if last:
        dq_ref[...] = dq_ref[...] * scale


def attn_bwd(scalars, qx, dox, blocks, dq, last, dims):
    kv_heads, repeat, width = dims
    rows = qx.shape[1]
    columns = kv_heads * repeat * width
    first = dq is None
    slots = len(blocks)
    args = [scalars, qx, dox, *blocks] + ([] if first else [dq])
    out_shape = [jax.ShapeDtypeStruct((rows, columns), F32)] + [
        jax.ShapeDtypeStruct(b.shape, BF16) for b in blocks
    ]
    return pl.pallas_call(
        functools.partial(
            attn_bwd_kernel,
            slots=slots,
            kv_heads=kv_heads,
            repeat=repeat,
            width=width,
            coef=math.log2(math.e) / math.sqrt(width),
            scale=1.0 / math.sqrt(width),
            first=first,
            last=last,
        ),
        out_shape=out_shape,
        in_specs=[pl.BlockSpec(memory_space=pltpu.SMEM)] + vmem(len(args) - 1),
        out_specs=vmem(len(out_shape)),
        compiler_params=params(),
        cost_estimate=pl.CostEstimate(
            flops=slots * 20 * rows * rows * columns,
            bytes_accessed=16 * rows * columns,
            transcendentals=slots * rows * rows * kv_heads * repeat,
        ),
        name="attn_bwd",
    )(*args)


def rms_parts(value):
    r = lax.rsqrt(jnp.mean(value * value, axis=-1, keepdims=True) + EPS)
    return r, value * r


def rms_back(r, n, gain, c):
    gc = gain * c
    return r * (gc - n * jnp.mean(n * gc, axis=-1, keepdims=True))


def shards(
    dp_size,
    tensor_size,
    tokens,
    norm_attn,
    w_query,
    key_weight,
    value_weight,
    query_gain,
    key_gain,
    w_out,
    norm_mlp,
    w_gate,
    w_up,
    w_down,
    out_grad,
    prefix_len,
):
    rows, model = tokens.shape
    width = query_gain.shape[0]
    kv_heads = key_weight.shape[1] // width
    repeat = w_query.shape[1] // key_weight.shape[1]
    dims = (kv_heads, repeat, width)
    group = dp_size // prefix_len.shape[0]
    planes = dp_size // 2
    group_planes = group // 2
    half = rows // 2
    shard = model // dp_size
    assert tensor_size == 4 and MAX_PREFIX <= 4 * rows

    device = lax.axis_index("dp")
    core = lax.axis_index("tensor") % 2
    x_at = device % 2
    z_at = device // 2
    sequence = device // group
    member = device % group
    plane = member // 2
    prefix = jnp.sum(jnp.where(jnp.arange(prefix_len.shape[0]) == sequence, prefix_len, 0))

    core_pairs = [(t, t ^ 1) for t in range(tensor_size)]
    y_pairs = [(t, t ^ 2) for t in range(tensor_size)]
    x_pairs = [(d, d ^ 1) for d in range(dp_size)]

    def core_swap(value):
        return lax.ppermute(value, "tensor", core_pairs)

    def y_swap(value):
        return lax.ppermute(value, "tensor", y_pairs)

    def x_swap(value):
        return lax.ppermute(value, "dp", x_pairs)

    def plane_of(d):
        return (d % group) // 2

    def own_half(value):
        return lax.dynamic_slice_in_dim(value, core * half, half, 0)

    def other_half(value):
        return lax.dynamic_slice_in_dim(value, (1 - core) * half, half, 0)

    def join(mine, theirs):
        return jnp.where(
            core == 0, jnp.concatenate([mine, theirs], 0), jnp.concatenate([theirs, mine], 0)
        )

    def sum_tensor(left, right):
        away = dot(other_half(left), right).astype(BF16)
        came = core_swap(away)
        both = (dot(own_half(left), right) + came.astype(F32)).astype(BF16)
        return both.astype(F32) + y_swap(both).astype(F32)

    def columns_of(value, side):
        cut = value.reshape(value.shape[0], planes, 2, shard)
        return lax.dynamic_index_in_dim(cut, side, 2, keepdims=False).reshape(
            value.shape[0], planes * shard
        )

    def gather_columns(mine):
        came = x_swap(columns_of(mine, 1 - x_at))
        return join(came, core_swap(came))

    def scatter_z(stack):
        up_carry = stack(jnp.clip(planes - 1 + z_at, 0, planes - 1))
        down_carry = stack(jnp.clip(1 - planes + z_at, 0, planes - 1))
        for step in range(1, planes):
            up_pairs = [
                (2 * z + x, 2 * z + 2 + x) for z in range(planes - 1) for x in range(2) if z <= step - 1
            ]
            down_pairs = [
                (2 * (planes - 1 - z) + x, 2 * (planes - 2 - z) + x)
                for z in range(planes - 1)
                for x in range(2)
                if z <= step - 1
            ]
            up = lax.ppermute(up_carry, "dp", up_pairs)
            down = lax.ppermute(down_carry, "dp", down_pairs)
            if step < planes - 1:
                up_carry = up + stack(jnp.clip(planes - step - 1 + z_at, 0, planes - 1))
                down_carry = down + stack(jnp.clip(step + 1 - planes + z_at, 0, planes - 1))
        return stack(z_at).astype(F32) + up.astype(F32) + down.astype(F32)

    def scatter_rows(left_own, left_came, right_own, right_came):
        part = dot(left_own, right_own, TN) + dot(left_came, right_came, TN)
        part = part.astype(BF16)
        return scatter_z(lambda j: lax.dynamic_slice_in_dim(part, j * shard, shard, 0))

    def scatter_columns(left_own, left_came, right_own, right_came):
        part = dot(left_own, right_own, TN) + dot(left_came, right_came, TN)
        part = part.astype(BF16)
        return scatter_z(lambda j: lax.dynamic_slice_in_dim(part, j * shard, shard, 1))

    def sum_all(value, axes):
        for axis, bit in axes:
            size = dp_size if axis == "dp" else tensor_size
            value = value + lax.ppermute(value, axis, [(d, d ^ bit) for d in range(size)])
        return value

    dp_bits = []
    bit = 1
    while bit < dp_size:
        dp_bits.append(("dp", bit))
        bit *= 2

    positions = (member * rows + jnp.arange(rows)).astype(F32)
    counter = jnp.arange(width // 2, dtype=F32)
    angles = positions[:, None] * (ROPE_BASE ** (-2.0 * counter / width))[None, :]
    cos, sin = jnp.cos(angles), jnp.sin(angles)
    cos = jnp.concatenate([cos, cos], axis=1)
    sin = jnp.concatenate([-sin, sin], axis=1)
    norm_attn_row = norm_attn[None, :]
    norm_mlp_row = norm_mlp[None, :]
    q_gain_row = query_gain[None, :]
    k_gain_row = key_gain[None, :]

    h_one, kv, k_raw = project(
        tokens,
        norm_attn_row,
        (key_weight, value_weight),
        (k_gain_row, k_gain_row),
        (True, False),
        cos,
        sin,
        "project_kv",
    )
    later_pairs = [(d, d + 2) for d in range(dp_size) if plane_of(d) < group_planes - 1]
    to_first_pairs = [(d, d - 2) for d in range(dp_size) if plane_of(d) == 1]
    kv_own = [kv]
    came = kv
    for step in range(1, group_planes):
        came = lax.ppermute(came, "dp", later_pairs)
        kv_own.append(came)
    if group_planes > 1:
        kv_own[1] = kv_own[1] + lax.ppermute(kv, "dp", to_first_pairs)
    kv_far = [x_swap(b) for b in kv_own]
    scalars = []
    for step in range(group_planes):
        if step == 1:
            there = jnp.where(plane == 0, 1, plane - 1)
        else:
            there = plane - step
        mine = jnp.where(there >= 0, 2 * there + x_at, -1)
        far = jnp.where(there >= 0, 2 * there + 1 - x_at, -1)
        scalars.append(jnp.stack([member, prefix, mine, far]).astype(jnp.int32))

    _, q, q_raw = project(
        tokens, norm_attn_row, (w_query,), (q_gain_row,), (True,), cos, sin, "project_q"
    )
    d_hidden = dot(out_grad, w_down, NT)

    acc = None
    for step in range(group_planes):
        last = step == group_planes - 1
        outs = attn_fwd(scalars[step], q, [kv_own[step], kv_far[step]], acc, last, dims)
        acc = outs[0]
    heads_b, lse = outs

    x_half = own_half(tokens).astype(F32)
    middle = x_half + sum_tensor(heads_b, w_out)
    r_two, n_two = rms_parts(middle)
    h_two_half = (n_two * norm_mlp_row).astype(BF16)
    h_two = join(h_two_half, core_swap(h_two_half))
    gate_proj = dot(h_two, w_gate)
    up_proj = dot(h_two, w_up)
    sig = jax.nn.sigmoid(gate_proj)
    silu = gate_proj * sig
    hidden = (silu * up_proj).astype(BF16)
    d_gate = (d_hidden * up_proj * sig * (1.0 + gate_proj * (1.0 - sig))).astype(BF16)
    d_up = (d_hidden * silu).astype(BF16)

    def d_h_two_part(which):
        return dot(which(d_gate), w_gate, NT) + dot(which(d_up), w_up, NT)

    away = d_h_two_part(other_half).astype(BF16)
    both = (d_h_two_part(own_half) + core_swap(away).astype(F32)).astype(BF16)
    d_h_two = both.astype(F32) + y_swap(both).astype(F32)
    out_grad_half = own_half(out_grad)
    d_middle_half = out_grad_half.astype(F32) + rms_back(r_two, n_two, norm_mlp_row, d_h_two)
    norm_mlp_part = jnp.sum(d_h_two * n_two, axis=0)
    d_attn_half = d_middle_half.astype(BF16)
    d_attn = join(d_attn_half, core_swap(d_attn_half))
    d_heads = dot(d_attn, w_out, NT).astype(BF16)

    og_came = gather_columns(out_grad_half)
    hidden_came = x_swap(hidden)
    w_down_grad = scatter_columns(hidden, hidden_came, columns_of(out_grad, x_at), og_came)
    h_two_came = gather_columns(h_two_half)
    h_two_cols = columns_of(h_two, x_at)
    w_gate_grad = scatter_rows(h_two_cols, h_two_came, d_gate, x_swap(d_gate))
    w_up_grad = scatter_rows(h_two_cols, h_two_came, d_up, x_swap(d_up))

    mlp_out = sum_tensor(hidden, w_down)
    block_half = (middle + mlp_out).astype(BF16)
    block_out = join(block_half, core_swap(block_half))

    qx, dox = attn_prep(q, d_heads, heads_b, lse, width)
    dq = None
    sums = [None] * group_planes
    for step in reversed(range(group_planes)):
        dq, d_own, d_far = attn_bwd(
            scalars[step], qx, dox, [kv_own[step], kv_far[step]], dq, step == 0, dims
        )
        sums[step] = (d_own, x_swap(d_far))
    earlier_pairs = [(d, d - 2) for d in range(dp_size) if plane_of(d) > 0]
    from_first_pairs = [(d, d + 2) for d in range(dp_size) if plane_of(d) == 0]
    came = None
    for step in reversed(range(1, group_planes)):
        carry = sums[step][0].astype(F32) + sums[step][1].astype(F32)
        if came is not None:
            carry = carry + came.astype(F32)
        carry = carry.astype(BF16)
        pairs = [(a, b) for a, b in earlier_pairs if plane_of(a) >= step]
        came = lax.ppermute(carry, "dp", pairs)
    kv_grad = sums[0][0].astype(F32) + sums[0][1].astype(F32)
    if group_planes > 1:
        kv_grad = kv_grad + came.astype(F32) + lax.ppermute(carry, "dp", from_first_pairs).astype(F32)

    d_attn_came = gather_columns(d_attn_half)
    w_out_grad = scatter_columns(heads_b, x_swap(heads_b), columns_of(d_attn, x_at), d_attn_came)

    kv_width = kv_heads * width
    dq_b, q_gain_part = unproject(dq, q_raw, q_gain_row, cos, sin, 0, "unproject_q")
    dkv_b, k_gain_part = unproject(kv_grad, k_raw, k_gain_row, cos, sin, kv_width, "unproject_kv")
    h_one_came = gather_columns(own_half(h_one))
    h_one_cols = columns_of(h_one, x_at)
    w_query_grad = scatter_rows(h_one_cols, h_one_came, dq_b, x_swap(dq_b))
    w_kv_grad = scatter_rows(h_one_cols, h_one_came, dkv_b, x_swap(dkv_b))

    def d_h_one_part(which):
        dkv_rows = which(dkv_b)
        return (
            dot(which(dq_b), w_query, NT)
            + dot(dkv_rows[:, :kv_width], key_weight, NT)
            + dot(dkv_rows[:, kv_width:], value_weight, NT)
        )

    away = d_h_one_part(other_half)
    mine = d_h_one_part(own_half)
    x_other = other_half(tokens).astype(F32)
    r_own, n_own = rms_parts(x_half)
    r_other, n_other = rms_parts(x_other)
    norm_attn_part = jnp.sum(away * n_other + mine * n_own, axis=0)
    both = (mine + core_swap(away.astype(BF16)).astype(F32)).astype(BF16)
    d_h_one = (both.astype(F32) + y_swap(both).astype(F32)).astype(BF16)
    d_h_one_other = core_swap(d_h_one)
    d_middle_other = core_swap(d_middle_half)
    grad_own = d_middle_half + rms_back(r_own, n_own, norm_attn_row, d_h_one.astype(F32))
    grad_other = d_middle_other + rms_back(r_other, n_other, norm_attn_row, d_h_one_other.astype(F32))
    tokens_grad = join(grad_own, grad_other)

    norm_mlp_sum = sum_all(norm_mlp_part, [("tensor", 1)] + dp_bits)
    small = jnp.concatenate([norm_attn_part, q_gain_part[0], k_gain_part[0]])
    small = sum_all(small, [("tensor", 1), ("tensor", 2)] + dp_bits)
    norm_mlp_grad = lax.dynamic_slice_in_dim(norm_mlp_sum, device * shard, shard, 0)
    norm_attn_grad = lax.dynamic_slice_in_dim(small, device * shard, shard, 0)
    return (
        block_out,
        tokens_grad,
        norm_attn_grad,
        w_query_grad,
        w_kv_grad[:, :kv_width],
        w_kv_grad[:, kv_width:],
        small[model : model + width],
        small[model + width :],
        w_out_grad,
        norm_mlp_grad,
        w_gate_grad,
        w_up_grad,
        w_down_grad,
    )


def solution(mesh):
    placed = (
        P("dp", None),
        P(),
        P(None, "tensor"),
        P(None, "tensor"),
        P(None, "tensor"),
        P(),
        P(),
        P("tensor", None),
        P(),
        P(None, "tensor"),
        P(None, "tensor"),
        P("tensor", None),
        P("dp", None),
        P(),
    )
    return jax.shard_map(
        functools.partial(shards, mesh.shape["dp"], mesh.shape["tensor"]),
        mesh=mesh,
        in_specs=placed,
        out_specs=(
            P("dp", None),
            P("dp", None),
            P("dp"),
            P("dp", "tensor"),
            P("dp", "tensor"),
            P("dp", "tensor"),
            P(),
            P(),
            P("tensor", "dp"),
            P("dp"),
            P("dp", "tensor"),
            P("dp", "tensor"),
            P("tensor", "dp"),
        ),
        check_vma=False,
    )
```

```python
import functools
import math

import jax
import jax.numpy as jnp
from jax import lax
from jax.experimental import pallas as pl
from jax.experimental.pallas import tpu as pltpu
from jax.sharding import PartitionSpec as P

F32 = jnp.float32
BF16 = jnp.bfloat16
EPS = 1e-06
ROPE_BASE = 1000000.0
MAX_PREFIX = 2048
VMEM_LIMIT = 56 * 2**20

NN = (((1,), (0,)), ((), ()))
NT = (((1,), (1,)), ((), ()))
TN = (((0,), (0,)), ((), ()))


def dot(left, right, dims=NN):
    return lax.dot_general(left, right, dims, preferred_element_type=F32)


def vmem(count):
    return [pl.BlockSpec(memory_space=pltpu.VMEM)] * count


def params():
    return pltpu.CompilerParams(vmem_limit_bytes=VMEM_LIMIT)


def roll_half(value):
    return pltpu.roll(value, value.shape[-1] // 2, 1)


def project_kernel(x_ref, g_ref, *refs, heads, normed, width):
    count = len(heads)
    w_refs = refs[:count]
    gain_refs = refs[count : 2 * count]
    cos_ref, sin_ref = refs[2 * count : 2 * count + 2]
    h_ref, out_ref = refs[2 * count + 2 : 2 * count + 4]
    raw_refs = refs[2 * count + 4 :]
    x = x_ref[...].astype(F32)
    h = (x * lax.rsqrt(jnp.mean(x * x, axis=1, keepdims=True) + EPS) * g_ref[...]).astype(BF16)
    h_ref[...] = h
    cos, sin = cos_ref[...], sin_ref[...]
    column = 0
    raw_at = 0
    for i in range(count):
        product = dot(h, w_refs[i][...])
        if normed[i]:
            raw_refs[raw_at][...] = product
            raw_at += 1
        for j in range(heads[i]):
            u = product[:, j * width : (j + 1) * width]
            if normed[i]:
                u = u * lax.rsqrt(jnp.mean(u * u, axis=1, keepdims=True) + EPS) * gain_refs[i][...]
                u = u * cos + roll_half(u) * sin
            out_ref[:, column : column + width] = u.astype(BF16)
            column += width


def project(x, gain, weights, gains, normed, cos, sin, name):
    rows, model = x.shape
    width = cos.shape[1]
    heads = tuple(w.shape[1] // width for w in weights)
    columns = sum(w.shape[1] for w in weights)
    raws = [w for w, n in zip(weights, normed) if n]
    return pl.pallas_call(
        functools.partial(project_kernel, heads=heads, normed=normed, width=width),
        out_shape=[
            jax.ShapeDtypeStruct((rows, model), BF16),
            jax.ShapeDtypeStruct((rows, columns), BF16),
        ]
        + [jax.ShapeDtypeStruct((rows, w.shape[1]), F32) for w in raws],
        in_specs=vmem(4 + 2 * len(weights)),
        out_specs=vmem(2 + len(raws)),
        compiler_params=params(),
        cost_estimate=pl.CostEstimate(
            flops=2 * rows * model * columns,
            bytes_accessed=4 * rows * model + 2 * model * columns,
            transcendentals=0,
        ),
        name=name,
    )(x, gain, *weights, *gains, cos, sin)


def unproject_kernel(d_ref, raw_ref, gain_ref, cos_ref, sin_ref, out_ref, gain_out_ref, *, width, plain):
    columns = d_ref.shape[1]
    cos, sin = cos_ref[...], sin_ref[...]
    gain = gain_ref[...]
    total = jnp.zeros((1, width), F32)
    for at in range(0, columns - plain, width):
        d = d_ref[:, at : at + width].astype(F32)
        c = d * cos - roll_half(d) * sin
        v = raw_ref[:, at : at + width]
        r = lax.rsqrt(jnp.mean(v * v, axis=1, keepdims=True) + EPS)
        n = v * r
        total = total + jnp.sum(c * n, axis=0, keepdims=True)
        gc = gain * c
        out_ref[:, at : at + width] = (r * (gc - n * jnp.mean(n * gc, axis=1, keepdims=True))).astype(BF16)
    if plain:
        out_ref[:, columns - plain :] = d_ref[:, columns - plain :].astype(BF16)
    gain_out_ref[...] = total


def unproject(d, raw, gain, cos, sin, plain, name):
    rows, columns = d.shape
    width = cos.shape[1]
    return pl.pallas_call(
        functools.partial(unproject_kernel, width=width, plain=plain),
        out_shape=[jax.ShapeDtypeStruct((rows, columns), BF16), jax.ShapeDtypeStruct((1, width), F32)],
        in_specs=vmem(5),
        out_specs=vmem(2),
        compiler_params=params(),
        cost_estimate=pl.CostEstimate(
            flops=20 * rows * columns, bytes_accessed=10 * rows * columns, transcendentals=0
        ),
        name=name,
    )(d, raw, gain, cos, sin)


def block_flags(scalar_ref, slot, rows):
    member, prefix = scalar_ref[0], scalar_ref[1]
    other = scalar_ref[2 + slot]
    key0 = other * rows
    needed = (other >= 0) & ((other <= member) | (key0 < prefix))
    full = (other < member) | (key0 + rows <= prefix)
    return key0, needed, full


def visible(shape, key0, row0, prefix):
    key_pos = key0 + lax.broadcasted_iota(jnp.int32, shape, 1)
    row_pos = row0 + lax.broadcasted_iota(jnp.int32, shape, 0)
    return (key_pos <= row_pos) | (key_pos < prefix)


def attn_fwd_kernel(
    prefix_ref,
    q_ref,
    kv_ref,
    o_ref,
    lse_ref,
    all_ref,
    acc,
    send_x,
    recv_x,
    send_z,
    recv_z,
    send_down,
    *,
    group,
    kv_heads,
    repeat,
    width,
    tile,
    coef,
):
    rows = q_ref.shape[0]
    kv_width = kv_heads * width
    planes = group // 2
    device = lax.axis_index("dp")
    member = device % group
    plane = member // 2
    x_at = member % 2
    x_other = device + 1 - 2 * x_at
    inner = plane < planes - 1
    prefix = prefix_ref[0]

    barrier = pltpu.get_barrier_semaphore()
    pl.semaphore_signal(barrier, 1, device_id={"dp": x_other}, device_id_type=pl.DeviceIdType.MESH)

    @pl.when(inner)
    def _():
        pl.semaphore_signal(
            barrier, 1, device_id={"dp": device + 2}, device_id_type=pl.DeviceIdType.MESH
        )

    @pl.when(plane > 0)
    def _():
        pl.semaphore_signal(
            barrier, 1, device_id={"dp": device - 2}, device_id_type=pl.DeviceIdType.MESH
        )

    pl.semaphore_wait(barrier, 1 + inner.astype(jnp.int32) + (plane > 0).astype(jnp.int32))

    def source(slot):
        return kv_ref if slot == 0 else all_ref.at[2 * slot]

    def to_x(slot):
        return pltpu.make_async_remote_copy(
            src_ref=source(slot),
            dst_ref=all_ref.at[2 * slot + 1],
            send_sem=send_x.at[slot],
            recv_sem=recv_x.at[slot],
            device_id={"dp": x_other},
            device_id_type=pl.DeviceIdType.MESH,
        )

    def to_z(slot):
        return pltpu.make_async_remote_copy(
            src_ref=source(slot - 1),
            dst_ref=all_ref.at[2 * slot],
            send_sem=send_z.at[slot],
            recv_sem=recv_z.at[slot],
            device_id={"dp": device + 2},
            device_id_type=pl.DeviceIdType.MESH,
        )

    def to_first():
        return pltpu.make_async_remote_copy(
            src_ref=kv_ref,
            dst_ref=all_ref.at[2],
            send_sem=send_down,
            recv_sem=recv_z.at[1],
            device_id={"dp": device - 2},
            device_id_type=pl.DeviceIdType.MESH,
        )

    ones = jnp.ones((rows, width), BF16)
    row0 = member * rows

    def work(block, other, masked, start=False):
        key0 = other * rows

        def head_pair(h, carry):
            k = block[:, pl.ds(pl.multiple_of(h * width, width), width)]
            v = block[:, pl.ds(pl.multiple_of(kv_width + h * width, width), width)]
            v = jnp.concatenate([v, ones], axis=1)
            for g in range(repeat):
                head = h * repeat + g
                for at in range(0, rows, tile):
                    q = q_ref[at : at + tile, pl.ds(pl.multiple_of(head * width, width), width)]
                    p = jnp.exp2(dot(q, k, NT) * coef)
                    if masked:
                        p = jnp.where(visible(p.shape, key0, row0 + at, prefix), p, 0.0)
                    term = dot(p.astype(BF16), v)
                    if start:
                        acc[head, at : at + tile, :] = term
                    else:
                        acc[head, at : at + tile, :] += term
            return carry

        lax.fori_loop(0, kv_heads, head_pair, 0)

    to_x(0).start()
    if planes > 1:

        @pl.when(inner)
        def _():
            to_z(1).start()

        @pl.when(plane == 1)
        def _():
            to_first().start()

    work(kv_ref, member, True, True)
    to_x(0).wait_recv()
    work(all_ref.at[1], member + 1 - 2 * x_at, True)
    for slot in range(1, planes):

        def step(slot=slot):
            to_z(slot).wait_recv()
            if slot < planes - 1:

                @pl.when(inner & (plane >= slot))
                def _():
                    to_z(slot + 1).start()

            to_x(slot).start()
            there = 2 * (plane - slot)
            if slot == 1:

                @pl.when(plane == 0)
                def _():
                    work(all_ref.at[2 * slot], 2 + x_at, True)

                @pl.when(plane > 0)
                def _():
                    work(all_ref.at[2 * slot], there + x_at, False)
            else:
                work(all_ref.at[2 * slot], there + x_at, False)
            to_x(slot).wait_recv()
            if slot == 1:

                @pl.when(plane == 0)
                def _():
                    work(all_ref.at[2 * slot + 1], 3 - x_at, True)

                @pl.when(plane > 0)
                def _():
                    work(all_ref.at[2 * slot + 1], there + 1 - x_at, False)
            else:
                work(all_ref.at[2 * slot + 1], there + 1 - x_at, False)

        if slot == 1:
            step()
        else:
            pl.when(plane >= slot)(step)

    for head in range(kv_heads * repeat):
        total = acc[head, :, width:]
        o_ref[:, head * width : (head + 1) * width] = (acc[head, :, :width] / total).astype(BF16)
        lse_ref[:, head * width : (head + 1) * width] = jnp.log2(total) * (1.0 / coef)

    to_x(0).wait_send()
    for slot in range(1, planes):

        @pl.when(inner & (plane >= slot - 1))
        def _(slot=slot):
            to_z(slot).wait_send()

        @pl.when((plane >= slot) | (slot == 1))
        def _(slot=slot):
            to_x(slot).wait_send()

    if planes > 1:

        @pl.when(plane == 1)
        def _():
            to_first().wait_send()


def attn_fwd(prefix, q, kv, group, dims):
    kv_heads, repeat, width = dims
    rows = q.shape[0]
    heads = kv_heads * repeat
    columns = heads * width
    planes = group // 2
    return pl.pallas_call(
        functools.partial(
            attn_fwd_kernel,
            group=group,
            kv_heads=kv_heads,
            repeat=repeat,
            width=width,
            tile=min(rows, 256),
            coef=math.log2(math.e) / math.sqrt(width),
        ),
        out_shape=[
            jax.ShapeDtypeStruct((rows, columns), BF16),
            jax.ShapeDtypeStruct((rows, columns), F32),
            jax.ShapeDtypeStruct((group,) + kv.shape, BF16),
        ],
        in_specs=[pl.BlockSpec(memory_space=pltpu.SMEM)] + vmem(2),
        out_specs=vmem(3),
        scratch_shapes=[pltpu.VMEM((heads, rows, 2 * width), F32)]
        + [pltpu.SemaphoreType.DMA((planes,))] * 4
        + [pltpu.SemaphoreType.DMA],
        compiler_params=pltpu.CompilerParams(
            vmem_limit_bytes=VMEM_LIMIT, collective_id=0, has_side_effects=True
        ),
        cost_estimate=pl.CostEstimate(
            flops=group * 8 * rows * rows * columns,
            bytes_accessed=40 * rows * columns,
            transcendentals=group * rows * rows * heads,
        ),
        name="attn_fwd",
    )(prefix, q, kv)


def split_three(value):
    high = value.astype(BF16)
    left = value - high.astype(F32)
    mid = left.astype(BF16)
    return high.astype(F32), mid.astype(F32), (left - mid.astype(F32)).astype(BF16).astype(F32)


def attn_prep_kernel(core_ref, own_ref, far_ref, w_ref, q_ref, o_ref, lse_ref, qx_ref, dox_ref, *, heads, width):
    half = own_ref.shape[0]
    core = core_ref[0]
    lane = lax.broadcasted_iota(jnp.int32, (half, width), 1)

    def extra(value):
        a, b, c = split_three(value)
        return jnp.where(lane == 0, a, jnp.where(lane == 1, b, jnp.where(lane == 2, c, 0.0))).astype(BF16)

    for ref, at_core in ((own_ref, core), (far_ref, 1 - core)):
        at_rows = pl.ds(pl.multiple_of(at_core * half, half), half)
        d_heads = dot(ref[...], w_ref[...], NT)
        for head in range(heads):
            at = slice(head * width, (head + 1) * width)
            qx_ref[head, at_rows, :width] = q_ref[at_rows, at]
            qx_ref[head, at_rows, width:] = extra(lse_ref[at_rows, at])
            d = d_heads[:, at].astype(BF16)
            delta = jnp.sum(d.astype(F32) * o_ref[at_rows, at].astype(F32), axis=1, keepdims=True)
            dox_ref[head, at_rows, :width] = d
            dox_ref[head, at_rows, width:] = extra(jnp.broadcast_to(delta, (half, width)))


def attn_prep(core, d_own, d_far, w_out, q, out, lse, width):
    rows, columns = q.shape
    heads = columns // width
    return pl.pallas_call(
        functools.partial(attn_prep_kernel, heads=heads, width=width),
        out_shape=[jax.ShapeDtypeStruct((heads, rows, 2 * width), BF16)] * 2,
        in_specs=[pl.BlockSpec(memory_space=pltpu.SMEM)] + vmem(6),
        out_specs=vmem(2),
        compiler_params=params(),
        cost_estimate=pl.CostEstimate(
            flops=2 * rows * columns * w_out.shape[1],
            bytes_accessed=14 * rows * columns,
            transcendentals=0,
        ),
        name="attn_prep",
    )(core, d_own, d_far, w_out, q, out, lse)


def attn_bwd_kernel(scalar_ref, qx_ref, dox_ref, *refs, slots, kv_heads, repeat, width, coef, scale, first, last):
    kv_refs = refs[:slots]
    rest = refs[slots:]
    if not first:
        dq_in, rest = rest[0], rest[1:]
    dq_ref = rest[0]
    dkv_refs = rest[1:]
    rows = qx_ref.shape[1]
    kv_width = kv_heads * width
    if first:
        dq_ref[...] = jnp.zeros_like(dq_ref)
    else:
        dq_ref[...] = dq_in[...]
    lane = lax.broadcasted_iota(jnp.int32, (rows, width), 1)
    minus = jnp.where(lane < 3, -1.0, 0.0).astype(BF16)
    row0 = scalar_ref[0] * rows
    prefix = scalar_ref[1]
    for slot in range(slots):
        key0, needed, full = block_flags(scalar_ref, slot, rows)

        def work(masked, slot=slot, key0=key0):
            for h in range(kv_heads):
                k_at = slice(h * width, (h + 1) * width)
                v_at = slice(kv_width + h * width, kv_width + (h + 1) * width)
                k = kv_refs[slot][:, k_at]
                v = kv_refs[slot][:, v_at]
                kx = jnp.concatenate([k, minus], axis=1)
                vx = jnp.concatenate([v, minus], axis=1)
                dk = jnp.zeros((rows, width), F32)
                dv = jnp.zeros((rows, width), F32)
                for g in range(repeat):
                    head = h * repeat + g
                    qx = qx_ref[head]
                    dox = dox_ref[head]
                    p = jnp.exp2(dot(qx, kx, NT) * coef)
                    if masked:
                        p = jnp.where(visible(p.shape, key0, row0, prefix), p, 0.0)
                    ds = (p * dot(dox, vx, NT)).astype(BF16)
                    dv += dot(p.astype(BF16), dox[:, :width], TN)
                    dk += dot(ds, qx[:, :width], TN)
                    dq_ref[:, head * width : (head + 1) * width] += dot(ds, k)
                dkv_refs[slot][:, k_at] = (dk * scale).astype(BF16)
                dkv_refs[slot][:, v_at] = dv.astype(BF16)

        pl.when(needed & full)(functools.partial(work, False))
        pl.when(needed & jnp.logical_not(full))(functools.partial(work, True))

        @pl.when(jnp.logical_not(needed))
        def _(slot=slot):
            dkv_refs[slot][...] = jnp.zeros_like(dkv_refs[slot])

    if last:
        dq_ref[...] = dq_ref[...] * scale


def attn_bwd(scalars, qx, dox, stack, at, dq, last, dims):
    kv_heads, repeat, width = dims
    rows = qx.shape[1]
    columns = kv_heads * repeat * width
    first = dq is None
    slots = len(at)
    args = [scalars, qx, dox] + [stack] * slots + ([] if first else [dq])
    block = stack.shape[1:]
    out_shape = [jax.ShapeDtypeStruct((rows, columns), F32)] + [jax.ShapeDtypeStruct(block, BF16)] * slots
    picks = [pl.BlockSpec((None,) + block, lambda i, j=j: (j, 0, 0)) for j in at]
    return pl.pallas_call(
        functools.partial(
            attn_bwd_kernel,
            slots=slots,
            kv_heads=kv_heads,
            repeat=repeat,
            width=width,
            coef=math.log2(math.e) / math.sqrt(width),
            scale=1.0 / math.sqrt(width),
            first=first,
            last=last,
        ),
        out_shape=out_shape,
        grid=(1,),
        in_specs=[pl.BlockSpec(memory_space=pltpu.SMEM)] + vmem(2) + picks + vmem(0 if first else 1),
        out_specs=vmem(len(out_shape)),
        compiler_params=params(),
        cost_estimate=pl.CostEstimate(
            flops=slots * 20 * rows * rows * columns,
            bytes_accessed=16 * rows * columns,
            transcendentals=slots * rows * rows * kv_heads * repeat,
        ),
        name="attn_bwd",
    )(*args)


def smem():
    return pl.BlockSpec(memory_space=pltpu.SMEM)


def cut_kernel(at_ref, *refs, halves, planes, shard):
    x_at, core = at_ref[0], at_ref[1]
    keep_ref, send_ref = refs[-2:]
    half = send_ref.shape[0]
    for z in range(planes):
        to = slice(z * shard, (z + 1) * shard)
        keep = pl.ds(pl.multiple_of((2 * z + x_at) * shard, shard), shard)
        send = pl.ds(pl.multiple_of((2 * z + 1 - x_at) * shard, shard), shard)
        if halves:
            own_ref, far_ref = refs[:2]
            keep_ref[pl.ds(pl.multiple_of(core * half, half), half), to] = own_ref[:, keep]
            keep_ref[pl.ds(pl.multiple_of((1 - core) * half, half), half), to] = far_ref[:, keep]
            send_ref[:, to] = own_ref[:, send]
        else:
            keep_ref[:, to] = refs[0][:, keep]
            send_ref[:, to] = refs[0][pl.ds(pl.multiple_of(core * half, half), half), send]


def cut(x_at, core, parts, planes, shard, join):
    halves = len(parts) == 2
    half = parts[0].shape[0] // (1 if halves else 2)
    if shard % 128:
        whole = join(*parts) if halves else parts[0]
        own = parts[0] if halves else lax.dynamic_slice_in_dim(whole, core * half, half, 0)

        def columns(value, side):
            view = value.reshape(value.shape[0], planes, 2, shard)
            return lax.dynamic_index_in_dim(view, side, 2, keepdims=False).reshape(
                value.shape[0], planes * shard
            )

        return columns(whole, x_at), columns(own, 1 - x_at)
    return pl.pallas_call(
        functools.partial(cut_kernel, halves=halves, planes=planes, shard=shard),
        out_shape=[
            jax.ShapeDtypeStruct((2 * half, planes * shard), BF16),
            jax.ShapeDtypeStruct((half, planes * shard), BF16),
        ],
        in_specs=[smem()] + vmem(len(parts)),
        out_specs=vmem(2),
        compiler_params=params(),
        cost_estimate=pl.CostEstimate(
            flops=0, bytes_accessed=10 * half * planes * shard, transcendentals=0
        ),
        name="cut",
    )(jnp.stack([x_at, core]).astype(jnp.int32), *parts)


def norm_kernel(core_ref, both_ref, y_ref, x_ref, gain_ref, middle_ref, h_ref):
    half = both_ref.shape[0]
    x = x_ref[pl.ds(pl.multiple_of(core_ref[0] * half, half), half), :].astype(F32)
    middle = x + both_ref[...].astype(F32) + y_ref[...].astype(F32)
    middle_ref[...] = middle
    r = lax.rsqrt(jnp.mean(middle * middle, axis=1, keepdims=True) + EPS)
    h_ref[...] = (middle * r * gain_ref[...]).astype(BF16)


def norm_forward(core, both, came, x, gain):
    return pl.pallas_call(
        norm_kernel,
        out_shape=[jax.ShapeDtypeStruct(both.shape, F32), jax.ShapeDtypeStruct(both.shape, BF16)],
        in_specs=[smem()] + vmem(4),
        out_specs=vmem(2),
        compiler_params=params(),
        cost_estimate=pl.CostEstimate(
            flops=10 * both.size, bytes_accessed=14 * both.size, transcendentals=0
        ),
        name="norm_forward",
    )(core, both, came, x, gain)


def norm_back_kernel(core_ref, both_ref, y_ref, middle_ref, add_ref, gain_ref, d_ref, d_low_ref, gain_out_ref):
    half = both_ref.shape[0]
    c = both_ref[...].astype(F32) + y_ref[...].astype(F32)
    v = middle_ref[...]
    r = lax.rsqrt(jnp.mean(v * v, axis=1, keepdims=True) + EPS)
    n = v * r
    gain_out_ref[...] = jnp.sum(c * n, axis=0, keepdims=True)
    gc = c * gain_ref[...]
    d = r * (gc - n * jnp.mean(n * gc, axis=1, keepdims=True))
    d = d + add_ref[pl.ds(pl.multiple_of(core_ref[0] * half, half), half), :].astype(F32)
    d_ref[...] = d
    d_low_ref[...] = d.astype(BF16)


def norm_back(core, both, came, middle, add, gain):
    return pl.pallas_call(
        norm_back_kernel,
        out_shape=[
            jax.ShapeDtypeStruct(both.shape, F32),
            jax.ShapeDtypeStruct(both.shape, BF16),
            jax.ShapeDtypeStruct((1, both.shape[1]), F32),
        ],
        in_specs=[smem()] + vmem(5),
        out_specs=vmem(3),
        compiler_params=params(),
        cost_estimate=pl.CostEstimate(
            flops=20 * both.size, bytes_accessed=18 * both.size, transcendentals=0
        ),
        name="norm_back",
    )(core, both, came, middle, add, gain)


def mlp_kernel(core_ref, own_ref, far_ref, gate_ref, up_ref, d_ref, hidden_ref, d_gate_ref, d_up_ref):
    half = own_ref.shape[0]
    core = core_ref[0]
    for ref, at_core in ((own_ref, core), (far_ref, 1 - core)):
        at = pl.ds(pl.multiple_of(at_core * half, half), half)
        gate = dot(ref[...], gate_ref[...])
        up = dot(ref[...], up_ref[...])
        sig = 1.0 / (1.0 + jnp.exp(-gate))
        silu = gate * sig
        d = d_ref[at, :]
        hidden_ref[at, :] = (silu * up).astype(BF16)
        d_up_ref[at, :] = (d * silu).astype(BF16)
        d_gate_ref[at, :] = (d * up * (sig * (1.0 + gate * (1.0 - sig)))).astype(BF16)


def mlp(core, own, far, w_gate, w_up, d_hidden):
    half, model = own.shape
    units = w_gate.shape[1]
    tile = math.gcd(units, 256)
    rows_spec = pl.BlockSpec((half, model), lambda i: (0, 0))
    weight_spec = pl.BlockSpec((model, tile), lambda i: (0, i))
    unit_spec = pl.BlockSpec((2 * half, tile), lambda i: (0, i))
    return pl.pallas_call(
        mlp_kernel,
        out_shape=[jax.ShapeDtypeStruct((2 * half, units), BF16)] * 3,
        grid=(units // tile,),
        in_specs=[smem(), rows_spec, rows_spec, weight_spec, weight_spec, unit_spec],
        out_specs=[unit_spec] * 3,
        compiler_params=params(),
        cost_estimate=pl.CostEstimate(
            flops=8 * half * model * units,
            bytes_accessed=4 * model * units + 20 * half * units,
            transcendentals=2 * half * units,
        ),
        name="mlp",
    )(core, own, far, w_gate, w_up, d_hidden)


def pair_kernel(core_ref, gate_ref, up_ref, w_gate_ref, w_up_ref, *refs):
    half = gate_ref.shape[0] // 2
    at = pl.ds(pl.multiple_of(core_ref[0] * half, half), half)
    total = dot(gate_ref[at, :], w_gate_ref[...], NT) + dot(up_ref[at, :], w_up_ref[...], NT)
    if len(refs) == 2:
        total = total + refs[0][...].astype(F32)
    refs[-1][...] = total.astype(BF16)


def pair(core, d_gate, d_up, w_gate, w_up, add):
    rows, units = d_gate.shape
    model = w_gate.shape[0]
    tile = math.gcd(model, 256)
    all_spec = pl.BlockSpec((rows, units), lambda i: (0, 0))
    weight_spec = pl.BlockSpec((tile, units), lambda i: (i, 0))
    out_spec = pl.BlockSpec((rows // 2, tile), lambda i: (0, i))
    return pl.pallas_call(
        pair_kernel,
        out_shape=jax.ShapeDtypeStruct((rows // 2, model), BF16),
        grid=(model // tile,),
        in_specs=[smem(), all_spec, all_spec, weight_spec, weight_spec] + [out_spec] * len(add),
        out_specs=out_spec,
        compiler_params=params(),
        cost_estimate=pl.CostEstimate(
            flops=2 * rows * units * model, bytes_accessed=4 * model * units, transcendentals=0
        ),
        name="pair",
    )(core, d_gate, d_up, w_gate, w_up, *add)


def rms_parts(value):
    r = lax.rsqrt(jnp.mean(value * value, axis=-1, keepdims=True) + EPS)
    return r, value * r


def rms_back(r, n, gain, c):
    gc = gain * c
    return r * (gc - n * jnp.mean(n * gc, axis=-1, keepdims=True))


def shards(
    dp_size,
    tensor_size,
    tokens,
    norm_attn,
    w_query,
    key_weight,
    value_weight,
    query_gain,
    key_gain,
    w_out,
    norm_mlp,
    w_gate,
    w_up,
    w_down,
    out_grad,
    prefix_len,
):
    rows, model = tokens.shape
    width = query_gain.shape[0]
    kv_heads = key_weight.shape[1] // width
    repeat = w_query.shape[1] // key_weight.shape[1]
    dims = (kv_heads, repeat, width)
    group = dp_size // prefix_len.shape[0]
    planes = dp_size // 2
    group_planes = group // 2
    half = rows // 2
    shard = model // dp_size
    assert tensor_size == 4 and MAX_PREFIX <= 4 * rows

    device = lax.axis_index("dp")
    core = lax.axis_index("tensor") % 2
    x_at = device % 2
    z_at = device // 2
    sequence = device // group
    member = device % group
    plane = member // 2
    prefix = jnp.sum(jnp.where(jnp.arange(prefix_len.shape[0]) == sequence, prefix_len, 0))

    core_pairs = [(t, t ^ 1) for t in range(tensor_size)]
    y_pairs = [(t, t ^ 2) for t in range(tensor_size)]
    x_pairs = [(d, d ^ 1) for d in range(dp_size)]

    def core_swap(value):
        return lax.ppermute(value, "tensor", core_pairs)

    def y_swap(value):
        return lax.ppermute(value, "tensor", y_pairs)

    def x_swap(value):
        return lax.ppermute(value, "dp", x_pairs)

    def plane_of(d):
        return (d % group) // 2

    def own_half(value):
        return lax.dynamic_slice_in_dim(value, core * half, half, 0)

    def other_half(value):
        return lax.dynamic_slice_in_dim(value, (1 - core) * half, half, 0)

    def join(mine, theirs):
        return jnp.where(
            core == 0, jnp.concatenate([mine, theirs], 0), jnp.concatenate([theirs, mine], 0)
        )

    def sum_tensor(left, right):
        away = dot(other_half(left), right).astype(BF16)
        came = core_swap(away)
        both = (dot(own_half(left), right) + came.astype(F32)).astype(BF16)
        return both, y_swap(both)

    def cut_columns(*parts):
        keep, send = cut(x_at, core, parts, planes, shard, join)
        came = x_swap(send)
        return keep, join(came, core_swap(came))

    def scatter_z(stack):
        up_carry = stack(jnp.clip(planes - 1 + z_at, 0, planes - 1))
        down_carry = stack(jnp.clip(1 - planes + z_at, 0, planes - 1))
        for step in range(1, planes):
            up_pairs = [
                (2 * z + x, 2 * z + 2 + x) for z in range(planes - 1) for x in range(2) if z <= step - 1
            ]
            down_pairs = [
                (2 * (planes - 1 - z) + x, 2 * (planes - 2 - z) + x)
                for z in range(planes - 1)
                for x in range(2)
                if z <= step - 1
            ]
            up = lax.ppermute(up_carry, "dp", up_pairs)
            down = lax.ppermute(down_carry, "dp", down_pairs)
            if step < planes - 1:
                up_carry = up + stack(jnp.clip(planes - step - 1 + z_at, 0, planes - 1))
                down_carry = down + stack(jnp.clip(step + 1 - planes + z_at, 0, planes - 1))
        return stack(z_at).astype(F32) + up.astype(F32) + down.astype(F32)

    def scatter_rows(left_own, left_came, right_own, right_came):
        part = dot(left_own, right_own, TN) + dot(left_came, right_came, TN)
        part = part.astype(BF16)
        return scatter_z(lambda j: lax.dynamic_slice_in_dim(part, j * shard, shard, 0))

    def scatter_columns(left_own, left_came, right_own, right_came):
        part = dot(left_own, right_own, TN) + dot(left_came, right_came, TN)
        part = part.astype(BF16)
        return scatter_z(lambda j: lax.dynamic_slice_in_dim(part, j * shard, shard, 1))

    def sum_all(value, axes):
        for axis, bit in axes:
            size = dp_size if axis == "dp" else tensor_size
            value = value + lax.ppermute(value, axis, [(d, d ^ bit) for d in range(size)])
        return value

    dp_bits = []
    bit = 1
    while bit < dp_size:
        dp_bits.append(("dp", bit))
        bit *= 2

    positions = (member * rows + jnp.arange(rows)).astype(F32)
    counter = jnp.arange(width // 2, dtype=F32)
    angles = positions[:, None] * (ROPE_BASE ** (-2.0 * counter / width))[None, :]
    cos, sin = jnp.cos(angles), jnp.sin(angles)
    cos = jnp.concatenate([cos, cos], axis=1)
    sin = jnp.concatenate([-sin, sin], axis=1)
    norm_attn_row = norm_attn[None, :]
    norm_mlp_row = norm_mlp[None, :]
    q_gain_row = query_gain[None, :]
    k_gain_row = key_gain[None, :]

    core_at = core[None].astype(jnp.int32)
    core_not = 1 - core_at
    h_one, qkv, q_raw, k_raw = project(
        tokens,
        norm_attn_row,
        (w_query, key_weight, value_weight),
        (q_gain_row, k_gain_row, k_gain_row),
        (True, True, False),
        cos,
        sin,
        "project",
    )
    q = qkv[:, : w_query.shape[1]]
    kv = qkv[:, w_query.shape[1] :]
    heads_b, lse, kv_all = attn_fwd(prefix[None].astype(jnp.int32), q, kv, group, dims)
    kv_all = lax.dynamic_update_slice(kv_all, kv[None], (0, 0, 0))
    scalars = []
    for step in range(group_planes):
        if step == 1:
            there = jnp.where(plane == 0, 1, plane - 1)
        else:
            there = plane - step
        mine = jnp.where(there >= 0, 2 * there + x_at, -1)
        far = jnp.where(there >= 0, 2 * there + 1 - x_at, -1)
        scalars.append(jnp.stack([member, prefix, mine, far]).astype(jnp.int32))

    both, came = sum_tensor(heads_b, w_out)
    d_hidden = dot(out_grad, w_down, NT)
    og_cols, og_came = cut_columns(out_grad)
    h_one_cols, h_one_came = cut_columns(h_one)
    middle, h_two_half = norm_forward(core_at, both, came, tokens, norm_mlp_row)
    h_two_far = core_swap(h_two_half)
    hidden, d_gate, d_up = mlp(core_at, h_two_half, h_two_far, w_gate, w_up, d_hidden)

    away = pair(core_not, d_gate, d_up, w_gate, w_up, [])
    both = pair(core_at, d_gate, d_up, w_gate, w_up, [core_swap(away)])
    came = y_swap(both)
    d_middle_half, d_attn_half, norm_mlp_part = norm_back(
        core_at, both, came, middle, out_grad, norm_mlp_row
    )
    d_attn_far = core_swap(d_attn_half)

    hidden_came = x_swap(hidden)
    w_down_grad = scatter_columns(hidden, hidden_came, og_cols, og_came)
    h_two_cols, h_two_came = cut_columns(h_two_half, h_two_far)
    w_gate_grad = scatter_rows(h_two_cols, h_two_came, d_gate, x_swap(d_gate))
    w_up_grad = scatter_rows(h_two_cols, h_two_came, d_up, x_swap(d_up))

    both, came = sum_tensor(hidden, w_down)
    block_half = (middle + (both.astype(F32) + came.astype(F32))).astype(BF16)
    block_out = join(block_half, core_swap(block_half))

    qx, dox = attn_prep(core_at, d_attn_half, d_attn_far, w_out, q, heads_b, lse, width)
    dq = None
    sums = [None] * group_planes
    for step in reversed(range(group_planes)):
        dq, d_own, d_far = attn_bwd(
            scalars[step], qx, dox, kv_all, (2 * step, 2 * step + 1), dq, step == 0, dims
        )
        sums[step] = (d_own, x_swap(d_far))
    earlier_pairs = [(d, d - 2) for d in range(dp_size) if plane_of(d) > 0]
    from_first_pairs = [(d, d + 2) for d in range(dp_size) if plane_of(d) == 0]
    came = None
    for step in reversed(range(1, group_planes)):
        carry = sums[step][0].astype(F32) + sums[step][1].astype(F32)
        if came is not None:
            carry = carry + came.astype(F32)
        carry = carry.astype(BF16)
        pairs = [(a, b) for a, b in earlier_pairs if plane_of(a) >= step]
        came = lax.ppermute(carry, "dp", pairs)
    kv_grad = sums[0][0].astype(F32) + sums[0][1].astype(F32)
    if group_planes > 1:
        kv_grad = kv_grad + came.astype(F32) + lax.ppermute(carry, "dp", from_first_pairs).astype(F32)

    d_attn_cols, d_attn_came = cut_columns(d_attn_half, d_attn_far)
    w_out_grad = scatter_columns(heads_b, x_swap(heads_b), d_attn_cols, d_attn_came)

    kv_width = kv_heads * width
    dq_b, q_gain_part = unproject(dq, q_raw, q_gain_row, cos, sin, 0, "unproject_q")
    dkv_b, k_gain_part = unproject(kv_grad, k_raw, k_gain_row, cos, sin, kv_width, "unproject_kv")
    w_query_grad = scatter_rows(h_one_cols, h_one_came, dq_b, x_swap(dq_b))
    w_kv_grad = scatter_rows(h_one_cols, h_one_came, dkv_b, x_swap(dkv_b))

    def d_h_one_part(which):
        dkv_rows = which(dkv_b)
        return (
            dot(which(dq_b), w_query, NT)
            + dot(dkv_rows[:, :kv_width], key_weight, NT)
            + dot(dkv_rows[:, kv_width:], value_weight, NT)
        )

    away = d_h_one_part(other_half)
    mine = d_h_one_part(own_half)
    x_half = own_half(tokens).astype(F32)
    x_other = other_half(tokens).astype(F32)
    r_own, n_own = rms_parts(x_half)
    r_other, n_other = rms_parts(x_other)
    norm_attn_part = jnp.sum(away * n_other + mine * n_own, axis=0)
    both = (mine + core_swap(away.astype(BF16)).astype(F32)).astype(BF16)
    d_h_one = (both.astype(F32) + y_swap(both).astype(F32)).astype(BF16)
    d_h_one_other = core_swap(d_h_one)
    d_middle_other = core_swap(d_middle_half)
    grad_own = d_middle_half + rms_back(r_own, n_own, norm_attn_row, d_h_one.astype(F32))
    grad_other = d_middle_other + rms_back(r_other, n_other, norm_attn_row, d_h_one_other.astype(F32))
    tokens_grad = join(grad_own, grad_other)

    norm_mlp_sum = sum_all(norm_mlp_part[0], [("tensor", 1)] + dp_bits)
    small = jnp.concatenate([norm_attn_part, q_gain_part[0], k_gain_part[0]])
    small = sum_all(small, [("tensor", 1), ("tensor", 2)] + dp_bits)
    norm_mlp_grad = lax.dynamic_slice_in_dim(norm_mlp_sum, device * shard, shard, 0)
    norm_attn_grad = lax.dynamic_slice_in_dim(small, device * shard, shard, 0)
    return (
        block_out,
        tokens_grad,
        norm_attn_grad,
        w_query_grad,
        w_kv_grad[:, :kv_width],
        w_kv_grad[:, kv_width:],
        small[model : model + width],
        small[model + width :],
        w_out_grad,
        norm_mlp_grad,
        w_gate_grad,
        w_up_grad,
        w_down_grad,
    )


def solution(mesh):
    placed = (
        P("dp", None),
        P(),
        P(None, "tensor"),
        P(None, "tensor"),
        P(None, "tensor"),
        P(),
        P(),
        P("tensor", None),
        P(),
        P(None, "tensor"),
        P(None, "tensor"),
        P("tensor", None),
        P("dp", None),
        P(),
    )
    return jax.shard_map(
        functools.partial(shards, mesh.shape["dp"], mesh.shape["tensor"]),
        mesh=mesh,
        in_specs=placed,
        out_specs=(
            P("dp", None),
            P("dp", None),
            P("dp"),
            P("dp", "tensor"),
            P("dp", "tensor"),
            P("dp", "tensor"),
            P(),
            P(),
            P("tensor", "dp"),
            P("dp"),
            P("dp", "tensor"),
            P("dp", "tensor"),
            P("tensor", "dp"),
        ),
        check_vma=False,
    )
```

```python
import functools
import math

import jax
import jax.numpy as jnp
from jax import lax
from jax.experimental import pallas as pl
from jax.experimental.pallas import tpu as pltpu
from jax.sharding import PartitionSpec as P

F32 = jnp.float32
BF16 = jnp.bfloat16
EPS = 1e-06
ROPE_BASE = 1000000.0
MAX_PREFIX = 2048
VMEM_LIMIT = 56 * 2**20
BACK_VMEM_LIMIT = 60 * 2**20

COST = pl.CostEstimate(flops=1000, bytes_accessed=1000, transcendentals=0)

NN = (((1,), (0,)), ((), ()))
NT = (((1,), (1,)), ((), ()))
TN = (((0,), (0,)), ((), ()))


def dot(left, right, dims=NN):
    return lax.dot_general(left, right, dims, preferred_element_type=F32)


def vmem(count):
    return [pl.BlockSpec(memory_space=pltpu.VMEM)] * count


def params():
    return pltpu.CompilerParams(vmem_limit_bytes=VMEM_LIMIT)


def greet(peers):
    barrier = pltpu.get_barrier_semaphore()
    count = 0
    for peer, there in peers:

        def signal(peer=peer):
            pl.semaphore_signal(barrier, 1, device_id=peer, device_id_type=pl.DeviceIdType.MESH)

        if there is True:
            signal()
            count = count + 1
        else:
            pl.when(there)(signal)
            count = count + there.astype(jnp.int32)
    pl.semaphore_wait(barrier, count)


def remote(src, dst, send, recv, peer):
    return pltpu.make_async_remote_copy(
        src_ref=src,
        dst_ref=dst,
        send_sem=send,
        recv_sem=recv,
        device_id=peer,
        device_id_type=pl.DeviceIdType.MESH,
    )


def tensor_peers():
    t = lax.axis_index("tensor")
    core = t % 2
    y = t // 2
    return core, {"tensor": t + 1 - 2 * core}, {"tensor": t + 2 - 4 * y}


def rows_of(core, half):
    return pl.ds(pl.multiple_of(core * half, half), half)


def cut_into(out, out_rows, ref, ref_rows, side, planes, shard):
    for z in range(planes):
        to = slice(z * shard, (z + 1) * shard)
        if shard % 128 == 0:
            at = pl.ds(pl.multiple_of((2 * z + side) * shard, shard), shard)
            out[out_rows, to] = ref[ref_rows, at]
        else:
            low = ref[ref_rows, 2 * z * shard : (2 * z + 1) * shard]
            high = ref[ref_rows, (2 * z + 1) * shard : (2 * z + 2) * shard]
            out[out_rows, to] = jnp.where(side == 0, low, high)


class Columns:
    def __init__(self, own, far, keep, came, scratch, x_at, core, x_peer, core_peer, planes, shard):
        self.own, self.far, self.keep, self.came = own, far, keep, came
        self.send_ref, self.recv_ref, self.sems = scratch[0], scratch[1], scratch[2:]
        self.x_at, self.core, self.cut = x_at, core, (planes, shard)
        self.x_peer, self.core_peer = x_peer, core_peer
        self.half = own.shape[0]

    @staticmethod
    def scratch(half, columns):
        return [pltpu.VMEM((half, columns), BF16)] * 2 + [pltpu.SemaphoreType.DMA] * 4

    def over_x(self):
        return remote(self.send_ref, self.recv_ref, self.sems[0], self.sems[1], self.x_peer)

    def over_core(self):
        there = self.came.at[rows_of(self.core, self.half), :]
        return remote(self.recv_ref, there, self.sems[2], self.sems[3], self.core_peer)

    def start(self):
        every = slice(None)
        cut_into(self.send_ref, every, self.own, every, 1 - self.x_at, *self.cut)
        self.over_x().start()

    def store(self):
        every = slice(None)
        for ref, core in ((self.own, self.core), (self.far, 1 - self.core)):
            cut_into(self.keep, rows_of(core, self.half), ref, every, self.x_at, *self.cut)

    def forward(self):
        self.over_x().wait_recv()
        self.over_core().start()
        self.came[rows_of(self.core, self.half), :] = self.recv_ref[...]

    def finish(self):
        self.over_core().wait_recv()
        self.over_x().wait_send()
        self.over_core().wait_send()


class TensorSum:
    def __init__(self, scratch, core, core_peer, y_peer):
        (self.away, self.core_came, self.both, self.y_came, self.mine) = scratch[:5]
        self.sems = scratch[5:]
        self.core, self.core_peer, self.y_peer = core, core_peer, y_peer
        self.chunks, self.half, self.width = self.away.shape

    @staticmethod
    def scratch(chunks, half, width):
        return (
            [pltpu.VMEM((chunks, half, width), BF16)] * 4
            + [pltpu.VMEM((2, 2 * half, width), F32)]
            + [pltpu.SemaphoreType.DMA((chunks,))] * 4
        )

    def over_core(self, i):
        s = self.sems
        return remote(self.away.at[i], self.core_came.at[i], s[0].at[i], s[1].at[i], self.core_peer)

    def over_y(self, i):
        s = self.sems
        return remote(self.both.at[i], self.y_came.at[i], s[2].at[i], s[3].at[i], self.y_peer)

    def add(self, i, value):
        self.mine[i % 2] = value
        self.away[i] = self.mine[i % 2, rows_of(1 - self.core, self.half), :].astype(BF16)
        self.over_core(i).start()
        if i > 0:
            self.pass_on(i - 1)
        if i == self.chunks - 1:
            self.pass_on(i)

    def pass_on(self, i):
        self.over_core(i).wait_recv()
        mine = self.mine[i % 2, rows_of(self.core, self.half), :]
        self.both[i] = (mine + self.core_came[i].astype(F32)).astype(BF16)
        self.over_y(i).start()

    def total(self, i):
        self.over_y(i).wait_recv()
        return self.both[i].astype(F32) + self.y_came[i].astype(F32)

    def finish(self):
        for i in range(self.chunks):
            self.over_core(i).wait_send()
            self.over_y(i).wait_send()


def roll_half(value):
    return pltpu.roll(value, value.shape[-1] // 2, 1)


def project_kernel(x_ref, g_ref, *refs, heads, normed, width):
    count = len(heads)
    w_refs = refs[:count]
    gain_refs = refs[count : 2 * count]
    cos_ref, sin_ref = refs[2 * count : 2 * count + 2]
    h_ref, out_ref = refs[2 * count + 2 : 2 * count + 4]
    raw_refs = refs[2 * count + 4 :]
    x = x_ref[...].astype(F32)
    h = (x * lax.rsqrt(jnp.mean(x * x, axis=1, keepdims=True) + EPS) * g_ref[...]).astype(BF16)
    h_ref[...] = h
    cos, sin = cos_ref[...], sin_ref[...]
    column = 0
    raw_at = 0
    for i in range(count):
        product = dot(h, w_refs[i][...])
        if normed[i]:
            raw_refs[raw_at][...] = product
            raw_at += 1
        for j in range(heads[i]):
            u = product[:, j * width : (j + 1) * width]
            if normed[i]:
                u = u * lax.rsqrt(jnp.mean(u * u, axis=1, keepdims=True) + EPS) * gain_refs[i][...]
                u = u * cos + roll_half(u) * sin
            out_ref[:, column : column + width] = u.astype(BF16)
            column += width


def project(x, gain, weights, gains, normed, cos, sin, name):
    rows, model = x.shape
    width = cos.shape[1]
    heads = tuple(w.shape[1] // width for w in weights)
    columns = sum(w.shape[1] for w in weights)
    raws = [w for w, n in zip(weights, normed) if n]
    return pl.pallas_call(
        functools.partial(project_kernel, heads=heads, normed=normed, width=width),
        out_shape=[
            jax.ShapeDtypeStruct((rows, model), BF16),
            jax.ShapeDtypeStruct((rows, columns), BF16),
        ]
        + [jax.ShapeDtypeStruct((rows, w.shape[1]), F32) for w in raws],
        in_specs=vmem(4 + 2 * len(weights)),
        out_specs=vmem(2 + len(raws)),
        compiler_params=params(),
        cost_estimate=COST,
        name=name,
    )(x, gain, *weights, *gains, cos, sin)


def unproject_kernel(d_ref, raw_ref, gain_ref, cos_ref, sin_ref, out_ref, gain_out_ref, *, width, plain):
    columns = d_ref.shape[1]
    cos, sin = cos_ref[...], sin_ref[...]
    gain = gain_ref[...]
    total = jnp.zeros((1, width), F32)
    for at in range(0, columns - plain, width):
        d = d_ref[:, at : at + width].astype(F32)
        c = d * cos - roll_half(d) * sin
        v = raw_ref[:, at : at + width]
        r = lax.rsqrt(jnp.mean(v * v, axis=1, keepdims=True) + EPS)
        n = v * r
        total = total + jnp.sum(c * n, axis=0, keepdims=True)
        gc = gain * c
        out_ref[:, at : at + width] = (r * (gc - n * jnp.mean(n * gc, axis=1, keepdims=True))).astype(BF16)
    if plain:
        out_ref[:, columns - plain :] = d_ref[:, columns - plain :].astype(BF16)
    gain_out_ref[...] = total


def unproject(d, raw, gain, cos, sin, plain, name):
    rows, columns = d.shape
    width = cos.shape[1]
    return pl.pallas_call(
        functools.partial(unproject_kernel, width=width, plain=plain),
        out_shape=[jax.ShapeDtypeStruct((rows, columns), BF16), jax.ShapeDtypeStruct((1, width), F32)],
        in_specs=vmem(5),
        out_specs=vmem(2),
        compiler_params=params(),
        cost_estimate=COST,
        name=name,
    )(d, raw, gain, cos, sin)


def visible(shape, key0, row0, prefix):
    key_pos = key0 + lax.broadcasted_iota(jnp.int32, shape, 1)
    row_pos = row0 + lax.broadcasted_iota(jnp.int32, shape, 0)
    return (key_pos <= row_pos) | (key_pos < prefix)


def attn_fwd_kernel(
    prefix_ref,
    q_ref,
    kv_ref,
    o_ref,
    lse_ref,
    all_ref,
    acc,
    send_x,
    recv_x,
    send_z,
    recv_z,
    send_down,
    *,
    group,
    kv_heads,
    repeat,
    width,
    tile,
    coef,
):
    rows = q_ref.shape[0]
    kv_width = kv_heads * width
    planes = group // 2
    device = lax.axis_index("dp")
    member = device % group
    plane = member // 2
    x_at = member % 2
    x_other = device + 1 - 2 * x_at
    inner = plane < planes - 1
    prefix = prefix_ref[0]

    barrier = pltpu.get_barrier_semaphore()
    pl.semaphore_signal(barrier, 1, device_id={"dp": x_other}, device_id_type=pl.DeviceIdType.MESH)

    @pl.when(inner)
    def _():
        pl.semaphore_signal(
            barrier, 1, device_id={"dp": device + 2}, device_id_type=pl.DeviceIdType.MESH
        )

    @pl.when(plane > 0)
    def _():
        pl.semaphore_signal(
            barrier, 1, device_id={"dp": device - 2}, device_id_type=pl.DeviceIdType.MESH
        )

    pl.semaphore_wait(barrier, 1 + inner.astype(jnp.int32) + (plane > 0).astype(jnp.int32))

    def source(slot):
        return kv_ref if slot == 0 else all_ref.at[2 * slot]

    def to_x(slot):
        return pltpu.make_async_remote_copy(
            src_ref=source(slot),
            dst_ref=all_ref.at[2 * slot + 1],
            send_sem=send_x.at[slot],
            recv_sem=recv_x.at[slot],
            device_id={"dp": x_other},
            device_id_type=pl.DeviceIdType.MESH,
        )

    def to_z(slot):
        return pltpu.make_async_remote_copy(
            src_ref=source(slot - 1),
            dst_ref=all_ref.at[2 * slot],
            send_sem=send_z.at[slot],
            recv_sem=recv_z.at[slot],
            device_id={"dp": device + 2},
            device_id_type=pl.DeviceIdType.MESH,
        )

    def to_first():
        return pltpu.make_async_remote_copy(
            src_ref=kv_ref,
            dst_ref=all_ref.at[2],
            send_sem=send_down,
            recv_sem=recv_z.at[1],
            device_id={"dp": device - 2},
            device_id_type=pl.DeviceIdType.MESH,
        )

    all_ref[0] = kv_ref[...]
    ones = jnp.ones((rows, width), BF16)
    row0 = member * rows

    def work(block, other, masked, start=False):
        key0 = other * rows

        def head_pair(h, carry):
            k = block[:, pl.ds(pl.multiple_of(h * width, width), width)]
            v = block[:, pl.ds(pl.multiple_of(kv_width + h * width, width), width)]
            v = jnp.concatenate([v, ones], axis=1)
            for g in range(repeat):
                head = h * repeat + g
                for at in range(0, rows, tile):
                    q = q_ref[at : at + tile, pl.ds(pl.multiple_of(head * width, width), width)]
                    p = jnp.exp2(dot(q, k, NT) * coef)
                    if masked:
                        p = jnp.where(visible(p.shape, key0, row0 + at, prefix), p, 0.0)
                    term = dot(p.astype(BF16), v)
                    if start:
                        acc[head, at : at + tile, :] = term
                    else:
                        acc[head, at : at + tile, :] += term
            return carry

        lax.fori_loop(0, kv_heads, head_pair, 0)

    to_x(0).start()
    if planes > 1:

        @pl.when(inner)
        def _():
            to_z(1).start()

        @pl.when(plane == 1)
        def _():
            to_first().start()

    work(kv_ref, member, True, True)
    to_x(0).wait_recv()
    work(all_ref.at[1], member + 1 - 2 * x_at, True)
    for slot in range(1, planes):

        def step(slot=slot):
            to_z(slot).wait_recv()
            if slot < planes - 1:

                @pl.when(inner & (plane >= slot))
                def _():
                    to_z(slot + 1).start()

            to_x(slot).start()
            there = 2 * (plane - slot)
            if slot == 1:

                @pl.when(plane == 0)
                def _():
                    work(all_ref.at[2 * slot], 2 + x_at, True)

                @pl.when(plane > 0)
                def _():
                    work(all_ref.at[2 * slot], there + x_at, False)
            else:
                work(all_ref.at[2 * slot], there + x_at, False)
            to_x(slot).wait_recv()
            if slot == 1:

                @pl.when(plane == 0)
                def _():
                    work(all_ref.at[2 * slot + 1], 3 - x_at, True)

                @pl.when(plane > 0)
                def _():
                    work(all_ref.at[2 * slot + 1], there + 1 - x_at, False)
            else:
                work(all_ref.at[2 * slot + 1], there + 1 - x_at, False)

        if slot == 1:
            step()
        else:
            pl.when(plane >= slot)(step)

    for head in range(kv_heads * repeat):
        total = acc[head, :, width:]
        o_ref[:, head * width : (head + 1) * width] = (acc[head, :, :width] / total).astype(BF16)
        lse_ref[:, head * width : (head + 1) * width] = jnp.log2(total) * (1.0 / coef)

    to_x(0).wait_send()
    for slot in range(1, planes):

        @pl.when(inner & (plane >= slot - 1))
        def _(slot=slot):
            to_z(slot).wait_send()

        @pl.when((plane >= slot) | (slot == 1))
        def _(slot=slot):
            to_x(slot).wait_send()

    if planes > 1:

        @pl.when(plane == 1)
        def _():
            to_first().wait_send()


def attn_fwd(prefix, q, kv, group, dims):
    kv_heads, repeat, width = dims
    rows = q.shape[0]
    heads = kv_heads * repeat
    columns = heads * width
    planes = group // 2
    return pl.pallas_call(
        functools.partial(
            attn_fwd_kernel,
            group=group,
            kv_heads=kv_heads,
            repeat=repeat,
            width=width,
            tile=min(rows, 256),
            coef=math.log2(math.e) / math.sqrt(width),
        ),
        out_shape=[
            jax.ShapeDtypeStruct((rows, columns), BF16),
            jax.ShapeDtypeStruct((rows, columns), F32),
            jax.ShapeDtypeStruct((group,) + kv.shape, BF16),
        ],
        in_specs=[pl.BlockSpec(memory_space=pltpu.SMEM)] + vmem(2),
        out_specs=vmem(3),
        scratch_shapes=[pltpu.VMEM((heads, rows, 2 * width), F32)]
        + [pltpu.SemaphoreType.DMA((planes,))] * 4
        + [pltpu.SemaphoreType.DMA],
        compiler_params=pltpu.CompilerParams(
            vmem_limit_bytes=VMEM_LIMIT, collective_id=0, has_side_effects=True
        ),
        cost_estimate=COST,
        name="attn_fwd",
    )(prefix, q, kv)


def split_three(value):
    high = value.astype(BF16)
    left = value - high.astype(F32)
    mid = left.astype(BF16)
    return high.astype(F32), mid.astype(F32), (left - mid.astype(F32)).astype(BF16).astype(F32)


def attn_prep_kernel(core_ref, own_ref, far_ref, w_ref, q_ref, o_ref, lse_ref, qx_ref, dox_ref, *, heads, width):
    half = own_ref.shape[0]
    core = core_ref[0]
    lane = lax.broadcasted_iota(jnp.int32, (half, width), 1)

    def extra(value):
        a, b, c = split_three(value)
        return jnp.where(lane == 0, a, jnp.where(lane == 1, b, jnp.where(lane == 2, c, 0.0))).astype(BF16)

    for ref, at_core in ((own_ref, core), (far_ref, 1 - core)):
        at_rows = pl.ds(pl.multiple_of(at_core * half, half), half)
        d_heads = dot(ref[...], w_ref[...], NT)
        for head in range(heads):
            at = slice(head * width, (head + 1) * width)
            qx_ref[head, at_rows, :width] = q_ref[at_rows, at]
            qx_ref[head, at_rows, width:] = extra(lse_ref[at_rows, at])
            d = d_heads[:, at].astype(BF16)
            delta = jnp.sum(d.astype(F32) * o_ref[at_rows, at].astype(F32), axis=1, keepdims=True)
            dox_ref[head, at_rows, :width] = d
            dox_ref[head, at_rows, width:] = extra(jnp.broadcast_to(delta, (half, width)))


def attn_prep(core, d_own, d_far, w_out, q, out, lse, width):
    rows, columns = q.shape
    heads = columns // width
    return pl.pallas_call(
        functools.partial(attn_prep_kernel, heads=heads, width=width),
        out_shape=[jax.ShapeDtypeStruct((heads, rows, 2 * width), BF16)] * 2,
        in_specs=[pl.BlockSpec(memory_space=pltpu.SMEM)] + vmem(6),
        out_specs=vmem(2),
        compiler_params=params(),
        cost_estimate=COST,
        name="attn_prep",
    )(core, d_own, d_far, w_out, q, out, lse)


def back_kernel(
    *refs, group, planes, all_planes, shard, kv_heads, repeat, width, coef, scale, sums
):
    refs = list(refs)

    def take(count):
        out = refs[:count]
        del refs[:count]
        return out

    prefix_ref, qx_ref, dox_ref, kv_ref = take(4)
    h_own_ref, h_far_ref, a_own_ref, a_far_ref, heads_ref, up_ref = take(6)
    if sums:
        hid_ref, hid_came_ref, og_ref, og_came_ref, gate_ref = take(5)
    dq_ref, grad_ref, h_ref, h_came_ref, a_ref, a_came_ref, heads_came_ref, up_came_ref = take(8)
    if sums:
        w_down_ref, w_gate_ref, w_out_ref = take(3)
    own_ref, far_ref, xr_ref, zr_ref, first_ref = take(5)
    send_x, recv_x, send_z, recv_z, send_first, recv_first = take(6)
    swap_sems = take(4)
    h_scratch, a_scratch = take(6), take(6)
    if sums:
        gate_came_ref, send_gate, recv_gate = take(3)
        down_sum, gate_sum, out_sum = take(6), take(6), take(6)

    rows = qx_ref.shape[1]
    kv_width = kv_heads * width
    device = lax.axis_index("dp")
    member = device % group
    plane = member // 2
    last = planes - 1
    x_at = member % 2
    x_other = device + 1 - 2 * x_at
    inner = plane < last
    prefix = prefix_ref[0]

    core, core_peer, _ = tensor_peers()
    x_peer = {"dp": x_other}
    greet(
        [(x_peer, True), (core_peer, True), ({"dp": device + 2}, inner), ({"dp": device - 2}, plane > 0)]
    )

    def copy(src, dst, send, recv, there):
        return remote(src, dst, send, recv, {"dp": there})

    def columns(own, far, keep, came, scratch):
        return Columns(
            own, far, keep, came, scratch, x_at, core, x_peer, core_peer, all_planes, shard
        )

    h_two = columns(h_own_ref, h_far_ref, h_ref, h_came_ref, h_scratch)
    d_attn = columns(a_own_ref, a_far_ref, a_ref, a_came_ref, a_scratch)
    heads_swap = copy(heads_ref, heads_came_ref, swap_sems[0], swap_sems[1], x_other)
    up_swap = copy(up_ref, up_came_ref, swap_sems[2], swap_sems[3], x_other)

    def up(parts, j):
        stack, came, send_up, recv_up = parts[:4]
        return copy(stack.at[j], came.at[j], send_up.at[j], recv_up.at[j], device + 2)

    def down(parts, j):
        stack, came, _, _, send_down, recv_down = parts
        slot = jnp.where(plane - 1 == j, planes, j)
        return copy(stack.at[j], came.at[slot], send_down.at[j], recv_down.at[j], device - 2)

    def sum_start(parts):
        @pl.when(plane == 0)
        def _():
            for j in range(last, 0, -1):
                up(parts, j).start()

        @pl.when(plane == last)
        def _():
            for j in range(last):
                down(parts, j).start()

    def sum_wave(parts, wave):
        stack, came = parts[:2]
        j = last - wave
        i = wave

        @pl.when((plane > 0) & (plane < j))
        def _():
            up(parts, j).wait_recv()
            stack[j] += came[j]
            up(parts, j).start()

        @pl.when((plane < last) & (plane > i))
        def _():
            down(parts, i).wait_recv()
            stack[i] += came[i]
            down(parts, i).start()

    def sum_finish(parts, out):
        stack, came = parts[:2]
        out[...] = stack[plane].astype(F32)

        @pl.when(plane > 0)
        def _():
            up(parts, plane).wait_recv()
            out[...] += came[plane].astype(F32)

        @pl.when(plane < last)
        def _():
            down(parts, plane).wait_recv()
            out[...] += came[planes].astype(F32)

        for j in range(planes):
            pl.when(plane < j)(lambda j=j: up(parts, j).wait_send())
            pl.when(plane > j)(lambda j=j: down(parts, j).wait_send())

    def gate_swap():
        return copy(gate_ref, gate_came_ref, send_gate, recv_gate, x_other)

    def column_terms(stack, left, left_came, right, right_came):
        tile = 256

        def body(t, carry):
            at = pl.ds(pl.multiple_of(t * tile, tile), tile)
            term = dot(left[:, at], right[...], TN) + dot(left_came[:, at], right_came[...], TN)
            for j in range(planes):
                stack[j, at, :] = term[:, j * shard : (j + 1) * shard].astype(BF16)
            return carry

        lax.fori_loop(0, left.shape[1] // tile, body, 0)

    def down_terms():
        column_terms(down_sum[0], hid_ref, hid_came_ref, og_ref, og_came_ref)

    def out_terms():
        column_terms(out_sum[0], heads_ref, heads_came_ref, a_ref, a_came_ref)

    def gate_terms():
        stack = gate_sum[0]

        def body(j, carry):
            at = pl.ds(pl.multiple_of(j * shard, shard), shard)
            stack[j] = (
                dot(h_ref[:, at], gate_ref[...], TN) + dot(h_came_ref[:, at], gate_came_ref[...], TN)
            ).astype(BF16)
            return carry

        lax.fori_loop(0, planes, body, 0)

    lane = lax.broadcasted_iota(jnp.int32, (rows, width), 1)
    minus = jnp.where(lane < 3, -1.0, 0.0).astype(BF16)
    row0 = member * rows

    def work(block, other, masked, out):
        key0 = other * rows

        def head_group(h, carry):
            k_at = pl.ds(pl.multiple_of(h * width, width), width)
            v_at = pl.ds(pl.multiple_of(kv_width + h * width, width), width)
            k = kv_ref[block, :, k_at]
            v = kv_ref[block, :, v_at]
            kx = jnp.concatenate([k, minus], axis=1)
            vx = jnp.concatenate([v, minus], axis=1)
            dk = jnp.zeros((rows, width), F32)
            dv = jnp.zeros((rows, width), F32)
            for g in range(repeat):
                head = h * repeat + g
                qx = qx_ref[head]
                dox = dox_ref[head]
                p = jnp.exp2(dot(qx, kx, NT) * coef)
                if masked:
                    p = jnp.where(visible(p.shape, key0, row0, prefix), p, 0.0)
                ds = (p * dot(dox, vx, NT)).astype(BF16)
                dv += dot(p.astype(BF16), dox[:, :width], TN)
                dk += dot(ds, qx[:, :width], TN)
                dq_ref[:, pl.ds(pl.multiple_of(head * width, width), width)] += dot(ds, k)
            out[:, k_at] = (dk * scale).astype(BF16)
            out[:, v_at] = dv.astype(BF16)
            return carry

        lax.fori_loop(0, kv_heads, head_group, 0)

    def far_swap(slot):
        return copy(far_ref.at[slot], xr_ref.at[slot], send_x.at[slot], recv_x.at[slot], x_other)

    def to_plane(slot):
        return copy(own_ref.at[slot], zr_ref.at[slot], send_z.at[slot], recv_z.at[slot], device - 2)

    def from_first():
        return copy(own_ref.at[1], first_ref, send_first, recv_first, device + 2)

    def attend(slot):
        there = 2 * (plane - slot)
        far, own = there + 1 - x_at, there + x_at

        def both(far, own, masked):
            work(2 * slot + 1, far, masked, far_ref.at[slot])
            far_swap(slot).start()
            work(2 * slot, own, masked, own_ref.at[slot])

        if slot == 0:
            both(far, own, True)
        elif slot == 1:
            pl.when(plane == 0)(lambda: both(3 - x_at, 2 + x_at, True))
            pl.when(plane > 0)(lambda: both(far, own, False))
        else:
            pl.when(plane >= slot)(lambda: both(far, own, False))

    def pass_back(slot):
        def go():
            far_swap(slot).wait_recv()
            own_ref[slot] += xr_ref[slot]
            if slot < last:

                @pl.when(inner & (plane >= slot))
                def _():
                    to_plane(slot + 1).wait_recv()
                    own_ref[slot] += zr_ref[slot + 1]

            if slot == 1:
                pl.when(plane == 0)(lambda: from_first().start())
                pl.when(plane > 0)(lambda: to_plane(slot).start())
            else:
                to_plane(slot).start()

        if slot == 1:
            go()
        else:
            pl.when(plane >= slot)(go)

    dq_ref[...] = jnp.zeros_like(dq_ref)
    if sums:
        gate_swap().start()
        down_terms()
        sum_start(down_sum)
    h_two.start()
    h_two.store()
    d_attn.store()
    pending = list(range(last, 0, -1))
    waves = list(range(max(last - 1, 0)))
    for count, slot in enumerate(range(last, -1, -1)):
        attend(slot)
        if sums and count >= 1 and count - 1 < len(waves):
            sum_wave(down_sum, waves[count - 1])
        if count >= 1 and slot >= 1:
            pass_back(pending.pop(0))
        if slot == min(1, last):
            h_two.forward()
            d_attn.start()
            heads_swap.start()
            if sums:
                gate_swap().wait_recv()
                h_two.over_core().wait_recv()
                gate_terms()
                sum_start(gate_sum)
    up_swap.start()
    while pending:
        pass_back(pending.pop(0))
    dq_ref[...] = dq_ref[...] * scale
    d_attn.forward()
    heads_swap.wait_recv()
    d_attn.over_core().wait_recv()
    if sums:
        out_terms()
        sum_start(out_sum)
        for wave in waves:
            sum_wave(gate_sum, wave)
        for wave in waves:
            sum_wave(out_sum, wave)

    far_swap(0).wait_recv()
    grad_ref[...] = own_ref[0].astype(F32) + xr_ref[0].astype(F32)
    if last > 0:

        @pl.when(inner)
        def _():
            to_plane(1).wait_recv()
            grad_ref[...] += zr_ref[1].astype(F32)

        @pl.when(plane == 1)
        def _():
            from_first().wait_recv()
            grad_ref[...] += first_ref[...].astype(F32)

    if sums:
        sum_finish(down_sum, w_down_ref)
        sum_finish(gate_sum, w_gate_ref)
        sum_finish(out_sum, w_out_ref)
        gate_swap().wait_send()
    up_swap.wait_recv()
    up_swap.wait_send()
    heads_swap.wait_send()
    for part in (h_two, d_attn):
        part.over_x().wait_send()
        part.over_core().wait_send()
    if not sums:
        h_two.over_core().wait_recv()
    for slot in range(planes):
        if slot <= 1:
            far_swap(slot).wait_send()
        else:
            pl.when(plane >= slot)(lambda slot=slot: far_swap(slot).wait_send())
        if slot >= 1:
            pl.when(plane >= slot)(lambda slot=slot: to_plane(slot).wait_send())
    if last > 0:
        pl.when(plane == 0)(lambda: from_first().wait_send())


def back(prefix, qx, dox, kv_all, shared, grads, group, all_planes, shard, dims):
    kv_heads, repeat, width = dims
    rows = qx.shape[1]
    columns = kv_heads * repeat * width
    planes = group // 2
    block = kv_all.shape[1:]
    dma = pltpu.SemaphoreType.DMA
    heads, d_up = shared[4:]
    units = d_up.shape[1]
    cut_shape = jax.ShapeDtypeStruct((rows, all_planes * shard), BF16)
    out_shape = [jax.ShapeDtypeStruct((rows, columns), F32), jax.ShapeDtypeStruct(block, F32)]
    out_shape += [cut_shape] * 4
    out_shape += [jax.ShapeDtypeStruct(heads.shape, BF16), jax.ShapeDtypeStruct(d_up.shape, BF16)]
    scratch = [pltpu.VMEM((planes,) + block, BF16)] * 4 + [pltpu.VMEM(block, BF16)]
    scratch += [dma((planes,))] * 4 + [dma, dma] + [dma] * 4
    scratch += Columns.scratch(rows // 2, all_planes * shard) * 2
    args = [prefix, qx, dox, kv_all, *shared]
    if grads is not None:
        args += grads
        shapes = (units, shard), (shard, units), (heads.shape[1], shard)
        out_shape += [jax.ShapeDtypeStruct(s, F32) for s in shapes]
        scratch += [pltpu.VMEM((rows, units), BF16), dma, dma]
        for shape in shapes:
            scratch += [pltpu.VMEM((n,) + shape, BF16) for n in (planes, planes + 1)]
            scratch += [dma((planes,))] * 4
    return pl.pallas_call(
        functools.partial(
            back_kernel,
            group=group,
            planes=planes,
            all_planes=all_planes,
            shard=shard,
            kv_heads=kv_heads,
            repeat=repeat,
            width=width,
            coef=math.log2(math.e) / math.sqrt(width),
            scale=1.0 / math.sqrt(width),
            sums=grads is not None,
        ),
        out_shape=out_shape,
        in_specs=[smem()] + vmem(8) + [pl.BlockSpec(memory_space=pl.ANY)] + vmem(len(args) - 10),
        out_specs=vmem(7) + [pl.BlockSpec(memory_space=pl.ANY)] + vmem(len(out_shape) - 8),
        scratch_shapes=scratch,
        compiler_params=pltpu.CompilerParams(
            vmem_limit_bytes=BACK_VMEM_LIMIT, collective_id=1, has_side_effects=True
        ),
        cost_estimate=COST,
        name="back",
    )(*args)


def smem():
    return pl.BlockSpec(memory_space=pltpu.SMEM)


def cut_kernel(at_ref, *refs, halves, planes, shard):
    x_at, core = at_ref[0], at_ref[1]
    keep_ref, send_ref = refs[-2:]
    half = send_ref.shape[0]
    for z in range(planes):
        to = slice(z * shard, (z + 1) * shard)
        keep = pl.ds(pl.multiple_of((2 * z + x_at) * shard, shard), shard)
        send = pl.ds(pl.multiple_of((2 * z + 1 - x_at) * shard, shard), shard)
        if halves:
            own_ref, far_ref = refs[:2]
            keep_ref[pl.ds(pl.multiple_of(core * half, half), half), to] = own_ref[:, keep]
            keep_ref[pl.ds(pl.multiple_of((1 - core) * half, half), half), to] = far_ref[:, keep]
            send_ref[:, to] = own_ref[:, send]
        else:
            keep_ref[:, to] = refs[0][:, keep]
            send_ref[:, to] = refs[0][pl.ds(pl.multiple_of(core * half, half), half), send]


def cut(x_at, core, parts, planes, shard, join):
    halves = len(parts) == 2
    half = parts[0].shape[0] // (1 if halves else 2)
    if shard % 128:
        whole = join(*parts) if halves else parts[0]
        own = parts[0] if halves else lax.dynamic_slice_in_dim(whole, core * half, half, 0)

        def columns(value, side):
            view = value.reshape(value.shape[0], planes, 2, shard)
            return lax.dynamic_index_in_dim(view, side, 2, keepdims=False).reshape(
                value.shape[0], planes * shard
            )

        return columns(whole, x_at), columns(own, 1 - x_at)
    return pl.pallas_call(
        functools.partial(cut_kernel, halves=halves, planes=planes, shard=shard),
        out_shape=[
            jax.ShapeDtypeStruct((2 * half, planes * shard), BF16),
            jax.ShapeDtypeStruct((half, planes * shard), BF16),
        ],
        in_specs=[smem()] + vmem(len(parts)),
        out_specs=vmem(2),
        compiler_params=params(),
        cost_estimate=COST,
        name="cut",
    )(jnp.stack([x_at, core]).astype(jnp.int32), *parts)


def norm_kernel(core_ref, both_ref, y_ref, x_ref, gain_ref, middle_ref, h_ref):
    half = both_ref.shape[0]
    x = x_ref[pl.ds(pl.multiple_of(core_ref[0] * half, half), half), :].astype(F32)
    middle = x + both_ref[...].astype(F32) + y_ref[...].astype(F32)
    middle_ref[...] = middle
    r = lax.rsqrt(jnp.mean(middle * middle, axis=1, keepdims=True) + EPS)
    h_ref[...] = (middle * r * gain_ref[...]).astype(BF16)


def norm_forward(core, both, came, x, gain):
    return pl.pallas_call(
        norm_kernel,
        out_shape=[jax.ShapeDtypeStruct(both.shape, F32), jax.ShapeDtypeStruct(both.shape, BF16)],
        in_specs=[smem()] + vmem(4),
        out_specs=vmem(2),
        compiler_params=params(),
        cost_estimate=COST,
        name="norm_forward",
    )(core, both, came, x, gain)


def mlp_kernel(core_ref, own_ref, far_ref, gate_ref, up_ref, d_ref, hidden_ref, d_gate_ref, d_up_ref):
    half = own_ref.shape[0]
    core = core_ref[0]
    for ref, at_core in ((own_ref, core), (far_ref, 1 - core)):
        at = pl.ds(pl.multiple_of(at_core * half, half), half)
        gate = dot(ref[...], gate_ref[...])
        up = dot(ref[...], up_ref[...])
        sig = 1.0 / (1.0 + jnp.exp(-gate))
        silu = gate * sig
        d = d_ref[at, :]
        hidden_ref[at, :] = (silu * up).astype(BF16)
        d_up_ref[at, :] = (d * silu).astype(BF16)
        d_gate_ref[at, :] = (d * up * (sig * (1.0 + gate * (1.0 - sig)))).astype(BF16)


def mlp(core, own, far, w_gate, w_up, d_hidden):
    half, model = own.shape
    units = w_gate.shape[1]
    tile = math.gcd(units, 256)
    rows_spec = pl.BlockSpec((half, model), lambda i: (0, 0))
    weight_spec = pl.BlockSpec((model, tile), lambda i: (0, i))
    unit_spec = pl.BlockSpec((2 * half, tile), lambda i: (0, i))
    return pl.pallas_call(
        mlp_kernel,
        out_shape=[jax.ShapeDtypeStruct((2 * half, units), BF16)] * 3,
        grid=(units // tile,),
        in_specs=[smem(), rows_spec, rows_spec, weight_spec, weight_spec, unit_spec],
        out_specs=[unit_spec] * 3,
        compiler_params=params(),
        cost_estimate=COST,
        name="mlp",
    )(core, own, far, w_gate, w_up, d_hidden)


def d_middle_kernel(
    hid_ref,
    d_gate_ref,
    d_up_ref,
    w_gate_ref,
    w_up_ref,
    middle_ref,
    add_ref,
    gain_ref,
    hid_came_ref,
    d_ref,
    own_ref,
    far_ref,
    gain_out_ref,
    gate_buf,
    up_buf,
    load_sems,
    c_ref,
    hid_send,
    hid_recv,
    far_send,
    far_recv,
    *scratch,
    blocks,
):
    device = lax.axis_index("dp")
    core, core_peer, y_peer = tensor_peers()
    x_peer = {"dp": device + 1 - 2 * (device % 2)}
    half = middle_ref.shape[0]
    total = TensorSum(scratch, core, core_peer, y_peer)
    chunks, width = total.chunks, total.width

    def loads(i):
        at = pl.ds(i * width, width)
        return (
            pltpu.make_async_copy(w_gate_ref.at[at, :], gate_buf.at[i], load_sems.at[2 * i]),
            pltpu.make_async_copy(w_up_ref.at[at, :], up_buf.at[i], load_sems.at[2 * i + 1]),
        )

    for i in range(chunks):
        for load in loads(i):
            load.start()
    greet([(x_peer, True), (core_peer, True), (y_peer, True)])
    swap = remote(hid_ref, hid_came_ref, hid_send, hid_recv, x_peer)
    swap.start()
    for i in range(chunks):
        for load in loads(i):
            load.wait()
        total.add(i, dot(d_gate_ref[...], gate_buf[i], NT) + dot(d_up_ref[...], up_buf[i], NT))
    for i in range(chunks):
        c_ref[:, i * width : (i + 1) * width] = total.total(i)

    step = half // blocks

    def to_core(b):
        at = slice(b * step, (b + 1) * step)
        return remote(own_ref.at[at, :], far_ref.at[at, :], far_send.at[b], far_recv.at[b], core_peer)

    gain_out_ref[...] = jnp.zeros_like(gain_out_ref)
    for b in range(blocks):
        at = slice(b * step, (b + 1) * step)
        add_at = pl.ds(pl.multiple_of(core * half + b * step, step), step)
        c = c_ref[at, :]
        v = middle_ref[at, :]
        r = lax.rsqrt(jnp.mean(v * v, axis=1, keepdims=True) + EPS)
        n = v * r
        gain_out_ref[...] += jnp.sum(c * n, axis=0, keepdims=True)
        gc = c * gain_ref[...]
        d = r * (gc - n * jnp.mean(n * gc, axis=1, keepdims=True)) + add_ref[add_at, :].astype(F32)
        d_ref[at, :] = d
        own_ref[at, :] = d.astype(BF16)
        to_core(b).start()
    for b in range(blocks):
        to_core(b).wait_recv()
        to_core(b).wait_send()
    total.finish()
    swap.wait_recv()
    swap.wait_send()


def d_middle_of(hidden, d_gate, d_up, w_gate, w_up, middle, out_grad, gain):
    half, model = middle.shape
    units = hidden.shape[1]
    chunks, blocks = 4, 4
    width = model // chunks
    dma = pltpu.SemaphoreType.DMA
    anywhere = pl.BlockSpec(memory_space=pl.ANY)
    return pl.pallas_call(
        functools.partial(d_middle_kernel, blocks=blocks),
        out_shape=[
            jax.ShapeDtypeStruct(hidden.shape, BF16),
            jax.ShapeDtypeStruct((half, model), F32),
            jax.ShapeDtypeStruct((half, model), BF16),
            jax.ShapeDtypeStruct((half, model), BF16),
            jax.ShapeDtypeStruct((1, model), F32),
        ],
        in_specs=vmem(3) + [anywhere] * 2 + vmem(3),
        out_specs=vmem(5),
        scratch_shapes=[pltpu.VMEM((chunks, width, units), BF16)] * 2
        + [dma((2 * chunks,)), pltpu.VMEM((half, model), F32), dma, dma, dma((blocks,)), dma((blocks,))]
        + TensorSum.scratch(chunks, half, width),
        compiler_params=pltpu.CompilerParams(
            vmem_limit_bytes=VMEM_LIMIT, collective_id=2, has_side_effects=True
        ),
        cost_estimate=COST,
        name="d_middle",
    )(hidden, d_gate, d_up, w_gate, w_up, middle, out_grad, gain)


def rms_parts(value):
    r = lax.rsqrt(jnp.mean(value * value, axis=-1, keepdims=True) + EPS)
    return r, value * r


def rms_back(r, n, gain, c):
    gc = gain * c
    return r * (gc - n * jnp.mean(n * gc, axis=-1, keepdims=True))


class Chain:
    def __init__(self):
        self.last = None

    def mark(self, value):
        self.last = value

    def __call__(self, *values):
        if self.last is None:
            return values
        return lax.optimization_barrier((*values, self.last))[:-1]


class ZSum:
    def __init__(self, part, dim, shard, planes, z_at):
        self.part, self.dim, self.shard, self.planes, self.z_at = part, dim, shard, planes, z_at
        self.at = 0
        self.came = None

    def term(self, j):
        j = jnp.clip(j, 0, self.planes - 1)
        return lax.dynamic_slice_in_dim(self.part, j * self.shard, self.shard, self.dim)

    def send(self, up, down):
        last = self.planes - 1
        self.at += 1
        up_pairs = [(2 * z + x, 2 * z + 2 + x) for z in range(last) for x in range(2) if z < self.at]
        down_pairs = [
            (2 * (last - z) + x, 2 * (last - 1 - z) + x)
            for z in range(last)
            for x in range(2)
            if z < self.at
        ]
        self.came = lax.ppermute(up, "dp", up_pairs), lax.ppermute(down, "dp", down_pairs)

    def terms(self):
        planes, z_at, at = self.planes, self.z_at, self.at
        return self.term(planes - 1 - at + z_at), self.term(at + 1 - planes + z_at)

    def start(self):
        self.send(*self.terms())

    def step(self, chain):
        if self.at >= self.planes - 1:
            return
        up, down = chain(*self.came)
        up_term, down_term = self.terms()
        up, down = up + up_term, down + down_term
        chain.mark(up)
        self.send(up, down)

    def finish(self, chain):
        if self.at == 0:
            self.start()
        while self.at < self.planes - 1:
            self.step(chain)
        up, down = chain(*self.came)
        total = self.term(self.z_at).astype(F32) + up.astype(F32) + down.astype(F32)
        chain.mark(total)
        return total


def shards(
    dp_size,
    tensor_size,
    tokens,
    norm_attn,
    w_query,
    key_weight,
    value_weight,
    query_gain,
    key_gain,
    w_out,
    norm_mlp,
    w_gate,
    w_up,
    w_down,
    out_grad,
    prefix_len,
):
    rows, model = tokens.shape
    width = query_gain.shape[0]
    kv_heads = key_weight.shape[1] // width
    repeat = w_query.shape[1] // key_weight.shape[1]
    dims = (kv_heads, repeat, width)
    group = dp_size // prefix_len.shape[0]
    planes = dp_size // 2
    group_planes = group // 2
    half = rows // 2
    shard = model // dp_size
    assert tensor_size == 4 and MAX_PREFIX <= 4 * rows

    device = lax.axis_index("dp")
    core = lax.axis_index("tensor") % 2
    x_at = device % 2
    z_at = device // 2
    sequence = device // group
    member = device % group
    plane = member // 2
    prefix = jnp.sum(jnp.where(jnp.arange(prefix_len.shape[0]) == sequence, prefix_len, 0))

    core_pairs = [(t, t ^ 1) for t in range(tensor_size)]
    y_pairs = [(t, t ^ 2) for t in range(tensor_size)]
    x_pairs = [(d, d ^ 1) for d in range(dp_size)]

    def core_swap(value):
        return lax.ppermute(value, "tensor", core_pairs)

    def y_swap(value):
        return lax.ppermute(value, "tensor", y_pairs)

    def x_swap(value):
        return lax.ppermute(value, "dp", x_pairs)

    def plane_of(d):
        return (d % group) // 2

    def own_half(value):
        return lax.dynamic_slice_in_dim(value, core * half, half, 0)

    def other_half(value):
        return lax.dynamic_slice_in_dim(value, (1 - core) * half, half, 0)

    def join(mine, theirs):
        return jnp.where(
            core == 0, jnp.concatenate([mine, theirs], 0), jnp.concatenate([theirs, mine], 0)
        )

    def sum_all(value, axes):
        for axis, bit in axes:
            size = dp_size if axis == "dp" else tensor_size
            value = value + lax.ppermute(value, axis, [(d, d ^ bit) for d in range(size)])
        return value

    dp_bits = []
    bit = 1
    while bit < dp_size:
        dp_bits.append(("dp", bit))
        bit *= 2

    positions = (member * rows + jnp.arange(rows)).astype(F32)
    counter = jnp.arange(width // 2, dtype=F32)
    angles = positions[:, None] * (ROPE_BASE ** (-2.0 * counter / width))[None, :]
    cos, sin = jnp.cos(angles), jnp.sin(angles)
    cos = jnp.concatenate([cos, cos], axis=1)
    sin = jnp.concatenate([-sin, sin], axis=1)
    norm_attn_row = norm_attn[None, :]
    norm_mlp_row = norm_mlp[None, :]
    q_gain_row = query_gain[None, :]
    k_gain_row = key_gain[None, :]

    core_at = core[None].astype(jnp.int32)
    core_not = 1 - core_at
    h_one, qkv, q_raw, k_raw = project(
        tokens,
        norm_attn_row,
        (w_query, key_weight, value_weight),
        (q_gain_row, k_gain_row, k_gain_row),
        (True, True, False),
        cos,
        sin,
        "project",
    )
    q = qkv[:, : w_query.shape[1]]
    kv = qkv[:, w_query.shape[1] :]
    prefix_at = prefix[None].astype(jnp.int32)
    heads_b, lse, kv_all = attn_fwd(prefix_at, q, kv, group, dims)
    chain = Chain()

    away = dot(other_half(heads_b), w_out).astype(BF16)
    came = core_swap(away)
    both = (dot(own_half(heads_b), w_out) + came.astype(F32)).astype(BF16)
    chain.mark(both)
    y_came = y_swap(both)
    (og,) = chain(out_grad)
    og_keep, og_send = cut(x_at, core, [og], planes, shard, join)
    og_came = x_swap(og_send)
    chain.mark(og_keep)
    d_hidden = dot(chain(out_grad)[0], w_down, NT)
    chain.mark(d_hidden)
    h_one_keep, h_one_send = cut(x_at, core, chain(h_one), planes, shard, join)
    h_one_came = x_swap(h_one_send)
    chain.mark(h_one_keep)
    middle, h_two_half = norm_forward(core_at, both, *chain(y_came), tokens, norm_mlp_row)
    chain.mark(h_two_half)
    h_two_far = core_swap(h_two_half)
    og_came = join(og_came, core_swap(og_came))
    h_one_came = join(h_one_came, core_swap(h_one_came))
    hidden, d_gate, d_up = mlp(core_at, h_two_half, *chain(h_two_far), w_gate, w_up, d_hidden)
    chain.mark(hidden)

    hidden_came, d_middle_half, d_attn_half, d_attn_far, norm_mlp_part = d_middle_of(
        hidden, d_gate, d_up, w_gate, w_up, middle, out_grad, norm_mlp_row
    )
    chain.mark(d_attn_far)
    qx, dox = attn_prep(core_at, d_attn_half, d_attn_far, w_out, q, heads_b, lse, width)
    chain.mark(dox)

    fused = planes == group_planes and shard % 128 == 0
    shared = [h_two_half, h_two_far, d_attn_half, d_attn_far, heads_b, d_up]
    grads = [hidden, hidden_came, og_keep, og_came, d_gate] if fused else None
    outs = back(prefix_at, qx, *chain(dox), kv_all, shared, grads, group, planes, shard, dims)
    dq, kv_grad, h_two_keep, h_two_came, d_attn_keep, d_attn_came, heads_came, up_came = outs[:8]
    chain.mark(dq)
    if fused:
        w_down_grad, w_gate_grad, w_out_grad = outs[8:]
    else:
        down_part = (dot(hidden, og_keep, TN) + dot(hidden_came, og_came, TN)).astype(BF16)
        w_down_grad = ZSum(down_part, 1, shard, planes, z_at).finish(chain)
        gate_part = dot(h_two_keep, d_gate, TN) + dot(h_two_came, x_swap(d_gate), TN)
        w_gate_grad = ZSum(gate_part.astype(BF16), 0, shard, planes, z_at).finish(chain)
        out_part = dot(heads_b, d_attn_keep, TN) + dot(heads_came, d_attn_came, TN)
        w_out_grad = ZSum(out_part.astype(BF16), 1, shard, planes, z_at).finish(chain)

    d_middle_far = core_swap(chain(d_middle_half)[0])
    dq_b, q_gain_part = unproject(chain(dq)[0], q_raw, q_gain_row, cos, sin, 0, "unproject_q")
    chain.mark(dq_b)
    dq_came = x_swap(chain(dq_b)[0])
    up_part = (dot(h_two_keep, d_up, TN) + dot(h_two_came, *chain(up_came), TN)).astype(BF16)
    chain.mark(up_part)
    up = ZSum(up_part, 0, shard, planes, z_at)
    up.start()

    dkv_b, k_gain_part = unproject(
        chain(kv_grad)[0], k_raw, k_gain_row, cos, sin, kv_heads * width, "unproject_kv"
    )
    kv_width = kv_heads * width
    chain.mark(dkv_b)
    dkv_came = x_swap(dkv_b)

    def d_h_one_part(which):
        dkv_rows = which(dkv_b)
        return (
            dot(which(dq_b), w_query, NT)
            + dot(dkv_rows[:, :kv_width], key_weight, NT)
            + dot(dkv_rows[:, kv_width:], value_weight, NT)
        )

    away = d_h_one_part(other_half)
    came = core_swap(away.astype(BF16))
    mine = d_h_one_part(own_half)
    both = (mine + came.astype(F32)).astype(BF16)
    chain.mark(both)
    one_y = y_swap(both)
    x_half = own_half(tokens).astype(F32)
    x_other = other_half(tokens).astype(F32)
    r_own, n_own = rms_parts(x_half)
    r_other, n_other = rms_parts(x_other)
    norm_attn_part = jnp.sum(away * n_other + mine * n_own, axis=0)

    up.step(chain)
    mlp_away = dot(other_half(chain(hidden)[0]), w_down).astype(BF16)
    mlp_came = core_swap(mlp_away)
    chain.mark(mlp_away)
    mlp_both = (dot(own_half(chain(hidden)[0]), w_down) + mlp_came.astype(F32)).astype(BF16)
    chain.mark(mlp_both)
    mlp_y = y_swap(mlp_both)
    (dq_came,) = chain(dq_came)
    q_part = (dot(h_one_keep, dq_b, TN) + dot(h_one_came, dq_came, TN)).astype(BF16)
    chain.mark(q_part)
    query = ZSum(q_part, 0, shard, planes, z_at)
    query.start()
    (dkv_came,) = chain(dkv_came)
    kv_part = (dot(h_one_keep, dkv_b, TN) + dot(h_one_came, dkv_came, TN)).astype(BF16)
    chain.mark(kv_part)
    key_value = ZSum(kv_part, 0, shard, planes, z_at)
    key_value.start()
    up.step(chain)
    query.step(chain)
    key_value.step(chain)
    w_up_grad = up.finish(chain)
    query.step(chain)
    key_value.step(chain)

    d_h_one = (both.astype(F32) + one_y.astype(F32)).astype(BF16)
    d_h_one_other = core_swap(d_h_one)
    grad_own = d_middle_half + rms_back(r_own, n_own, norm_attn_row, d_h_one.astype(F32))
    grad_other = d_middle_far + rms_back(r_other, n_other, norm_attn_row, d_h_one_other.astype(F32))
    tokens_grad = join(grad_own, grad_other)
    block_half = (middle + (mlp_both.astype(F32) + mlp_y.astype(F32))).astype(BF16)
    block_out = join(block_half, core_swap(block_half))
    w_query_grad = query.finish(chain)
    w_kv_grad = key_value.finish(chain)

    small = jnp.concatenate([norm_attn_part, q_gain_part[0], k_gain_part[0]])
    norm_mlp_part, small = chain(norm_mlp_part[0], small)
    norm_mlp_sum = sum_all(norm_mlp_part, [("tensor", 1)] + dp_bits)
    small = sum_all(small, [("tensor", 1), ("tensor", 2)] + dp_bits)
    norm_mlp_grad = lax.dynamic_slice_in_dim(norm_mlp_sum, device * shard, shard, 0)
    norm_attn_grad = lax.dynamic_slice_in_dim(small, device * shard, shard, 0)
    return (
        block_out,
        tokens_grad,
        norm_attn_grad,
        w_query_grad,
        w_kv_grad[:, :kv_width],
        w_kv_grad[:, kv_width:],
        small[model : model + width],
        small[model + width :],
        w_out_grad,
        norm_mlp_grad,
        w_gate_grad,
        w_up_grad,
        w_down_grad,
    )


def solution(mesh):
    placed = (
        P("dp", None),
        P(),
        P(None, "tensor"),
        P(None, "tensor"),
        P(None, "tensor"),
        P(),
        P(),
        P("tensor", None),
        P(),
        P(None, "tensor"),
        P(None, "tensor"),
        P("tensor", None),
        P("dp", None),
        P(),
    )
    return jax.shard_map(
        functools.partial(shards, mesh.shape["dp"], mesh.shape["tensor"]),
        mesh=mesh,
        in_specs=placed,
        out_specs=(
            P("dp", None),
            P("dp", None),
            P("dp"),
            P("dp", "tensor"),
            P("dp", "tensor"),
            P("dp", "tensor"),
            P(),
            P(),
            P("tensor", "dp"),
            P("dp"),
            P("dp", "tensor"),
            P("dp", "tensor"),
            P("tensor", "dp"),
        ),
        check_vma=False,
    )
```

```python
import functools
import math

import jax
import jax.numpy as jnp
from jax import lax
from jax.experimental import pallas as pl
from jax.experimental.pallas import tpu as pltpu
from jax.sharding import PartitionSpec as P

F32 = jnp.float32
BF16 = jnp.bfloat16
EPS = 1e-06
ROPE_BASE = 1000000.0
MAX_PREFIX = 2048
VMEM_LIMIT = 56 * 2**20
BACK_VMEM_LIMIT = 60 * 2**20

COST = pl.CostEstimate(flops=1000, bytes_accessed=1000, transcendentals=0)

NN = (((1,), (0,)), ((), ()))
NT = (((1,), (1,)), ((), ()))
TN = (((0,), (0,)), ((), ()))


def dot(left, right, dims=NN):
    return lax.dot_general(left, right, dims, preferred_element_type=F32)


def vmem(count):
    return [pl.BlockSpec(memory_space=pltpu.VMEM)] * count


def params():
    return pltpu.CompilerParams(vmem_limit_bytes=VMEM_LIMIT)


def greet(peers):
    barrier = pltpu.get_barrier_semaphore()
    count = 0
    for peer, there in peers:

        def signal(peer=peer):
            pl.semaphore_signal(barrier, 1, device_id=peer, device_id_type=pl.DeviceIdType.MESH)

        if there is True:
            signal()
            count = count + 1
        else:
            pl.when(there)(signal)
            count = count + there.astype(jnp.int32)
    pl.semaphore_wait(barrier, count)


def remote(src, dst, send, recv, peer):
    return pltpu.make_async_remote_copy(
        src_ref=src,
        dst_ref=dst,
        send_sem=send,
        recv_sem=recv,
        device_id=peer,
        device_id_type=pl.DeviceIdType.MESH,
    )


def tensor_peers():
    t = lax.axis_index("tensor")
    core = t % 2
    y = t // 2
    return core, {"tensor": t + 1 - 2 * core}, {"tensor": t + 2 - 4 * y}


def rows_of(core, half):
    return pl.ds(pl.multiple_of(core * half, half), half)


def cut_into(out, out_rows, ref, ref_rows, side, planes, shard):
    for z in range(planes):
        to = slice(z * shard, (z + 1) * shard)
        if shard % 128 == 0:
            at = pl.ds(pl.multiple_of((2 * z + side) * shard, shard), shard)
            out[out_rows, to] = ref[ref_rows, at]
        else:
            low = ref[ref_rows, 2 * z * shard : (2 * z + 1) * shard]
            high = ref[ref_rows, (2 * z + 1) * shard : (2 * z + 2) * shard]
            out[out_rows, to] = jnp.where(side == 0, low, high)


class Columns:
    def __init__(self, own, far, keep, came, scratch, x_at, core, x_peer, core_peer, planes, shard):
        self.own, self.far, self.keep, self.came = own, far, keep, came
        self.send_ref, self.recv_ref, self.sems = scratch[0], scratch[1], scratch[2:]
        self.x_at, self.core, self.cut = x_at, core, (planes, shard)
        self.x_peer, self.core_peer = x_peer, core_peer
        self.half = own.shape[0]

    @staticmethod
    def scratch(half, columns):
        return [pltpu.VMEM((half, columns), BF16)] * 2 + [pltpu.SemaphoreType.DMA] * 4

    def over_x(self):
        return remote(self.send_ref, self.recv_ref, self.sems[0], self.sems[1], self.x_peer)

    def over_core(self):
        there = self.came.at[rows_of(self.core, self.half), :]
        return remote(self.recv_ref, there, self.sems[2], self.sems[3], self.core_peer)

    def start(self):
        every = slice(None)
        cut_into(self.send_ref, every, self.own, every, 1 - self.x_at, *self.cut)
        self.over_x().start()

    def store(self):
        every = slice(None)
        for ref, core in ((self.own, self.core), (self.far, 1 - self.core)):
            cut_into(self.keep, rows_of(core, self.half), ref, every, self.x_at, *self.cut)

    def forward(self):
        self.over_x().wait_recv()
        self.over_core().start()
        self.came[rows_of(self.core, self.half), :] = self.recv_ref[...]

    def finish(self):
        self.over_core().wait_recv()
        self.over_x().wait_send()
        self.over_core().wait_send()


class LineSum:
    def __init__(self, scratch, device, plane, planes):
        self.stack, self.came = scratch[:2]
        self.sems = scratch[2:]
        self.device, self.plane, self.planes = device, plane, planes

    @staticmethod
    def scratch(planes, shape):
        return [pltpu.VMEM((n,) + shape, BF16) for n in (planes, planes + 1)] + [
            pltpu.SemaphoreType.DMA((planes,))
        ] * 4

    def up(self, j):
        s = self.sems
        peer = {"dp": self.device + 2}
        return remote(self.stack.at[j], self.came.at[j], s[0].at[j], s[1].at[j], peer)

    def down(self, j):
        s = self.sems
        slot = jnp.where(self.plane - 1 == j, self.planes, j)
        peer = {"dp": self.device - 2}
        return remote(self.stack.at[j], self.came.at[slot], s[2].at[j], s[3].at[j], peer)

    def start(self):
        last = self.planes - 1

        @pl.when(self.plane == 0)
        def _():
            for j in range(last, 0, -1):
                self.up(j).start()

        @pl.when(self.plane == last)
        def _():
            for j in range(last):
                self.down(j).start()

    def wave(self, i):
        last = self.planes - 1
        j = last - i

        @pl.when((self.plane > 0) & (self.plane < j))
        def _():
            self.up(j).wait_recv()
            self.stack[j] += self.came[j]
            self.up(j).start()

        @pl.when((self.plane < last) & (self.plane > i))
        def _():
            self.down(i).wait_recv()
            self.stack[i] += self.came[i]
            self.down(i).start()

    def finish(self, out):
        plane, planes = self.plane, self.planes
        out[...] = self.stack[plane].astype(F32)

        @pl.when(plane > 0)
        def _():
            self.up(plane).wait_recv()
            out[...] += self.came[plane].astype(F32)

        @pl.when(plane < planes - 1)
        def _():
            self.down(plane).wait_recv()
            out[...] += self.came[planes].astype(F32)

        for j in range(planes):
            pl.when(plane < j)(lambda j=j: self.up(j).wait_send())
            pl.when(plane > j)(lambda j=j: self.down(j).wait_send())

    def fill_rows(self, left, left_came, right, right_came):
        shard = self.stack.shape[1]

        def body(j, carry):
            at = pl.ds(pl.multiple_of(j * shard, shard), shard)
            self.stack[j] = (
                dot(left[:, at], right[...], TN) + dot(left_came[:, at], right_came[...], TN)
            ).astype(BF16)
            return carry

        lax.fori_loop(0, self.planes, body, 0)

    def fill_columns(self, left, left_came, right, right_came):
        shard = self.stack.shape[2]
        tile = 256

        def body(t, carry):
            at = pl.ds(pl.multiple_of(t * tile, tile), tile)
            term = dot(left[:, at], right[...], TN) + dot(left_came[:, at], right_came[...], TN)
            for j in range(self.planes):
                self.stack[j, at, :] = term[:, j * shard : (j + 1) * shard].astype(BF16)
            return carry

        lax.fori_loop(0, left.shape[1] // tile, body, 0)


class TensorSum:
    def __init__(self, scratch, mine, core, core_peer, y_peer):
        self.away, self.core_came, self.both, self.y_came = scratch[:4]
        self.sems = scratch[4:]
        self.mine = mine
        self.core, self.core_peer, self.y_peer = core, core_peer, y_peer
        self.chunks, self.half, self.width = self.away.shape

    @staticmethod
    def scratch(chunks, half, width):
        return [pltpu.VMEM((chunks, half, width), BF16)] * 4 + [
            pltpu.SemaphoreType.DMA((chunks,))
        ] * 4

    def over_core(self, i):
        s = self.sems
        return remote(self.away.at[i], self.core_came.at[i], s[0].at[i], s[1].at[i], self.core_peer)

    def over_y(self, i):
        s = self.sems
        return remote(self.both.at[i], self.y_came.at[i], s[2].at[i], s[3].at[i], self.y_peer)

    def add(self, i, value):
        self.mine[i % 2] = value
        self.away[i] = self.mine[i % 2, rows_of(1 - self.core, self.half), :].astype(BF16)
        self.over_core(i).start()
        if i > 0:
            self.pass_on(i - 1)
        if i == self.chunks - 1:
            self.pass_on(i)

    def pass_on(self, i):
        self.over_core(i).wait_recv()
        mine = self.mine[i % 2, rows_of(self.core, self.half), :]
        self.both[i] = (mine + self.core_came[i].astype(F32)).astype(BF16)
        self.over_y(i).start()

    def total(self, i):
        self.over_y(i).wait_recv()
        return self.both[i].astype(F32) + self.y_came[i].astype(F32)

    def finish(self):
        for i in range(self.chunks):
            self.over_core(i).wait_send()
            self.over_y(i).wait_send()


def roll_half(value):
    return pltpu.roll(value, value.shape[-1] // 2, 1)


def project_kernel(x_ref, g_ref, *refs, heads, normed, width):
    count = len(heads)
    w_refs = refs[:count]
    gain_refs = refs[count : 2 * count]
    cos_ref, sin_ref = refs[2 * count : 2 * count + 2]
    h_ref, out_ref = refs[2 * count + 2 : 2 * count + 4]
    raw_refs = refs[2 * count + 4 :]
    x = x_ref[...].astype(F32)
    h = (x * lax.rsqrt(jnp.mean(x * x, axis=1, keepdims=True) + EPS) * g_ref[...]).astype(BF16)
    h_ref[...] = h
    cos, sin = cos_ref[...], sin_ref[...]
    column = 0
    raw_at = 0
    for i in range(count):
        product = dot(h, w_refs[i][...])
        if normed[i]:
            raw_refs[raw_at][...] = product
            raw_at += 1
        for j in range(heads[i]):
            u = product[:, j * width : (j + 1) * width]
            if normed[i]:
                u = u * lax.rsqrt(jnp.mean(u * u, axis=1, keepdims=True) + EPS) * gain_refs[i][...]
                u = u * cos + roll_half(u) * sin
            out_ref[:, column : column + width] = u.astype(BF16)
            column += width


def project(x, gain, weights, gains, normed, cos, sin, name):
    rows, model = x.shape
    width = cos.shape[1]
    heads = tuple(w.shape[1] // width for w in weights)
    columns = sum(w.shape[1] for w in weights)
    raws = [w for w, n in zip(weights, normed) if n]
    return pl.pallas_call(
        functools.partial(project_kernel, heads=heads, normed=normed, width=width),
        out_shape=[
            jax.ShapeDtypeStruct((rows, model), BF16),
            jax.ShapeDtypeStruct((rows, columns), BF16),
        ]
        + [jax.ShapeDtypeStruct((rows, w.shape[1]), F32) for w in raws],
        in_specs=vmem(4 + 2 * len(weights)),
        out_specs=vmem(2 + len(raws)),
        compiler_params=params(),
        cost_estimate=COST,
        name=name,
    )(x, gain, *weights, *gains, cos, sin)


def visible(shape, key0, row0, prefix):
    key_pos = key0 + lax.broadcasted_iota(jnp.int32, shape, 1)
    row_pos = row0 + lax.broadcasted_iota(jnp.int32, shape, 0)
    return (key_pos <= row_pos) | (key_pos < prefix)


def attn_fwd_kernel(
    prefix_ref,
    q_ref,
    kv_ref,
    o_ref,
    lse_ref,
    all_ref,
    acc,
    send_x,
    recv_x,
    send_z,
    recv_z,
    send_down,
    *,
    group,
    kv_heads,
    repeat,
    width,
    tile,
    coef,
):
    rows = q_ref.shape[0]
    kv_width = kv_heads * width
    planes = group // 2
    device = lax.axis_index("dp")
    member = device % group
    plane = member // 2
    x_at = member % 2
    x_other = device + 1 - 2 * x_at
    inner = plane < planes - 1
    prefix = prefix_ref[0]

    barrier = pltpu.get_barrier_semaphore()
    pl.semaphore_signal(barrier, 1, device_id={"dp": x_other}, device_id_type=pl.DeviceIdType.MESH)

    @pl.when(inner)
    def _():
        pl.semaphore_signal(
            barrier, 1, device_id={"dp": device + 2}, device_id_type=pl.DeviceIdType.MESH
        )

    @pl.when(plane > 0)
    def _():
        pl.semaphore_signal(
            barrier, 1, device_id={"dp": device - 2}, device_id_type=pl.DeviceIdType.MESH
        )

    pl.semaphore_wait(barrier, 1 + inner.astype(jnp.int32) + (plane > 0).astype(jnp.int32))

    def source(slot):
        return kv_ref if slot == 0 else all_ref.at[2 * slot]

    def to_x(slot):
        return pltpu.make_async_remote_copy(
            src_ref=source(slot),
            dst_ref=all_ref.at[2 * slot + 1],
            send_sem=send_x.at[slot],
            recv_sem=recv_x.at[slot],
            device_id={"dp": x_other},
            device_id_type=pl.DeviceIdType.MESH,
        )

    def to_z(slot):
        return pltpu.make_async_remote_copy(
            src_ref=source(slot - 1),
            dst_ref=all_ref.at[2 * slot],
            send_sem=send_z.at[slot],
            recv_sem=recv_z.at[slot],
            device_id={"dp": device + 2},
            device_id_type=pl.DeviceIdType.MESH,
        )

    def to_first():
        return pltpu.make_async_remote_copy(
            src_ref=kv_ref,
            dst_ref=all_ref.at[2],
            send_sem=send_down,
            recv_sem=recv_z.at[1],
            device_id={"dp": device - 2},
            device_id_type=pl.DeviceIdType.MESH,
        )

    all_ref[0] = kv_ref[...]
    ones = jnp.ones((rows, width), BF16)
    row0 = member * rows

    def work(block, other, masked, start=False):
        key0 = other * rows

        def head_pair(h, carry):
            k = block[:, pl.ds(pl.multiple_of(h * width, width), width)]
            v = block[:, pl.ds(pl.multiple_of(kv_width + h * width, width), width)]
            v = jnp.concatenate([v, ones], axis=1)
            for g in range(repeat):
                head = h * repeat + g
                for at in range(0, rows, tile):
                    q = q_ref[at : at + tile, pl.ds(pl.multiple_of(head * width, width), width)]
                    p = jnp.exp2(dot(q, k, NT) * coef)
                    if masked:
                        p = jnp.where(visible(p.shape, key0, row0 + at, prefix), p, 0.0)
                    term = dot(p.astype(BF16), v)
                    if start:
                        acc[head, at : at + tile, :] = term
                    else:
                        acc[head, at : at + tile, :] += term
            return carry

        lax.fori_loop(0, kv_heads, head_pair, 0)

    to_x(0).start()
    if planes > 1:

        @pl.when(inner)
        def _():
            to_z(1).start()

        @pl.when(plane == 1)
        def _():
            to_first().start()

    work(kv_ref, member, True, True)
    to_x(0).wait_recv()
    work(all_ref.at[1], member + 1 - 2 * x_at, True)
    for slot in range(1, planes):

        def step(slot=slot):
            to_z(slot).wait_recv()
            if slot < planes - 1:

                @pl.when(inner & (plane >= slot))
                def _():
                    to_z(slot + 1).start()

            to_x(slot).start()
            there = 2 * (plane - slot)
            if slot == 1:

                @pl.when(plane == 0)
                def _():
                    work(all_ref.at[2 * slot], 2 + x_at, True)

                @pl.when(plane > 0)
                def _():
                    work(all_ref.at[2 * slot], there + x_at, False)
            else:
                work(all_ref.at[2 * slot], there + x_at, False)
            to_x(slot).wait_recv()
            if slot == 1:

                @pl.when(plane == 0)
                def _():
                    work(all_ref.at[2 * slot + 1], 3 - x_at, True)

                @pl.when(plane > 0)
                def _():
                    work(all_ref.at[2 * slot + 1], there + 1 - x_at, False)
            else:
                work(all_ref.at[2 * slot + 1], there + 1 - x_at, False)

        if slot == 1:
            step()
        else:
            pl.when(plane >= slot)(step)

    for head in range(kv_heads * repeat):
        total = acc[head, :, width:]
        o_ref[:, head * width : (head + 1) * width] = (acc[head, :, :width] / total).astype(BF16)
        lse_ref[:, head * width : (head + 1) * width] = jnp.log2(total) * (1.0 / coef)

    to_x(0).wait_send()
    for slot in range(1, planes):

        @pl.when(inner & (plane >= slot - 1))
        def _(slot=slot):
            to_z(slot).wait_send()

        @pl.when((plane >= slot) | (slot == 1))
        def _(slot=slot):
            to_x(slot).wait_send()

    if planes > 1:

        @pl.when(plane == 1)
        def _():
            to_first().wait_send()


def attn_fwd(prefix, q, kv, group, dims):
    kv_heads, repeat, width = dims
    rows = q.shape[0]
    heads = kv_heads * repeat
    columns = heads * width
    planes = group // 2
    return pl.pallas_call(
        functools.partial(
            attn_fwd_kernel,
            group=group,
            kv_heads=kv_heads,
            repeat=repeat,
            width=width,
            tile=min(rows, 256),
            coef=math.log2(math.e) / math.sqrt(width),
        ),
        out_shape=[
            jax.ShapeDtypeStruct((rows, columns), BF16),
            jax.ShapeDtypeStruct((rows, columns), F32),
            jax.ShapeDtypeStruct((group,) + kv.shape, BF16),
        ],
        in_specs=[pl.BlockSpec(memory_space=pltpu.SMEM)] + vmem(2),
        out_specs=vmem(3),
        scratch_shapes=[pltpu.VMEM((heads, rows, 2 * width), F32)]
        + [pltpu.SemaphoreType.DMA((planes,))] * 4
        + [pltpu.SemaphoreType.DMA],
        compiler_params=pltpu.CompilerParams(
            vmem_limit_bytes=VMEM_LIMIT, collective_id=0, has_side_effects=True
        ),
        cost_estimate=COST,
        name="attn_fwd",
    )(prefix, q, kv)


def split_three(value):
    high = value.astype(BF16)
    left = value - high.astype(F32)
    mid = left.astype(BF16)
    return high.astype(F32), mid.astype(F32), (left - mid.astype(F32)).astype(BF16).astype(F32)


def attn_prep_kernel(core_ref, own_ref, far_ref, w_ref, q_ref, o_ref, lse_ref, qx_ref, dox_ref, *, heads, width):
    half = own_ref.shape[0]
    core = core_ref[0]
    lane = lax.broadcasted_iota(jnp.int32, (half, width), 1)

    def extra(value):
        a, b, c = split_three(value)
        return jnp.where(lane == 0, a, jnp.where(lane == 1, b, jnp.where(lane == 2, c, 0.0))).astype(BF16)

    for ref, at_core in ((own_ref, core), (far_ref, 1 - core)):
        at_rows = pl.ds(pl.multiple_of(at_core * half, half), half)
        d_heads = dot(ref[...], w_ref[...], NT)
        for head in range(heads):
            at = slice(head * width, (head + 1) * width)
            qx_ref[head, at_rows, :width] = q_ref[at_rows, at]
            qx_ref[head, at_rows, width:] = extra(lse_ref[at_rows, at])
            d = d_heads[:, at].astype(BF16)
            delta = jnp.sum(d.astype(F32) * o_ref[at_rows, at].astype(F32), axis=1, keepdims=True)
            dox_ref[head, at_rows, :width] = d
            dox_ref[head, at_rows, width:] = extra(jnp.broadcast_to(delta, (half, width)))


def attn_prep(core, d_own, d_far, w_out, q, out, lse, width):
    rows, columns = q.shape
    heads = columns // width
    return pl.pallas_call(
        functools.partial(attn_prep_kernel, heads=heads, width=width),
        out_shape=[jax.ShapeDtypeStruct((heads, rows, 2 * width), BF16)] * 2,
        in_specs=[pl.BlockSpec(memory_space=pltpu.SMEM)] + vmem(6),
        out_specs=vmem(2),
        compiler_params=params(),
        cost_estimate=COST,
        name="attn_prep",
    )(core, d_own, d_far, w_out, q, out, lse)


def back_kernel(
    *refs, group, planes, all_planes, shard, kv_heads, repeat, width, coef, scale, sums
):
    refs = list(refs)

    def take(count):
        out = refs[:count]
        del refs[:count]
        return out

    prefix_ref, qx_ref, dox_ref, kv_ref = take(4)
    h_own_ref, h_far_ref, a_own_ref, a_far_ref, heads_ref, up_ref = take(6)
    if sums:
        hid_ref, hid_came_ref, og_ref, og_came_ref, gate_ref = take(5)
    dq_ref, grad_ref, h_ref, h_came_ref, a_ref, a_came_ref, heads_came_ref, up_came_ref = take(8)
    if sums:
        w_down_ref, w_gate_ref, w_out_ref = take(3)
    own_ref, far_ref, xr_ref, zr_ref, first_ref = take(5)
    send_x, recv_x, send_z, recv_z, send_first, recv_first = take(6)
    swap_sems = take(4)
    h_scratch, a_scratch = take(6), take(6)
    rows = qx_ref.shape[1]
    kv_width = kv_heads * width
    device = lax.axis_index("dp")
    member = device % group
    plane = member // 2
    last = planes - 1
    if sums:
        gate_came_ref, send_gate, recv_gate = take(3)
        down_sum, gate_sum, out_sum = (LineSum(take(6), device, plane, planes) for _ in range(3))
    x_at = member % 2
    x_other = device + 1 - 2 * x_at
    inner = plane < last
    prefix = prefix_ref[0]

    core, core_peer, _ = tensor_peers()
    x_peer = {"dp": x_other}
    greet(
        [(x_peer, True), (core_peer, True), ({"dp": device + 2}, inner), ({"dp": device - 2}, plane > 0)]
    )

    def copy(src, dst, send, recv, there):
        return remote(src, dst, send, recv, {"dp": there})

    def columns(own, far, keep, came, scratch):
        return Columns(
            own, far, keep, came, scratch, x_at, core, x_peer, core_peer, all_planes, shard
        )

    h_two = columns(h_own_ref, h_far_ref, h_ref, h_came_ref, h_scratch)
    d_attn = columns(a_own_ref, a_far_ref, a_ref, a_came_ref, a_scratch)
    heads_swap = copy(heads_ref, heads_came_ref, swap_sems[0], swap_sems[1], x_other)
    up_swap = copy(up_ref, up_came_ref, swap_sems[2], swap_sems[3], x_other)

    def gate_swap():
        return copy(gate_ref, gate_came_ref, send_gate, recv_gate, x_other)

    lane = lax.broadcasted_iota(jnp.int32, (rows, width), 1)
    minus = jnp.where(lane < 3, -1.0, 0.0).astype(BF16)
    row0 = member * rows

    def work(block, other, masked, out):
        key0 = other * rows

        def head_group(h, carry):
            k_at = pl.ds(pl.multiple_of(h * width, width), width)
            v_at = pl.ds(pl.multiple_of(kv_width + h * width, width), width)
            k = kv_ref[block, :, k_at]
            v = kv_ref[block, :, v_at]
            kx = jnp.concatenate([k, minus], axis=1)
            vx = jnp.concatenate([v, minus], axis=1)
            dk = jnp.zeros((rows, width), F32)
            dv = jnp.zeros((rows, width), F32)
            for g in range(repeat):
                head = h * repeat + g
                qx = qx_ref[head]
                dox = dox_ref[head]
                p = jnp.exp2(dot(qx, kx, NT) * coef)
                if masked:
                    p = jnp.where(visible(p.shape, key0, row0, prefix), p, 0.0)
                ds = (p * dot(dox, vx, NT)).astype(BF16)
                dv += dot(p.astype(BF16), dox[:, :width], TN)
                dk += dot(ds, qx[:, :width], TN)
                dq_ref[:, pl.ds(pl.multiple_of(head * width, width), width)] += dot(ds, k)
            out[:, k_at] = (dk * scale).astype(BF16)
            out[:, v_at] = dv.astype(BF16)
            return carry

        lax.fori_loop(0, kv_heads, head_group, 0)

    def far_swap(slot):
        return copy(far_ref.at[slot], xr_ref.at[slot], send_x.at[slot], recv_x.at[slot], x_other)

    def to_plane(slot):
        return copy(own_ref.at[slot], zr_ref.at[slot], send_z.at[slot], recv_z.at[slot], device - 2)

    def from_first():
        return copy(own_ref.at[1], first_ref, send_first, recv_first, device + 2)

    def attend(slot):
        there = 2 * (plane - slot)
        far, own = there + 1 - x_at, there + x_at

        def both(far, own, masked):
            work(2 * slot + 1, far, masked, far_ref.at[slot])
            far_swap(slot).start()
            work(2 * slot, own, masked, own_ref.at[slot])

        if slot == 0:
            both(far, own, True)
        elif slot == 1:
            pl.when(plane == 0)(lambda: both(3 - x_at, 2 + x_at, True))
            pl.when(plane > 0)(lambda: both(far, own, False))
        else:
            pl.when(plane >= slot)(lambda: both(far, own, False))

    def pass_back(slot):
        def go():
            far_swap(slot).wait_recv()
            own_ref[slot] += xr_ref[slot]
            if slot < last:

                @pl.when(inner & (plane >= slot))
                def _():
                    to_plane(slot + 1).wait_recv()
                    own_ref[slot] += zr_ref[slot + 1]

            if slot == 1:
                pl.when(plane == 0)(lambda: from_first().start())
                pl.when(plane > 0)(lambda: to_plane(slot).start())
            else:
                to_plane(slot).start()

        if slot == 1:
            go()
        else:
            pl.when(plane >= slot)(go)

    dq_ref[...] = jnp.zeros_like(dq_ref)
    if sums:
        gate_swap().start()
        down_sum.fill_columns(hid_ref, hid_came_ref, og_ref, og_came_ref)
        down_sum.start()
    h_two.start()
    h_two.store()
    d_attn.store()
    pending = list(range(last, 0, -1))
    waves = list(range(max(last - 1, 0)))
    for count, slot in enumerate(range(last, -1, -1)):
        attend(slot)
        if sums and count >= 1 and count - 1 < len(waves):
            down_sum.wave(waves[count - 1])
        if count >= 1 and slot >= 1:
            pass_back(pending.pop(0))
        if slot == min(1, last):
            h_two.forward()
            d_attn.start()
            heads_swap.start()
            if sums:
                gate_swap().wait_recv()
                h_two.over_core().wait_recv()
                gate_sum.fill_rows(h_ref, h_came_ref, gate_ref, gate_came_ref)
                gate_sum.start()
    up_swap.start()
    while pending:
        pass_back(pending.pop(0))
    dq_ref[...] = dq_ref[...] * scale
    d_attn.forward()
    heads_swap.wait_recv()
    d_attn.over_core().wait_recv()
    if sums:
        out_sum.fill_columns(heads_ref, heads_came_ref, a_ref, a_came_ref)
        out_sum.start()
        for wave in waves:
            gate_sum.wave(wave)
        for wave in waves:
            out_sum.wave(wave)

    far_swap(0).wait_recv()
    grad_ref[...] = own_ref[0].astype(F32) + xr_ref[0].astype(F32)
    if last > 0:

        @pl.when(inner)
        def _():
            to_plane(1).wait_recv()
            grad_ref[...] += zr_ref[1].astype(F32)

        @pl.when(plane == 1)
        def _():
            from_first().wait_recv()
            grad_ref[...] += first_ref[...].astype(F32)

    if sums:
        down_sum.finish(w_down_ref)
        gate_sum.finish(w_gate_ref)
        out_sum.finish(w_out_ref)
        gate_swap().wait_send()
    up_swap.wait_recv()
    up_swap.wait_send()
    heads_swap.wait_send()
    for part in (h_two, d_attn):
        part.over_x().wait_send()
        part.over_core().wait_send()
    if not sums:
        h_two.over_core().wait_recv()
    for slot in range(planes):
        if slot <= 1:
            far_swap(slot).wait_send()
        else:
            pl.when(plane >= slot)(lambda slot=slot: far_swap(slot).wait_send())
        if slot >= 1:
            pl.when(plane >= slot)(lambda slot=slot: to_plane(slot).wait_send())
    if last > 0:
        pl.when(plane == 0)(lambda: from_first().wait_send())


def back(prefix, qx, dox, kv_all, shared, grads, group, all_planes, shard, dims):
    kv_heads, repeat, width = dims
    rows = qx.shape[1]
    columns = kv_heads * repeat * width
    planes = group // 2
    block = kv_all.shape[1:]
    dma = pltpu.SemaphoreType.DMA
    heads, d_up = shared[4:]
    units = d_up.shape[1]
    cut_shape = jax.ShapeDtypeStruct((rows, all_planes * shard), BF16)
    out_shape = [jax.ShapeDtypeStruct((rows, columns), F32), jax.ShapeDtypeStruct(block, F32)]
    out_shape += [cut_shape] * 4
    out_shape += [jax.ShapeDtypeStruct(heads.shape, BF16), jax.ShapeDtypeStruct(d_up.shape, BF16)]
    scratch = [pltpu.VMEM((planes,) + block, BF16)] * 4 + [pltpu.VMEM(block, BF16)]
    scratch += [dma((planes,))] * 4 + [dma, dma] + [dma] * 4
    scratch += Columns.scratch(rows // 2, all_planes * shard) * 2
    args = [prefix, qx, dox, kv_all, *shared]
    if grads is not None:
        args += grads
        shapes = (units, shard), (shard, units), (heads.shape[1], shard)
        out_shape += [jax.ShapeDtypeStruct(s, F32) for s in shapes]
        scratch += [pltpu.VMEM((rows, units), BF16), dma, dma]
        for shape in shapes:
            scratch += LineSum.scratch(planes, shape)
    return pl.pallas_call(
        functools.partial(
            back_kernel,
            group=group,
            planes=planes,
            all_planes=all_planes,
            shard=shard,
            kv_heads=kv_heads,
            repeat=repeat,
            width=width,
            coef=math.log2(math.e) / math.sqrt(width),
            scale=1.0 / math.sqrt(width),
            sums=grads is not None,
        ),
        out_shape=out_shape,
        in_specs=[smem()] + vmem(8) + [pl.BlockSpec(memory_space=pl.ANY)] + vmem(len(args) - 10),
        out_specs=vmem(7) + [pl.BlockSpec(memory_space=pl.ANY)] + vmem(len(out_shape) - 8),
        scratch_shapes=scratch,
        compiler_params=pltpu.CompilerParams(
            vmem_limit_bytes=BACK_VMEM_LIMIT, collective_id=1, has_side_effects=True
        ),
        cost_estimate=COST,
        name="back",
    )(*args)


def smem():
    return pl.BlockSpec(memory_space=pltpu.SMEM)


def cut_kernel(at_ref, *refs, halves, planes, shard):
    x_at, core = at_ref[0], at_ref[1]
    keep_ref, send_ref = refs[-2:]
    half = send_ref.shape[0]
    for z in range(planes):
        to = slice(z * shard, (z + 1) * shard)
        keep = pl.ds(pl.multiple_of((2 * z + x_at) * shard, shard), shard)
        send = pl.ds(pl.multiple_of((2 * z + 1 - x_at) * shard, shard), shard)
        if halves:
            own_ref, far_ref = refs[:2]
            keep_ref[pl.ds(pl.multiple_of(core * half, half), half), to] = own_ref[:, keep]
            keep_ref[pl.ds(pl.multiple_of((1 - core) * half, half), half), to] = far_ref[:, keep]
            send_ref[:, to] = own_ref[:, send]
        else:
            keep_ref[:, to] = refs[0][:, keep]
            send_ref[:, to] = refs[0][pl.ds(pl.multiple_of(core * half, half), half), send]


def cut(x_at, core, parts, planes, shard, join):
    halves = len(parts) == 2
    half = parts[0].shape[0] // (1 if halves else 2)
    if shard % 128:
        whole = join(*parts) if halves else parts[0]
        own = parts[0] if halves else lax.dynamic_slice_in_dim(whole, core * half, half, 0)

        def columns(value, side):
            view = value.reshape(value.shape[0], planes, 2, shard)
            return lax.dynamic_index_in_dim(view, side, 2, keepdims=False).reshape(
                value.shape[0], planes * shard
            )

        return columns(whole, x_at), columns(own, 1 - x_at)
    return pl.pallas_call(
        functools.partial(cut_kernel, halves=halves, planes=planes, shard=shard),
        out_shape=[
            jax.ShapeDtypeStruct((2 * half, planes * shard), BF16),
            jax.ShapeDtypeStruct((half, planes * shard), BF16),
        ],
        in_specs=[smem()] + vmem(len(parts)),
        out_specs=vmem(2),
        compiler_params=params(),
        cost_estimate=COST,
        name="cut",
    )(jnp.stack([x_at, core]).astype(jnp.int32), *parts)


def norm_kernel(core_ref, both_ref, y_ref, x_ref, gain_ref, middle_ref, h_ref):
    half = both_ref.shape[0]
    x = x_ref[pl.ds(pl.multiple_of(core_ref[0] * half, half), half), :].astype(F32)
    middle = x + both_ref[...].astype(F32) + y_ref[...].astype(F32)
    middle_ref[...] = middle
    r = lax.rsqrt(jnp.mean(middle * middle, axis=1, keepdims=True) + EPS)
    h_ref[...] = (middle * r * gain_ref[...]).astype(BF16)


def norm_forward(core, both, came, x, gain):
    return pl.pallas_call(
        norm_kernel,
        out_shape=[jax.ShapeDtypeStruct(both.shape, F32), jax.ShapeDtypeStruct(both.shape, BF16)],
        in_specs=[smem()] + vmem(4),
        out_specs=vmem(2),
        compiler_params=params(),
        cost_estimate=COST,
        name="norm_forward",
    )(core, both, came, x, gain)


def mlp_kernel(core_ref, own_ref, far_ref, gate_ref, up_ref, d_ref, hidden_ref, d_gate_ref, d_up_ref):
    half = own_ref.shape[0]
    core = core_ref[0]
    for ref, at_core in ((own_ref, core), (far_ref, 1 - core)):
        at = pl.ds(pl.multiple_of(at_core * half, half), half)
        gate = dot(ref[...], gate_ref[...])
        up = dot(ref[...], up_ref[...])
        sig = 1.0 / (1.0 + jnp.exp(-gate))
        silu = gate * sig
        d = d_ref[at, :]
        hidden_ref[at, :] = (silu * up).astype(BF16)
        d_up_ref[at, :] = (d * silu).astype(BF16)
        d_gate_ref[at, :] = (d * up * (sig * (1.0 + gate * (1.0 - sig)))).astype(BF16)


def mlp(core, own, far, w_gate, w_up, d_hidden):
    half, model = own.shape
    units = w_gate.shape[1]
    tile = math.gcd(units, 256)
    rows_spec = pl.BlockSpec((half, model), lambda i: (0, 0))
    weight_spec = pl.BlockSpec((model, tile), lambda i: (0, i))
    unit_spec = pl.BlockSpec((2 * half, tile), lambda i: (0, i))
    return pl.pallas_call(
        mlp_kernel,
        out_shape=[jax.ShapeDtypeStruct((2 * half, units), BF16)] * 3,
        grid=(units // tile,),
        in_specs=[smem(), rows_spec, rows_spec, weight_spec, weight_spec, unit_spec],
        out_specs=[unit_spec] * 3,
        compiler_params=params(),
        cost_estimate=COST,
        name="mlp",
    )(core, own, far, w_gate, w_up, d_hidden)


def d_middle_kernel(
    hid_ref,
    d_gate_ref,
    d_up_ref,
    w_gate_ref,
    w_up_ref,
    middle_ref,
    add_ref,
    gain_ref,
    hid_came_ref,
    own_ref,
    far_ref,
    gain_out_ref,
    gate_buf,
    up_buf,
    load_sems,
    c_ref,
    mine_ref,
    hid_send,
    hid_recv,
    far_send,
    far_recv,
    *scratch,
    blocks,
):
    device = lax.axis_index("dp")
    core, core_peer, y_peer = tensor_peers()
    x_peer = {"dp": device + 1 - 2 * (device % 2)}
    half = middle_ref.shape[0]
    total = TensorSum(scratch, mine_ref, core, core_peer, y_peer)
    chunks, width = total.chunks, total.width

    def loads(i):
        at = pl.ds(i * width, width)
        return (
            pltpu.make_async_copy(w_gate_ref.at[at, :], gate_buf.at[i], load_sems.at[2 * i]),
            pltpu.make_async_copy(w_up_ref.at[at, :], up_buf.at[i], load_sems.at[2 * i + 1]),
        )

    for i in range(chunks):
        for load in loads(i):
            load.start()
    greet([(x_peer, True), (core_peer, True), (y_peer, True)])
    swap = remote(hid_ref, hid_came_ref, hid_send, hid_recv, x_peer)
    swap.start()
    for i in range(chunks):
        for load in loads(i):
            load.wait()
        total.add(i, dot(d_gate_ref[...], gate_buf[i], NT) + dot(d_up_ref[...], up_buf[i], NT))
    for i in range(chunks):
        c_ref[:, i * width : (i + 1) * width] = total.total(i)

    step = half // blocks

    def to_core(b):
        at = slice(b * step, (b + 1) * step)
        return remote(own_ref.at[at, :], far_ref.at[at, :], far_send.at[b], far_recv.at[b], core_peer)

    gain_out_ref[...] = jnp.zeros_like(gain_out_ref)
    for b in range(blocks):
        at = slice(b * step, (b + 1) * step)
        add_at = pl.ds(pl.multiple_of(core * half + b * step, step), step)
        c = c_ref[at, :]
        v = middle_ref[at, :]
        r = lax.rsqrt(jnp.mean(v * v, axis=1, keepdims=True) + EPS)
        n = v * r
        gain_out_ref[...] += jnp.sum(c * n, axis=0, keepdims=True)
        gc = c * gain_ref[...]
        d = r * (gc - n * jnp.mean(n * gc, axis=1, keepdims=True)) + add_ref[add_at, :].astype(F32)
        own_ref[at, :] = d.astype(BF16)
        to_core(b).start()
    for b in range(blocks):
        to_core(b).wait_recv()
        to_core(b).wait_send()
    total.finish()
    swap.wait_recv()
    swap.wait_send()


def d_middle_of(hidden, d_gate, d_up, w_gate, w_up, middle, out_grad, gain):
    half, model = middle.shape
    units = hidden.shape[1]
    chunks, blocks = 4, 4
    width = model // chunks
    dma = pltpu.SemaphoreType.DMA
    anywhere = pl.BlockSpec(memory_space=pl.ANY)
    return pl.pallas_call(
        functools.partial(d_middle_kernel, blocks=blocks),
        out_shape=[
            jax.ShapeDtypeStruct(hidden.shape, BF16),
            jax.ShapeDtypeStruct((half, model), BF16),
            jax.ShapeDtypeStruct((half, model), BF16),
            jax.ShapeDtypeStruct((1, model), F32),
        ],
        in_specs=vmem(3) + [anywhere] * 2 + vmem(3),
        out_specs=vmem(4),
        scratch_shapes=[pltpu.VMEM((chunks, width, units), BF16)] * 2
        + [dma((2 * chunks,)), pltpu.VMEM((half, model), F32)]
        + [pltpu.VMEM((2, 2 * half, width), F32)]
        + [dma, dma, dma((blocks,)), dma((blocks,))]
        + TensorSum.scratch(chunks, half, width),
        compiler_params=pltpu.CompilerParams(
            vmem_limit_bytes=VMEM_LIMIT, collective_id=2, has_side_effects=True
        ),
        cost_estimate=COST,
        name="d_middle",
    )(hidden, d_gate, d_up, w_gate, w_up, middle, out_grad, gain)


def through_rope(d_ref, raw_ref, gain, cos, sin, out_ref, width, plain):
    columns = d_ref.shape[1]
    total = jnp.zeros((1, width), F32)
    for at in range(0, columns - plain, width):
        d = d_ref[:, at : at + width]
        c = d * cos - roll_half(d) * sin
        v = raw_ref[:, at : at + width]
        r = lax.rsqrt(jnp.mean(v * v, axis=1, keepdims=True) + EPS)
        n = v * r
        total = total + jnp.sum(c * n, axis=0, keepdims=True)
        gc = gain * c
        out_ref[:, at : at + width] = (r * (gc - n * jnp.mean(n * gc, axis=1, keepdims=True))).astype(BF16)
    if plain:
        out_ref[:, columns - plain :] = d_ref[:, columns - plain :].astype(BF16)
    return total


def front_kernel(*refs, dp_size, planes, chunks, sums):
    refs = list(refs)

    def take(count):
        out = refs[:count]
        del refs[:count]
        return out

    dq_in, dkv_in, q_raw, k_raw, q_gain, k_gain, cos_ref, sin_ref = take(8)
    w_q, w_k, w_v, x_ref, mlp_gain_ref, middle_ref, hid_ref, w_down_ref = take(8)
    if sums:
        one_ref, one_came, two_ref, two_came, up_ref, up_came = take(6)
    d_one, block_out, gains, dq_ref, dq_came, dkv_ref, dkv_came = take(7)
    if sums:
        w_up_out, w_q_out, w_kv_out = take(3)
    mine, down_buf, down_sems, gain_came = take(4)
    swap_sems, one_sems, block_sems, gain_sems = take(4), take(2), take(2), take(2)
    one_sum_scratch, out_sum_scratch = take(8), take(8)
    half = x_ref.shape[0] // 2
    model = x_ref.shape[1]
    width = model // chunks
    head = cos_ref.shape[1]
    kv_width = w_k.shape[1]

    device = lax.axis_index("dp")
    core, core_peer, y_peer = tensor_peers()
    x_peer = {"dp": device + 1 - 2 * (device % 2)}
    plane = device // 2
    bits = [1 << i for i in range(dp_size.bit_length() - 1)]
    dp_peers = [{"dp": device + bit - 2 * bit * ((device // bit) % 2)} for bit in bits]
    gain_peers = [core_peer, y_peer] + dp_peers
    meets = [(peer, True) for peer in gain_peers]
    if sums:
        up_sum, q_sum, kv_sum = (LineSum(take(6), device, plane, planes) for _ in range(3))
        meets += [({"dp": device + 2}, plane < planes - 1), ({"dp": device - 2}, plane > 0)]

    def load(i):
        at = pl.ds(i * width, width)
        return pltpu.make_async_copy(w_down_ref.at[:, at], down_buf.at[i % 2], down_sems.at[i])

    load(0).start()
    load(1).start()
    greet(meets)
    if sums:
        up_sum.fill_rows(two_ref, two_came, up_ref, up_came)
        up_sum.start()
    cos, sin = cos_ref[...], sin_ref[...]
    k_total = through_rope(dkv_in, k_raw, k_gain[...], cos, sin, dkv_ref, head, kv_width)
    kv_swap = remote(dkv_ref, dkv_came, swap_sems[0], swap_sems[1], x_peer)
    kv_swap.start()
    q_total = through_rope(dq_in, q_raw, q_gain[...], cos, sin, dq_ref, head, 0)
    q_swap = remote(dq_ref, dq_came, swap_sems[2], swap_sems[3], x_peer)
    q_swap.start()

    one_sum = TensorSum(one_sum_scratch, mine, core, core_peer, y_peer)
    x = x_ref[...].astype(F32)
    r = lax.rsqrt(jnp.mean(x * x, axis=1, keepdims=True) + EPS)
    for i in range(chunks):
        at = slice(i * width, (i + 1) * width)
        part = (
            dot(dq_ref[...], w_q[at, :], NT)
            + dot(dkv_ref[:, :kv_width], w_k[at, :], NT)
            + dot(dkv_ref[:, kv_width:], w_v[at, :], NT)
        )
        one_sum.add(i, part)
        gains[0, :, at] = jnp.sum(part * (x_ref[:, at].astype(F32) * r), axis=0, keepdims=True)
    gains[0, :, model : 2 * model] = mlp_gain_ref[...]
    gains[0, :, 2 * model : 2 * model + head] = q_total
    gains[0, :, 2 * model + head :] = k_total

    def gain_swap(k):
        return remote(
            gains.at[k], gain_came.at[k], gain_sems[0].at[k], gain_sems[1].at[k], gain_peers[k]
        )

    def gain_add(k):
        gain_swap(k).wait_recv()
        gains[k + 1] = gains[k] + gain_came[k]
        if k + 1 < len(gain_peers):
            gain_swap(k + 1).start()

    gain_swap(0).start()

    out_sum = TensorSum(out_sum_scratch, mine, core, core_peer, y_peer)
    for i in range(chunks):
        load(i).wait()
        out_sum.add(i, dot(hid_ref[...], down_buf[i % 2]))
        if i + 2 < chunks:
            load(i + 2).start()
    gain_add(0)
    if sums:
        if planes > 2:
            up_sum.wave(0)
        kv_swap.wait_recv()
        kv_sum.fill_rows(one_ref, one_came, dkv_ref, dkv_came)
        kv_sum.start()
    gain_add(1)
    if sums:
        q_swap.wait_recv()
        q_sum.fill_rows(one_ref, one_came, dq_ref, dq_came)
        q_sum.start()
    gain_add(2)

    mine_rows = rows_of(core, half)

    def give(out, sems):
        rows = out.at[mine_rows, :]
        return remote(rows, rows, sems[0], sems[1], core_peer)

    for i in range(chunks):
        d_one[mine_rows, i * width : (i + 1) * width] = one_sum.total(i).astype(BF16)
    give(d_one, one_sems).start()
    if sums:
        for wave in range(1, planes - 2):
            up_sum.wave(wave)
    for k in range(3, len(gain_peers)):
        gain_add(k)
    for i in range(chunks):
        at = slice(i * width, (i + 1) * width)
        block_out[mine_rows, at] = (middle_ref[:, at] + out_sum.total(i)).astype(BF16)
    give(block_out, block_sems).start()
    if sums:
        for wave in range(planes - 2):
            kv_sum.wave(wave)
            q_sum.wave(wave)
        up_sum.finish(w_up_out)
        kv_sum.finish(w_kv_out)
        q_sum.finish(w_q_out)
    else:
        kv_swap.wait_recv()
        q_swap.wait_recv()
    kv_swap.wait_send()
    q_swap.wait_send()
    for out, sems in ((d_one, one_sems), (block_out, block_sems)):
        give(out, sems).wait_recv()
        give(out, sems).wait_send()
    for k in range(len(gain_peers)):
        gain_swap(k).wait_send()
    one_sum.finish()
    out_sum.finish()


def front(dq, dkv, q_raw, k_raw, q_gain, k_gain, cos, sin, weights, x, mlp_gain, middle, hidden, w_down, grads, dp_size, shard):
    rows, model = x.shape
    half = rows // 2
    planes = dp_size // 2
    chunks = 4
    width = model // chunks
    units = hidden.shape[1]
    stages = dp_size.bit_length() + 1
    dma = pltpu.SemaphoreType.DMA
    gains = (2 * model + 2 * cos.shape[1],)
    args = [dq, dkv, q_raw, k_raw, q_gain, k_gain, cos, sin, *weights, x, mlp_gain, middle, hidden, w_down]
    whole = jax.ShapeDtypeStruct((rows, model), BF16)
    q_shape, kv_shape = jax.ShapeDtypeStruct(dq.shape, BF16), jax.ShapeDtypeStruct(dkv.shape, BF16)
    out_shape = [whole, whole, jax.ShapeDtypeStruct((stages + 1, 1) + gains, F32)]
    out_shape += [q_shape, q_shape, kv_shape, kv_shape]
    scratch = [pltpu.VMEM((2, rows, width), F32), pltpu.VMEM((2, units, width), BF16), dma((chunks,))]
    scratch += [pltpu.VMEM((stages, 1) + gains, F32)]
    scratch += [dma] * 8 + [dma((stages,))] * 2
    scratch += TensorSum.scratch(chunks, half, width) * 2
    if grads is not None:
        args += grads
        for columns in (units, dq.shape[1], dkv.shape[1]):
            out_shape.append(jax.ShapeDtypeStruct((shard, columns), F32))
            scratch += LineSum.scratch(planes, (shard, columns))
    return pl.pallas_call(
        functools.partial(
            front_kernel, dp_size=dp_size, planes=planes, chunks=chunks, sums=grads is not None
        ),
        out_shape=out_shape,
        in_specs=vmem(15) + [pl.BlockSpec(memory_space=pl.ANY)] + vmem(len(args) - 16),
        out_specs=vmem(len(out_shape)),
        scratch_shapes=scratch,
        compiler_params=pltpu.CompilerParams(
            vmem_limit_bytes=BACK_VMEM_LIMIT, collective_id=3, has_side_effects=True
        ),
        cost_estimate=COST,
        name="front",
    )(*args)


def last_kernel(core_ref, d_ref, x_ref, gain_ref, own_ref, far_ref, out_ref, *, steps):
    c = d_ref[...].astype(F32)
    x = x_ref[...].astype(F32)
    r = lax.rsqrt(jnp.mean(x * x, axis=1, keepdims=True) + EPS)
    n = x * r
    gc = c * gain_ref[...]
    d = r * (gc - n * jnp.mean(n * gc, axis=1, keepdims=True))
    mine = (pl.program_id(0) // steps) == core_ref[0]
    out_ref[...] = d + jnp.where(mine, own_ref[...].astype(F32), far_ref[...].astype(F32))


def tokens_grad_of(core, d_one, x, gain, own, far):
    rows, model = x.shape
    half = rows // 2
    tile = math.gcd(half, 128)
    steps = half // tile
    row_spec = pl.BlockSpec((tile, model), lambda i: (i, 0))
    half_spec = pl.BlockSpec((tile, model), lambda i: (i % steps, 0))
    return pl.pallas_call(
        functools.partial(last_kernel, steps=steps),
        out_shape=jax.ShapeDtypeStruct((rows, model), F32),
        grid=(2 * steps,),
        in_specs=[smem(), row_spec, row_spec, pl.BlockSpec((1, model), lambda i: (0, 0))] + [half_spec] * 2,
        out_specs=row_spec,
        compiler_params=params(),
        cost_estimate=COST,
        name="tokens_grad",
    )(core, d_one, x, gain, own, far)


class Chain:
    def __init__(self):
        self.last = None

    def mark(self, value):
        self.last = value

    def __call__(self, *values):
        if self.last is None:
            return values
        return lax.optimization_barrier((*values, self.last))[:-1]


class ZSum:
    def __init__(self, part, dim, shard, planes, z_at):
        self.part, self.dim, self.shard, self.planes, self.z_at = part, dim, shard, planes, z_at
        self.at = 0
        self.came = None

    def term(self, j):
        j = jnp.clip(j, 0, self.planes - 1)
        return lax.dynamic_slice_in_dim(self.part, j * self.shard, self.shard, self.dim)

    def send(self, up, down):
        last = self.planes - 1
        self.at += 1
        up_pairs = [(2 * z + x, 2 * z + 2 + x) for z in range(last) for x in range(2) if z < self.at]
        down_pairs = [
            (2 * (last - z) + x, 2 * (last - 1 - z) + x)
            for z in range(last)
            for x in range(2)
            if z < self.at
        ]
        self.came = lax.ppermute(up, "dp", up_pairs), lax.ppermute(down, "dp", down_pairs)

    def terms(self):
        planes, z_at, at = self.planes, self.z_at, self.at
        return self.term(planes - 1 - at + z_at), self.term(at + 1 - planes + z_at)

    def start(self):
        self.send(*self.terms())

    def step(self, chain):
        if self.at >= self.planes - 1:
            return
        up, down = chain(*self.came)
        up_term, down_term = self.terms()
        up, down = up + up_term, down + down_term
        chain.mark(up)
        self.send(up, down)

    def finish(self, chain):
        if self.at == 0:
            self.start()
        while self.at < self.planes - 1:
            self.step(chain)
        up, down = chain(*self.came)
        total = self.term(self.z_at).astype(F32) + up.astype(F32) + down.astype(F32)
        chain.mark(total)
        return total


def shards(
    dp_size,
    tensor_size,
    tokens,
    norm_attn,
    w_query,
    key_weight,
    value_weight,
    query_gain,
    key_gain,
    w_out,
    norm_mlp,
    w_gate,
    w_up,
    w_down,
    out_grad,
    prefix_len,
):
    rows, model = tokens.shape
    width = query_gain.shape[0]
    kv_heads = key_weight.shape[1] // width
    repeat = w_query.shape[1] // key_weight.shape[1]
    dims = (kv_heads, repeat, width)
    group = dp_size // prefix_len.shape[0]
    planes = dp_size // 2
    group_planes = group // 2
    half = rows // 2
    shard = model // dp_size
    assert tensor_size == 4 and MAX_PREFIX <= 4 * rows

    device = lax.axis_index("dp")
    core = lax.axis_index("tensor") % 2
    x_at = device % 2
    z_at = device // 2
    sequence = device // group
    member = device % group
    plane = member // 2
    prefix = jnp.sum(jnp.where(jnp.arange(prefix_len.shape[0]) == sequence, prefix_len, 0))

    core_pairs = [(t, t ^ 1) for t in range(tensor_size)]
    y_pairs = [(t, t ^ 2) for t in range(tensor_size)]
    x_pairs = [(d, d ^ 1) for d in range(dp_size)]

    def core_swap(value):
        return lax.ppermute(value, "tensor", core_pairs)

    def y_swap(value):
        return lax.ppermute(value, "tensor", y_pairs)

    def x_swap(value):
        return lax.ppermute(value, "dp", x_pairs)

    def plane_of(d):
        return (d % group) // 2

    def own_half(value):
        return lax.dynamic_slice_in_dim(value, core * half, half, 0)

    def other_half(value):
        return lax.dynamic_slice_in_dim(value, (1 - core) * half, half, 0)

    def join(mine, theirs):
        return jnp.where(
            core == 0, jnp.concatenate([mine, theirs], 0), jnp.concatenate([theirs, mine], 0)
        )

    positions = (member * rows + jnp.arange(rows)).astype(F32)
    counter = jnp.arange(width // 2, dtype=F32)
    angles = positions[:, None] * (ROPE_BASE ** (-2.0 * counter / width))[None, :]
    cos, sin = jnp.cos(angles), jnp.sin(angles)
    cos = jnp.concatenate([cos, cos], axis=1)
    sin = jnp.concatenate([-sin, sin], axis=1)
    norm_attn_row = norm_attn[None, :]
    norm_mlp_row = norm_mlp[None, :]
    q_gain_row = query_gain[None, :]
    k_gain_row = key_gain[None, :]

    core_at = core[None].astype(jnp.int32)
    core_not = 1 - core_at
    h_one, qkv, q_raw, k_raw = project(
        tokens,
        norm_attn_row,
        (w_query, key_weight, value_weight),
        (q_gain_row, k_gain_row, k_gain_row),
        (True, True, False),
        cos,
        sin,
        "project",
    )
    q = qkv[:, : w_query.shape[1]]
    kv = qkv[:, w_query.shape[1] :]
    prefix_at = prefix[None].astype(jnp.int32)
    heads_b, lse, kv_all = attn_fwd(prefix_at, q, kv, group, dims)
    chain = Chain()

    away = dot(other_half(heads_b), w_out).astype(BF16)
    came = core_swap(away)
    both = (dot(own_half(heads_b), w_out) + came.astype(F32)).astype(BF16)
    chain.mark(both)
    y_came = y_swap(both)
    (og,) = chain(out_grad)
    og_keep, og_send = cut(x_at, core, [og], planes, shard, join)
    og_came = x_swap(og_send)
    chain.mark(og_keep)
    d_hidden = dot(chain(out_grad)[0], w_down, NT)
    chain.mark(d_hidden)
    h_one_keep, h_one_send = cut(x_at, core, chain(h_one), planes, shard, join)
    h_one_came = x_swap(h_one_send)
    chain.mark(h_one_keep)
    middle, h_two_half = norm_forward(core_at, both, *chain(y_came), tokens, norm_mlp_row)
    chain.mark(h_two_half)
    h_two_far = core_swap(h_two_half)
    og_came = join(og_came, core_swap(og_came))
    h_one_came = join(h_one_came, core_swap(h_one_came))
    hidden, d_gate, d_up = mlp(core_at, h_two_half, *chain(h_two_far), w_gate, w_up, d_hidden)
    chain.mark(hidden)

    hidden_came, d_attn_half, d_attn_far, norm_mlp_part = d_middle_of(
        hidden, d_gate, d_up, w_gate, w_up, middle, out_grad, norm_mlp_row
    )
    chain.mark(d_attn_far)
    qx, dox = attn_prep(core_at, d_attn_half, d_attn_far, w_out, q, heads_b, lse, width)
    chain.mark(dox)

    fused = planes == group_planes and shard % 128 == 0
    shared = [h_two_half, h_two_far, d_attn_half, d_attn_far, heads_b, d_up]
    grads = [hidden, hidden_came, og_keep, og_came, d_gate] if fused else None
    outs = back(prefix_at, qx, *chain(dox), kv_all, shared, grads, group, planes, shard, dims)
    dq, kv_grad, h_two_keep, h_two_came, d_attn_keep, d_attn_came, heads_came, up_came = outs[:8]
    chain.mark(dq)
    if fused:
        w_down_grad, w_gate_grad, w_out_grad = outs[8:]
    else:
        down_part = (dot(hidden, og_keep, TN) + dot(hidden_came, og_came, TN)).astype(BF16)
        w_down_grad = ZSum(down_part, 1, shard, planes, z_at).finish(chain)
        gate_part = dot(h_two_keep, d_gate, TN) + dot(h_two_came, x_swap(d_gate), TN)
        w_gate_grad = ZSum(gate_part.astype(BF16), 0, shard, planes, z_at).finish(chain)
        out_part = dot(heads_b, d_attn_keep, TN) + dot(heads_came, d_attn_came, TN)
        w_out_grad = ZSum(out_part.astype(BF16), 1, shard, planes, z_at).finish(chain)

    up_grads = [h_one_keep, h_one_came, h_two_keep, h_two_came, d_up, up_came] if fused else None
    outs = front(
        *chain(dq),
        kv_grad,
        q_raw,
        k_raw,
        q_gain_row,
        k_gain_row,
        cos,
        sin,
        (w_query, key_weight, value_weight),
        tokens,
        0.5 * norm_mlp_part,
        middle,
        hidden,
        w_down,
        up_grads,
        dp_size,
        shard,
    )
    d_h_one, block_out, gains, dq_b, dq_came, dkv_b, dkv_came = outs[:7]
    if fused:
        w_up_grad, w_query_grad, w_kv_grad = outs[7:]
    else:
        chain.mark(d_h_one)

        def by_rows(left, left_came, right, right_came):
            part = dot(left, right, TN) + dot(left_came, right_came, TN)
            return ZSum(part.astype(BF16), 0, shard, planes, z_at).finish(chain)

        w_up_grad = by_rows(h_two_keep, h_two_came, d_up, up_came)
        w_query_grad = by_rows(h_one_keep, h_one_came, dq_b, dq_came)
        w_kv_grad = by_rows(h_one_keep, h_one_came, dkv_b, dkv_came)
    kv_width = kv_heads * width
    tokens_grad = tokens_grad_of(core_at, d_h_one, tokens, norm_attn_row, d_attn_half, d_attn_far)
    gains = gains[-1, 0]
    return (
        block_out,
        tokens_grad,
        lax.dynamic_slice_in_dim(gains, device * shard, shard, 0),
        w_query_grad,
        w_kv_grad[:, :kv_width],
        w_kv_grad[:, kv_width:],
        gains[2 * model : 2 * model + width],
        gains[2 * model + width :],
        w_out_grad,
        lax.dynamic_slice_in_dim(gains, model + device * shard, shard, 0),
        w_gate_grad,
        w_up_grad,
        w_down_grad,
    )


def solution(mesh):
    placed = (
        P("dp", None),
        P(),
        P(None, "tensor"),
        P(None, "tensor"),
        P(None, "tensor"),
        P(),
        P(),
        P("tensor", None),
        P(),
        P(None, "tensor"),
        P(None, "tensor"),
        P("tensor", None),
        P("dp", None),
        P(),
    )
    return jax.shard_map(
        functools.partial(shards, mesh.shape["dp"], mesh.shape["tensor"]),
        mesh=mesh,
        in_specs=placed,
        out_specs=(
            P("dp", None),
            P("dp", None),
            P("dp"),
            P("dp", "tensor"),
            P("dp", "tensor"),
            P("dp", "tensor"),
            P(),
            P(),
            P("tensor", "dp"),
            P("dp"),
            P("dp", "tensor"),
            P("dp", "tensor"),
            P("tensor", "dp"),
        ),
        check_vma=False,
    )
```

```python
import functools
import math

import jax
import jax.numpy as jnp
from jax import lax
from jax.experimental import pallas as pl
from jax.experimental.pallas import tpu as pltpu
from jax.sharding import PartitionSpec as P

F32 = jnp.float32
BF16 = jnp.bfloat16
EPS = 1e-06
ROPE_BASE = 1000000.0
MAX_PREFIX = 2048
VMEM_LIMIT = 56 * 2**20
BACK_VMEM_LIMIT = 60 * 2**20

COST = pl.CostEstimate(flops=1000, bytes_accessed=1000, transcendentals=0)

NN = (((1,), (0,)), ((), ()))
NT = (((1,), (1,)), ((), ()))
TN = (((0,), (0,)), ((), ()))


def dot(left, right, dims=NN):
    return lax.dot_general(left, right, dims, preferred_element_type=F32)


def vmem(count):
    return [pl.BlockSpec(memory_space=pltpu.VMEM)] * count


def params():
    return pltpu.CompilerParams(vmem_limit_bytes=VMEM_LIMIT)


def greet(peers):
    barrier = pltpu.get_barrier_semaphore()
    count = 0
    for peer, there in peers:

        def signal(peer=peer):
            pl.semaphore_signal(barrier, 1, device_id=peer, device_id_type=pl.DeviceIdType.MESH)

        if there is True:
            signal()
            count = count + 1
        else:
            pl.when(there)(signal)
            count = count + there.astype(jnp.int32)
    pl.semaphore_wait(barrier, count)


def remote(src, dst, send, recv, peer):
    return pltpu.make_async_remote_copy(
        src_ref=src,
        dst_ref=dst,
        send_sem=send,
        recv_sem=recv,
        device_id=peer,
        device_id_type=pl.DeviceIdType.MESH,
    )


class Staged:
    def __init__(self, arrays, buffers, sems, out=False):
        self.copies = []
        for i, (array, buffer) in enumerate(zip(arrays, buffers)):
            ends = (buffer, array) if out else (array, buffer)
            self.copies.append((buffer, pltpu.make_async_copy(*ends, sems.at[i])))

    @staticmethod
    def scratch(shapes):
        return [pltpu.VMEM(s.shape, s.dtype) for s in shapes] + [pltpu.SemaphoreType.DMA((len(shapes),))]

    def start(self, *buffers):
        for buffer, copy in self.copies:
            if not buffers or any(buffer is b for b in buffers):
                copy.start()

    def wait(self, *buffers):
        for buffer, copy in self.copies:
            if not buffers or any(buffer is b for b in buffers):
                copy.wait()


ANYWHERE = pl.BlockSpec(memory_space=pl.ANY)


def tensor_peers():
    t = lax.axis_index("tensor")
    core = t % 2
    y = t // 2
    return core, {"tensor": t + 1 - 2 * core}, {"tensor": t + 2 - 4 * y}


def rows_of(core, half):
    return pl.ds(pl.multiple_of(core * half, half), half)


def cut_into(out, out_rows, ref, ref_rows, side, planes, shard):
    for z in range(planes):
        to = slice(z * shard, (z + 1) * shard)
        if shard % 128 == 0:
            at = pl.ds(pl.multiple_of((2 * z + side) * shard, shard), shard)
            out[out_rows, to] = ref[ref_rows, at]
        else:
            low = ref[ref_rows, 2 * z * shard : (2 * z + 1) * shard]
            high = ref[ref_rows, (2 * z + 1) * shard : (2 * z + 2) * shard]
            out[out_rows, to] = jnp.where(side == 0, low, high)


class Columns:
    def __init__(self, whole, keep, came, scratch, x_at, core, x_peer, core_peer, planes, shard):
        self.whole, self.keep, self.came = whole, keep, came
        self.send_ref, self.recv_ref, self.sems = scratch[0], scratch[1], scratch[2:]
        self.x_at, self.core, self.cut = x_at, core, (planes, shard)
        self.x_peer, self.core_peer = x_peer, core_peer
        self.half = whole.shape[0] // 2

    @staticmethod
    def scratch(half, columns):
        return [pltpu.VMEM((half, columns), BF16)] * 2 + [pltpu.SemaphoreType.DMA] * 4

    def over_x(self):
        return remote(self.send_ref, self.recv_ref, self.sems[0], self.sems[1], self.x_peer)

    def over_core(self):
        there = self.came.at[rows_of(self.core, self.half), :]
        return remote(self.recv_ref, there, self.sems[2], self.sems[3], self.core_peer)

    def start(self):
        mine = rows_of(self.core, self.half)
        cut_into(self.send_ref, slice(None), self.whole, mine, 1 - self.x_at, *self.cut)
        self.over_x().start()

    def store(self):
        cut_into(self.keep, slice(None), self.whole, slice(None), self.x_at, *self.cut)

    def forward(self):
        self.over_x().wait_recv()
        self.over_core().start()
        self.came[rows_of(self.core, self.half), :] = self.recv_ref[...]

    def finish(self):
        self.over_core().wait_recv()
        self.over_x().wait_send()
        self.over_core().wait_send()


class LineSum:
    def __init__(self, scratch, device, plane, planes):
        self.stack, self.came = scratch[:2]
        self.sems = scratch[2:]
        self.device, self.plane, self.planes = device, plane, planes

    @staticmethod
    def scratch(planes, shape):
        return [pltpu.VMEM((n,) + shape, BF16) for n in (planes, planes + 1)] + [
            pltpu.SemaphoreType.DMA((planes,))
        ] * 4

    def up(self, j):
        s = self.sems
        peer = {"dp": self.device + 2}
        return remote(self.stack.at[j], self.came.at[j], s[0].at[j], s[1].at[j], peer)

    def down(self, j):
        s = self.sems
        slot = jnp.where(self.plane - 1 == j, self.planes, j)
        peer = {"dp": self.device - 2}
        return remote(self.stack.at[j], self.came.at[slot], s[2].at[j], s[3].at[j], peer)

    def start(self):
        last = self.planes - 1

        @pl.when(self.plane == 0)
        def _():
            for j in range(last, 0, -1):
                self.up(j).start()

        @pl.when(self.plane == last)
        def _():
            for j in range(last):
                self.down(j).start()

    def wave(self, i):
        last = self.planes - 1
        j = last - i

        @pl.when((self.plane > 0) & (self.plane < j))
        def _():
            self.up(j).wait_recv()
            self.stack[j] += self.came[j]
            self.up(j).start()

        @pl.when((self.plane < last) & (self.plane > i))
        def _():
            self.down(i).wait_recv()
            self.stack[i] += self.came[i]
            self.down(i).start()

    def finish(self, out):
        plane, planes = self.plane, self.planes
        out[...] = self.stack[plane].astype(F32)

        @pl.when(plane > 0)
        def _():
            self.up(plane).wait_recv()
            out[...] += self.came[plane].astype(F32)

        @pl.when(plane < planes - 1)
        def _():
            self.down(plane).wait_recv()
            out[...] += self.came[planes].astype(F32)

        for j in range(planes):
            pl.when(plane < j)(lambda j=j: self.up(j).wait_send())
            pl.when(plane > j)(lambda j=j: self.down(j).wait_send())

    def fill_rows(self, left, left_came, right, right_came):
        shard = self.stack.shape[1]

        def body(j, carry):
            at = pl.ds(pl.multiple_of(j * shard, shard), shard)
            self.stack[j] = (
                dot(left[:, at], right[...], TN) + dot(left_came[:, at], right_came[...], TN)
            ).astype(BF16)
            return carry

        lax.fori_loop(0, self.planes, body, 0)

    def fill_columns(self, left, left_came, right, right_came):
        shard = self.stack.shape[2]
        tile = 256

        def body(t, carry):
            at = pl.ds(pl.multiple_of(t * tile, tile), tile)
            term = dot(left[:, at], right[...], TN) + dot(left_came[:, at], right_came[...], TN)
            for j in range(self.planes):
                self.stack[j, at, :] = term[:, j * shard : (j + 1) * shard].astype(BF16)
            return carry

        lax.fori_loop(0, left.shape[1] // tile, body, 0)


class TensorSum:
    def __init__(self, scratch, mine, core, core_peer, y_peer):
        self.away, self.core_came, self.both, self.y_came = scratch[:4]
        self.sems = scratch[4:]
        self.mine = mine
        self.core, self.core_peer, self.y_peer = core, core_peer, y_peer
        self.chunks, self.half, self.width = self.away.shape

    @staticmethod
    def scratch(chunks, half, width):
        return [pltpu.VMEM((chunks, half, width), BF16)] * 4 + [
            pltpu.SemaphoreType.DMA((chunks,))
        ] * 4

    def over_core(self, i):
        s = self.sems
        return remote(self.away.at[i], self.core_came.at[i], s[0].at[i], s[1].at[i], self.core_peer)

    def over_y(self, i):
        s = self.sems
        return remote(self.both.at[i], self.y_came.at[i], s[2].at[i], s[3].at[i], self.y_peer)

    def add(self, i, value):
        self.mine[i % 2] = value
        self.away[i] = self.mine[i % 2, rows_of(1 - self.core, self.half), :].astype(BF16)
        self.over_core(i).start()
        if i > 0:
            self.pass_on(i - 1)
        if i == self.chunks - 1:
            self.pass_on(i)

    def pass_on(self, i):
        self.over_core(i).wait_recv()
        mine = self.mine[i % 2, rows_of(self.core, self.half), :]
        self.both[i] = (mine + self.core_came[i].astype(F32)).astype(BF16)
        self.over_y(i).start()

    def total(self, i):
        self.over_y(i).wait_recv()
        return self.both[i].astype(F32) + self.y_came[i].astype(F32)

    def finish(self):
        for i in range(self.chunks):
            self.over_core(i).wait_send()
            self.over_y(i).wait_send()


def roll_half(value):
    return pltpu.roll(value, value.shape[-1] // 2, 1)


def project_kernel(x_ref, g_ref, *refs, heads, normed, width):
    count = len(heads)
    w_refs = refs[:count]
    gain_refs = refs[count : 2 * count]
    cos_ref, sin_ref = refs[2 * count : 2 * count + 2]
    h_ref, q_ref, kv_ref = refs[2 * count + 2 : 2 * count + 5]
    raw_refs = refs[2 * count + 5 :]
    x = x_ref[...].astype(F32)
    h = (x * lax.rsqrt(jnp.mean(x * x, axis=1, keepdims=True) + EPS) * g_ref[...]).astype(BF16)
    h_ref[...] = h
    cos, sin = cos_ref[...], sin_ref[...]
    column = 0
    raw_at = 0
    for i in range(count):
        out_ref = q_ref if i == 0 else kv_ref
        column = 0 if i < 2 else column
        product = dot(h, w_refs[i][...])
        if normed[i]:
            raw_refs[raw_at][...] = product
            raw_at += 1
        for j in range(heads[i]):
            u = product[:, j * width : (j + 1) * width]
            if normed[i]:
                u = u * lax.rsqrt(jnp.mean(u * u, axis=1, keepdims=True) + EPS) * gain_refs[i][...]
                u = u * cos + roll_half(u) * sin
            out_ref[:, column : column + width] = u.astype(BF16)
            column += width


def project(x, gain, weights, gains, normed, cos, sin, name):
    rows, model = x.shape
    width = cos.shape[1]
    heads = tuple(w.shape[1] // width for w in weights)
    columns = sum(w.shape[1] for w in weights)
    raws = [w for w, n in zip(weights, normed) if n]
    return pl.pallas_call(
        functools.partial(project_kernel, heads=heads, normed=normed, width=width),
        out_shape=[
            jax.ShapeDtypeStruct((rows, model), BF16),
            jax.ShapeDtypeStruct((rows, weights[0].shape[1]), BF16),
            jax.ShapeDtypeStruct((rows, columns - weights[0].shape[1]), BF16),
        ]
        + [jax.ShapeDtypeStruct((rows, w.shape[1]), F32) for w in raws],
        in_specs=vmem(4 + 2 * len(weights)),
        out_specs=vmem(3 + len(raws)),
        compiler_params=params(),
        cost_estimate=COST,
        name=name,
    )(x, gain, *weights, *gains, cos, sin)


def visible(shape, key0, row0, prefix):
    key_pos = key0 + lax.broadcasted_iota(jnp.int32, shape, 1)
    row_pos = row0 + lax.broadcasted_iota(jnp.int32, shape, 0)
    return (key_pos <= row_pos) | (key_pos < prefix)


def attn_fwd_kernel(
    prefix_ref,
    q_ref,
    kv_ref,
    o_ref,
    lse_ref,
    all_ref,
    acc,
    send_x,
    recv_x,
    send_z,
    recv_z,
    send_down,
    *,
    group,
    kv_heads,
    repeat,
    width,
    tile,
    coef,
):
    rows = q_ref.shape[0]
    kv_width = kv_heads * width
    planes = group // 2
    device = lax.axis_index("dp")
    member = device % group
    plane = member // 2
    x_at = member % 2
    x_other = device + 1 - 2 * x_at
    inner = plane < planes - 1
    prefix = prefix_ref[0]

    barrier = pltpu.get_barrier_semaphore()
    pl.semaphore_signal(barrier, 1, device_id={"dp": x_other}, device_id_type=pl.DeviceIdType.MESH)

    @pl.when(inner)
    def _():
        pl.semaphore_signal(
            barrier, 1, device_id={"dp": device + 2}, device_id_type=pl.DeviceIdType.MESH
        )

    @pl.when(plane > 0)
    def _():
        pl.semaphore_signal(
            barrier, 1, device_id={"dp": device - 2}, device_id_type=pl.DeviceIdType.MESH
        )

    pl.semaphore_wait(barrier, 1 + inner.astype(jnp.int32) + (plane > 0).astype(jnp.int32))

    def source(slot):
        return kv_ref if slot == 0 else all_ref.at[2 * slot]

    def to_x(slot):
        return pltpu.make_async_remote_copy(
            src_ref=source(slot),
            dst_ref=all_ref.at[2 * slot + 1],
            send_sem=send_x.at[slot],
            recv_sem=recv_x.at[slot],
            device_id={"dp": x_other},
            device_id_type=pl.DeviceIdType.MESH,
        )

    def to_z(slot):
        return pltpu.make_async_remote_copy(
            src_ref=source(slot - 1),
            dst_ref=all_ref.at[2 * slot],
            send_sem=send_z.at[slot],
            recv_sem=recv_z.at[slot],
            device_id={"dp": device + 2},
            device_id_type=pl.DeviceIdType.MESH,
        )

    def to_first():
        return pltpu.make_async_remote_copy(
            src_ref=kv_ref,
            dst_ref=all_ref.at[2],
            send_sem=send_down,
            recv_sem=recv_z.at[1],
            device_id={"dp": device - 2},
            device_id_type=pl.DeviceIdType.MESH,
        )

    all_ref[0] = kv_ref[...]
    ones = jnp.ones((rows, width), BF16)
    row0 = member * rows

    def work(block, other, masked, start=False):
        key0 = other * rows

        def head_pair(h, carry):
            k = block[:, pl.ds(pl.multiple_of(h * width, width), width)]
            v = block[:, pl.ds(pl.multiple_of(kv_width + h * width, width), width)]
            v = jnp.concatenate([v, ones], axis=1)
            for g in range(repeat):
                head = h * repeat + g
                for at in range(0, rows, tile):
                    q = q_ref[at : at + tile, pl.ds(pl.multiple_of(head * width, width), width)]
                    p = jnp.exp2(dot(q, k, NT) * coef)
                    if masked:
                        p = jnp.where(visible(p.shape, key0, row0 + at, prefix), p, 0.0)
                    term = dot(p.astype(BF16), v)
                    if start:
                        acc[head, at : at + tile, :] = term
                    else:
                        acc[head, at : at + tile, :] += term
            return carry

        lax.fori_loop(0, kv_heads, head_pair, 0)

    to_x(0).start()
    if planes > 1:

        @pl.when(inner)
        def _():
            to_z(1).start()

        @pl.when(plane == 1)
        def _():
            to_first().start()

    work(kv_ref, member, True, True)
    to_x(0).wait_recv()
    work(all_ref.at[1], member + 1 - 2 * x_at, True)
    for slot in range(1, planes):

        def step(slot=slot):
            to_z(slot).wait_recv()
            if slot < planes - 1:

                @pl.when(inner & (plane >= slot))
                def _():
                    to_z(slot + 1).start()

            to_x(slot).start()
            there = 2 * (plane - slot)
            if slot == 1:

                @pl.when(plane == 0)
                def _():
                    work(all_ref.at[2 * slot], 2 + x_at, True)

                @pl.when(plane > 0)
                def _():
                    work(all_ref.at[2 * slot], there + x_at, False)
            else:
                work(all_ref.at[2 * slot], there + x_at, False)
            to_x(slot).wait_recv()
            if slot == 1:

                @pl.when(plane == 0)
                def _():
                    work(all_ref.at[2 * slot + 1], 3 - x_at, True)

                @pl.when(plane > 0)
                def _():
                    work(all_ref.at[2 * slot + 1], there + 1 - x_at, False)
            else:
                work(all_ref.at[2 * slot + 1], there + 1 - x_at, False)

        if slot == 1:
            step()
        else:
            pl.when(plane >= slot)(step)

    for head in range(kv_heads * repeat):
        total = acc[head, :, width:]
        o_ref[:, head * width : (head + 1) * width] = (acc[head, :, :width] / total).astype(BF16)
        lse_ref[:, head * width : (head + 1) * width] = jnp.log2(total) * (1.0 / coef)

    to_x(0).wait_send()
    for slot in range(1, planes):

        @pl.when(inner & (plane >= slot - 1))
        def _(slot=slot):
            to_z(slot).wait_send()

        @pl.when((plane >= slot) | (slot == 1))
        def _(slot=slot):
            to_x(slot).wait_send()

    if planes > 1:

        @pl.when(plane == 1)
        def _():
            to_first().wait_send()


def attn_fwd(prefix, q, kv, group, dims):
    kv_heads, repeat, width = dims
    rows = q.shape[0]
    heads = kv_heads * repeat
    columns = heads * width
    planes = group // 2
    return pl.pallas_call(
        functools.partial(
            attn_fwd_kernel,
            group=group,
            kv_heads=kv_heads,
            repeat=repeat,
            width=width,
            tile=min(rows, 256),
            coef=math.log2(math.e) / math.sqrt(width),
        ),
        out_shape=[
            jax.ShapeDtypeStruct((rows, columns), BF16),
            jax.ShapeDtypeStruct((rows, columns), F32),
            jax.ShapeDtypeStruct((group,) + kv.shape, BF16),
        ],
        in_specs=[pl.BlockSpec(memory_space=pltpu.SMEM)] + vmem(2),
        out_specs=vmem(3),
        scratch_shapes=[pltpu.VMEM((heads, rows, 2 * width), F32)]
        + [pltpu.SemaphoreType.DMA((planes,))] * 4
        + [pltpu.SemaphoreType.DMA],
        compiler_params=pltpu.CompilerParams(
            vmem_limit_bytes=VMEM_LIMIT, collective_id=0, has_side_effects=True
        ),
        cost_estimate=COST,
        name="attn_fwd",
    )(prefix, q, kv)


def split_three(value):
    high = value.astype(BF16)
    left = value - high.astype(F32)
    mid = left.astype(BF16)
    return high.astype(F32), mid.astype(F32), (left - mid.astype(F32)).astype(BF16).astype(F32)


def back_kernel(
    *refs, group, planes, all_planes, shard, kv_heads, repeat, width, coef, scale, sums
):
    refs = list(refs)

    def take(count):
        out = refs[:count]
        del refs[:count]
        return out

    device = lax.axis_index("dp")
    member = device % group
    plane = member // 2
    last = planes - 1
    prefix_ref, up_ref = take(2)
    if sums:
        hid_arrays = take(2)
    count = 11 if sums else 4
    arrays = take(count)
    dq_ref, grad_ref, a_ref, a_came_ref, up_came_ref = take(5)
    if sums:
        w_down_ref, w_gate_ref, w_out_ref = take(3)
    if sums:
        hid_ref, hid_came_ref = hid_buffers = take(2)
        hid_sems = take(1)[0]
    buffers = take(count)
    inputs = Staged(arrays, buffers, *take(1))
    a_all_ref, qx_ref, dox_ref, kv_ref = buffers[:4]
    if sums:
        og_ref, og_came_ref, gate_ref, h_ref, h_came_ref, heads_ref, heads_came_ref = buffers[4:]
    own_ref, far_ref, xr_ref, zr_ref, first_ref = take(5)
    send_x, recv_x, send_z, recv_z, send_first, recv_first = take(6)
    swap_sems = take(2)
    a_scratch = take(6)
    rows = qx_ref.shape[1]
    kv_width = kv_heads * width
    if sums:
        gate_came_ref, send_gate, recv_gate = take(3)
        left = w_down_ref.shape[0]
        rest = pl.ds(hid_arrays[0].shape[1] - left, left)
        hid_inputs = Staged([h.at[:, rest] for h in hid_arrays], hid_buffers, hid_sems)
        down_sum, out_sum = (LineSum(take(6), device, plane, planes) for _ in range(2))
        piece = gate_came_ref.shape[2]
        pieces = gate_ref.shape[1] // piece
        gate_sums = [LineSum(take(6), device, plane, planes) for _ in range(pieces)]
    x_at = member % 2
    x_other = device + 1 - 2 * x_at
    inner = plane < last
    prefix = prefix_ref[0]

    core, core_peer, _ = tensor_peers()
    x_peer = {"dp": x_other}
    inputs.start(a_all_ref)
    if sums:
        hid_inputs.start()
        inputs.start(*buffers[4:6])
    inputs.start(*buffers[1:4])
    if sums:
        inputs.start(*buffers[6:])
    greet(
        [(x_peer, True), (core_peer, True), ({"dp": device + 2}, inner), ({"dp": device - 2}, plane > 0)]
    )

    def copy(src, dst, send, recv, there):
        return remote(src, dst, send, recv, {"dp": there})

    place = (x_at, core, x_peer, core_peer, all_planes, shard)
    d_attn = Columns(a_all_ref, a_ref, a_came_ref, a_scratch, *place)
    up_swap = copy(up_ref, up_came_ref, swap_sems[0], swap_sems[1], x_other)

    def gate_swap(k):
        part = gate_ref.at[:, pl.ds(k * piece, piece)]
        return copy(part, gate_came_ref.at[k], send_gate.at[k], recv_gate.at[k], x_other)

    def gate_start(k):
        gate_swap(k).wait_recv()
        part = gate_ref.at[:, pl.ds(k * piece, piece)]
        gate_sums[k].fill_rows(h_ref, h_came_ref, part, gate_came_ref.at[k])
        gate_sums[k].start()

    lane = lax.broadcasted_iota(jnp.int32, (rows, width), 1)
    minus = jnp.where(lane < 3, -1.0, 0.0).astype(BF16)
    row0 = member * rows

    def work(block, other, masked, out):
        key0 = other * rows

        def head_group(h, carry):
            k_at = pl.ds(pl.multiple_of(h * width, width), width)
            v_at = pl.ds(pl.multiple_of(kv_width + h * width, width), width)
            k = kv_ref[block, :, k_at]
            v = kv_ref[block, :, v_at]
            kx = jnp.concatenate([k, minus], axis=1)
            vx = jnp.concatenate([v, minus], axis=1)
            dk = jnp.zeros((rows, width), F32)
            dv = jnp.zeros((rows, width), F32)
            for g in range(repeat):
                head = h * repeat + g
                qx = qx_ref[head]
                dox = dox_ref[head]
                p = jnp.exp2(dot(qx, kx, NT) * coef)
                if masked:
                    p = jnp.where(visible(p.shape, key0, row0, prefix), p, 0.0)
                ds = (p * dot(dox, vx, NT)).astype(BF16)
                dv += dot(p.astype(BF16), dox[:, :width], TN)
                dk += dot(ds, qx[:, :width], TN)
                dq_ref[:, pl.ds(pl.multiple_of(head * width, width), width)] += dot(ds, k)
            out[:, k_at] = (dk * scale).astype(BF16)
            out[:, v_at] = dv.astype(BF16)
            return carry

        lax.fori_loop(0, kv_heads, head_group, 0)

    def far_swap(slot):
        return copy(far_ref.at[slot], xr_ref.at[slot], send_x.at[slot], recv_x.at[slot], x_other)

    def to_plane(slot):
        return copy(own_ref.at[slot], zr_ref.at[slot], send_z.at[slot], recv_z.at[slot], device - 2)

    def from_first():
        return copy(own_ref.at[1], first_ref, send_first, recv_first, device + 2)

    def attend(slot):
        there = 2 * (plane - slot)
        far, own = there + 1 - x_at, there + x_at

        def both(far, own, masked):
            work(2 * slot + 1, far, masked, far_ref.at[slot])
            far_swap(slot).start()
            work(2 * slot, own, masked, own_ref.at[slot])

        if slot == 0:
            both(far, own, True)
        elif slot == 1:
            pl.when(plane == 0)(lambda: both(3 - x_at, 2 + x_at, True))
            pl.when(plane > 0)(lambda: both(far, own, False))
        else:
            pl.when(plane >= slot)(lambda: both(far, own, False))

    def pass_back(slot):
        def go():
            far_swap(slot).wait_recv()
            own_ref[slot] += xr_ref[slot]
            if slot < last:

                @pl.when(inner & (plane >= slot))
                def _():
                    to_plane(slot + 1).wait_recv()
                    own_ref[slot] += zr_ref[slot + 1]

            if slot == 1:
                pl.when(plane == 0)(lambda: from_first().start())
                pl.when(plane > 0)(lambda: to_plane(slot).start())
            else:
                to_plane(slot).start()

        if slot == 1:
            go()
        else:
            pl.when(plane >= slot)(go)

    dq_ref[...] = jnp.zeros_like(dq_ref)
    inputs.wait(a_all_ref)
    d_attn.start()
    if sums:
        hid_inputs.wait()
        inputs.wait(og_ref, og_came_ref)
        down_sum.fill_columns(hid_ref, hid_came_ref, og_ref, og_came_ref)
        down_sum.start()
    inputs.wait(*buffers[1:4])
    attend(last)
    d_attn.forward()
    if sums:
        inputs.wait(*buffers[6:])
        gate_swap(0).start()
    d_attn.store()
    pending = list(range(last, 0, -1))
    waves = range(max(last - 1, 0))
    for slot in range(last - 1, -1, -1):
        attend(slot)
        if slot == last - 1:
            if sums:
                d_attn.over_core().wait_recv()
                out_sum.fill_columns(heads_ref, heads_came_ref, a_ref, a_came_ref)
                out_sum.start()
                down_sum.wave(0)
                gate_start(0)
                gate_swap(1).start()
            pass_back(pending.pop(0))
        if slot == last - 2:
            if sums:
                for wave in waves[1:]:
                    down_sum.wave(wave)
                out_sum.wave(0)
                gate_start(1)
                gate_swap(2).start()
                gate_sums[0].wave(0)
            pass_back(pending.pop(0))
    if sums:
        for wave in waves[1:]:
            out_sum.wave(wave)
            gate_sums[0].wave(wave)
    while pending:
        pass_back(pending.pop(0))
    if sums:
        gate_start(2)
    up_swap.start()
    if sums:
        for k in (1, 2):
            for wave in waves:
                gate_sums[k].wave(wave)
    dq_ref[...] = dq_ref[...] * scale

    far_swap(0).wait_recv()
    grad_ref[...] = own_ref[0].astype(F32) + xr_ref[0].astype(F32)
    if last > 0:

        @pl.when(inner)
        def _():
            to_plane(1).wait_recv()
            grad_ref[...] += zr_ref[1].astype(F32)

        @pl.when(plane == 1)
        def _():
            from_first().wait_recv()
            grad_ref[...] += first_ref[...].astype(F32)

    if sums:
        down_sum.finish(w_down_ref)
        out_sum.finish(w_out_ref)
        for k in range(pieces):
            gate_sums[k].finish(w_gate_ref.at[:, pl.ds(k * piece, piece)])
            gate_swap(k).wait_send()
    else:
        d_attn.over_core().wait_recv()
    up_swap.wait_recv()
    up_swap.wait_send()
    d_attn.over_x().wait_send()
    d_attn.over_core().wait_send()
    for slot in range(planes):
        if slot <= 1:
            far_swap(slot).wait_send()
        else:
            pl.when(plane >= slot)(lambda slot=slot: far_swap(slot).wait_send())
        if slot >= 1:
            pl.when(plane >= slot)(lambda slot=slot: to_plane(slot).wait_send())
    if last > 0:
        pl.when(plane == 0)(lambda: from_first().wait_send())


def back(prefix, qx, dox, kv_all, shared, grads, group, all_planes, shard, pieces, dims):
    kv_heads, repeat, width = dims
    rows = qx.shape[1]
    columns = kv_heads * repeat * width
    planes = group // 2
    block = kv_all.shape[1:]
    dma = pltpu.SemaphoreType.DMA
    d_up = shared[1]
    units = d_up.shape[1]
    cut_shape = jax.ShapeDtypeStruct((rows, all_planes * shard), BF16)
    out_shape = [jax.ShapeDtypeStruct((rows, columns), F32), jax.ShapeDtypeStruct(block, F32)]
    out_shape += [cut_shape] * 2 + [jax.ShapeDtypeStruct(d_up.shape, BF16)]
    scratch = [pltpu.VMEM((planes,) + block, BF16)] * 4 + [pltpu.VMEM(block, BF16)]
    scratch += [dma((planes,))] * 4 + [dma, dma] + [dma] * 2
    scratch += Columns.scratch(rows // 2, all_planes * shard)
    d_attn, d_up = shared
    staged = [d_attn, qx, dox, kv_all]
    args = [prefix, d_up]
    first = []
    if grads is not None:
        args += grads[:2]
        staged += grads[2:]
        first = [pltpu.VMEM((rows, units // pieces), BF16)] * 2 + [dma((2,))]
    args += staged
    scratch = first + Staged.scratch(staged) + scratch
    if grads is not None:
        piece = units // pieces
        shapes = (piece, shard), (shard, units), (columns, shard)
        out_shape += [jax.ShapeDtypeStruct(s, F32) for s in shapes]
        scratch += [pltpu.VMEM((pieces, rows, piece), BF16)] + [dma((pieces,))] * 2
        for shape in [(piece, shard), (columns, shard)] + [(shard, piece)] * pieces:
            scratch += LineSum.scratch(planes, shape)
    return pl.pallas_call(
        functools.partial(
            back_kernel,
            group=group,
            planes=planes,
            all_planes=all_planes,
            shard=shard,
            kv_heads=kv_heads,
            repeat=repeat,
            width=width,
            coef=math.log2(math.e) / math.sqrt(width),
            scale=1.0 / math.sqrt(width),
            sums=grads is not None,
        ),
        out_shape=out_shape,
        in_specs=[smem()] + [ANYWHERE] * (len(args) - 1),
        out_specs=vmem(4) + [pl.BlockSpec(memory_space=pl.ANY)] + vmem(len(out_shape) - 5),
        scratch_shapes=scratch,
        compiler_params=pltpu.CompilerParams(
            vmem_limit_bytes=BACK_VMEM_LIMIT, collective_id=1, has_side_effects=True
        ),
        cost_estimate=COST,
        name="back",
    )(*args)


def smem():
    return pl.BlockSpec(memory_space=pltpu.SMEM)


def out_kernel(*refs, planes, shard, blocks):
    refs = list(refs)

    def take(count):
        out = refs[:count]
        del refs[:count]
        return out

    arrays = take(4)
    gain_ref, w_down_ref = take(2)
    middle_ref, h_ref, d_hidden_out, og_keep, og_came, heads_came = take(6)
    buffers = take(4)
    heads_ref, w_ref, og_ref, x_ref = buffers
    inputs = Staged(arrays, buffers, *take(1))
    d_hidden_ref, d_hidden_sem = take(2)
    down_buf, down_sems, mine_ref, h_send, h_recv, heads_send, heads_recv = take(7)
    scratch = refs
    device = lax.axis_index("dp")
    core, core_peer, y_peer = tensor_peers()
    x_at = device % 2
    x_peer = {"dp": device + 1 - 2 * x_at}
    half = middle_ref.shape[0]
    total = TensorSum(scratch[:8], mine_ref, core, core_peer, y_peer)
    chunks, width = total.chunks, total.width
    place = (x_at, core, x_peer, core_peer, planes, shard)
    og = Columns(og_ref, og_keep, og_came, scratch[8:14], *place)
    tiles = down_sems.shape[0]
    tile = down_buf.shape[0] // tiles

    def load(t):
        at = pl.ds(t * tile, tile)
        return pltpu.make_async_copy(w_down_ref.at[at, :], down_buf.at[at, :], down_sems.at[t])

    inputs.start()
    for t in range(tiles):
        load(t).start()
    greet([(x_peer, True), (core_peer, True), (y_peer, True)])
    heads_swap = remote(heads_ref, heads_came, heads_send, heads_recv, x_peer)
    inputs.wait(heads_ref, w_ref)
    heads_swap.start()
    for i in range(chunks):
        total.add(i, dot(heads_ref[...], w_ref[:, i * width : (i + 1) * width]))
    inputs.wait(og_ref)
    og.start()
    og.store()
    for t in range(tiles):
        at = slice(t * tile, (t + 1) * tile)
        load(t).wait()
        d_hidden_ref[:, at] = dot(og_ref[...], down_buf[at, :], NT)
    d_hidden_copy = pltpu.make_async_copy(d_hidden_ref, d_hidden_out, d_hidden_sem)
    d_hidden_copy.start()
    mine = rows_of(core, half)
    inputs.wait(x_ref)
    for i in range(chunks):
        at = slice(i * width, (i + 1) * width)
        middle_ref[:, at] = x_ref[mine, at].astype(F32) + total.total(i)
    step = half // blocks

    def to_core(b):
        rows = h_ref.at[pl.ds(pl.multiple_of(core * half + b * step, step), step), :]
        return remote(rows, rows, h_send.at[b], h_recv.at[b], core_peer)

    for b in range(blocks):
        v = middle_ref[b * step : (b + 1) * step, :]
        r = lax.rsqrt(jnp.mean(v * v, axis=1, keepdims=True) + EPS)
        at = pl.ds(pl.multiple_of(core * half + b * step, step), step)
        h_ref[at, :] = (v * r * gain_ref[...]).astype(BF16)
        to_core(b).start()
    og.forward()
    og.finish()
    d_hidden_copy.wait()
    heads_swap.wait_recv()
    heads_swap.wait_send()
    for b in range(blocks):
        to_core(b).wait_recv()
        to_core(b).wait_send()
    total.finish()


def attention_out(heads, w_out, x, gain, out_grad, w_down, planes, shard):
    rows, model = x.shape
    half = rows // 2
    units = w_down.shape[0]
    chunks, blocks = 4, 4
    tiles = units // math.gcd(units, 256)
    dma = pltpu.SemaphoreType.DMA
    cut_shape = jax.ShapeDtypeStruct((rows, planes * shard), BF16)
    return pl.pallas_call(
        functools.partial(out_kernel, planes=planes, shard=shard, blocks=blocks),
        out_shape=[
            jax.ShapeDtypeStruct((half, model), F32),
            jax.ShapeDtypeStruct((rows, model), BF16),
            jax.ShapeDtypeStruct((rows, units), F32),
        ]
        + [cut_shape] * 2
        + [jax.ShapeDtypeStruct(heads.shape, BF16)],
        in_specs=[ANYWHERE] * 4 + vmem(1) + [ANYWHERE],
        out_specs=vmem(2) + [ANYWHERE] + vmem(3),
        scratch_shapes=Staged.scratch([heads, w_out, out_grad, x])
        + [pltpu.VMEM((rows, units), F32), dma]
        + [pltpu.VMEM((units, model), BF16), dma((tiles,))]
        + [pltpu.VMEM((2, rows, model // chunks), F32), dma((blocks,)), dma((blocks,)), dma, dma]
        + TensorSum.scratch(chunks, half, model // chunks)
        + Columns.scratch(half, planes * shard),
        compiler_params=pltpu.CompilerParams(
            vmem_limit_bytes=VMEM_LIMIT, collective_id=4, has_side_effects=True
        ),
        cost_estimate=COST,
        name="attention_out",
    )(heads, w_out, out_grad, x, gain, w_down)


def middle_kernel(*refs, planes, shard, heads, width, pieces, blocks, sums):
    refs = list(refs)

    def take(count):
        out = refs[:count]
        del refs[:count]
        return out

    w_gate_ref, w_up_ref, gain_ref = take(3)
    count = 10 if sums else 8
    arrays = take(count)
    outs = take(3)
    hid_came_ref, a_ref, gain_out_ref, qx_ref, dox_ref, h_keep, h_came = take(7)
    if sums:
        down_outs = take(pieces - 1)
    buffers = take(count)
    inputs = Staged(arrays, buffers, *take(1))
    h_ref, d_ref, middle_ref, og_ref, w_out_ref, q_ref, o_ref, lse_ref = buffers[:8]
    if sums:
        og_keep, og_came = buffers[8:]
    out_buffers = take(3)
    hid_ref, gate_ref, up_ref = out_buffers
    outputs = Staged(outs, out_buffers, *take(1), out=True)
    gate_buf, up_buf, load_sems, c_ref, mine_ref = take(5)
    hid_send, hid_recv, a_send, a_recv = take(4)
    sum_scratch, h_scratch = take(8), take(6)
    device = lax.axis_index("dp")
    core, core_peer, y_peer = tensor_peers()
    plane = device // 2
    x_at = device % 2
    x_peer = {"dp": device + 1 - 2 * x_at}
    meets = [(x_peer, True), (core_peer, True), (y_peer, True)]
    h_two = Columns(h_ref, h_keep, h_came, h_scratch, x_at, core, x_peer, core_peer, planes, shard)
    half = middle_ref.shape[0]
    total = TensorSum(sum_scratch, mine_ref, core, core_peer, y_peer)
    chunks, columns = total.chunks, total.width
    units = hid_ref.shape[1]
    piece = units // pieces
    tile = 256
    tiles = units // tile
    if sums:
        downs = [LineSum(take(6), device, plane, planes) for _ in range(pieces - 1)]
        meets += [({"dp": device + 2}, plane < planes - 1), ({"dp": device - 2}, plane > 0)]

    def loads(t):
        at = pl.ds(t * tile, tile)
        return (
            pltpu.make_async_copy(w_gate_ref.at[:, at], gate_buf.at[:, at], load_sems.at[2 * t]),
            pltpu.make_async_copy(w_up_ref.at[:, at], up_buf.at[:, at], load_sems.at[2 * t + 1]),
        )

    inputs.start(h_ref)
    for t in range(tiles):
        for load in loads(t):
            load.start()
        if t == 0:
            inputs.start(d_ref)
    inputs.start(*buffers[2:])
    greet(meets)
    inputs.wait(h_ref)

    def swap(k):
        at = pl.ds(k * piece, piece)
        return remote(hid_ref.at[:, at], hid_came_ref.at[:, at], hid_send.at[k], hid_recv.at[k], x_peer)

    for t in range(tiles):
        for load in loads(t):
            load.wait()
        if t == 0:
            inputs.wait(d_ref)
        at = slice(t * tile, (t + 1) * tile)
        gate = dot(h_ref[...], gate_buf[:, at])
        up = dot(h_ref[...], up_buf[:, at])
        sig = 1.0 / (1.0 + jnp.exp(-gate))
        silu = gate * sig
        d = d_ref[:, at]
        hid_ref[:, at] = (silu * up).astype(BF16)
        up_ref[:, at] = (d * silu).astype(BF16)
        gate_ref[:, at] = (d * up * (sig * (1.0 + gate * (1.0 - sig)))).astype(BF16)
        if (t + 1) * tile % piece == 0:
            swap((t + 1) * tile // piece - 1).start()

    outputs.start()
    inputs.wait(*buffers[2:])

    def down_start(k):
        if sums:
            at = pl.ds(k * piece, piece)
            swap(k).wait_recv()
            downs[k].fill_columns(hid_ref.at[:, at], hid_came_ref.at[:, at], og_keep, og_came)
            downs[k].start()

    def down_wave(k, wave):
        if sums and wave < planes - 2:
            downs[k].wave(wave)

    for i in range(chunks):
        at = slice(i * columns, (i + 1) * columns)
        total.add(i, dot(gate_ref[...], gate_buf[at, :], NT) + dot(up_ref[...], up_buf[at, :], NT))
        if i == chunks - 2:
            down_start(0)
    for i in range(chunks):
        if i == 1:
            down_start(1)
            h_two.start()
        if i == 2:
            down_wave(0, 0)
        c_ref[:, i * columns : (i + 1) * columns] = total.total(i)
    down_wave(0, 1)

    step = half // blocks

    def to_core(b):
        rows = a_ref.at[pl.ds(pl.multiple_of(core * half + b * step, step), step), :]
        return remote(rows, rows, a_send.at[b], a_recv.at[b], core_peer)

    gain_out_ref[...] = jnp.zeros_like(gain_out_ref)
    for b in range(blocks):
        at = slice(b * step, (b + 1) * step)
        whole_at = pl.ds(pl.multiple_of(core * half + b * step, step), step)
        c = c_ref[at, :]
        v = middle_ref[at, :]
        r = lax.rsqrt(jnp.mean(v * v, axis=1, keepdims=True) + EPS)
        n = v * r
        gain_out_ref[...] += jnp.sum(c * n, axis=0, keepdims=True)
        gc = c * gain_ref[...]
        d = r * (gc - n * jnp.mean(n * gc, axis=1, keepdims=True)) + og_ref[whole_at, :].astype(F32)
        a_ref[whole_at, :] = d.astype(BF16)
        to_core(b).start()

    lane = lax.broadcasted_iota(jnp.int32, (half, width), 1)

    def extra(value):
        a, b, c = split_three(value)
        return jnp.where(lane == 0, a, jnp.where(lane == 1, b, jnp.where(lane == 2, c, 0.0))).astype(BF16)

    def prepare(which):
        at_rows = rows_of(which, half)
        d_heads = dot(a_ref[at_rows, :], w_out_ref[...], NT)
        for head in range(heads):
            at = slice(head * width, (head + 1) * width)
            qx_ref[head, at_rows, :width] = q_ref[at_rows, at]
            qx_ref[head, at_rows, width:] = extra(lse_ref[at_rows, at])
            d = d_heads[:, at].astype(BF16)
            delta = jnp.sum(d.astype(F32) * o_ref[at_rows, at].astype(F32), axis=1, keepdims=True)
            dox_ref[head, at_rows, :width] = d
            dox_ref[head, at_rows, width:] = extra(jnp.broadcast_to(delta, (half, width)))

    down_wave(1, 0)
    h_two.store()
    prepare(core)
    h_two.forward()
    for b in range(blocks):
        to_core(b).wait_recv()
    prepare(1 - core)
    down_wave(1, 1)
    for b in range(blocks):
        to_core(b).wait_send()
    total.finish()
    h_two.finish()
    outputs.wait()
    for k in range(pieces):
        if k == pieces - 1 or not sums:
            swap(k).wait_recv()
        swap(k).wait_send()
    if sums:
        for k in range(pieces - 1):
            for wave in range(2, planes - 2):
                downs[k].wave(wave)
            downs[k].finish(down_outs[k])


def middle_of(w_gate, w_up, h_two, d_hidden, middle, out_grad, gain, w_out, q, out, lse, cuts, pieces, planes, shard, width):
    half, model = middle.shape
    rows, units = d_hidden.shape
    columns = q.shape[1]
    heads = columns // width
    chunks, blocks = 4, 4
    dma = pltpu.SemaphoreType.DMA
    staged = [h_two, d_hidden, middle, out_grad, w_out, q, out, lse] + ([] if cuts is None else cuts)
    args = [w_gate, w_up, gain, *staged]
    unit_shape = jax.ShapeDtypeStruct((rows, units), BF16)
    out_shape = [unit_shape] * 4 + [
        jax.ShapeDtypeStruct((rows, model), BF16),
        jax.ShapeDtypeStruct((1, model), F32),
    ]
    out_shape += [jax.ShapeDtypeStruct((heads, rows, 2 * width), BF16)] * 2
    out_shape += [jax.ShapeDtypeStruct((rows, planes * shard), BF16)] * 2
    scratch = Staged.scratch(staged) + Staged.scratch([unit_shape] * 3)
    scratch += [pltpu.VMEM((model, units), BF16)] * 2 + [dma((2 * units // 256,))]
    scratch += [pltpu.VMEM((half, model), F32), pltpu.VMEM((2, rows, model // chunks), F32)]
    scratch += [dma((pieces,))] * 2 + [dma((blocks,))] * 2
    scratch += TensorSum.scratch(chunks, half, model // chunks)
    scratch += Columns.scratch(half, planes * shard)
    if cuts is not None:
        out_shape += [jax.ShapeDtypeStruct((units // pieces, shard), F32)] * (pieces - 1)
        scratch += LineSum.scratch(planes, (units // pieces, shard)) * (pieces - 1)
    return pl.pallas_call(
        functools.partial(
            middle_kernel,
            planes=planes,
            shard=shard,
            heads=heads,
            width=width,
            pieces=pieces,
            blocks=blocks,
            sums=cuts is not None,
        ),
        out_shape=out_shape,
        in_specs=[ANYWHERE] * 2 + vmem(1) + [ANYWHERE] * len(staged),
        out_specs=[ANYWHERE] * 3 + vmem(len(out_shape) - 3),
        scratch_shapes=scratch,
        compiler_params=pltpu.CompilerParams(
            vmem_limit_bytes=BACK_VMEM_LIMIT, collective_id=2, has_side_effects=True
        ),
        cost_estimate=COST,
        name="middle",
    )(*args)


def through_rope(d_ref, raw_ref, gain, cos, sin, out_ref, width, plain):
    columns = d_ref.shape[1]
    total = jnp.zeros((1, width), F32)
    for at in range(0, columns - plain, width):
        d = d_ref[:, at : at + width]
        c = d * cos - roll_half(d) * sin
        v = raw_ref[:, at : at + width]
        r = lax.rsqrt(jnp.mean(v * v, axis=1, keepdims=True) + EPS)
        n = v * r
        total = total + jnp.sum(c * n, axis=0, keepdims=True)
        gc = gain * c
        out_ref[:, at : at + width] = (r * (gc - n * jnp.mean(n * gc, axis=1, keepdims=True))).astype(BF16)
    if plain:
        out_ref[:, columns - plain :] = d_ref[:, columns - plain :].astype(BF16)
    return total


def front_kernel(*refs, dp_size, planes, shard, chunks, sums):
    refs = list(refs)

    def take(count):
        out = refs[:count]
        del refs[:count]
        return out

    q_gain, k_gain, mlp_gain_ref, w_down_ref = take(4)
    count = 17 if sums else 13
    arrays = take(count)
    d_one, block_out, gains, dq_ref, dq_came, dkv_ref, dkv_came, one_ref, one_came = take(9)
    if sums:
        w_up_out, w_q_out, w_kv_out = take(3)
    buffers = take(count)
    inputs = Staged(arrays, buffers, *take(1))
    dkv_in, k_raw, cos_ref, sin_ref, dq_in, q_raw, one_all = buffers[:7]
    x_ref, w_q, w_k, w_v, hid_ref, middle_ref = buffers[7:13]
    if sums:
        two_ref, two_came, up_ref, up_came = buffers[13:]
    mine, down_buf, down_sems, gain_came = take(4)
    swap_sems, one_sems, block_sems, gain_sems = take(4), take(2), take(2), take(2)
    one_sum_scratch, out_sum_scratch, one_scratch = take(8), take(8), take(6)
    half = x_ref.shape[0] // 2
    model = x_ref.shape[1]
    width = model // chunks
    head = cos_ref.shape[1]
    kv_width = w_k.shape[1]

    device = lax.axis_index("dp")
    core, core_peer, y_peer = tensor_peers()
    x_at = device % 2
    x_peer = {"dp": device + 1 - 2 * x_at}
    plane = device // 2
    one = Columns(one_all, one_ref, one_came, one_scratch, x_at, core, x_peer, core_peer, planes, shard)
    bits = [1 << i for i in range(dp_size.bit_length() - 1)]
    dp_peers = [{"dp": device + bit - 2 * bit * ((device // bit) % 2)} for bit in bits]
    gain_peers = [core_peer, y_peer] + dp_peers
    meets = [(peer, True) for peer in gain_peers]
    if sums:
        up_sum, q_sum, kv_sum = (LineSum(take(6), device, plane, planes) for _ in range(3))
        meets += [({"dp": device + 2}, plane < planes - 1), ({"dp": device - 2}, plane > 0)]

    narrow = down_buf.shape[2]
    parts = model // narrow

    def load(i):
        at = pl.ds(i * narrow, narrow)
        return pltpu.make_async_copy(w_down_ref.at[:, at], down_buf.at[i % 2], down_sems.at[i])

    if sums:
        inputs.start(*buffers[13:])
    inputs.start(*buffers[:13])
    load(0).start()
    load(1).start()
    greet(meets)
    if sums:
        inputs.wait(*buffers[13:])
        up_sum.fill_rows(two_ref, two_came, up_ref, up_came)
        up_sum.start()
    inputs.wait(*buffers[:7])
    cos, sin = cos_ref[...], sin_ref[...]
    k_total = through_rope(dkv_in, k_raw, k_gain[...], cos, sin, dkv_ref, head, kv_width)
    kv_swap = remote(dkv_ref, dkv_came, swap_sems[0], swap_sems[1], x_peer)
    kv_swap.start()
    q_total = through_rope(dq_in, q_raw, q_gain[...], cos, sin, dq_ref, head, 0)
    q_swap = remote(dq_ref, dq_came, swap_sems[2], swap_sems[3], x_peer)
    q_swap.start()
    one.start()
    inputs.wait(*buffers[7:13])

    one_sum = TensorSum(one_sum_scratch, mine, core, core_peer, y_peer)
    x = x_ref[...].astype(F32)
    r = lax.rsqrt(jnp.mean(x * x, axis=1, keepdims=True) + EPS)
    for i in range(chunks):
        at = slice(i * width, (i + 1) * width)
        part = (
            dot(dq_ref[...], w_q[at, :], NT)
            + dot(dkv_ref[:, :kv_width], w_k[at, :], NT)
            + dot(dkv_ref[:, kv_width:], w_v[at, :], NT)
        )
        one_sum.add(i, part)
        gains[0, :, at] = jnp.sum(part * (x_ref[:, at].astype(F32) * r), axis=0, keepdims=True)
    gains[0, :, model : 2 * model] = mlp_gain_ref[...]
    gains[0, :, 2 * model : 2 * model + head] = q_total
    gains[0, :, 2 * model + head :] = k_total

    def gain_swap(k):
        return remote(
            gains.at[k], gain_came.at[k], gain_sems[0].at[k], gain_sems[1].at[k], gain_peers[k]
        )

    def gain_add(k):
        gain_swap(k).wait_recv()
        gains[k + 1] = gains[k] + gain_came[k]
        if k + 1 < len(gain_peers):
            gain_swap(k + 1).start()

    gain_swap(0).start()

    out_sum = TensorSum(out_sum_scratch, mine.at[:, :, pl.ds(0, narrow)], core, core_peer, y_peer)
    for i in range(parts):
        load(i).wait()
        out_sum.add(i, dot(hid_ref[...], down_buf[i % 2]))
        if i + 2 < parts:
            load(i + 2).start()
    gain_add(0)
    one.store()
    one.forward()
    if sums:
        if planes > 2:
            up_sum.wave(0)
        kv_swap.wait_recv()
        one.over_core().wait_recv()
        kv_sum.fill_rows(one_ref, one_came, dkv_ref, dkv_came)
        kv_sum.start()
    gain_add(1)
    if sums:
        q_swap.wait_recv()
        q_sum.fill_rows(one_ref, one_came, dq_ref, dq_came)
        q_sum.start()
    gain_add(2)

    mine_rows = rows_of(core, half)

    def give(out, sems):
        rows = out.at[mine_rows, :]
        return remote(rows, rows, sems[0], sems[1], core_peer)

    for i in range(chunks):
        d_one[mine_rows, i * width : (i + 1) * width] = one_sum.total(i).astype(BF16)
    give(d_one, one_sems).start()
    if sums:
        for wave in range(1, planes - 2):
            up_sum.wave(wave)
    for k in range(3, len(gain_peers)):
        gain_add(k)
    for i in range(parts):
        at = slice(i * narrow, (i + 1) * narrow)
        block_out[mine_rows, at] = (middle_ref[:, at] + out_sum.total(i)).astype(BF16)
    give(block_out, block_sems).start()
    if sums:
        for wave in range(planes - 2):
            kv_sum.wave(wave)
            q_sum.wave(wave)
        up_sum.finish(w_up_out)
        kv_sum.finish(w_kv_out)
        q_sum.finish(w_q_out)
    else:
        kv_swap.wait_recv()
        q_swap.wait_recv()
        one.over_core().wait_recv()
    one.over_x().wait_send()
    one.over_core().wait_send()
    kv_swap.wait_send()
    q_swap.wait_send()
    for out, sems in ((d_one, one_sems), (block_out, block_sems)):
        give(out, sems).wait_recv()
        give(out, sems).wait_send()
    for k in range(len(gain_peers)):
        gain_swap(k).wait_send()
    one_sum.finish()
    out_sum.finish()


def front(dq, dkv, q_raw, k_raw, q_gain, k_gain, cos, sin, h_one, weights, x, mlp_gain, middle, hidden, w_down, grads, dp_size, shard):
    rows, model = x.shape
    half = rows // 2
    planes = dp_size // 2
    chunks = 4
    width = model // chunks
    units = hidden.shape[1]
    stages = dp_size.bit_length() + 1
    dma = pltpu.SemaphoreType.DMA
    gains = (2 * model + 2 * cos.shape[1],)
    staged = [dkv, k_raw, cos, sin, dq, q_raw, h_one, x, *weights, hidden, middle]
    if grads is not None:
        staged += grads
    args = [q_gain, k_gain, mlp_gain, w_down, *staged]
    cut_shape = jax.ShapeDtypeStruct((rows, planes * shard), BF16)
    whole = jax.ShapeDtypeStruct((rows, model), BF16)
    q_shape, kv_shape = jax.ShapeDtypeStruct(dq.shape, BF16), jax.ShapeDtypeStruct(dkv.shape, BF16)
    out_shape = [whole, whole, jax.ShapeDtypeStruct((stages + 1, 1) + gains, F32)]
    out_shape += [q_shape, q_shape, kv_shape, kv_shape, cut_shape, cut_shape]
    scratch = Staged.scratch(staged)
    scratch += [pltpu.VMEM((2, rows, width), F32)]
    scratch += [pltpu.VMEM((2, units, width // 2), BF16), dma((2 * chunks,))]
    scratch += [pltpu.VMEM((stages, 1) + gains, F32)]
    scratch += [dma] * 8 + [dma((stages,))] * 2
    scratch += TensorSum.scratch(chunks, half, width) + TensorSum.scratch(2 * chunks, half, width // 2)
    scratch += Columns.scratch(half, planes * shard)
    if grads is not None:
        for columns in (units, dq.shape[1], dkv.shape[1]):
            out_shape.append(jax.ShapeDtypeStruct((shard, columns), F32))
            scratch += LineSum.scratch(planes, (shard, columns))
    return pl.pallas_call(
        functools.partial(
            front_kernel,
            dp_size=dp_size,
            planes=planes,
            shard=shard,
            chunks=chunks,
            sums=grads is not None,
        ),
        out_shape=out_shape,
        in_specs=vmem(3) + [ANYWHERE] * (len(args) - 3),
        out_specs=vmem(len(out_shape)),
        scratch_shapes=scratch,
        compiler_params=pltpu.CompilerParams(
            vmem_limit_bytes=BACK_VMEM_LIMIT, collective_id=3, has_side_effects=True
        ),
        cost_estimate=COST,
        name="front",
    )(*args)


def last_kernel(d_ref, x_ref, gain_ref, add_ref, out_ref):
    c = d_ref[...].astype(F32)
    x = x_ref[...].astype(F32)
    r = lax.rsqrt(jnp.mean(x * x, axis=1, keepdims=True) + EPS)
    n = x * r
    gc = c * gain_ref[...]
    out_ref[...] = add_ref[...].astype(F32) + r * (gc - n * jnp.mean(n * gc, axis=1, keepdims=True))


def tokens_grad_of(d_one, x, gain, add):
    rows, model = x.shape
    tile = math.gcd(rows, 128)
    row_spec = pl.BlockSpec((tile, model), lambda i: (i, 0))
    return pl.pallas_call(
        last_kernel,
        out_shape=jax.ShapeDtypeStruct((rows, model), F32),
        grid=(rows // tile,),
        in_specs=[row_spec, row_spec, pl.BlockSpec((1, model), lambda i: (0, 0)), row_spec],
        out_specs=row_spec,
        compiler_params=params(),
        cost_estimate=COST,
        name="tokens_grad",
    )(d_one, x, gain, add)


class Chain:
    def __init__(self):
        self.last = None

    def mark(self, value):
        self.last = value

    def __call__(self, *values):
        if self.last is None:
            return values
        return lax.optimization_barrier((*values, self.last))[:-1]


class ZSum:
    def __init__(self, part, dim, shard, planes, z_at):
        self.part, self.dim, self.shard, self.planes, self.z_at = part, dim, shard, planes, z_at
        self.at = 0
        self.came = None

    def term(self, j):
        j = jnp.clip(j, 0, self.planes - 1)
        return lax.dynamic_slice_in_dim(self.part, j * self.shard, self.shard, self.dim)

    def send(self, up, down):
        last = self.planes - 1
        self.at += 1
        up_pairs = [(2 * z + x, 2 * z + 2 + x) for z in range(last) for x in range(2) if z < self.at]
        down_pairs = [
            (2 * (last - z) + x, 2 * (last - 1 - z) + x)
            for z in range(last)
            for x in range(2)
            if z < self.at
        ]
        self.came = lax.ppermute(up, "dp", up_pairs), lax.ppermute(down, "dp", down_pairs)

    def terms(self):
        planes, z_at, at = self.planes, self.z_at, self.at
        return self.term(planes - 1 - at + z_at), self.term(at + 1 - planes + z_at)

    def start(self):
        self.send(*self.terms())

    def step(self, chain):
        if self.at >= self.planes - 1:
            return
        up, down = chain(*self.came)
        up_term, down_term = self.terms()
        up, down = up + up_term, down + down_term
        chain.mark(up)
        self.send(up, down)

    def finish(self, chain):
        if self.at == 0:
            self.start()
        while self.at < self.planes - 1:
            self.step(chain)
        up, down = chain(*self.came)
        total = self.term(self.z_at).astype(F32) + up.astype(F32) + down.astype(F32)
        chain.mark(total)
        return total


def shards(
    dp_size,
    tensor_size,
    tokens,
    norm_attn,
    w_query,
    key_weight,
    value_weight,
    query_gain,
    key_gain,
    w_out,
    norm_mlp,
    w_gate,
    w_up,
    w_down,
    out_grad,
    prefix_len,
):
    rows, model = tokens.shape
    width = query_gain.shape[0]
    kv_heads = key_weight.shape[1] // width
    repeat = w_query.shape[1] // key_weight.shape[1]
    dims = (kv_heads, repeat, width)
    group = dp_size // prefix_len.shape[0]
    planes = dp_size // 2
    group_planes = group // 2
    half = rows // 2
    shard = model // dp_size
    assert tensor_size == 4 and MAX_PREFIX <= 4 * rows

    device = lax.axis_index("dp")
    x_at = device % 2
    z_at = device // 2
    sequence = device // group
    member = device % group
    plane = member // 2
    prefix = jnp.sum(jnp.where(jnp.arange(prefix_len.shape[0]) == sequence, prefix_len, 0))

    x_pairs = [(d, d ^ 1) for d in range(dp_size)]

    def x_swap(value):
        return lax.ppermute(value, "dp", x_pairs)

    positions = (member * rows + jnp.arange(rows)).astype(F32)
    counter = jnp.arange(width // 2, dtype=F32)
    angles = positions[:, None] * (ROPE_BASE ** (-2.0 * counter / width))[None, :]
    cos, sin = jnp.cos(angles), jnp.sin(angles)
    cos = jnp.concatenate([cos, cos], axis=1)
    sin = jnp.concatenate([-sin, sin], axis=1)
    norm_attn_row = norm_attn[None, :]
    norm_mlp_row = norm_mlp[None, :]
    q_gain_row = query_gain[None, :]
    k_gain_row = key_gain[None, :]

    h_one, q, kv, q_raw, k_raw = project(
        tokens,
        norm_attn_row,
        (w_query, key_weight, value_weight),
        (q_gain_row, k_gain_row, k_gain_row),
        (True, True, False),
        cos,
        sin,
        "project",
    )
    prefix_at = prefix[None].astype(jnp.int32)
    heads_b, lse, kv_all = attn_fwd(prefix_at, q, kv, group, dims)
    fused = planes == group_planes and shard % 128 == 0
    pieces = 3
    middle, h_two, d_hidden, og_keep, og_came, heads_came = attention_out(
        heads_b, w_out, tokens, norm_mlp_row, out_grad, w_down, planes, shard
    )
    outs = middle_of(
        w_gate,
        w_up,
        h_two,
        d_hidden,
        middle,
        out_grad,
        norm_mlp_row,
        w_out,
        q,
        heads_b,
        lse,
        [og_keep, og_came] if fused else None,
        pieces,
        planes,
        shard,
        width,
    )
    hidden, d_gate, d_up, hidden_came, d_attn, norm_mlp_part, qx, dox, h_two_keep, h_two_came = outs[:10]

    grads = None
    if fused:
        grads = [hidden, hidden_came, og_keep, og_came, d_gate, h_two_keep, h_two_came]
        grads += [heads_b, heads_came]
        w_down_parts = outs[10:]
    outs = back(prefix_at, qx, dox, kv_all, [d_attn, d_up], grads, group, planes, shard, pieces, dims)
    dq, kv_grad, d_attn_keep, d_attn_came, up_came = outs[:5]
    chain = Chain()
    chain.mark(dq)
    if fused:
        w_down_grad = jnp.concatenate([*w_down_parts, outs[5]], axis=0)
        w_gate_grad, w_out_grad = outs[6:]
    else:
        down_part = (dot(hidden, og_keep, TN) + dot(hidden_came, og_came, TN)).astype(BF16)
        w_down_grad = ZSum(down_part, 1, shard, planes, z_at).finish(chain)
        gate_part = dot(h_two_keep, d_gate, TN) + dot(h_two_came, x_swap(d_gate), TN)
        w_gate_grad = ZSum(gate_part.astype(BF16), 0, shard, planes, z_at).finish(chain)
        out_part = dot(heads_b, d_attn_keep, TN) + dot(heads_came, d_attn_came, TN)
        w_out_grad = ZSum(out_part.astype(BF16), 1, shard, planes, z_at).finish(chain)

    up_grads = [h_two_keep, h_two_came, d_up, up_came] if fused else None
    outs = front(
        *chain(dq),
        kv_grad,
        q_raw,
        k_raw,
        q_gain_row,
        k_gain_row,
        cos,
        sin,
        h_one,
        (w_query, key_weight, value_weight),
        tokens,
        0.5 * norm_mlp_part,
        middle,
        hidden,
        w_down,
        up_grads,
        dp_size,
        shard,
    )
    d_h_one, block_out, gains, dq_b, dq_came, dkv_b, dkv_came, h_one_keep, h_one_came = outs[:9]
    if fused:
        w_up_grad, w_query_grad, w_kv_grad = outs[9:]
    else:
        chain.mark(d_h_one)

        def by_rows(left, left_came, right, right_came):
            part = dot(left, right, TN) + dot(left_came, right_came, TN)
            return ZSum(part.astype(BF16), 0, shard, planes, z_at).finish(chain)

        w_up_grad = by_rows(h_two_keep, h_two_came, d_up, up_came)
        w_query_grad = by_rows(h_one_keep, h_one_came, dq_b, dq_came)
        w_kv_grad = by_rows(h_one_keep, h_one_came, dkv_b, dkv_came)
    kv_width = kv_heads * width
    tokens_grad = tokens_grad_of(d_h_one, tokens, norm_attn_row, d_attn)
    gains = gains[-1, 0]
    return (
        block_out,
        tokens_grad,
        lax.dynamic_slice_in_dim(gains, device * shard, shard, 0),
        w_query_grad,
        w_kv_grad[:, :kv_width],
        w_kv_grad[:, kv_width:],
        gains[2 * model : 2 * model + width],
        gains[2 * model + width :],
        w_out_grad,
        lax.dynamic_slice_in_dim(gains, model + device * shard, shard, 0),
        w_gate_grad,
        w_up_grad,
        w_down_grad,
    )


def solution(mesh):
    placed = (
        P("dp", None),
        P(),
        P(None, "tensor"),
        P(None, "tensor"),
        P(None, "tensor"),
        P(),
        P(),
        P("tensor", None),
        P(),
        P(None, "tensor"),
        P(None, "tensor"),
        P("tensor", None),
        P("dp", None),
        P(),
    )
    return jax.shard_map(
        functools.partial(shards, mesh.shape["dp"], mesh.shape["tensor"]),
        mesh=mesh,
        in_specs=placed,
        out_specs=(
            P("dp", None),
            P("dp", None),
            P("dp"),
            P("dp", "tensor"),
            P("dp", "tensor"),
            P("dp", "tensor"),
            P(),
            P(),
            P("tensor", "dp"),
            P("dp"),
            P("dp", "tensor"),
            P("dp", "tensor"),
            P("tensor", "dp"),
        ),
        check_vma=False,
    )
```

```python
import functools
import math

import jax
import jax.numpy as jnp
from jax import lax
from jax.experimental import pallas as pl
from jax.experimental.pallas import tpu as pltpu
from jax.sharding import PartitionSpec as P

F32 = jnp.float32
BF16 = jnp.bfloat16
EPS = 1e-06
ROPE_BASE = 1000000.0
MAX_PREFIX = 2048
VMEM_LIMIT = 56 * 2**20
BACK_VMEM_LIMIT = 60 * 2**20

COST = pl.CostEstimate(flops=1000, bytes_accessed=1000, transcendentals=0)

NN = (((1,), (0,)), ((), ()))
NT = (((1,), (1,)), ((), ()))
TN = (((0,), (0,)), ((), ()))


def dot(left, right, dims=NN):
    return lax.dot_general(left, right, dims, preferred_element_type=F32)


def vmem(count):
    return [pl.BlockSpec(memory_space=pltpu.VMEM)] * count


def params():
    return pltpu.CompilerParams(vmem_limit_bytes=VMEM_LIMIT)


def greet(peers):
    barrier = pltpu.get_barrier_semaphore()
    count = 0
    for peer, there in peers:

        def signal(peer=peer):
            pl.semaphore_signal(barrier, 1, device_id=peer, device_id_type=pl.DeviceIdType.MESH)

        if there is True:
            signal()
            count = count + 1
        else:
            pl.when(there)(signal)
            count = count + there.astype(jnp.int32)
    pl.semaphore_wait(barrier, count)


def remote(src, dst, send, recv, peer):
    return pltpu.make_async_remote_copy(
        src_ref=src,
        dst_ref=dst,
        send_sem=send,
        recv_sem=recv,
        device_id=peer,
        device_id_type=pl.DeviceIdType.MESH,
    )


class Staged:
    def __init__(self, arrays, buffers, sems, out=False):
        self.copies = []
        for i, (array, buffer) in enumerate(zip(arrays, buffers)):
            ends = (buffer, array) if out else (array, buffer)
            self.copies.append((buffer, pltpu.make_async_copy(*ends, sems.at[i])))

    @staticmethod
    def scratch(shapes):
        return [pltpu.VMEM(s.shape, s.dtype) for s in shapes] + [pltpu.SemaphoreType.DMA((len(shapes),))]

    def start(self, *buffers):
        for buffer, copy in self.copies:
            if not buffers or any(buffer is b for b in buffers):
                copy.start()

    def wait(self, *buffers):
        for buffer, copy in self.copies:
            if not buffers or any(buffer is b for b in buffers):
                copy.wait()


ANYWHERE = pl.BlockSpec(memory_space=pl.ANY)


def tensor_peers():
    t = lax.axis_index("tensor")
    core = t % 2
    y = t // 2
    return core, {"tensor": t + 1 - 2 * core}, {"tensor": t + 2 - 4 * y}


def rows_of(core, half):
    return pl.ds(pl.multiple_of(core * half, half), half)


def cut_into(out, out_rows, ref, ref_rows, side, planes, shard):
    for z in range(planes):
        to = slice(z * shard, (z + 1) * shard)
        if shard % 128 == 0:
            at = pl.ds(pl.multiple_of((2 * z + side) * shard, shard), shard)
            out[out_rows, to] = ref[ref_rows, at]
        else:
            low = ref[ref_rows, 2 * z * shard : (2 * z + 1) * shard]
            high = ref[ref_rows, (2 * z + 1) * shard : (2 * z + 2) * shard]
            out[out_rows, to] = jnp.where(side == 0, low, high)


class Columns:
    def __init__(self, whole, keep, came, scratch, x_at, core, x_peer, core_peer, planes, shard):
        self.whole, self.keep, self.came = whole, keep, came
        self.send_ref, self.recv_ref, self.sems = scratch[0], scratch[1], scratch[2:]
        self.x_at, self.core, self.cut = x_at, core, (planes, shard)
        self.x_peer, self.core_peer = x_peer, core_peer
        self.half = whole.shape[0] // 2

    @staticmethod
    def scratch(half, columns):
        return [pltpu.VMEM((half, columns), BF16)] * 2 + [pltpu.SemaphoreType.DMA] * 4

    def over_x(self):
        return remote(self.send_ref, self.recv_ref, self.sems[0], self.sems[1], self.x_peer)

    def over_core(self):
        there = self.came.at[rows_of(self.core, self.half), :]
        return remote(self.recv_ref, there, self.sems[2], self.sems[3], self.core_peer)

    def start(self):
        mine = rows_of(self.core, self.half)
        cut_into(self.send_ref, slice(None), self.whole, mine, 1 - self.x_at, *self.cut)
        self.over_x().start()

    def store(self):
        cut_into(self.keep, slice(None), self.whole, slice(None), self.x_at, *self.cut)

    def forward(self):
        self.over_x().wait_recv()
        self.over_core().start()
        self.came[rows_of(self.core, self.half), :] = self.recv_ref[...]

    def finish(self):
        self.over_core().wait_recv()
        self.over_x().wait_send()
        self.over_core().wait_send()


class LineSum:
    def __init__(self, scratch, device, plane, planes, paced=False):
        self.paced = paced
        self.stack, self.came = scratch[:2]
        self.sems = scratch[2:]
        self.device, self.plane, self.planes = device, plane, planes

    @staticmethod
    def scratch(planes, shape):
        return [pltpu.VMEM((n,) + shape, BF16) for n in (planes, planes + 1)] + [
            pltpu.SemaphoreType.DMA((planes,))
        ] * 4

    def up(self, j):
        s = self.sems
        peer = {"dp": self.device + 2}
        return remote(self.stack.at[j], self.came.at[j], s[0].at[j], s[1].at[j], peer)

    def down(self, j):
        s = self.sems
        slot = jnp.where(self.plane - 1 == j, self.planes, j)
        peer = {"dp": self.device - 2}
        return remote(self.stack.at[j], self.came.at[slot], s[2].at[j], s[3].at[j], peer)

    def start(self):
        last = self.planes - 1

        @pl.when(self.plane == 0)
        def _():
            for j in range(last, last - 1 if self.paced else 0, -1):
                self.up(j).start()

        @pl.when(self.plane == last)
        def _():
            for j in range(1 if self.paced else last):
                self.down(j).start()

    def advance(self, step):
        plane, last = self.plane, self.planes - 1
        low, high = last - step + plane, step - last + plane
        if self.paced:

            @pl.when(plane == 0)
            def _():
                self.up(last - step + 1).wait_send()
                self.up(last - step).start()

            @pl.when(plane == last)
            def _():
                self.down(step - 1).wait_send()
                self.down(step).start()

        @pl.when((plane >= 1) & (plane <= step))
        def _():
            self.up(low).wait_recv()
            self.stack[low] += self.came[low]
            self.up(low).start()

        @pl.when((plane < last) & (plane >= last - step))
        def _():
            self.down(high).wait_recv()
            self.stack[high] += self.came[high]
            self.down(high).start()

    def finish(self, out):
        plane, planes = self.plane, self.planes

        @pl.when(plane == 0)
        def _():
            self.down(plane).wait_recv()
            out[...] = self.stack[plane] + self.came[planes]

        @pl.when(plane == planes - 1)
        def _():
            self.up(plane).wait_recv()
            out[...] = self.stack[plane] + self.came[plane]

        @pl.when((plane > 0) & (plane < planes - 1))
        def _():
            self.up(plane).wait_recv()
            self.down(plane).wait_recv()
            total = self.stack[plane].astype(F32) + self.came[plane].astype(F32)
            out[...] = (total + self.came[planes].astype(F32)).astype(BF16)

        for j in range(planes):
            ups, downs = plane < j, plane > j
            if self.paced and j > 1:
                ups = ups & (plane > 0)
            if self.paced and j < planes - 2:
                downs = downs & (plane < planes - 1)
            pl.when(ups)(lambda j=j: self.up(j).wait_send())
            pl.when(downs)(lambda j=j: self.down(j).wait_send())

    def fill_rows(self, left, left_came, right, right_came):
        shard = self.stack.shape[1]

        def body(j, carry):
            at = pl.ds(pl.multiple_of(j * shard, shard), shard)
            self.stack[j] = (
                dot(left[:, at], right[...], TN) + dot(left_came[:, at], right_came[...], TN)
            ).astype(BF16)
            return carry

        lax.fori_loop(0, self.planes, body, 0)

    def fill_columns(self, left, left_came, right, right_came):
        shard = self.stack.shape[2]
        tile = 256

        def body(t, carry):
            at = pl.ds(pl.multiple_of(t * tile, tile), tile)
            term = dot(left[:, at], right[...], TN) + dot(left_came[:, at], right_came[...], TN)
            for j in range(self.planes):
                self.stack[j, at, :] = term[:, j * shard : (j + 1) * shard].astype(BF16)
            return carry

        lax.fori_loop(0, left.shape[1] // tile, body, 0)


class TensorSum:
    def __init__(self, scratch, mine, core, core_peer, y_peer):
        self.away, self.core_came, self.both, self.y_came = scratch[:4]
        self.sems = scratch[4:]
        self.mine = mine
        self.core, self.core_peer, self.y_peer = core, core_peer, y_peer
        self.chunks, self.half, self.width = self.away.shape

    @staticmethod
    def scratch(chunks, half, width):
        return [pltpu.VMEM((chunks, half, width), BF16)] * 4 + [
            pltpu.SemaphoreType.DMA((chunks,))
        ] * 4

    def over_core(self, i):
        s = self.sems
        return remote(self.away.at[i], self.core_came.at[i], s[0].at[i], s[1].at[i], self.core_peer)

    def over_y(self, i):
        s = self.sems
        return remote(self.both.at[i], self.y_came.at[i], s[2].at[i], s[3].at[i], self.y_peer)

    def add(self, i, value):
        self.mine[i % 2] = value
        self.away[i] = self.mine[i % 2, rows_of(1 - self.core, self.half), :].astype(BF16)
        self.over_core(i).start()
        if i > 0:
            self.pass_on(i - 1)
        if i == self.chunks - 1:
            self.pass_on(i)

    def pass_on(self, i):
        self.over_core(i).wait_recv()
        mine = self.mine[i % 2, rows_of(self.core, self.half), :]
        self.both[i] = (mine + self.core_came[i].astype(F32)).astype(BF16)
        self.over_y(i).start()

    def total(self, i):
        self.over_y(i).wait_recv()
        return self.both[i].astype(F32) + self.y_came[i].astype(F32)

    def finish(self):
        for i in range(self.chunks):
            self.over_core(i).wait_send()
            self.over_y(i).wait_send()


def roll_half(value):
    return pltpu.roll(value, value.shape[-1] // 2, 1)


def project_kernel(x_ref, g_ref, *refs, heads, normed, width):
    count = len(heads)
    w_refs = refs[:count]
    gain_refs = refs[count : 2 * count]
    cos_ref, sin_ref = refs[2 * count : 2 * count + 2]
    h_ref, q_ref, kv_ref = refs[2 * count + 2 : 2 * count + 5]
    raw_refs = refs[2 * count + 5 :]
    x = x_ref[...].astype(F32)
    h = (x * lax.rsqrt(jnp.mean(x * x, axis=1, keepdims=True) + EPS) * g_ref[...]).astype(BF16)
    h_ref[...] = h
    cos, sin = cos_ref[...], sin_ref[...]
    column = 0
    raw_at = 0
    for i in range(count):
        out_ref = q_ref if i == 0 else kv_ref
        column = 0 if i < 2 else column
        product = dot(h, w_refs[i][...])
        if normed[i]:
            raw_refs[raw_at][...] = product
            raw_at += 1
        for j in range(heads[i]):
            u = product[:, j * width : (j + 1) * width]
            if normed[i]:
                u = u * lax.rsqrt(jnp.mean(u * u, axis=1, keepdims=True) + EPS) * gain_refs[i][...]
                u = u * cos + roll_half(u) * sin
            out_ref[:, column : column + width] = u.astype(BF16)
            column += width


def project(x, gain, weights, gains, normed, cos, sin, name):
    rows, model = x.shape
    width = cos.shape[1]
    heads = tuple(w.shape[1] // width for w in weights)
    columns = sum(w.shape[1] for w in weights)
    raws = [w for w, n in zip(weights, normed) if n]
    return pl.pallas_call(
        functools.partial(project_kernel, heads=heads, normed=normed, width=width),
        out_shape=[
            jax.ShapeDtypeStruct((rows, model), BF16),
            jax.ShapeDtypeStruct((rows, weights[0].shape[1]), BF16),
            jax.ShapeDtypeStruct((rows, columns - weights[0].shape[1]), BF16),
        ]
        + [jax.ShapeDtypeStruct((rows, w.shape[1]), F32) for w in raws],
        in_specs=vmem(4 + 2 * len(weights)),
        out_specs=vmem(3 + len(raws)),
        compiler_params=params(),
        cost_estimate=COST,
        name=name,
    )(x, gain, *weights, *gains, cos, sin)


def visible(shape, key0, row0, prefix):
    key_pos = key0 + lax.broadcasted_iota(jnp.int32, shape, 1)
    row_pos = row0 + lax.broadcasted_iota(jnp.int32, shape, 0)
    return (key_pos <= row_pos) | (key_pos < prefix)


def attn_fwd_kernel(
    prefix_ref,
    q_ref,
    kv_ref,
    o_ref,
    lse_ref,
    all_ref,
    acc,
    send_x,
    recv_x,
    send_z,
    recv_z,
    send_down,
    *,
    group,
    kv_heads,
    repeat,
    width,
    tile,
    coef,
):
    rows = q_ref.shape[0]
    kv_width = kv_heads * width
    planes = group // 2
    device = lax.axis_index("dp")
    member = device % group
    plane = member // 2
    x_at = member % 2
    x_other = device + 1 - 2 * x_at
    inner = plane < planes - 1
    prefix = prefix_ref[0]

    barrier = pltpu.get_barrier_semaphore()
    pl.semaphore_signal(barrier, 1, device_id={"dp": x_other}, device_id_type=pl.DeviceIdType.MESH)

    @pl.when(inner)
    def _():
        pl.semaphore_signal(
            barrier, 1, device_id={"dp": device + 2}, device_id_type=pl.DeviceIdType.MESH
        )

    @pl.when(plane > 0)
    def _():
        pl.semaphore_signal(
            barrier, 1, device_id={"dp": device - 2}, device_id_type=pl.DeviceIdType.MESH
        )

    pl.semaphore_wait(barrier, 1 + inner.astype(jnp.int32) + (plane > 0).astype(jnp.int32))

    def source(slot):
        return kv_ref if slot == 0 else all_ref.at[2 * slot]

    def to_x(slot):
        return pltpu.make_async_remote_copy(
            src_ref=source(slot),
            dst_ref=all_ref.at[2 * slot + 1],
            send_sem=send_x.at[slot],
            recv_sem=recv_x.at[slot],
            device_id={"dp": x_other},
            device_id_type=pl.DeviceIdType.MESH,
        )

    def to_z(slot):
        return pltpu.make_async_remote_copy(
            src_ref=source(slot - 1),
            dst_ref=all_ref.at[2 * slot],
            send_sem=send_z.at[slot],
            recv_sem=recv_z.at[slot],
            device_id={"dp": device + 2},
            device_id_type=pl.DeviceIdType.MESH,
        )

    def to_first():
        return pltpu.make_async_remote_copy(
            src_ref=kv_ref,
            dst_ref=all_ref.at[2],
            send_sem=send_down,
            recv_sem=recv_z.at[1],
            device_id={"dp": device - 2},
            device_id_type=pl.DeviceIdType.MESH,
        )

    all_ref[0] = kv_ref[...]
    ones = jnp.ones((rows, width), BF16)
    row0 = member * rows

    def work(block, other, masked, start=False):
        key0 = other * rows

        def head_pair(h, carry):
            k = block[:, pl.ds(pl.multiple_of(h * width, width), width)]
            v = block[:, pl.ds(pl.multiple_of(kv_width + h * width, width), width)]
            v = jnp.concatenate([v, ones], axis=1)
            for g in range(repeat):
                head = h * repeat + g
                for at in range(0, rows, tile):
                    q = q_ref[at : at + tile, pl.ds(pl.multiple_of(head * width, width), width)]
                    p = jnp.exp2(dot(q, k, NT) * coef)
                    if masked:
                        p = jnp.where(visible(p.shape, key0, row0 + at, prefix), p, 0.0)
                    term = dot(p.astype(BF16), v)
                    if start:
                        acc[head, at : at + tile, :] = term
                    else:
                        acc[head, at : at + tile, :] += term
            return carry

        lax.fori_loop(0, kv_heads, head_pair, 0)

    to_x(0).start()
    if planes > 1:

        @pl.when(inner)
        def _():
            to_z(1).start()

        @pl.when(plane == 1)
        def _():
            to_first().start()

    work(kv_ref, member, True, True)
    to_x(0).wait_recv()
    work(all_ref.at[1], member + 1 - 2 * x_at, True)
    for slot in range(1, planes):

        def step(slot=slot):
            to_z(slot).wait_recv()
            if slot < planes - 1:

                @pl.when(inner & (plane >= slot))
                def _():
                    to_z(slot + 1).start()

            to_x(slot).start()
            there = 2 * (plane - slot)
            if slot == 1:

                @pl.when(plane == 0)
                def _():
                    work(all_ref.at[2 * slot], 2 + x_at, True)

                @pl.when(plane > 0)
                def _():
                    work(all_ref.at[2 * slot], there + x_at, False)
            else:
                work(all_ref.at[2 * slot], there + x_at, False)
            to_x(slot).wait_recv()
            if slot == 1:

                @pl.when(plane == 0)
                def _():
                    work(all_ref.at[2 * slot + 1], 3 - x_at, True)

                @pl.when(plane > 0)
                def _():
                    work(all_ref.at[2 * slot + 1], there + 1 - x_at, False)
            else:
                work(all_ref.at[2 * slot + 1], there + 1 - x_at, False)

        if slot == 1:
            step()
        else:
            pl.when(plane >= slot)(step)

    for head in range(kv_heads * repeat):
        total = acc[head, :, width:]
        o_ref[:, head * width : (head + 1) * width] = (acc[head, :, :width] / total).astype(BF16)
        lse_ref[:, head * width : (head + 1) * width] = jnp.log2(total) * (1.0 / coef)

    to_x(0).wait_send()
    for slot in range(1, planes):

        @pl.when(inner & (plane >= slot - 1))
        def _(slot=slot):
            to_z(slot).wait_send()

        @pl.when((plane >= slot) | (slot == 1))
        def _(slot=slot):
            to_x(slot).wait_send()

    if planes > 1:

        @pl.when(plane == 1)
        def _():
            to_first().wait_send()


def attn_fwd(prefix, q, kv, group, dims):
    kv_heads, repeat, width = dims
    rows = q.shape[0]
    heads = kv_heads * repeat
    columns = heads * width
    planes = group // 2
    return pl.pallas_call(
        functools.partial(
            attn_fwd_kernel,
            group=group,
            kv_heads=kv_heads,
            repeat=repeat,
            width=width,
            tile=min(rows, 256),
            coef=math.log2(math.e) / math.sqrt(width),
        ),
        out_shape=[
            jax.ShapeDtypeStruct((rows, columns), BF16),
            jax.ShapeDtypeStruct((rows, columns), F32),
            jax.ShapeDtypeStruct((group,) + kv.shape, BF16),
        ],
        in_specs=[pl.BlockSpec(memory_space=pltpu.SMEM)] + vmem(2),
        out_specs=vmem(3),
        scratch_shapes=[pltpu.VMEM((heads, rows, 2 * width), F32)]
        + [pltpu.SemaphoreType.DMA((planes,))] * 4
        + [pltpu.SemaphoreType.DMA],
        compiler_params=pltpu.CompilerParams(
            vmem_limit_bytes=VMEM_LIMIT, collective_id=0, has_side_effects=True
        ),
        cost_estimate=COST,
        name="attn_fwd",
    )(prefix, q, kv)


def split_three(value):
    high = value.astype(BF16)
    left = value - high.astype(F32)
    mid = left.astype(BF16)
    return high.astype(F32), mid.astype(F32), (left - mid.astype(F32)).astype(BF16).astype(F32)


def back_kernel(
    *refs, group, planes, all_planes, shard, kv_heads, repeat, width, coef, scale, sums
):
    refs = list(refs)

    def take(count):
        out = refs[:count]
        del refs[:count]
        return out

    device = lax.axis_index("dp")
    member = device % group
    plane = member // 2
    last = planes - 1
    prefix_ref, up_ref, w_down_in, middle_in = take(4)
    if sums:
        hid_arrays = take(1)
    count = 12 if sums else 5
    arrays = take(count)
    dq_ref, grad_ref, a_ref, a_came_ref, up_came_ref, block_ref = take(6)
    if sums:
        w_down_ref, w_gate_ref, w_out_ref = take(3)
    if sums:
        hid_buffers = take(1)
        hid_sems = take(1)[0]
    buffers = take(count)
    inputs = Staged(arrays, buffers, *take(1))
    a_all_ref, qx_ref, dox_ref, kv_ref, hid_ref = buffers[:5]
    if sums:
        hid_came_ref = hid_buffers[0]
        og_ref, og_came_ref, gate_ref, h_ref, h_came_ref, heads_ref, heads_came_ref = buffers[5:]
    down_buf, down_sems, mine_ref, middle_buf, middle_sems = take(5)
    block_sems = take(3)
    total_scratch = take(8)
    own_ref, far_ref, xr_ref, zr_ref, first_ref = take(5)
    send_x, recv_x, send_z, recv_z, send_first, recv_first = take(6)
    swap_sems = take(2)
    a_scratch = take(6)
    rows = qx_ref.shape[1]
    kv_width = kv_heads * width
    if sums:
        gate_came_ref, send_gate, recv_gate = take(3)
        left = w_down_ref.shape[0]
        rest = pl.ds(hid_arrays[0].shape[1] - left, left)
        hid_inputs = Staged([h.at[:, rest] for h in hid_arrays], hid_buffers, hid_sems)
        down_sum, out_sum = (LineSum(take(6), device, plane, planes) for _ in range(2))
        piece = gate_came_ref.shape[2]
        pieces = gate_ref.shape[1] // piece
        gate_sums = [LineSum(take(6), device, plane, planes) for _ in range(pieces)]
    x_at = member % 2
    x_other = device + 1 - 2 * x_at
    inner = plane < last
    prefix = prefix_ref[0]

    core, core_peer, y_peer = tensor_peers()
    x_peer = {"dp": x_other}
    total = TensorSum(total_scratch, mine_ref, core, core_peer, y_peer)
    half = total.half
    parts, narrow = total.chunks, total.width

    def load(i):
        at = pl.ds(i * narrow, narrow)
        return pltpu.make_async_copy(w_down_in.at[:, at], down_buf.at[i % 2], down_sems.at[i % 2])

    def middle_load(i):
        at = pl.ds(i * narrow, narrow)
        return pltpu.make_async_copy(middle_in.at[:, at], middle_buf.at[i % 2], middle_sems.at[i % 2])

    def block_at(i):
        return block_ref.at[rows_of(core, half), pl.ds(i * narrow, narrow)]

    def block_store(i):
        return pltpu.make_async_copy(total.both.at[i], block_at(i), block_sems[0].at[i])

    def block_give(i):
        return remote(total.both.at[i], block_at(i), block_sems[1].at[i], block_sems[2].at[i], core_peer)

    def block_add(i):
        load(i).wait()
        total.add(i, dot(hid_ref[...], down_buf[i % 2]))
        if i + 2 < parts:
            load(i + 2).start()

    def block_finish(i):
        middle_load(i).wait()
        value = middle_buf[i % 2] + total.total(i)
        total.over_y(i).wait_send()
        total.both[i] = value.astype(BF16)
        if i + 2 < parts:
            middle_load(i + 2).start()
        block_store(i).start()
        block_give(i).start()

    inputs.start(a_all_ref)
    if sums:
        hid_inputs.start()
        inputs.start(hid_ref, *buffers[5:7])
    inputs.start(*buffers[1:4])
    if sums:
        inputs.start(*buffers[7:])
    else:
        inputs.start(hid_ref)
    for i in range(2):
        load(i).start()
        middle_load(i).start()
    greet(
        [
            (x_peer, True),
            (core_peer, True),
            (y_peer, True),
            ({"dp": device + 2}, inner),
            ({"dp": device - 2}, plane > 0),
        ]
    )

    def copy(src, dst, send, recv, there):
        return remote(src, dst, send, recv, {"dp": there})

    place = (x_at, core, x_peer, core_peer, all_planes, shard)
    d_attn = Columns(a_all_ref, a_ref, a_came_ref, a_scratch, *place)
    up_swap = copy(up_ref, up_came_ref, swap_sems[0], swap_sems[1], x_other)

    def gate_swap(k):
        part = gate_ref.at[:, pl.ds(k * piece, piece)]
        return copy(part, gate_came_ref.at[k], send_gate.at[k], recv_gate.at[k], x_other)

    def gate_start(k):
        gate_swap(k).wait_recv()
        part = gate_ref.at[:, pl.ds(k * piece, piece)]
        gate_sums[k].fill_rows(h_ref, h_came_ref, part, gate_came_ref.at[k])
        gate_sums[k].start()

    lane = lax.broadcasted_iota(jnp.int32, (rows, width), 1)
    minus = jnp.where(lane < 3, -1.0, 0.0).astype(BF16)
    row0 = member * rows

    def work(block, other, masked, out):
        key0 = other * rows

        def head_group(h, carry):
            k_at = pl.ds(pl.multiple_of(h * width, width), width)
            v_at = pl.ds(pl.multiple_of(kv_width + h * width, width), width)
            k = kv_ref[block, :, k_at]
            v = kv_ref[block, :, v_at]
            kx = jnp.concatenate([k, minus], axis=1)
            vx = jnp.concatenate([v, minus], axis=1)
            dk = jnp.zeros((rows, width), F32)
            dv = jnp.zeros((rows, width), F32)
            for g in range(repeat):
                head = h * repeat + g
                qx = qx_ref[head]
                dox = dox_ref[head]
                p = jnp.exp2(dot(qx, kx, NT) * coef)
                if masked:
                    p = jnp.where(visible(p.shape, key0, row0, prefix), p, 0.0)
                ds = (p * dot(dox, vx, NT)).astype(BF16)
                dv += dot(p.astype(BF16), dox[:, :width], TN)
                dk += dot(ds, qx[:, :width], TN)
                dq_ref[:, pl.ds(pl.multiple_of(head * width, width), width)] += dot(ds, k)
            out[:, k_at] = (dk * scale).astype(BF16)
            out[:, v_at] = dv.astype(BF16)
            return carry

        lax.fori_loop(0, kv_heads, head_group, 0)

    def far_swap(slot):
        return copy(far_ref.at[slot], xr_ref.at[slot], send_x.at[slot], recv_x.at[slot], x_other)

    def to_plane(slot):
        return copy(own_ref.at[slot], zr_ref.at[slot], send_z.at[slot], recv_z.at[slot], device - 2)

    def from_first():
        return copy(own_ref.at[1], first_ref, send_first, recv_first, device + 2)

    def attend(slot):
        there = 2 * (plane - slot)
        far, own = there + 1 - x_at, there + x_at

        def both(far, own, masked):
            work(2 * slot + 1, far, masked, far_ref.at[slot])
            far_swap(slot).start()
            work(2 * slot, own, masked, own_ref.at[slot])

        if slot == 0:
            both(far, own, True)
        elif slot == 1:
            pl.when(plane == 0)(lambda: both(3 - x_at, 2 + x_at, True))
            pl.when(plane > 0)(lambda: both(far, own, False))
        else:
            pl.when(plane >= slot)(lambda: both(far, own, False))

    def pass_back(slot):
        def go():
            far_swap(slot).wait_recv()
            own_ref[slot] += xr_ref[slot]
            if slot < last:

                @pl.when(inner & (plane >= slot))
                def _():
                    to_plane(slot + 1).wait_recv()
                    own_ref[slot] += zr_ref[slot + 1]

            if slot == 1:
                pl.when(plane == 0)(lambda: from_first().start())
                pl.when(plane > 0)(lambda: to_plane(slot).start())
            else:
                to_plane(slot).start()

        if slot == 1:
            go()
        else:
            pl.when(plane >= slot)(go)

    dq_ref[...] = jnp.zeros_like(dq_ref)
    inputs.wait(a_all_ref)
    d_attn.start()
    inputs.wait(hid_ref)
    if sums:
        hid_inputs.wait()
        inputs.wait(og_ref, og_came_ref)
        down_sum.fill_columns(hid_ref.at[:, rest], hid_came_ref, og_ref, og_came_ref)
        down_sum.start()
    inputs.wait(*buffers[1:4])
    attend(last)
    d_attn.forward()
    if sums:
        inputs.wait(*buffers[7:])
        gate_swap(0).start()
    d_attn.store()
    pending = list(range(last, 0, -1))
    steps = range(1, last)
    adds = list(range(parts))
    share = -(-parts // last)
    for slot in range(last - 1, -1, -1):
        attend(slot)
        if slot == last - 1:
            if sums:
                d_attn.over_core().wait_recv()
                out_sum.fill_columns(heads_ref, heads_came_ref, a_ref, a_came_ref)
                out_sum.start()
                down_sum.advance(1)
                gate_start(0)
                gate_swap(1).start()
            pass_back(pending.pop(0))
        if slot == last - 2:
            if sums:
                for step in steps[1:]:
                    down_sum.advance(step)
                out_sum.advance(1)
                gate_start(1)
                gate_swap(2).start()
                gate_sums[0].advance(1)
            pass_back(pending.pop(0))
        for i in adds[:share]:
            block_add(i)
        del adds[:share]
    for i in adds:
        block_add(i)
    if sums:
        for step in steps[1:]:
            out_sum.advance(step)
            gate_sums[0].advance(step)
    while pending:
        pass_back(pending.pop(0))
    if sums:
        gate_start(2)
    up_swap.start()
    if sums:
        gate_sums[1].advance(1)
    for i in range(parts // 2):
        block_finish(i)
    if sums:
        for step in steps[1:]:
            gate_sums[1].advance(step)
        gate_sums[2].advance(1)
    for i in range(parts // 2, parts):
        block_finish(i)
    if sums:
        for step in steps[1:]:
            gate_sums[2].advance(step)
    dq_ref[...] = dq_ref[...] * scale

    far_swap(0).wait_recv()
    grad_ref[...] = own_ref[0].astype(F32) + xr_ref[0].astype(F32)
    if last > 0:

        @pl.when(inner)
        def _():
            to_plane(1).wait_recv()
            grad_ref[...] += zr_ref[1].astype(F32)

        @pl.when(plane == 1)
        def _():
            from_first().wait_recv()
            grad_ref[...] += first_ref[...].astype(F32)

    if sums:
        down_sum.finish(w_down_ref)
        out_sum.finish(w_out_ref)
        for k in range(pieces):
            gate_sums[k].finish(w_gate_ref.at[:, pl.ds(k * piece, piece)])
            gate_swap(k).wait_send()
    else:
        d_attn.over_core().wait_recv()
    up_swap.wait_recv()
    up_swap.wait_send()
    for i in range(parts):
        total.over_core(i).wait_send()
        block_store(i).wait()
        block_give(i).wait_recv()
        block_give(i).wait_send()
    d_attn.over_x().wait_send()
    d_attn.over_core().wait_send()
    for slot in range(planes):
        if slot <= 1:
            far_swap(slot).wait_send()
        else:
            pl.when(plane >= slot)(lambda slot=slot: far_swap(slot).wait_send())
        if slot >= 1:
            pl.when(plane >= slot)(lambda slot=slot: to_plane(slot).wait_send())
    if last > 0:
        pl.when(plane == 0)(lambda: from_first().wait_send())


def back(prefix, qx, dox, kv_all, shared, grads, group, all_planes, shard, pieces, dims):
    kv_heads, repeat, width = dims
    rows = qx.shape[1]
    columns = kv_heads * repeat * width
    planes = group // 2
    block = kv_all.shape[1:]
    dma = pltpu.SemaphoreType.DMA
    d_attn, d_up, hidden, w_down, middle = shared
    half, model = middle.shape
    parts = 8
    narrow = model // parts
    units = d_up.shape[1]
    cut_shape = jax.ShapeDtypeStruct((rows, all_planes * shard), BF16)
    out_shape = [jax.ShapeDtypeStruct((rows, columns), F32), jax.ShapeDtypeStruct(block, F32)]
    out_shape += [cut_shape] * 2 + [jax.ShapeDtypeStruct(d_up.shape, BF16)]
    out_shape.append(jax.ShapeDtypeStruct((rows, model), BF16))
    scratch = [pltpu.VMEM((planes,) + block, BF16)] * 4 + [pltpu.VMEM(block, BF16)]
    scratch += [dma((planes,))] * 4 + [dma, dma] + [dma] * 2
    scratch += Columns.scratch(rows // 2, all_planes * shard)
    staged = [d_attn, qx, dox, kv_all, hidden]
    args = [prefix, d_up, w_down, middle]
    first = []
    if grads is not None:
        args += grads[:1]
        staged += grads[1:]
        first = [pltpu.VMEM((rows, units // pieces), BF16), dma((1,))]
    args += staged
    product = [pltpu.VMEM((2, units, narrow), BF16), dma((2,)), pltpu.VMEM((2, rows, narrow), F32)]
    product += [pltpu.VMEM((2, half, narrow), F32), dma((2,))] + [dma((parts,))] * 3
    product += TensorSum.scratch(parts, half, narrow)
    scratch = first + Staged.scratch(staged) + product + scratch
    if grads is not None:
        piece = units // pieces
        shapes = (piece, shard), (shard, units), (columns, shard)
        out_shape += [jax.ShapeDtypeStruct(s, BF16) for s in shapes]
        scratch += [pltpu.VMEM((pieces, rows, piece), BF16)] + [dma((pieces,))] * 2
        for shape in [(piece, shard), (columns, shard)] + [(shard, piece)] * pieces:
            scratch += LineSum.scratch(planes, shape)
    return pl.pallas_call(
        functools.partial(
            back_kernel,
            group=group,
            planes=planes,
            all_planes=all_planes,
            shard=shard,
            kv_heads=kv_heads,
            repeat=repeat,
            width=width,
            coef=math.log2(math.e) / math.sqrt(width),
            scale=1.0 / math.sqrt(width),
            sums=grads is not None,
        ),
        out_shape=out_shape,
        in_specs=[smem()] + [ANYWHERE] * (len(args) - 1),
        out_specs=vmem(4) + [ANYWHERE] * 2 + vmem(len(out_shape) - 6),
        scratch_shapes=scratch,
        compiler_params=pltpu.CompilerParams(
            vmem_limit_bytes=BACK_VMEM_LIMIT, collective_id=1, has_side_effects=True
        ),
        cost_estimate=COST,
        name="back",
    )(*args)


def smem():
    return pl.BlockSpec(memory_space=pltpu.SMEM)


def out_kernel(*refs, planes, shard, blocks):
    refs = list(refs)

    def take(count):
        out = refs[:count]
        del refs[:count]
        return out

    arrays = take(4)
    gain_ref, w_down_ref = take(2)
    middle_ref, h_ref, d_hidden_out, og_keep, og_came, heads_came = take(6)
    buffers = take(4)
    heads_ref, w_ref, og_ref, x_ref = buffers
    inputs = Staged(arrays, buffers, *take(1))
    d_hidden_ref, d_hidden_sem = take(2)
    down_buf, down_sems, mine_ref, h_send, h_recv, heads_send, heads_recv = take(7)
    scratch = refs
    device = lax.axis_index("dp")
    core, core_peer, y_peer = tensor_peers()
    x_at = device % 2
    x_peer = {"dp": device + 1 - 2 * x_at}
    half = middle_ref.shape[0]
    total = TensorSum(scratch[:8], mine_ref, core, core_peer, y_peer)
    chunks, width = total.chunks, total.width
    place = (x_at, core, x_peer, core_peer, planes, shard)
    og = Columns(og_ref, og_keep, og_came, scratch[8:14], *place)
    tiles = down_sems.shape[0]
    tile = down_buf.shape[0] // tiles

    def load(t):
        at = pl.ds(t * tile, tile)
        return pltpu.make_async_copy(w_down_ref.at[at, :], down_buf.at[at, :], down_sems.at[t])

    inputs.start()
    for t in range(tiles):
        load(t).start()
    greet([(x_peer, True), (core_peer, True), (y_peer, True)])
    heads_swap = remote(heads_ref, heads_came, heads_send, heads_recv, x_peer)
    inputs.wait(heads_ref, w_ref)
    heads_swap.start()
    for i in range(chunks):
        total.add(i, dot(heads_ref[...], w_ref[:, i * width : (i + 1) * width]))
    inputs.wait(og_ref)
    og.start()
    og.store()
    for t in range(tiles):
        at = slice(t * tile, (t + 1) * tile)
        load(t).wait()
        d_hidden_ref[:, at] = dot(og_ref[...], down_buf[at, :], NT)
    d_hidden_copy = pltpu.make_async_copy(d_hidden_ref, d_hidden_out, d_hidden_sem)
    d_hidden_copy.start()
    mine = rows_of(core, half)
    inputs.wait(x_ref)
    for i in range(chunks):
        at = slice(i * width, (i + 1) * width)
        middle_ref[:, at] = x_ref[mine, at].astype(F32) + total.total(i)
    step = half // blocks

    def to_core(b):
        rows = h_ref.at[pl.ds(pl.multiple_of(core * half + b * step, step), step), :]
        return remote(rows, rows, h_send.at[b], h_recv.at[b], core_peer)

    for b in range(blocks):
        v = middle_ref[b * step : (b + 1) * step, :]
        r = lax.rsqrt(jnp.mean(v * v, axis=1, keepdims=True) + EPS)
        at = pl.ds(pl.multiple_of(core * half + b * step, step), step)
        h_ref[at, :] = (v * r * gain_ref[...]).astype(BF16)
        to_core(b).start()
    og.forward()
    og.finish()
    d_hidden_copy.wait()
    heads_swap.wait_recv()
    heads_swap.wait_send()
    for b in range(blocks):
        to_core(b).wait_recv()
        to_core(b).wait_send()
    total.finish()


def attention_out(heads, w_out, x, gain, out_grad, w_down, planes, shard):
    rows, model = x.shape
    half = rows // 2
    units = w_down.shape[0]
    chunks, blocks = 4, 4
    tiles = units // math.gcd(units, 256)
    dma = pltpu.SemaphoreType.DMA
    cut_shape = jax.ShapeDtypeStruct((rows, planes * shard), BF16)
    return pl.pallas_call(
        functools.partial(out_kernel, planes=planes, shard=shard, blocks=blocks),
        out_shape=[
            jax.ShapeDtypeStruct((half, model), F32),
            jax.ShapeDtypeStruct((rows, model), BF16),
            jax.ShapeDtypeStruct((rows, units), F32),
        ]
        + [cut_shape] * 2
        + [jax.ShapeDtypeStruct(heads.shape, BF16)],
        in_specs=[ANYWHERE] * 4 + vmem(1) + [ANYWHERE],
        out_specs=vmem(2) + [ANYWHERE] + vmem(3),
        scratch_shapes=Staged.scratch([heads, w_out, out_grad, x])
        + [pltpu.VMEM((rows, units), F32), dma]
        + [pltpu.VMEM((units, model), BF16), dma((tiles,))]
        + [pltpu.VMEM((2, rows, model // chunks), F32), dma((blocks,)), dma((blocks,)), dma, dma]
        + TensorSum.scratch(chunks, half, model // chunks)
        + Columns.scratch(half, planes * shard),
        compiler_params=pltpu.CompilerParams(
            vmem_limit_bytes=VMEM_LIMIT, collective_id=4, has_side_effects=True
        ),
        cost_estimate=COST,
        name="attention_out",
    )(heads, w_out, out_grad, x, gain, w_down)


def middle_kernel(*refs, planes, shard, heads, width, pieces, blocks, sums):
    refs = list(refs)

    def take(count):
        out = refs[:count]
        del refs[:count]
        return out

    w_gate_ref, w_up_ref, gain_ref = take(3)
    count = 10 if sums else 8
    arrays = take(count)
    outs = take(3)
    hid_came_ref, a_ref, gain_out_ref, qx_ref, dox_ref, h_keep, h_came = take(7)
    if sums:
        down_outs = take(pieces - 1)
    buffers = take(count)
    inputs = Staged(arrays, buffers, *take(1))
    h_ref, d_ref, middle_ref, og_ref, w_out_ref, q_ref, o_ref, lse_ref = buffers[:8]
    if sums:
        og_keep, og_came = buffers[8:]
    out_buffers = take(3)
    hid_ref, gate_ref, up_ref = out_buffers
    outputs = Staged(outs, out_buffers, *take(1), out=True)
    gate_buf, up_buf, load_sems, c_ref, mine_ref = take(5)
    hid_send, hid_recv, a_send, a_recv = take(4)
    sum_scratch, h_scratch = take(8), take(6)
    device = lax.axis_index("dp")
    core, core_peer, y_peer = tensor_peers()
    plane = device // 2
    x_at = device % 2
    x_peer = {"dp": device + 1 - 2 * x_at}
    meets = [(x_peer, True), (core_peer, True), (y_peer, True)]
    h_two = Columns(h_ref, h_keep, h_came, h_scratch, x_at, core, x_peer, core_peer, planes, shard)
    half = middle_ref.shape[0]
    total = TensorSum(sum_scratch, mine_ref, core, core_peer, y_peer)
    chunks, columns = total.chunks, total.width
    units = hid_ref.shape[1]
    piece = units // pieces
    tile = 256
    tiles = units // tile
    if sums:
        downs = [LineSum(take(6), device, plane, planes) for _ in range(pieces - 1)]
        meets += [({"dp": device + 2}, plane < planes - 1), ({"dp": device - 2}, plane > 0)]

    def loads(t):
        at = pl.ds(t * tile, tile)
        return (
            pltpu.make_async_copy(w_gate_ref.at[:, at], gate_buf.at[:, at], load_sems.at[2 * t]),
            pltpu.make_async_copy(w_up_ref.at[:, at], up_buf.at[:, at], load_sems.at[2 * t + 1]),
        )

    inputs.start(h_ref)
    for t in range(tiles):
        for load in loads(t):
            load.start()
        if t == 0:
            inputs.start(d_ref)
    inputs.start(*buffers[2:])
    greet(meets)
    inputs.wait(h_ref)

    def swap(k):
        at = pl.ds(k * piece, piece)
        return remote(hid_ref.at[:, at], hid_came_ref.at[:, at], hid_send.at[k], hid_recv.at[k], x_peer)

    for t in range(tiles):
        for load in loads(t):
            load.wait()
        if t == 0:
            inputs.wait(d_ref)
        at = slice(t * tile, (t + 1) * tile)
        gate = dot(h_ref[...], gate_buf[:, at])
        up = dot(h_ref[...], up_buf[:, at])
        sig = 1.0 / (1.0 + jnp.exp(-gate))
        silu = gate * sig
        d = d_ref[:, at]
        hid_ref[:, at] = (silu * up).astype(BF16)
        up_ref[:, at] = (d * silu).astype(BF16)
        gate_ref[:, at] = (d * up * (sig * (1.0 + gate * (1.0 - sig)))).astype(BF16)
        if (t + 1) * tile % piece == 0:
            swap((t + 1) * tile // piece - 1).start()

    outputs.start()
    inputs.wait(*buffers[2:])

    def down_start(k):
        if sums:
            at = pl.ds(k * piece, piece)
            swap(k).wait_recv()
            downs[k].fill_columns(hid_ref.at[:, at], hid_came_ref.at[:, at], og_keep, og_came)
            downs[k].start()

    def down_advance(k, step):
        if sums and step <= planes - 2:
            downs[k].advance(step)

    for i in range(chunks):
        at = slice(i * columns, (i + 1) * columns)
        total.add(i, dot(gate_ref[...], gate_buf[at, :], NT) + dot(up_ref[...], up_buf[at, :], NT))
        if i == chunks - 2:
            down_start(0)
    for i in range(chunks):
        if i == 1:
            down_start(1)
            h_two.start()
        if i == 2:
            down_advance(0, 1)
        c_ref[:, i * columns : (i + 1) * columns] = total.total(i)
    down_advance(0, 2)

    step = half // blocks

    def to_core(b):
        rows = a_ref.at[pl.ds(pl.multiple_of(core * half + b * step, step), step), :]
        return remote(rows, rows, a_send.at[b], a_recv.at[b], core_peer)

    gain_out_ref[...] = jnp.zeros_like(gain_out_ref)
    for b in range(blocks):
        at = slice(b * step, (b + 1) * step)
        whole_at = pl.ds(pl.multiple_of(core * half + b * step, step), step)
        c = c_ref[at, :]
        v = middle_ref[at, :]
        r = lax.rsqrt(jnp.mean(v * v, axis=1, keepdims=True) + EPS)
        n = v * r
        gain_out_ref[...] += jnp.sum(c * n, axis=0, keepdims=True)
        gc = c * gain_ref[...]
        d = r * (gc - n * jnp.mean(n * gc, axis=1, keepdims=True)) + og_ref[whole_at, :].astype(F32)
        a_ref[whole_at, :] = d.astype(BF16)
        to_core(b).start()

    lane = lax.broadcasted_iota(jnp.int32, (half, width), 1)

    def extra(value):
        a, b, c = split_three(value)
        return jnp.where(lane == 0, a, jnp.where(lane == 1, b, jnp.where(lane == 2, c, 0.0))).astype(BF16)

    def prepare(which):
        at_rows = rows_of(which, half)
        d_heads = dot(a_ref[at_rows, :], w_out_ref[...], NT)
        for head in range(heads):
            at = slice(head * width, (head + 1) * width)
            qx_ref[head, at_rows, :width] = q_ref[at_rows, at]
            qx_ref[head, at_rows, width:] = extra(lse_ref[at_rows, at])
            d = d_heads[:, at].astype(BF16)
            delta = jnp.sum(d.astype(F32) * o_ref[at_rows, at].astype(F32), axis=1, keepdims=True)
            dox_ref[head, at_rows, :width] = d
            dox_ref[head, at_rows, width:] = extra(jnp.broadcast_to(delta, (half, width)))

    down_advance(1, 1)
    h_two.store()
    prepare(core)
    h_two.forward()
    for b in range(blocks):
        to_core(b).wait_recv()
    prepare(1 - core)
    down_advance(1, 2)
    for b in range(blocks):
        to_core(b).wait_send()
    total.finish()
    h_two.finish()
    outputs.wait()
    for k in range(pieces):
        if k == pieces - 1 or not sums:
            swap(k).wait_recv()
        swap(k).wait_send()
    if sums:
        for k in range(pieces - 1):
            for step in range(3, planes - 1):
                downs[k].advance(step)
            downs[k].finish(down_outs[k])


def middle_of(w_gate, w_up, h_two, d_hidden, middle, out_grad, gain, w_out, q, out, lse, cuts, pieces, planes, shard, width):
    half, model = middle.shape
    rows, units = d_hidden.shape
    columns = q.shape[1]
    heads = columns // width
    chunks, blocks = 4, 4
    dma = pltpu.SemaphoreType.DMA
    staged = [h_two, d_hidden, middle, out_grad, w_out, q, out, lse] + ([] if cuts is None else cuts)
    args = [w_gate, w_up, gain, *staged]
    unit_shape = jax.ShapeDtypeStruct((rows, units), BF16)
    out_shape = [unit_shape] * 4 + [
        jax.ShapeDtypeStruct((rows, model), BF16),
        jax.ShapeDtypeStruct((1, model), F32),
    ]
    out_shape += [jax.ShapeDtypeStruct((heads, rows, 2 * width), BF16)] * 2
    out_shape += [jax.ShapeDtypeStruct((rows, planes * shard), BF16)] * 2
    scratch = Staged.scratch(staged) + Staged.scratch([unit_shape] * 3)
    scratch += [pltpu.VMEM((model, units), BF16)] * 2 + [dma((2 * units // 256,))]
    scratch += [pltpu.VMEM((half, model), F32), pltpu.VMEM((2, rows, model // chunks), F32)]
    scratch += [dma((pieces,))] * 2 + [dma((blocks,))] * 2
    scratch += TensorSum.scratch(chunks, half, model // chunks)
    scratch += Columns.scratch(half, planes * shard)
    if cuts is not None:
        out_shape += [jax.ShapeDtypeStruct((units // pieces, shard), BF16)] * (pieces - 1)
        scratch += LineSum.scratch(planes, (units // pieces, shard)) * (pieces - 1)
    return pl.pallas_call(
        functools.partial(
            middle_kernel,
            planes=planes,
            shard=shard,
            heads=heads,
            width=width,
            pieces=pieces,
            blocks=blocks,
            sums=cuts is not None,
        ),
        out_shape=out_shape,
        in_specs=[ANYWHERE] * 2 + vmem(1) + [ANYWHERE] * len(staged),
        out_specs=[ANYWHERE] * 3 + vmem(len(out_shape) - 3),
        scratch_shapes=scratch,
        compiler_params=pltpu.CompilerParams(
            vmem_limit_bytes=BACK_VMEM_LIMIT, collective_id=2, has_side_effects=True
        ),
        cost_estimate=COST,
        name="middle",
    )(*args)


def through_rope(d_ref, raw_ref, gain, cos, sin, out_ref, width, plain):
    columns = d_ref.shape[1]
    total = jnp.zeros((1, width), F32)
    for at in range(0, columns - plain, width):
        d = d_ref[:, at : at + width]
        c = d * cos - roll_half(d) * sin
        v = raw_ref[:, at : at + width]
        r = lax.rsqrt(jnp.mean(v * v, axis=1, keepdims=True) + EPS)
        n = v * r
        total = total + jnp.sum(c * n, axis=0, keepdims=True)
        gc = gain * c
        out_ref[:, at : at + width] = (r * (gc - n * jnp.mean(n * gc, axis=1, keepdims=True))).astype(BF16)
    if plain:
        out_ref[:, columns - plain :] = d_ref[:, columns - plain :].astype(BF16)
    return total


def front_kernel(*refs, dp_size, planes, shard, chunks, blocks, sums):
    refs = list(refs)

    def take(count):
        out = refs[:count]
        del refs[:count]
        return out

    q_gain, k_gain, attn_gain, mlp_gain_ref, add_array = take(5)
    count = 15 if sums else 11
    arrays = take(count)
    x_grad, gains, dq_ref, dq_came, dkv_ref, dkv_came, one_ref, one_came = take(8)
    if sums:
        w_up_out, w_q_out, w_kv_out = take(3)
    buffers = take(count)
    inputs = Staged(arrays, buffers, *take(1))
    dkv_in, k_raw, cos_ref, sin_ref, dq_in, q_raw, one_all = buffers[:7]
    x_ref, w_q, w_k, w_v = buffers[7:11]
    if sums:
        two_ref, two_came, up_ref, up_came = buffers[11:]
    mine, gain_came, c_ref, add_ref, add_sem = take(5)
    swap_sems, one_sems, gain_sems = take(4), take(2), take(2)
    one_sum_scratch, one_scratch = take(8), take(6)
    half = x_ref.shape[0] // 2
    model = x_ref.shape[1]
    width = model // chunks
    head = cos_ref.shape[1]
    kv_width = w_k.shape[1]

    device = lax.axis_index("dp")
    core, core_peer, y_peer = tensor_peers()
    x_at = device % 2
    x_peer = {"dp": device + 1 - 2 * x_at}
    plane = device // 2
    one = Columns(one_all, one_ref, one_came, one_scratch, x_at, core, x_peer, core_peer, planes, shard)
    bits = [1 << i for i in range(dp_size.bit_length() - 1)]
    dp_peers = [{"dp": device + bit - 2 * bit * ((device // bit) % 2)} for bit in bits]
    gain_peers = [core_peer, y_peer] + dp_peers
    meets = [(peer, True) for peer in gain_peers]
    if sums:
        up_sum, q_sum, kv_sum = (LineSum(take(6), device, plane, planes, True) for _ in range(3))
        meets += [({"dp": device + 2}, plane < planes - 1), ({"dp": device - 2}, plane > 0)]

    mine_rows = rows_of(core, half)
    add_load = pltpu.make_async_copy(add_array.at[mine_rows, :], add_ref, add_sem)
    inputs.start(one_all)
    if sums:
        inputs.start(*buffers[11:])
    inputs.start(*buffers[:6])
    inputs.start(*buffers[7:11])
    add_load.start()
    greet(meets)
    inputs.wait(one_all)
    one.start()
    if sums:
        inputs.wait(*buffers[11:])
        up_sum.fill_rows(two_ref, two_came, up_ref, up_came)
        up_sum.start()
    inputs.wait(*buffers[:6])
    cos, sin = cos_ref[...], sin_ref[...]
    k_total = through_rope(dkv_in, k_raw, k_gain[...], cos, sin, dkv_ref, head, kv_width)
    kv_swap = remote(dkv_ref, dkv_came, swap_sems[0], swap_sems[1], x_peer)
    kv_swap.start()
    q_total = through_rope(dq_in, q_raw, q_gain[...], cos, sin, dq_ref, head, 0)
    q_swap = remote(dq_ref, dq_came, swap_sems[2], swap_sems[3], x_peer)
    q_swap.start()
    inputs.wait(*buffers[7:11])

    one_sum = TensorSum(one_sum_scratch, mine, core, core_peer, y_peer)
    x = x_ref[...].astype(F32)
    r = lax.rsqrt(jnp.mean(x * x, axis=1, keepdims=True) + EPS)
    for i in range(chunks):
        at = slice(i * width, (i + 1) * width)
        part = (
            dot(dq_ref[...], w_q[at, :], NT)
            + dot(dkv_ref[:, :kv_width], w_k[at, :], NT)
            + dot(dkv_ref[:, kv_width:], w_v[at, :], NT)
        )
        one_sum.add(i, part)
        gains[0, :, at] = jnp.sum(part * (x_ref[:, at].astype(F32) * r), axis=0, keepdims=True)
    gains[0, :, model : 2 * model] = mlp_gain_ref[...]
    gains[0, :, 2 * model : 2 * model + head] = q_total
    gains[0, :, 2 * model + head :] = k_total
    one.forward()
    one.store()

    def gain_swap(k):
        return remote(
            gains.at[k], gain_came.at[k], gain_sems[0].at[k], gain_sems[1].at[k], gain_peers[k]
        )

    def gain_add(k):
        gain_swap(k).wait_recv()
        gains[k + 1] = gains[k] + gain_came[k]
        if k + 1 < len(gain_peers):
            gain_swap(k + 1).start()

    gain_swap(0).start()

    def advance(line, step):
        if sums and step <= planes - 2:
            line.advance(step)

    gain_add(0)
    if sums:
        advance(up_sum, 1)
        kv_swap.wait_recv()
        one.over_core().wait_recv()
        kv_sum.fill_rows(one_ref, one_came, dkv_ref, dkv_came)
        kv_sum.start()
    gain_add(1)
    if sums:
        q_swap.wait_recv()
        q_sum.fill_rows(one_ref, one_came, dq_ref, dq_came)
        q_sum.start()
        advance(up_sum, 2)
    gain_add(2)

    def give(out, sems):
        rows = out.at[mine_rows, :]
        return remote(rows, rows, sems[0], sems[1], core_peer)

    for i in range(chunks):
        c_ref[:, i * width : (i + 1) * width] = one_sum.total(i)
    add_load.wait()
    step = half // blocks
    for b in range(blocks):
        at = slice(b * step, (b + 1) * step)
        whole_at = pl.ds(pl.multiple_of(core * half + b * step, step), step)
        v = x_ref[whole_at, :].astype(F32)
        v_r = lax.rsqrt(jnp.mean(v * v, axis=1, keepdims=True) + EPS)
        n = v * v_r
        gc = c_ref[at, :] * attn_gain[...]
        d = v_r * (gc - n * jnp.mean(n * gc, axis=1, keepdims=True))
        x_grad[whole_at, :] = (d + add_ref[at, :].astype(F32)).astype(BF16)
    give(x_grad, one_sems).start()
    for k in range(3, len(gain_peers)):
        gain_add(k)
    if sums:
        advance(kv_sum, 1)
        advance(q_sum, 1)
    if sums:
        advance(kv_sum, 2)
        advance(q_sum, 2)
        for line in (up_sum, kv_sum, q_sum):
            for step in range(3, planes - 1):
                advance(line, step)
        up_sum.finish(w_up_out)
        kv_sum.finish(w_kv_out)
        q_sum.finish(w_q_out)
    else:
        kv_swap.wait_recv()
        q_swap.wait_recv()
        one.over_core().wait_recv()
    one.over_x().wait_send()
    one.over_core().wait_send()
    kv_swap.wait_send()
    q_swap.wait_send()
    give(x_grad, one_sems).wait_recv()
    give(x_grad, one_sems).wait_send()
    for k in range(len(gain_peers)):
        gain_swap(k).wait_send()
    one_sum.finish()


def front(dq, dkv, q_raw, k_raw, q_gain, k_gain, cos, sin, h_one, weights, x, d_attn, attn_gain, mlp_gain, grads, dp_size, shard):
    rows, model = x.shape
    half = rows // 2
    planes = dp_size // 2
    chunks = 4
    width = model // chunks
    stages = dp_size.bit_length() + 1
    dma = pltpu.SemaphoreType.DMA
    gains = (2 * model + 2 * cos.shape[1],)
    staged = [dkv, k_raw, cos, sin, dq, q_raw, h_one, x, *weights]
    if grads is not None:
        staged += grads
    args = [q_gain, k_gain, attn_gain, mlp_gain, d_attn, *staged]
    cut_shape = jax.ShapeDtypeStruct((rows, planes * shard), BF16)
    whole = jax.ShapeDtypeStruct((rows, model), BF16)
    q_shape, kv_shape = jax.ShapeDtypeStruct(dq.shape, BF16), jax.ShapeDtypeStruct(dkv.shape, BF16)
    out_shape = [whole, jax.ShapeDtypeStruct((stages + 1, 1) + gains, F32)]
    out_shape += [q_shape, q_shape, kv_shape, kv_shape, cut_shape, cut_shape]
    scratch = Staged.scratch(staged)
    scratch += [pltpu.VMEM((2, rows, width), F32)]
    scratch += [pltpu.VMEM((stages, 1) + gains, F32), pltpu.VMEM((half, model), F32)]
    scratch += [pltpu.VMEM((half, model), BF16), dma]
    scratch += [dma] * 6 + [dma((stages,))] * 2
    scratch += TensorSum.scratch(chunks, half, width)
    scratch += Columns.scratch(half, planes * shard)
    if grads is not None:
        for columns in (grads[2].shape[1], dq.shape[1], dkv.shape[1]):
            out_shape.append(jax.ShapeDtypeStruct((shard, columns), BF16))
            scratch += LineSum.scratch(planes, (shard, columns))
    return pl.pallas_call(
        functools.partial(
            front_kernel,
            dp_size=dp_size,
            planes=planes,
            shard=shard,
            chunks=chunks,
            blocks=4,
            sums=grads is not None,
        ),
        out_shape=out_shape,
        in_specs=vmem(4) + [ANYWHERE] * (len(args) - 4),
        out_specs=vmem(len(out_shape)),
        scratch_shapes=scratch,
        compiler_params=pltpu.CompilerParams(
            vmem_limit_bytes=BACK_VMEM_LIMIT, collective_id=3, has_side_effects=True
        ),
        cost_estimate=COST,
        name="front",
    )(*args)


class Chain:
    def __init__(self):
        self.last = None

    def mark(self, value):
        self.last = value

    def __call__(self, *values):
        if self.last is None:
            return values
        return lax.optimization_barrier((*values, self.last))[:-1]


class ZSum:
    def __init__(self, part, dim, shard, planes, z_at):
        self.part, self.dim, self.shard, self.planes, self.z_at = part, dim, shard, planes, z_at
        self.at = 0
        self.came = None

    def term(self, j):
        j = jnp.clip(j, 0, self.planes - 1)
        return lax.dynamic_slice_in_dim(self.part, j * self.shard, self.shard, self.dim)

    def send(self, up, down):
        last = self.planes - 1
        self.at += 1
        up_pairs = [(2 * z + x, 2 * z + 2 + x) for z in range(last) for x in range(2) if z < self.at]
        down_pairs = [
            (2 * (last - z) + x, 2 * (last - 1 - z) + x)
            for z in range(last)
            for x in range(2)
            if z < self.at
        ]
        self.came = lax.ppermute(up, "dp", up_pairs), lax.ppermute(down, "dp", down_pairs)

    def terms(self):
        planes, z_at, at = self.planes, self.z_at, self.at
        return self.term(planes - 1 - at + z_at), self.term(at + 1 - planes + z_at)

    def start(self):
        self.send(*self.terms())

    def step(self, chain):
        if self.at >= self.planes - 1:
            return
        up, down = chain(*self.came)
        up_term, down_term = self.terms()
        up, down = up + up_term, down + down_term
        chain.mark(up)
        self.send(up, down)

    def finish(self, chain):
        if self.at == 0:
            self.start()
        while self.at < self.planes - 1:
            self.step(chain)
        up, down = chain(*self.came)
        total = self.term(self.z_at).astype(F32) + up.astype(F32) + down.astype(F32)
        chain.mark(total)
        return total


def shards(
    dp_size,
    tensor_size,
    tokens,
    norm_attn,
    w_query,
    key_weight,
    value_weight,
    query_gain,
    key_gain,
    w_out,
    norm_mlp,
    w_gate,
    w_up,
    w_down,
    out_grad,
    prefix_len,
):
    rows, model = tokens.shape
    width = query_gain.shape[0]
    kv_heads = key_weight.shape[1] // width
    repeat = w_query.shape[1] // key_weight.shape[1]
    dims = (kv_heads, repeat, width)
    group = dp_size // prefix_len.shape[0]
    planes = dp_size // 2
    group_planes = group // 2
    half = rows // 2
    shard = model // dp_size
    assert tensor_size == 4 and MAX_PREFIX <= 4 * rows

    device = lax.axis_index("dp")
    x_at = device % 2
    z_at = device // 2
    sequence = device // group
    member = device % group
    plane = member // 2
    prefix = jnp.sum(jnp.where(jnp.arange(prefix_len.shape[0]) == sequence, prefix_len, 0))

    x_pairs = [(d, d ^ 1) for d in range(dp_size)]

    def x_swap(value):
        return lax.ppermute(value, "dp", x_pairs)

    positions = (member * rows + jnp.arange(rows)).astype(F32)
    counter = jnp.arange(width // 2, dtype=F32)
    angles = positions[:, None] * (ROPE_BASE ** (-2.0 * counter / width))[None, :]
    cos, sin = jnp.cos(angles), jnp.sin(angles)
    cos = jnp.concatenate([cos, cos], axis=1)
    sin = jnp.concatenate([-sin, sin], axis=1)
    norm_attn_row = norm_attn[None, :]
    norm_mlp_row = norm_mlp[None, :]
    q_gain_row = query_gain[None, :]
    k_gain_row = key_gain[None, :]

    h_one, q, kv, q_raw, k_raw = project(
        tokens,
        norm_attn_row,
        (w_query, key_weight, value_weight),
        (q_gain_row, k_gain_row, k_gain_row),
        (True, True, False),
        cos,
        sin,
        "project",
    )
    prefix_at = prefix[None].astype(jnp.int32)
    heads_b, lse, kv_all = attn_fwd(prefix_at, q, kv, group, dims)
    fused = planes == group_planes and shard % 128 == 0
    pieces = 3
    middle, h_two, d_hidden, og_keep, og_came, heads_came = attention_out(
        heads_b, w_out, tokens, norm_mlp_row, out_grad, w_down, planes, shard
    )
    outs = middle_of(
        w_gate,
        w_up,
        h_two,
        d_hidden,
        middle,
        out_grad,
        norm_mlp_row,
        w_out,
        q,
        heads_b,
        lse,
        [og_keep, og_came] if fused else None,
        pieces,
        planes,
        shard,
        width,
    )
    hidden, d_gate, d_up, hidden_came, d_attn, norm_mlp_part, qx, dox, h_two_keep, h_two_came = outs[:10]

    grads = None
    if fused:
        grads = [hidden_came, og_keep, og_came, d_gate, h_two_keep, h_two_came]
        grads += [heads_b, heads_came]
        w_down_parts = outs[10:]
    shared = [d_attn, d_up, hidden, w_down, middle]
    outs = back(prefix_at, qx, dox, kv_all, shared, grads, group, planes, shard, pieces, dims)
    dq, kv_grad, d_attn_keep, d_attn_came, up_came, block_out = outs[:6]
    chain = Chain()
    chain.mark(dq)
    if fused:
        w_down_grad = jnp.concatenate([*w_down_parts, outs[6]], axis=0)
        w_gate_grad, w_out_grad = outs[7:]
    else:
        down_part = (dot(hidden, og_keep, TN) + dot(hidden_came, og_came, TN)).astype(BF16)
        w_down_grad = ZSum(down_part, 1, shard, planes, z_at).finish(chain)
        gate_part = dot(h_two_keep, d_gate, TN) + dot(h_two_came, x_swap(d_gate), TN)
        w_gate_grad = ZSum(gate_part.astype(BF16), 0, shard, planes, z_at).finish(chain)
        out_part = dot(heads_b, d_attn_keep, TN) + dot(heads_came, d_attn_came, TN)
        w_out_grad = ZSum(out_part.astype(BF16), 1, shard, planes, z_at).finish(chain)

    up_grads = [h_two_keep, h_two_came, d_up, up_came] if fused else None
    outs = front(
        *chain(dq),
        kv_grad,
        q_raw,
        k_raw,
        q_gain_row,
        k_gain_row,
        cos,
        sin,
        h_one,
        (w_query, key_weight, value_weight),
        tokens,
        d_attn,
        norm_attn_row,
        0.5 * norm_mlp_part,
        up_grads,
        dp_size,
        shard,
    )
    tokens_grad, gains, dq_b, dq_came, dkv_b, dkv_came, h_one_keep, h_one_came = outs[:8]
    if fused:
        w_up_grad, w_query_grad, w_kv_grad = outs[8:]
    else:
        chain.mark(tokens_grad)

        def by_rows(left, left_came, right, right_came):
            part = dot(left, right, TN) + dot(left_came, right_came, TN)
            return ZSum(part.astype(BF16), 0, shard, planes, z_at).finish(chain)

        w_up_grad = by_rows(h_two_keep, h_two_came, d_up, up_came)
        w_query_grad = by_rows(h_one_keep, h_one_came, dq_b, dq_came)
        w_kv_grad = by_rows(h_one_keep, h_one_came, dkv_b, dkv_came)
    kv_width = kv_heads * width
    gains = gains[-1, 0]
    w_kv_grad = w_kv_grad.astype(F32)
    return (
        block_out,
        tokens_grad.astype(F32),
        lax.dynamic_slice_in_dim(gains, device * shard, shard, 0),
        w_query_grad.astype(F32),
        w_kv_grad[:, :kv_width],
        w_kv_grad[:, kv_width:],
        gains[2 * model : 2 * model + width],
        gains[2 * model + width :],
        w_out_grad.astype(F32),
        lax.dynamic_slice_in_dim(gains, model + device * shard, shard, 0),
        w_gate_grad.astype(F32),
        w_up_grad.astype(F32),
        w_down_grad.astype(F32),
    )


def solution(mesh):
    placed = (
        P("dp", None),
        P(),
        P(None, "tensor"),
        P(None, "tensor"),
        P(None, "tensor"),
        P(),
        P(),
        P("tensor", None),
        P(),
        P(None, "tensor"),
        P(None, "tensor"),
        P("tensor", None),
        P("dp", None),
        P(),
    )
    return jax.shard_map(
        functools.partial(shards, mesh.shape["dp"], mesh.shape["tensor"]),
        mesh=mesh,
        in_specs=placed,
        out_specs=(
            P("dp", None),
            P("dp", None),
            P("dp"),
            P("dp", "tensor"),
            P("dp", "tensor"),
            P("dp", "tensor"),
            P(),
            P(),
            P("tensor", "dp"),
            P("dp"),
            P("dp", "tensor"),
            P("dp", "tensor"),
            P("tensor", "dp"),
        ),
        check_vma=False,
    )
```

```python
import functools
import math

import jax
import jax.numpy as jnp
from jax import lax
from jax.experimental import pallas as pl
from jax.experimental.pallas import tpu as pltpu
from jax.sharding import PartitionSpec as P

F32 = jnp.float32
BF16 = jnp.bfloat16
EPS = 1e-06
ROPE_BASE = 1000000.0
MAX_PREFIX = 2048
VMEM_LIMIT = 56 * 2**20
BACK_VMEM_LIMIT = 60 * 2**20

COST = pl.CostEstimate(flops=1000, bytes_accessed=1000, transcendentals=0)

NN = (((1,), (0,)), ((), ()))
NT = (((1,), (1,)), ((), ()))
TN = (((0,), (0,)), ((), ()))


def dot(left, right, dims=NN):
    return lax.dot_general(left, right, dims, preferred_element_type=F32)


def vmem(count):
    return [pl.BlockSpec(memory_space=pltpu.VMEM)] * count


def params():
    return pltpu.CompilerParams(vmem_limit_bytes=VMEM_LIMIT)


def greet(peers):
    barrier = pltpu.get_barrier_semaphore()
    count = 0
    for peer, there in peers:

        def signal(peer=peer):
            pl.semaphore_signal(barrier, 1, device_id=peer, device_id_type=pl.DeviceIdType.MESH)

        if there is True:
            signal()
            count = count + 1
        else:
            pl.when(there)(signal)
            count = count + there.astype(jnp.int32)
    pl.semaphore_wait(barrier, count)


def remote(src, dst, send, recv, peer):
    return pltpu.make_async_remote_copy(
        src_ref=src,
        dst_ref=dst,
        send_sem=send,
        recv_sem=recv,
        device_id=peer,
        device_id_type=pl.DeviceIdType.MESH,
    )


class Staged:
    def __init__(self, arrays, buffers, sems, out=False):
        self.copies = []
        for i, (array, buffer) in enumerate(zip(arrays, buffers)):
            ends = (buffer, array) if out else (array, buffer)
            self.copies.append((buffer, pltpu.make_async_copy(*ends, sems.at[i])))

    @staticmethod
    def scratch(shapes):
        return [pltpu.VMEM(s.shape, s.dtype) for s in shapes] + [pltpu.SemaphoreType.DMA((len(shapes),))]

    def start(self, *buffers):
        for buffer, copy in self.copies:
            if not buffers or any(buffer is b for b in buffers):
                copy.start()

    def wait(self, *buffers):
        for buffer, copy in self.copies:
            if not buffers or any(buffer is b for b in buffers):
                copy.wait()


ANYWHERE = pl.BlockSpec(memory_space=pl.ANY)


def tensor_peers():
    t = lax.axis_index("tensor")
    core = t % 2
    y = t // 2
    return core, {"tensor": t + 1 - 2 * core}, {"tensor": t + 2 - 4 * y}


def rows_of(core, half):
    return pl.ds(pl.multiple_of(core * half, half), half)


def cut_into(out, out_rows, ref, ref_rows, side, planes, shard):
    for z in range(planes):
        to = slice(z * shard, (z + 1) * shard)
        if shard % 128 == 0:
            at = pl.ds(pl.multiple_of((2 * z + side) * shard, shard), shard)
            out[out_rows, to] = ref[ref_rows, at]
        else:
            low = ref[ref_rows, 2 * z * shard : (2 * z + 1) * shard]
            high = ref[ref_rows, (2 * z + 1) * shard : (2 * z + 2) * shard]
            out[out_rows, to] = jnp.where(side == 0, low, high)


class Columns:
    def __init__(self, whole, keep, came, scratch, x_at, core, x_peer, core_peer, planes, shard):
        self.whole, self.keep, self.came = whole, keep, came
        self.send_ref, self.recv_ref, self.sems = scratch[0], scratch[1], scratch[2:]
        self.x_at, self.core, self.cut = x_at, core, (planes, shard)
        self.x_peer, self.core_peer = x_peer, core_peer
        self.half = whole.shape[0] // 2

    @staticmethod
    def scratch(half, columns):
        return [pltpu.VMEM((half, columns), BF16)] * 2 + [pltpu.SemaphoreType.DMA] * 4

    def over_x(self):
        return remote(self.send_ref, self.recv_ref, self.sems[0], self.sems[1], self.x_peer)

    def over_core(self):
        there = self.came.at[rows_of(self.core, self.half), :]
        return remote(self.recv_ref, there, self.sems[2], self.sems[3], self.core_peer)

    def start(self):
        mine = rows_of(self.core, self.half)
        cut_into(self.send_ref, slice(None), self.whole, mine, 1 - self.x_at, *self.cut)
        self.over_x().start()

    def store(self):
        cut_into(self.keep, slice(None), self.whole, slice(None), self.x_at, *self.cut)

    def forward(self):
        self.over_x().wait_recv()
        self.over_core().start()
        self.came[rows_of(self.core, self.half), :] = self.recv_ref[...]

    def finish(self):
        self.over_core().wait_recv()
        self.over_x().wait_send()
        self.over_core().wait_send()


class LineSum:
    def __init__(self, scratch, device, plane, planes, paced=False):
        self.paced = paced
        self.stack, self.came = scratch[:2]
        self.sems = scratch[2:]
        self.device, self.plane, self.planes = device, plane, planes

    @staticmethod
    def scratch(planes, shape):
        return [pltpu.VMEM((n,) + shape, BF16) for n in (planes, planes + 1)] + [
            pltpu.SemaphoreType.DMA((planes,))
        ] * 4

    def up(self, j):
        s = self.sems
        peer = {"dp": self.device + 2}
        return remote(self.stack.at[j], self.came.at[j], s[0].at[j], s[1].at[j], peer)

    def down(self, j):
        s = self.sems
        slot = jnp.where(self.plane - 1 == j, self.planes, j)
        peer = {"dp": self.device - 2}
        return remote(self.stack.at[j], self.came.at[slot], s[2].at[j], s[3].at[j], peer)

    def start(self):
        last = self.planes - 1

        @pl.when(self.plane == 0)
        def _():
            for j in range(last, last - 1 if self.paced else 0, -1):
                self.up(j).start()

        @pl.when(self.plane == last)
        def _():
            for j in range(1 if self.paced else last):
                self.down(j).start()

    def advance(self, step):
        plane, last = self.plane, self.planes - 1
        low, high = last - step + plane, step - last + plane
        if self.paced:

            @pl.when(plane == 0)
            def _():
                self.up(last - step + 1).wait_send()
                self.up(last - step).start()

            @pl.when(plane == last)
            def _():
                self.down(step - 1).wait_send()
                self.down(step).start()

        @pl.when((plane >= 1) & (plane <= step))
        def _():
            self.up(low).wait_recv()
            self.stack[low] += self.came[low]
            self.up(low).start()

        @pl.when((plane < last) & (plane >= last - step))
        def _():
            self.down(high).wait_recv()
            self.stack[high] += self.came[high]
            self.down(high).start()

    def finish(self, out):
        plane, planes = self.plane, self.planes

        @pl.when(plane == 0)
        def _():
            self.down(plane).wait_recv()
            out[...] = self.stack[plane] + self.came[planes]

        @pl.when(plane == planes - 1)
        def _():
            self.up(plane).wait_recv()
            out[...] = self.stack[plane] + self.came[plane]

        @pl.when((plane > 0) & (plane < planes - 1))
        def _():
            self.up(plane).wait_recv()
            self.down(plane).wait_recv()
            total = self.stack[plane].astype(F32) + self.came[plane].astype(F32)
            out[...] = (total + self.came[planes].astype(F32)).astype(BF16)

        for j in range(planes):
            ups, downs = plane < j, plane > j
            if self.paced and j > 1:
                ups = ups & (plane > 0)
            if self.paced and j < planes - 2:
                downs = downs & (plane < planes - 1)
            pl.when(ups)(lambda j=j: self.up(j).wait_send())
            pl.when(downs)(lambda j=j: self.down(j).wait_send())

    def fill_rows(self, left, left_came, right, right_came):
        shard = self.stack.shape[1]

        def body(j, carry):
            at = pl.ds(pl.multiple_of(j * shard, shard), shard)
            self.stack[j] = (
                dot(left[:, at], right[...], TN) + dot(left_came[:, at], right_came[...], TN)
            ).astype(BF16)
            return carry

        lax.fori_loop(0, self.planes, body, 0)

    def fill_columns(self, left, left_came, right, right_came):
        shard = self.stack.shape[2]
        tile = 256

        def body(t, carry):
            at = pl.ds(pl.multiple_of(t * tile, tile), tile)
            term = dot(left[:, at], right[...], TN) + dot(left_came[:, at], right_came[...], TN)
            for j in range(self.planes):
                self.stack[j, at, :] = term[:, j * shard : (j + 1) * shard].astype(BF16)
            return carry

        lax.fori_loop(0, left.shape[1] // tile, body, 0)


class TensorSum:
    def __init__(self, scratch, mine, core, core_peer, y_peer):
        self.away, self.core_came, self.both, self.y_came = scratch[:4]
        self.sems = scratch[4:]
        self.mine = mine
        self.core, self.core_peer, self.y_peer = core, core_peer, y_peer
        self.chunks, self.half, self.width = self.away.shape

    @staticmethod
    def scratch(chunks, half, width):
        return [pltpu.VMEM((chunks, half, width), BF16)] * 4 + [
            pltpu.SemaphoreType.DMA((chunks,))
        ] * 4

    def over_core(self, i):
        s = self.sems
        return remote(self.away.at[i], self.core_came.at[i], s[0].at[i], s[1].at[i], self.core_peer)

    def over_y(self, i):
        s = self.sems
        return remote(self.both.at[i], self.y_came.at[i], s[2].at[i], s[3].at[i], self.y_peer)

    def add(self, i, value):
        self.mine[i % 2] = value
        self.away[i] = self.mine[i % 2, rows_of(1 - self.core, self.half), :].astype(BF16)
        self.over_core(i).start()
        if i > 0:
            self.pass_on(i - 1)
        if i == self.chunks - 1:
            self.pass_on(i)

    def pass_on(self, i):
        self.over_core(i).wait_recv()
        mine = self.mine[i % 2, rows_of(self.core, self.half), :]
        self.both[i] = (mine + self.core_came[i].astype(F32)).astype(BF16)
        self.over_y(i).start()

    def total(self, i):
        self.over_y(i).wait_recv()
        return self.both[i].astype(F32) + self.y_came[i].astype(F32)

    def finish(self):
        for i in range(self.chunks):
            self.over_core(i).wait_send()
            self.over_y(i).wait_send()


def roll_half(value):
    return pltpu.roll(value, value.shape[-1] // 2, 1)


def visible(shape, key0, row0, prefix):
    key_pos = key0 + lax.broadcasted_iota(jnp.int32, shape, 1)
    row_pos = row0 + lax.broadcasted_iota(jnp.int32, shape, 0)
    return (key_pos <= row_pos) | (key_pos < prefix)


def attn_fwd_kernel(*refs, group, kv_heads, repeat, width, tile, coef):
    refs = list(refs)

    def take(count):
        out = refs[:count]
        del refs[:count]
        return out

    prefix_ref, gain_ref, q_gain, k_gain = take(4)
    arrays = take(6)
    o_ref, lse_ref, all_out = take(3)
    outs = take(4)
    buffers = take(6)
    inputs = Staged(arrays, buffers, *take(1))
    x_ref, w_k, w_v, cos_ref, sin_ref, w_q = buffers
    out_buffers = take(4)
    h_ref, q_ref, q_raw, k_raw = out_buffers
    outputs = Staged(outs, out_buffers, *take(1), out=True)
    kv_ref, all_ref, all_sems, acc, send_x, recv_x, send_z, recv_z, send_down = take(9)
    rows = q_ref.shape[0]
    kv_width = kv_heads * width
    planes = group // 2
    device = lax.axis_index("dp")
    member = device % group
    plane = member // 2
    x_at = member % 2
    x_other = device + 1 - 2 * x_at
    inner = plane < planes - 1
    prefix = prefix_ref[0]
    inputs.start()
    greet([({"dp": x_other}, True), ({"dp": device + 2}, inner), ({"dp": device - 2}, plane > 0)])

    def store(slot):
        return pltpu.make_async_copy(all_ref.at[slot], all_out.at[slot], all_sems.at[slot])

    def source(slot):
        return kv_ref if slot == 0 else all_ref.at[2 * slot]

    def to_x(slot):
        return pltpu.make_async_remote_copy(
            src_ref=source(slot),
            dst_ref=all_ref.at[2 * slot + 1],
            send_sem=send_x.at[slot],
            recv_sem=recv_x.at[slot],
            device_id={"dp": x_other},
            device_id_type=pl.DeviceIdType.MESH,
        )

    def to_z(slot):
        return pltpu.make_async_remote_copy(
            src_ref=source(slot - 1),
            dst_ref=all_ref.at[2 * slot],
            send_sem=send_z.at[slot],
            recv_sem=recv_z.at[slot],
            device_id={"dp": device + 2},
            device_id_type=pl.DeviceIdType.MESH,
        )

    def to_first():
        return pltpu.make_async_remote_copy(
            src_ref=kv_ref,
            dst_ref=all_ref.at[2],
            send_sem=send_down,
            recv_sem=recv_z.at[1],
            device_id={"dp": device - 2},
            device_id_type=pl.DeviceIdType.MESH,
        )

    inputs.wait(x_ref, w_k, w_v, cos_ref, sin_ref)
    x = x_ref[...].astype(F32)
    r = lax.rsqrt(jnp.mean(x * x, axis=1, keepdims=True) + EPS)
    h_ref[...] = (x * r * gain_ref[...]).astype(BF16)
    cos, sin = cos_ref[...], sin_ref[...]

    def rotate(u, gain):
        u = u * lax.rsqrt(jnp.mean(u * u, axis=1, keepdims=True) + EPS) * gain[...]
        return (u * cos + roll_half(u) * sin).astype(BF16)

    keys = dot(h_ref[...], w_k[...])
    k_raw[...] = keys
    for at in range(0, kv_width, width):
        kv_ref[:, at : at + width] = rotate(keys[:, at : at + width], k_gain)
    kv_ref[:, kv_width:] = dot(h_ref[...], w_v[...]).astype(BF16)
    ones = jnp.ones((rows, width), BF16)
    row0 = member * rows

    def work(block, other, masked, start=False):
        key0 = other * rows

        def head_pair(h, carry):
            k = block[:, pl.ds(pl.multiple_of(h * width, width), width)]
            v = block[:, pl.ds(pl.multiple_of(kv_width + h * width, width), width)]
            v = jnp.concatenate([v, ones], axis=1)
            for g in range(repeat):
                head = h * repeat + g
                for at in range(0, rows, tile):
                    q = q_ref[at : at + tile, pl.ds(pl.multiple_of(head * width, width), width)]
                    p = jnp.exp2(dot(q, k, NT) * coef)
                    if masked:
                        p = jnp.where(visible(p.shape, key0, row0 + at, prefix), p, 0.0)
                    term = dot(p.astype(BF16), v)
                    if start:
                        acc[head, at : at + tile, :] = term
                    else:
                        acc[head, at : at + tile, :] += term
            return carry

        lax.fori_loop(0, kv_heads, head_pair, 0)

    to_x(0).start()
    if planes > 1:

        @pl.when(inner)
        def _():
            to_z(1).start()

        @pl.when(plane == 1)
        def _():
            to_first().start()

    inputs.wait(w_q)
    queries = dot(h_ref[...], w_q[...])
    q_raw[...] = queries
    for at in range(0, queries.shape[1], width):
        q_ref[:, at : at + width] = rotate(queries[:, at : at + width], q_gain)
    outputs.start()
    all_ref[0] = kv_ref[...]
    store(0).start()
    work(kv_ref, member, True, True)
    to_x(0).wait_recv()
    store(1).start()
    work(all_ref.at[1], member + 1 - 2 * x_at, True)
    for slot in range(1, planes):

        def step(slot=slot):
            to_z(slot).wait_recv()
            if slot < planes - 1:

                @pl.when(inner & (plane >= slot))
                def _():
                    to_z(slot + 1).start()

            to_x(slot).start()
            store(2 * slot).start()
            there = 2 * (plane - slot)
            if slot == 1:

                @pl.when(plane == 0)
                def _():
                    work(all_ref.at[2 * slot], 2 + x_at, True)

                @pl.when(plane > 0)
                def _():
                    work(all_ref.at[2 * slot], there + x_at, False)
            else:
                work(all_ref.at[2 * slot], there + x_at, False)
            to_x(slot).wait_recv()
            store(2 * slot + 1).start()
            if slot == 1:

                @pl.when(plane == 0)
                def _():
                    work(all_ref.at[2 * slot + 1], 3 - x_at, True)

                @pl.when(plane > 0)
                def _():
                    work(all_ref.at[2 * slot + 1], there + 1 - x_at, False)
            else:
                work(all_ref.at[2 * slot + 1], there + 1 - x_at, False)

        if slot == 1:
            step()
        else:
            pl.when(plane >= slot)(step)

    for head in range(kv_heads * repeat):
        total = acc[head, :, width:]
        o_ref[:, head * width : (head + 1) * width] = (acc[head, :, :width] / total).astype(BF16)
        lse_ref[:, head * width : (head + 1) * width] = jnp.log2(total) * (1.0 / coef)

    outputs.wait()
    to_x(0).wait_send()
    for slot in range(planes):

        @pl.when((plane >= slot) | (slot <= 1))
        def _(slot=slot):
            store(2 * slot).wait()
            store(2 * slot + 1).wait()

    for slot in range(1, planes):

        @pl.when(inner & (plane >= slot - 1))
        def _(slot=slot):
            to_z(slot).wait_send()

        @pl.when((plane >= slot) | (slot == 1))
        def _(slot=slot):
            to_x(slot).wait_send()

    if planes > 1:

        @pl.when(plane == 1)
        def _():
            to_first().wait_send()


def attn_fwd(prefix, x, gain, w_query, key_weight, value_weight, q_gain, k_gain, cos, sin, group, dims):
    kv_heads, repeat, width = dims
    rows = x.shape[0]
    heads = kv_heads * repeat
    columns = heads * width
    planes = group // 2
    dma = pltpu.SemaphoreType.DMA
    block = (rows, 2 * kv_heads * width)
    staged = [x, key_weight, value_weight, cos, sin, w_query]
    early = [
        jax.ShapeDtypeStruct(x.shape, BF16),
        jax.ShapeDtypeStruct((rows, columns), BF16),
        jax.ShapeDtypeStruct((rows, columns), F32),
        jax.ShapeDtypeStruct((rows, kv_heads * width), F32),
    ]
    return pl.pallas_call(
        functools.partial(
            attn_fwd_kernel,
            group=group,
            kv_heads=kv_heads,
            repeat=repeat,
            width=width,
            tile=min(rows, 256),
            coef=math.log2(math.e) / math.sqrt(width),
        ),
        out_shape=[
            jax.ShapeDtypeStruct((rows, columns), BF16),
            jax.ShapeDtypeStruct((rows, columns), F32),
            jax.ShapeDtypeStruct((group,) + block, BF16),
        ]
        + early,
        in_specs=[smem()] + vmem(3) + [ANYWHERE] * 6,
        out_specs=vmem(2) + [ANYWHERE] * 5,
        scratch_shapes=Staged.scratch(staged)
        + Staged.scratch(early)
        + [pltpu.VMEM(block, BF16), pltpu.VMEM((group,) + block, BF16), dma((group,))]
        + [pltpu.VMEM((heads, rows, 2 * width), F32)]
        + [dma((planes,))] * 4
        + [dma],
        compiler_params=pltpu.CompilerParams(
            vmem_limit_bytes=VMEM_LIMIT, collective_id=0, has_side_effects=True
        ),
        cost_estimate=COST,
        name="attn_fwd",
    )(prefix, gain, q_gain, k_gain, *staged)


def split_three(value):
    high = value.astype(BF16)
    left = value - high.astype(F32)
    mid = left.astype(BF16)
    return high.astype(F32), mid.astype(F32), (left - mid.astype(F32)).astype(BF16).astype(F32)


def back_kernel(
    *refs, group, planes, all_planes, shard, kv_heads, repeat, width, coef, scale, sums
):
    refs = list(refs)

    def take(count):
        out = refs[:count]
        del refs[:count]
        return out

    device = lax.axis_index("dp")
    member = device % group
    plane = member // 2
    last = planes - 1
    prefix_ref, up_ref, w_down_in, middle_in = take(4)
    if sums:
        hid_arrays = take(1)
    count = 12 if sums else 5
    arrays = take(count)
    dq_ref, grad_ref, a_ref, a_came_ref, up_came_ref, block_ref = take(6)
    if sums:
        w_down_ref, w_gate_ref, w_out_ref = take(3)
    if sums:
        hid_buffers = take(1)
        hid_sems = take(1)[0]
    buffers = take(count)
    inputs = Staged(arrays, buffers, *take(1))
    a_all_ref, qx_ref, dox_ref, kv_ref, hid_ref = buffers[:5]
    if sums:
        hid_came_ref = hid_buffers[0]
        og_ref, og_came_ref, gate_ref, h_ref, h_came_ref, heads_ref, heads_came_ref = buffers[5:]
    down_buf, down_sems, mine_ref, middle_buf, middle_sems = take(5)
    block_sems = take(3)
    total_scratch = take(8)
    own_ref, far_ref, xr_ref, zr_ref, first_ref = take(5)
    send_x, recv_x, send_z, recv_z, send_first, recv_first = take(6)
    swap_sems = take(2)
    a_scratch = take(6)
    rows = qx_ref.shape[1]
    kv_width = kv_heads * width
    if sums:
        gate_came_ref, send_gate, recv_gate = take(3)
        left = w_down_ref.shape[0]
        rest = pl.ds(hid_arrays[0].shape[1] - left, left)
        hid_inputs = Staged([h.at[:, rest] for h in hid_arrays], hid_buffers, hid_sems)
        down_sum, out_sum = (LineSum(take(6), device, plane, planes) for _ in range(2))
        piece = gate_came_ref.shape[2]
        pieces = gate_ref.shape[1] // piece
        gate_sums = [LineSum(take(6), device, plane, planes) for _ in range(pieces)]
    x_at = member % 2
    x_other = device + 1 - 2 * x_at
    inner = plane < last
    prefix = prefix_ref[0]

    core, core_peer, y_peer = tensor_peers()
    x_peer = {"dp": x_other}
    total = TensorSum(total_scratch, mine_ref, core, core_peer, y_peer)
    half = total.half
    parts, narrow = total.chunks, total.width

    def load(i):
        at = pl.ds(i * narrow, narrow)
        return pltpu.make_async_copy(w_down_in.at[:, at], down_buf.at[i % 2], down_sems.at[i % 2])

    def middle_load(i):
        at = pl.ds(i * narrow, narrow)
        return pltpu.make_async_copy(middle_in.at[:, at], middle_buf.at[i % 2], middle_sems.at[i % 2])

    def block_at(i):
        return block_ref.at[rows_of(core, half), pl.ds(i * narrow, narrow)]

    def block_store(i):
        return pltpu.make_async_copy(total.both.at[i], block_at(i), block_sems[0].at[i])

    def block_give(i):
        return remote(total.both.at[i], block_at(i), block_sems[1].at[i], block_sems[2].at[i], core_peer)

    def block_add(i):
        load(i).wait()
        total.add(i, dot(hid_ref[...], down_buf[i % 2]))
        if i + 2 < parts:
            load(i + 2).start()

    def block_finish(i):
        middle_load(i).wait()
        value = middle_buf[i % 2] + total.total(i)
        total.over_y(i).wait_send()
        total.both[i] = value.astype(BF16)
        if i + 2 < parts:
            middle_load(i + 2).start()
        block_store(i).start()
        block_give(i).start()

    inputs.start(a_all_ref)
    if sums:
        hid_inputs.start()
        inputs.start(hid_ref, *buffers[5:7])
    inputs.start(*buffers[1:4])
    if sums:
        inputs.start(*buffers[7:])
    else:
        inputs.start(hid_ref)
    for i in range(2):
        load(i).start()
        middle_load(i).start()
    greet(
        [
            (x_peer, True),
            (core_peer, True),
            (y_peer, True),
            ({"dp": device + 2}, inner),
            ({"dp": device - 2}, plane > 0),
        ]
    )

    def copy(src, dst, send, recv, there):
        return remote(src, dst, send, recv, {"dp": there})

    place = (x_at, core, x_peer, core_peer, all_planes, shard)
    d_attn = Columns(a_all_ref, a_ref, a_came_ref, a_scratch, *place)
    up_swap = copy(up_ref, up_came_ref, swap_sems[0], swap_sems[1], x_other)

    def gate_swap(k):
        part = gate_ref.at[:, pl.ds(k * piece, piece)]
        return copy(part, gate_came_ref.at[k], send_gate.at[k], recv_gate.at[k], x_other)

    def gate_start(k):
        gate_swap(k).wait_recv()
        part = gate_ref.at[:, pl.ds(k * piece, piece)]
        gate_sums[k].fill_rows(h_ref, h_came_ref, part, gate_came_ref.at[k])
        gate_sums[k].start()

    lane = lax.broadcasted_iota(jnp.int32, (rows, width), 1)
    minus = jnp.where(lane < 3, -1.0, 0.0).astype(BF16)
    row0 = member * rows

    def work(block, other, masked, out):
        key0 = other * rows

        def head_group(h, carry):
            k_at = pl.ds(pl.multiple_of(h * width, width), width)
            v_at = pl.ds(pl.multiple_of(kv_width + h * width, width), width)
            k = kv_ref[block, :, k_at]
            v = kv_ref[block, :, v_at]
            kx = jnp.concatenate([k, minus], axis=1)
            vx = jnp.concatenate([v, minus], axis=1)
            dk = jnp.zeros((rows, width), F32)
            dv = jnp.zeros((rows, width), F32)
            for g in range(repeat):
                head = h * repeat + g
                qx = qx_ref[head]
                dox = dox_ref[head]
                p = jnp.exp2(dot(qx, kx, NT) * coef)
                if masked:
                    p = jnp.where(visible(p.shape, key0, row0, prefix), p, 0.0)
                ds = (p * dot(dox, vx, NT)).astype(BF16)
                dv += dot(p.astype(BF16), dox[:, :width], TN)
                dk += dot(ds, qx[:, :width], TN)
                dq_ref[:, pl.ds(pl.multiple_of(head * width, width), width)] += dot(ds, k)
            out[:, k_at] = (dk * scale).astype(BF16)
            out[:, v_at] = dv.astype(BF16)
            return carry

        lax.fori_loop(0, kv_heads, head_group, 0)

    def far_swap(slot):
        return copy(far_ref.at[slot], xr_ref.at[slot], send_x.at[slot], recv_x.at[slot], x_other)

    def to_plane(slot):
        return copy(own_ref.at[slot], zr_ref.at[slot], send_z.at[slot], recv_z.at[slot], device - 2)

    def from_first():
        return copy(own_ref.at[1], first_ref, send_first, recv_first, device + 2)

    def attend(slot):
        there = 2 * (plane - slot)
        far, own = there + 1 - x_at, there + x_at

        def both(far, own, masked):
            work(2 * slot + 1, far, masked, far_ref.at[slot])
            far_swap(slot).start()
            work(2 * slot, own, masked, own_ref.at[slot])

        if slot == 0:
            both(far, own, True)
        elif slot == 1:
            pl.when(plane == 0)(lambda: both(3 - x_at, 2 + x_at, True))
            pl.when(plane > 0)(lambda: both(far, own, False))
        else:
            pl.when(plane >= slot)(lambda: both(far, own, False))

    def pass_back(slot):
        def go():
            far_swap(slot).wait_recv()
            own_ref[slot] += xr_ref[slot]
            if slot < last:

                @pl.when(inner & (plane >= slot))
                def _():
                    to_plane(slot + 1).wait_recv()
                    own_ref[slot] += zr_ref[slot + 1]

            if slot == 1:
                pl.when(plane == 0)(lambda: from_first().start())
                pl.when(plane > 0)(lambda: to_plane(slot).start())
            else:
                to_plane(slot).start()

        if slot == 1:
            go()
        else:
            pl.when(plane >= slot)(go)

    dq_ref[...] = jnp.zeros_like(dq_ref)
    inputs.wait(a_all_ref)
    d_attn.start()
    inputs.wait(hid_ref)
    if sums:
        hid_inputs.wait()
        inputs.wait(og_ref, og_came_ref)
        down_sum.fill_columns(hid_ref.at[:, rest], hid_came_ref, og_ref, og_came_ref)
        down_sum.start()
    inputs.wait(*buffers[1:4])
    attend(last)
    d_attn.forward()
    if sums:
        inputs.wait(*buffers[7:])
        gate_swap(0).start()
    d_attn.store()
    pending = list(range(last, 0, -1))
    steps = range(1, last)
    adds = list(range(parts))
    share = -(-parts // last)
    for slot in range(last - 1, -1, -1):
        attend(slot)
        if slot == last - 1:
            if sums:
                d_attn.over_core().wait_recv()
                out_sum.fill_columns(heads_ref, heads_came_ref, a_ref, a_came_ref)
                out_sum.start()
                down_sum.advance(1)
                gate_start(0)
                gate_swap(1).start()
            pass_back(pending.pop(0))
        if slot == last - 2:
            if sums:
                for step in steps[1:]:
                    down_sum.advance(step)
                out_sum.advance(1)
                gate_start(1)
                gate_swap(2).start()
                gate_sums[0].advance(1)
            pass_back(pending.pop(0))
        for i in adds[:share]:
            block_add(i)
        del adds[:share]
    for i in adds:
        block_add(i)
    if sums:
        for step in steps[1:]:
            out_sum.advance(step)
            gate_sums[0].advance(step)
    while pending:
        pass_back(pending.pop(0))
    if sums:
        gate_start(2)
    up_swap.start()
    if sums:
        gate_sums[1].advance(1)
    for i in range(parts // 2):
        block_finish(i)
    if sums:
        for step in steps[1:]:
            gate_sums[1].advance(step)
        gate_sums[2].advance(1)
    for i in range(parts // 2, parts):
        block_finish(i)
    if sums:
        for step in steps[1:]:
            gate_sums[2].advance(step)
    dq_ref[...] = dq_ref[...] * scale

    far_swap(0).wait_recv()
    grad_ref[...] = own_ref[0].astype(F32) + xr_ref[0].astype(F32)
    if last > 0:

        @pl.when(inner)
        def _():
            to_plane(1).wait_recv()
            grad_ref[...] += zr_ref[1].astype(F32)

        @pl.when(plane == 1)
        def _():
            from_first().wait_recv()
            grad_ref[...] += first_ref[...].astype(F32)

    if sums:
        down_sum.finish(w_down_ref)
        out_sum.finish(w_out_ref)
        for k in range(pieces):
            gate_sums[k].finish(w_gate_ref.at[:, pl.ds(k * piece, piece)])
            gate_swap(k).wait_send()
    else:
        d_attn.over_core().wait_recv()
    up_swap.wait_recv()
    up_swap.wait_send()
    for i in range(parts):
        total.over_core(i).wait_send()
        block_store(i).wait()
        block_give(i).wait_recv()
        block_give(i).wait_send()
    d_attn.over_x().wait_send()
    d_attn.over_core().wait_send()
    for slot in range(planes):
        if slot <= 1:
            far_swap(slot).wait_send()
        else:
            pl.when(plane >= slot)(lambda slot=slot: far_swap(slot).wait_send())
        if slot >= 1:
            pl.when(plane >= slot)(lambda slot=slot: to_plane(slot).wait_send())
    if last > 0:
        pl.when(plane == 0)(lambda: from_first().wait_send())


def back(prefix, qx, dox, kv_all, shared, grads, group, all_planes, shard, pieces, dims):
    kv_heads, repeat, width = dims
    rows = qx.shape[1]
    columns = kv_heads * repeat * width
    planes = group // 2
    block = kv_all.shape[1:]
    dma = pltpu.SemaphoreType.DMA
    d_attn, d_up, hidden, w_down, middle = shared
    half, model = middle.shape
    parts = 8
    narrow = model // parts
    units = d_up.shape[1]
    cut_shape = jax.ShapeDtypeStruct((rows, all_planes * shard), BF16)
    out_shape = [jax.ShapeDtypeStruct((rows, columns), F32), jax.ShapeDtypeStruct(block, F32)]
    out_shape += [cut_shape] * 2 + [jax.ShapeDtypeStruct(d_up.shape, BF16)]
    out_shape.append(jax.ShapeDtypeStruct((rows, model), BF16))
    scratch = [pltpu.VMEM((planes,) + block, BF16)] * 4 + [pltpu.VMEM(block, BF16)]
    scratch += [dma((planes,))] * 4 + [dma, dma] + [dma] * 2
    scratch += Columns.scratch(rows // 2, all_planes * shard)
    staged = [d_attn, qx, dox, kv_all, hidden]
    args = [prefix, d_up, w_down, middle]
    first = []
    if grads is not None:
        args += grads[:1]
        staged += grads[1:]
        first = [pltpu.VMEM((rows, units // pieces), BF16), dma((1,))]
    args += staged
    product = [pltpu.VMEM((2, units, narrow), BF16), dma((2,)), pltpu.VMEM((2, rows, narrow), F32)]
    product += [pltpu.VMEM((2, half, narrow), F32), dma((2,))] + [dma((parts,))] * 3
    product += TensorSum.scratch(parts, half, narrow)
    scratch = first + Staged.scratch(staged) + product + scratch
    if grads is not None:
        piece = units // pieces
        shapes = (piece, shard), (shard, units), (columns, shard)
        out_shape += [jax.ShapeDtypeStruct(s, BF16) for s in shapes]
        scratch += [pltpu.VMEM((pieces, rows, piece), BF16)] + [dma((pieces,))] * 2
        for shape in [(piece, shard), (columns, shard)] + [(shard, piece)] * pieces:
            scratch += LineSum.scratch(planes, shape)
    return pl.pallas_call(
        functools.partial(
            back_kernel,
            group=group,
            planes=planes,
            all_planes=all_planes,
            shard=shard,
            kv_heads=kv_heads,
            repeat=repeat,
            width=width,
            coef=math.log2(math.e) / math.sqrt(width),
            scale=1.0 / math.sqrt(width),
            sums=grads is not None,
        ),
        out_shape=out_shape,
        in_specs=[smem()] + [ANYWHERE] * (len(args) - 1),
        out_specs=vmem(4) + [ANYWHERE] * 2 + vmem(len(out_shape) - 6),
        scratch_shapes=scratch,
        compiler_params=pltpu.CompilerParams(
            vmem_limit_bytes=BACK_VMEM_LIMIT, collective_id=1, has_side_effects=True
        ),
        cost_estimate=COST,
        name="back",
    )(*args)


def smem():
    return pl.BlockSpec(memory_space=pltpu.SMEM)


def out_kernel(*refs, planes, shard, blocks):
    refs = list(refs)

    def take(count):
        out = refs[:count]
        del refs[:count]
        return out

    arrays = take(4)
    gain_ref, w_down_ref = take(2)
    middle_ref, h_ref, d_hidden_out, og_keep, og_came, heads_came = take(6)
    buffers = take(4)
    heads_ref, w_ref, og_ref, x_ref = buffers
    inputs = Staged(arrays, buffers, *take(1))
    d_hidden_ref, d_hidden_sem = take(2)
    down_buf, down_sems, mine_ref, h_send, h_recv, heads_send, heads_recv = take(7)
    scratch = refs
    device = lax.axis_index("dp")
    core, core_peer, y_peer = tensor_peers()
    x_at = device % 2
    x_peer = {"dp": device + 1 - 2 * x_at}
    half = middle_ref.shape[0]
    total = TensorSum(scratch[:8], mine_ref, core, core_peer, y_peer)
    chunks, width = total.chunks, total.width
    place = (x_at, core, x_peer, core_peer, planes, shard)
    og = Columns(og_ref, og_keep, og_came, scratch[8:14], *place)
    tiles = down_sems.shape[0]
    tile = down_buf.shape[0] // tiles

    def load(t):
        at = pl.ds(t * tile, tile)
        return pltpu.make_async_copy(w_down_ref.at[at, :], down_buf.at[at, :], down_sems.at[t])

    inputs.start()
    for t in range(tiles):
        load(t).start()
    greet([(x_peer, True), (core_peer, True), (y_peer, True)])
    heads_swap = remote(heads_ref, heads_came, heads_send, heads_recv, x_peer)
    inputs.wait(heads_ref, w_ref)
    heads_swap.start()
    for i in range(chunks):
        total.add(i, dot(heads_ref[...], w_ref[:, i * width : (i + 1) * width]))
    inputs.wait(og_ref)
    og.start()
    og.store()
    for t in range(tiles):
        at = slice(t * tile, (t + 1) * tile)
        load(t).wait()
        d_hidden_ref[:, at] = dot(og_ref[...], down_buf[at, :], NT)
    d_hidden_copy = pltpu.make_async_copy(d_hidden_ref, d_hidden_out, d_hidden_sem)
    d_hidden_copy.start()
    mine = rows_of(core, half)
    inputs.wait(x_ref)
    for i in range(chunks):
        at = slice(i * width, (i + 1) * width)
        middle_ref[:, at] = x_ref[mine, at].astype(F32) + total.total(i)
    step = half // blocks

    def to_core(b):
        rows = h_ref.at[pl.ds(pl.multiple_of(core * half + b * step, step), step), :]
        return remote(rows, rows, h_send.at[b], h_recv.at[b], core_peer)

    for b in range(blocks):
        v = middle_ref[b * step : (b + 1) * step, :]
        r = lax.rsqrt(jnp.mean(v * v, axis=1, keepdims=True) + EPS)
        at = pl.ds(pl.multiple_of(core * half + b * step, step), step)
        h_ref[at, :] = (v * r * gain_ref[...]).astype(BF16)
        to_core(b).start()
    og.forward()
    og.finish()
    d_hidden_copy.wait()
    heads_swap.wait_recv()
    heads_swap.wait_send()
    for b in range(blocks):
        to_core(b).wait_recv()
        to_core(b).wait_send()
    total.finish()


def attention_out(heads, w_out, x, gain, out_grad, w_down, planes, shard):
    rows, model = x.shape
    half = rows // 2
    units = w_down.shape[0]
    chunks, blocks = 4, 4
    tiles = units // math.gcd(units, 256)
    dma = pltpu.SemaphoreType.DMA
    cut_shape = jax.ShapeDtypeStruct((rows, planes * shard), BF16)
    return pl.pallas_call(
        functools.partial(out_kernel, planes=planes, shard=shard, blocks=blocks),
        out_shape=[
            jax.ShapeDtypeStruct((half, model), F32),
            jax.ShapeDtypeStruct((rows, model), BF16),
            jax.ShapeDtypeStruct((rows, units), F32),
        ]
        + [cut_shape] * 2
        + [jax.ShapeDtypeStruct(heads.shape, BF16)],
        in_specs=[ANYWHERE] * 4 + vmem(1) + [ANYWHERE],
        out_specs=vmem(2) + [ANYWHERE] + vmem(3),
        scratch_shapes=Staged.scratch([heads, w_out, out_grad, x])
        + [pltpu.VMEM((rows, units), F32), dma]
        + [pltpu.VMEM((units, model), BF16), dma((tiles,))]
        + [pltpu.VMEM((2, rows, model // chunks), F32), dma((blocks,)), dma((blocks,)), dma, dma]
        + TensorSum.scratch(chunks, half, model // chunks)
        + Columns.scratch(half, planes * shard),
        compiler_params=pltpu.CompilerParams(
            vmem_limit_bytes=VMEM_LIMIT, collective_id=4, has_side_effects=True
        ),
        cost_estimate=COST,
        name="attention_out",
    )(heads, w_out, out_grad, x, gain, w_down)


def middle_kernel(*refs, planes, shard, heads, width, pieces, blocks, sums):
    refs = list(refs)

    def take(count):
        out = refs[:count]
        del refs[:count]
        return out

    w_gate_ref, w_up_ref, gain_ref = take(3)
    count = 10 if sums else 8
    arrays = take(count)
    outs = take(3)
    hid_came_ref, a_ref, gain_out_ref, qx_ref, dox_ref, h_keep, h_came = take(7)
    if sums:
        down_outs = take(pieces - 1)
    buffers = take(count)
    inputs = Staged(arrays, buffers, *take(1))
    h_ref, d_ref, middle_ref, og_ref, w_out_ref, q_ref, o_ref, lse_ref = buffers[:8]
    if sums:
        og_keep, og_came = buffers[8:]
    out_buffers = take(3)
    hid_ref, gate_ref, up_ref = out_buffers
    outputs = Staged(outs, out_buffers, *take(1), out=True)
    gate_buf, up_buf, load_sems, c_ref, mine_ref = take(5)
    hid_send, hid_recv, a_send, a_recv = take(4)
    sum_scratch, h_scratch = take(8), take(6)
    device = lax.axis_index("dp")
    core, core_peer, y_peer = tensor_peers()
    plane = device // 2
    x_at = device % 2
    x_peer = {"dp": device + 1 - 2 * x_at}
    meets = [(x_peer, True), (core_peer, True), (y_peer, True)]
    h_two = Columns(h_ref, h_keep, h_came, h_scratch, x_at, core, x_peer, core_peer, planes, shard)
    half = middle_ref.shape[0]
    total = TensorSum(sum_scratch, mine_ref, core, core_peer, y_peer)
    chunks, columns = total.chunks, total.width
    units = hid_ref.shape[1]
    piece = units // pieces
    tile = 256
    tiles = units // tile
    if sums:
        downs = [LineSum(take(6), device, plane, planes) for _ in range(pieces - 1)]
        meets += [({"dp": device + 2}, plane < planes - 1), ({"dp": device - 2}, plane > 0)]

    def loads(t):
        at = pl.ds(t * tile, tile)
        return (
            pltpu.make_async_copy(w_gate_ref.at[:, at], gate_buf.at[:, at], load_sems.at[2 * t]),
            pltpu.make_async_copy(w_up_ref.at[:, at], up_buf.at[:, at], load_sems.at[2 * t + 1]),
        )

    inputs.start(h_ref)
    for t in range(tiles):
        for load in loads(t):
            load.start()
        if t == 0:
            inputs.start(d_ref)
    inputs.start(*buffers[2:])
    greet(meets)
    inputs.wait(h_ref)

    def swap(k):
        at = pl.ds(k * piece, piece)
        return remote(hid_ref.at[:, at], hid_came_ref.at[:, at], hid_send.at[k], hid_recv.at[k], x_peer)

    for t in range(tiles):
        for load in loads(t):
            load.wait()
        if t == 0:
            inputs.wait(d_ref)
        at = slice(t * tile, (t + 1) * tile)
        gate = dot(h_ref[...], gate_buf[:, at])
        up = dot(h_ref[...], up_buf[:, at])
        sig = 1.0 / (1.0 + jnp.exp(-gate))
        silu = gate * sig
        d = d_ref[:, at]
        hid_ref[:, at] = (silu * up).astype(BF16)
        up_ref[:, at] = (d * silu).astype(BF16)
        gate_ref[:, at] = (d * up * (sig * (1.0 + gate * (1.0 - sig)))).astype(BF16)
        if (t + 1) * tile % piece == 0:
            swap((t + 1) * tile // piece - 1).start()

    outputs.start()
    inputs.wait(*buffers[2:])

    def down_start(k):
        if sums:
            at = pl.ds(k * piece, piece)
            swap(k).wait_recv()
            downs[k].fill_columns(hid_ref.at[:, at], hid_came_ref.at[:, at], og_keep, og_came)
            downs[k].start()

    def down_advance(k, step):
        if sums and step <= planes - 2:
            downs[k].advance(step)

    for i in range(chunks):
        at = slice(i * columns, (i + 1) * columns)
        total.add(i, dot(gate_ref[...], gate_buf[at, :], NT) + dot(up_ref[...], up_buf[at, :], NT))
        if i == chunks - 2:
            down_start(0)
    for i in range(chunks):
        if i == 1:
            down_start(1)
            h_two.start()
        if i == 2:
            down_advance(0, 1)
        c_ref[:, i * columns : (i + 1) * columns] = total.total(i)
    down_advance(0, 2)

    step = half // blocks

    def to_core(b):
        rows = a_ref.at[pl.ds(pl.multiple_of(core * half + b * step, step), step), :]
        return remote(rows, rows, a_send.at[b], a_recv.at[b], core_peer)

    gain_out_ref[...] = jnp.zeros_like(gain_out_ref)
    for b in range(blocks):
        at = slice(b * step, (b + 1) * step)
        whole_at = pl.ds(pl.multiple_of(core * half + b * step, step), step)
        c = c_ref[at, :]
        v = middle_ref[at, :]
        r = lax.rsqrt(jnp.mean(v * v, axis=1, keepdims=True) + EPS)
        n = v * r
        gain_out_ref[...] += jnp.sum(c * n, axis=0, keepdims=True)
        gc = c * gain_ref[...]
        d = r * (gc - n * jnp.mean(n * gc, axis=1, keepdims=True)) + og_ref[whole_at, :].astype(F32)
        a_ref[whole_at, :] = d.astype(BF16)
        to_core(b).start()

    lane = lax.broadcasted_iota(jnp.int32, (half, width), 1)

    def extra(value):
        a, b, c = split_three(value)
        return jnp.where(lane == 0, a, jnp.where(lane == 1, b, jnp.where(lane == 2, c, 0.0))).astype(BF16)

    def prepare(which):
        at_rows = rows_of(which, half)
        d_heads = dot(a_ref[at_rows, :], w_out_ref[...], NT)
        for head in range(heads):
            at = slice(head * width, (head + 1) * width)
            qx_ref[head, at_rows, :width] = q_ref[at_rows, at]
            qx_ref[head, at_rows, width:] = extra(lse_ref[at_rows, at])
            d = d_heads[:, at].astype(BF16)
            delta = jnp.sum(d.astype(F32) * o_ref[at_rows, at].astype(F32), axis=1, keepdims=True)
            dox_ref[head, at_rows, :width] = d
            dox_ref[head, at_rows, width:] = extra(jnp.broadcast_to(delta, (half, width)))

    down_advance(1, 1)
    h_two.store()
    prepare(core)
    h_two.forward()
    for b in range(blocks):
        to_core(b).wait_recv()
    prepare(1 - core)
    down_advance(1, 2)
    for b in range(blocks):
        to_core(b).wait_send()
    total.finish()
    h_two.finish()
    outputs.wait()
    for k in range(pieces):
        if k == pieces - 1 or not sums:
            swap(k).wait_recv()
        swap(k).wait_send()
    if sums:
        for k in range(pieces - 1):
            for step in range(3, planes - 1):
                downs[k].advance(step)
            downs[k].finish(down_outs[k])


def middle_of(w_gate, w_up, h_two, d_hidden, middle, out_grad, gain, w_out, q, out, lse, cuts, pieces, planes, shard, width):
    half, model = middle.shape
    rows, units = d_hidden.shape
    columns = q.shape[1]
    heads = columns // width
    chunks, blocks = 4, 4
    dma = pltpu.SemaphoreType.DMA
    staged = [h_two, d_hidden, middle, out_grad, w_out, q, out, lse] + ([] if cuts is None else cuts)
    args = [w_gate, w_up, gain, *staged]
    unit_shape = jax.ShapeDtypeStruct((rows, units), BF16)
    out_shape = [unit_shape] * 4 + [
        jax.ShapeDtypeStruct((rows, model), BF16),
        jax.ShapeDtypeStruct((1, model), F32),
    ]
    out_shape += [jax.ShapeDtypeStruct((heads, rows, 2 * width), BF16)] * 2
    out_shape += [jax.ShapeDtypeStruct((rows, planes * shard), BF16)] * 2
    scratch = Staged.scratch(staged) + Staged.scratch([unit_shape] * 3)
    scratch += [pltpu.VMEM((model, units), BF16)] * 2 + [dma((2 * units // 256,))]
    scratch += [pltpu.VMEM((half, model), F32), pltpu.VMEM((2, rows, model // chunks), F32)]
    scratch += [dma((pieces,))] * 2 + [dma((blocks,))] * 2
    scratch += TensorSum.scratch(chunks, half, model // chunks)
    scratch += Columns.scratch(half, planes * shard)
    if cuts is not None:
        out_shape += [jax.ShapeDtypeStruct((units // pieces, shard), BF16)] * (pieces - 1)
        scratch += LineSum.scratch(planes, (units // pieces, shard)) * (pieces - 1)
    return pl.pallas_call(
        functools.partial(
            middle_kernel,
            planes=planes,
            shard=shard,
            heads=heads,
            width=width,
            pieces=pieces,
            blocks=blocks,
            sums=cuts is not None,
        ),
        out_shape=out_shape,
        in_specs=[ANYWHERE] * 2 + vmem(1) + [ANYWHERE] * len(staged),
        out_specs=[ANYWHERE] * 3 + vmem(len(out_shape) - 3),
        scratch_shapes=scratch,
        compiler_params=pltpu.CompilerParams(
            vmem_limit_bytes=BACK_VMEM_LIMIT, collective_id=2, has_side_effects=True
        ),
        cost_estimate=COST,
        name="middle",
    )(*args)


def through_rope(d_ref, raw_ref, gain, cos, sin, out_ref, width, plain):
    columns = d_ref.shape[1]
    total = jnp.zeros((1, width), F32)
    for at in range(0, columns - plain, width):
        d = d_ref[:, at : at + width]
        c = d * cos - roll_half(d) * sin
        v = raw_ref[:, at : at + width]
        r = lax.rsqrt(jnp.mean(v * v, axis=1, keepdims=True) + EPS)
        n = v * r
        total = total + jnp.sum(c * n, axis=0, keepdims=True)
        gc = gain * c
        out_ref[:, at : at + width] = (r * (gc - n * jnp.mean(n * gc, axis=1, keepdims=True))).astype(BF16)
    if plain:
        out_ref[:, columns - plain :] = d_ref[:, columns - plain :].astype(BF16)
    return total


def front_kernel(*refs, dp_size, planes, shard, chunks, blocks, sums):
    refs = list(refs)

    def take(count):
        out = refs[:count]
        del refs[:count]
        return out

    q_gain, k_gain, attn_gain, mlp_gain_ref, add_array = take(5)
    count = 15 if sums else 11
    arrays = take(count)
    x_grad, gains, dq_ref, dq_came, dkv_ref, dkv_came, one_ref, one_came = take(8)
    if sums:
        w_up_out, w_q_out, w_kv_out = take(3)
    buffers = take(count)
    inputs = Staged(arrays, buffers, *take(1))
    dkv_in, k_raw, cos_ref, sin_ref, dq_in, q_raw, one_all = buffers[:7]
    x_ref, w_q, w_k, w_v = buffers[7:11]
    if sums:
        two_ref, two_came, up_ref, up_came = buffers[11:]
    mine, gain_came, c_ref, add_ref, add_sem = take(5)
    swap_sems, one_sems, gain_sems = take(4), take(2), take(2)
    one_sum_scratch, one_scratch = take(8), take(6)
    half = x_ref.shape[0] // 2
    model = x_ref.shape[1]
    width = model // chunks
    head = cos_ref.shape[1]
    kv_width = w_k.shape[1]

    device = lax.axis_index("dp")
    core, core_peer, y_peer = tensor_peers()
    x_at = device % 2
    x_peer = {"dp": device + 1 - 2 * x_at}
    plane = device // 2
    one = Columns(one_all, one_ref, one_came, one_scratch, x_at, core, x_peer, core_peer, planes, shard)
    bits = [1 << i for i in range(dp_size.bit_length() - 1)]
    dp_peers = [{"dp": device + bit - 2 * bit * ((device // bit) % 2)} for bit in bits]
    gain_peers = [core_peer, y_peer] + dp_peers
    meets = [(peer, True) for peer in gain_peers]
    if sums:
        up_sum, q_sum, kv_sum = (LineSum(take(6), device, plane, planes, True) for _ in range(3))
        meets += [({"dp": device + 2}, plane < planes - 1), ({"dp": device - 2}, plane > 0)]

    mine_rows = rows_of(core, half)
    add_load = pltpu.make_async_copy(add_array.at[mine_rows, :], add_ref, add_sem)
    inputs.start(one_all)
    if sums:
        inputs.start(*buffers[11:])
    inputs.start(*buffers[:6])
    inputs.start(*buffers[7:11])
    add_load.start()
    greet(meets)
    inputs.wait(one_all)
    one.start()
    if sums:
        inputs.wait(*buffers[11:])
        up_sum.fill_rows(two_ref, two_came, up_ref, up_came)
        up_sum.start()
    inputs.wait(*buffers[:6])
    cos, sin = cos_ref[...], sin_ref[...]
    k_total = through_rope(dkv_in, k_raw, k_gain[...], cos, sin, dkv_ref, head, kv_width)
    kv_swap = remote(dkv_ref, dkv_came, swap_sems[0], swap_sems[1], x_peer)
    kv_swap.start()
    q_total = through_rope(dq_in, q_raw, q_gain[...], cos, sin, dq_ref, head, 0)
    q_swap = remote(dq_ref, dq_came, swap_sems[2], swap_sems[3], x_peer)
    q_swap.start()
    inputs.wait(*buffers[7:11])

    one_sum = TensorSum(one_sum_scratch, mine, core, core_peer, y_peer)
    x = x_ref[...].astype(F32)
    r = lax.rsqrt(jnp.mean(x * x, axis=1, keepdims=True) + EPS)
    for i in range(chunks):
        at = slice(i * width, (i + 1) * width)
        part = (
            dot(dq_ref[...], w_q[at, :], NT)
            + dot(dkv_ref[:, :kv_width], w_k[at, :], NT)
            + dot(dkv_ref[:, kv_width:], w_v[at, :], NT)
        )
        one_sum.add(i, part)
        gains[0, :, at] = jnp.sum(part * (x_ref[:, at].astype(F32) * r), axis=0, keepdims=True)
    gains[0, :, model : 2 * model] = mlp_gain_ref[...]
    gains[0, :, 2 * model : 2 * model + head] = q_total
    gains[0, :, 2 * model + head :] = k_total
    one.forward()
    one.store()

    def gain_swap(k):
        return remote(
            gains.at[k], gain_came.at[k], gain_sems[0].at[k], gain_sems[1].at[k], gain_peers[k]
        )

    def gain_add(k):
        gain_swap(k).wait_recv()
        gains[k + 1] = gains[k] + gain_came[k]
        if k + 1 < len(gain_peers):
            gain_swap(k + 1).start()

    gain_swap(0).start()

    def advance(line, step):
        if sums and step <= planes - 2:
            line.advance(step)

    gain_add(0)
    if sums:
        advance(up_sum, 1)
        kv_swap.wait_recv()
        one.over_core().wait_recv()
        kv_sum.fill_rows(one_ref, one_came, dkv_ref, dkv_came)
        kv_sum.start()
    gain_add(1)
    if sums:
        q_swap.wait_recv()
        q_sum.fill_rows(one_ref, one_came, dq_ref, dq_came)
        q_sum.start()
        advance(up_sum, 2)
    gain_add(2)

    def give(out, sems):
        rows = out.at[mine_rows, :]
        return remote(rows, rows, sems[0], sems[1], core_peer)

    for i in range(chunks):
        c_ref[:, i * width : (i + 1) * width] = one_sum.total(i)
    add_load.wait()
    step = half // blocks
    for b in range(blocks):
        at = slice(b * step, (b + 1) * step)
        whole_at = pl.ds(pl.multiple_of(core * half + b * step, step), step)
        v = x_ref[whole_at, :].astype(F32)
        v_r = lax.rsqrt(jnp.mean(v * v, axis=1, keepdims=True) + EPS)
        n = v * v_r
        gc = c_ref[at, :] * attn_gain[...]
        d = v_r * (gc - n * jnp.mean(n * gc, axis=1, keepdims=True))
        x_grad[whole_at, :] = (d + add_ref[at, :].astype(F32)).astype(BF16)
    give(x_grad, one_sems).start()
    for k in range(3, len(gain_peers)):
        gain_add(k)
    if sums:
        advance(kv_sum, 1)
        advance(q_sum, 1)
    if sums:
        advance(kv_sum, 2)
        advance(q_sum, 2)
        for line in (up_sum, kv_sum, q_sum):
            for step in range(3, planes - 1):
                advance(line, step)
        up_sum.finish(w_up_out)
        kv_sum.finish(w_kv_out)
        q_sum.finish(w_q_out)
    else:
        kv_swap.wait_recv()
        q_swap.wait_recv()
        one.over_core().wait_recv()
    one.over_x().wait_send()
    one.over_core().wait_send()
    kv_swap.wait_send()
    q_swap.wait_send()
    give(x_grad, one_sems).wait_recv()
    give(x_grad, one_sems).wait_send()
    for k in range(len(gain_peers)):
        gain_swap(k).wait_send()
    one_sum.finish()


def front(dq, dkv, q_raw, k_raw, q_gain, k_gain, cos, sin, h_one, weights, x, d_attn, attn_gain, mlp_gain, grads, dp_size, shard):
    rows, model = x.shape
    half = rows // 2
    planes = dp_size // 2
    chunks = 4
    width = model // chunks
    stages = dp_size.bit_length() + 1
    dma = pltpu.SemaphoreType.DMA
    gains = (2 * model + 2 * cos.shape[1],)
    staged = [dkv, k_raw, cos, sin, dq, q_raw, h_one, x, *weights]
    if grads is not None:
        staged += grads
    args = [q_gain, k_gain, attn_gain, mlp_gain, d_attn, *staged]
    cut_shape = jax.ShapeDtypeStruct((rows, planes * shard), BF16)
    whole = jax.ShapeDtypeStruct((rows, model), BF16)
    q_shape, kv_shape = jax.ShapeDtypeStruct(dq.shape, BF16), jax.ShapeDtypeStruct(dkv.shape, BF16)
    out_shape = [whole, jax.ShapeDtypeStruct((stages + 1, 1) + gains, F32)]
    out_shape += [q_shape, q_shape, kv_shape, kv_shape, cut_shape, cut_shape]
    scratch = Staged.scratch(staged)
    scratch += [pltpu.VMEM((2, rows, width), F32)]
    scratch += [pltpu.VMEM((stages, 1) + gains, F32), pltpu.VMEM((half, model), F32)]
    scratch += [pltpu.VMEM((half, model), BF16), dma]
    scratch += [dma] * 6 + [dma((stages,))] * 2
    scratch += TensorSum.scratch(chunks, half, width)
    scratch += Columns.scratch(half, planes * shard)
    if grads is not None:
        for columns in (grads[2].shape[1], dq.shape[1], dkv.shape[1]):
            out_shape.append(jax.ShapeDtypeStruct((shard, columns), BF16))
            scratch += LineSum.scratch(planes, (shard, columns))
    return pl.pallas_call(
        functools.partial(
            front_kernel,
            dp_size=dp_size,
            planes=planes,
            shard=shard,
            chunks=chunks,
            blocks=4,
            sums=grads is not None,
        ),
        out_shape=out_shape,
        in_specs=vmem(4) + [ANYWHERE] * (len(args) - 4),
        out_specs=vmem(len(out_shape)),
        scratch_shapes=scratch,
        compiler_params=pltpu.CompilerParams(
            vmem_limit_bytes=BACK_VMEM_LIMIT, collective_id=3, has_side_effects=True
        ),
        cost_estimate=COST,
        name="front",
    )(*args)


def widen_kernel(*refs, results, gains):
    refs = list(refs)

    def take(count):
        out = refs[:count]
        del refs[:count]
        return out

    count = 1 + max(i for parts in results for i, _ in parts)
    block_in = take(1)[0]
    arrays = take(count)
    if gains:
        gain_ref = take(1)[0]
    block_out = take(1)[0]
    outs = take(len(results))
    if gains:
        attn_out, mlp_out, q_out, k_out = take(4)
    buffers = take(count)
    inputs = Staged(arrays, buffers, *take(1))
    out_buffers = take(len(results))
    outputs = Staged(outs, out_buffers, *take(1), out=True)
    block, block_sems = take(2)
    block_load = pltpu.make_async_copy(block_in, block, block_sems.at[0])
    block_copy = pltpu.make_async_copy(block, block_out, block_sems.at[1])
    block_load.start()
    inputs.start()
    if gains:
        shard, head = attn_out.shape[1], q_out.shape[1]
        model = (gain_ref.shape[1] - 2 * head) // 2
        at = pl.multiple_of(lax.axis_index("dp") * shard, shard)
        attn_out[...] = gain_ref[:, pl.ds(at, shard)]
        mlp_out[...] = gain_ref[:, pl.ds(pl.multiple_of(model + at, shard), shard)]
        q_out[...] = gain_ref[:, 2 * model : 2 * model + head]
        k_out[...] = gain_ref[:, 2 * model + head :]
    block_load.wait()
    block_copy.start()
    waited = set()
    for parts, out in zip(results, out_buffers):
        row = 0
        for i, column in parts:
            part = buffers[i]
            if i not in waited:
                inputs.wait(part)
                waited.add(i)
            height = part.shape[0]
            out[row : row + height, :] = part[:, column : column + out.shape[1]].astype(F32)
            row += height
        outputs.start(out)
    block_copy.wait()
    outputs.wait()


def widen(block_out, arrays, results, shapes, gains, shard, head):
    out_shape = [jax.ShapeDtypeStruct(block_out.shape, BF16)]
    out_shape += [jax.ShapeDtypeStruct(s, F32) for s in shapes]
    args = [block_out, *arrays]
    rows = [] if gains is None else [(1, shard), (1, shard), (1, head), (1, head)]
    if gains is not None:
        args.append(gains)
    return pl.pallas_call(
        functools.partial(widen_kernel, results=results, gains=gains is not None),
        out_shape=out_shape + [jax.ShapeDtypeStruct(s, F32) for s in rows],
        in_specs=[ANYWHERE] * (1 + len(arrays)) + vmem(0 if gains is None else 1),
        out_specs=[ANYWHERE] * (1 + len(shapes)) + vmem(len(rows)),
        scratch_shapes=Staged.scratch(arrays)
        + Staged.scratch(out_shape[1:])
        + [pltpu.VMEM(block_out.shape, BF16), pltpu.SemaphoreType.DMA((2,))],
        compiler_params=params(),
        cost_estimate=COST,
        name="widen",
    )(*args)


class Chain:
    def __init__(self):
        self.last = None

    def mark(self, value):
        self.last = value

    def __call__(self, *values):
        if self.last is None:
            return values
        return lax.optimization_barrier((*values, self.last))[:-1]


class ZSum:
    def __init__(self, part, dim, shard, planes, z_at):
        self.part, self.dim, self.shard, self.planes, self.z_at = part, dim, shard, planes, z_at
        self.at = 0
        self.came = None

    def term(self, j):
        j = jnp.clip(j, 0, self.planes - 1)
        return lax.dynamic_slice_in_dim(self.part, j * self.shard, self.shard, self.dim)

    def send(self, up, down):
        last = self.planes - 1
        self.at += 1
        up_pairs = [(2 * z + x, 2 * z + 2 + x) for z in range(last) for x in range(2) if z < self.at]
        down_pairs = [
            (2 * (last - z) + x, 2 * (last - 1 - z) + x)
            for z in range(last)
            for x in range(2)
            if z < self.at
        ]
        self.came = lax.ppermute(up, "dp", up_pairs), lax.ppermute(down, "dp", down_pairs)

    def terms(self):
        planes, z_at, at = self.planes, self.z_at, self.at
        return self.term(planes - 1 - at + z_at), self.term(at + 1 - planes + z_at)

    def start(self):
        self.send(*self.terms())

    def step(self, chain):
        if self.at >= self.planes - 1:
            return
        up, down = chain(*self.came)
        up_term, down_term = self.terms()
        up, down = up + up_term, down + down_term
        chain.mark(up)
        self.send(up, down)

    def finish(self, chain):
        if self.at == 0:
            self.start()
        while self.at < self.planes - 1:
            self.step(chain)
        up, down = chain(*self.came)
        total = self.term(self.z_at).astype(F32) + up.astype(F32) + down.astype(F32)
        chain.mark(total)
        return total


def shards(
    dp_size,
    tensor_size,
    tokens,
    norm_attn,
    w_query,
    key_weight,
    value_weight,
    query_gain,
    key_gain,
    w_out,
    norm_mlp,
    w_gate,
    w_up,
    w_down,
    out_grad,
    prefix_len,
):
    rows, model = tokens.shape
    width = query_gain.shape[0]
    kv_heads = key_weight.shape[1] // width
    repeat = w_query.shape[1] // key_weight.shape[1]
    dims = (kv_heads, repeat, width)
    group = dp_size // prefix_len.shape[0]
    planes = dp_size // 2
    group_planes = group // 2
    half = rows // 2
    shard = model // dp_size
    assert tensor_size == 4 and MAX_PREFIX <= 4 * rows

    device = lax.axis_index("dp")
    x_at = device % 2
    z_at = device // 2
    sequence = device // group
    member = device % group
    plane = member // 2
    prefix = jnp.sum(jnp.where(jnp.arange(prefix_len.shape[0]) == sequence, prefix_len, 0))

    x_pairs = [(d, d ^ 1) for d in range(dp_size)]

    def x_swap(value):
        return lax.ppermute(value, "dp", x_pairs)

    positions = (member * rows + jnp.arange(rows)).astype(F32)
    counter = jnp.arange(width // 2, dtype=F32)
    angles = positions[:, None] * (ROPE_BASE ** (-2.0 * counter / width))[None, :]
    cos, sin = jnp.cos(angles), jnp.sin(angles)
    cos = jnp.concatenate([cos, cos], axis=1)
    sin = jnp.concatenate([-sin, sin], axis=1)
    norm_attn_row = norm_attn[None, :]
    norm_mlp_row = norm_mlp[None, :]
    q_gain_row = query_gain[None, :]
    k_gain_row = key_gain[None, :]

    prefix_at = prefix[None].astype(jnp.int32)
    heads_b, lse, kv_all, h_one, q, q_raw, k_raw = attn_fwd(
        prefix_at,
        tokens,
        norm_attn_row,
        w_query,
        key_weight,
        value_weight,
        q_gain_row,
        k_gain_row,
        cos,
        sin,
        group,
        dims,
    )
    fused = planes == group_planes and shard % 128 == 0
    pieces = 3
    middle, h_two, d_hidden, og_keep, og_came, heads_came = attention_out(
        heads_b, w_out, tokens, norm_mlp_row, out_grad, w_down, planes, shard
    )
    outs = middle_of(
        w_gate,
        w_up,
        h_two,
        d_hidden,
        middle,
        out_grad,
        norm_mlp_row,
        w_out,
        q,
        heads_b,
        lse,
        [og_keep, og_came] if fused else None,
        pieces,
        planes,
        shard,
        width,
    )
    hidden, d_gate, d_up, hidden_came, d_attn, norm_mlp_part, qx, dox, h_two_keep, h_two_came = outs[:10]

    grads = None
    if fused:
        grads = [hidden_came, og_keep, og_came, d_gate, h_two_keep, h_two_came]
        grads += [heads_b, heads_came]
        w_down_parts = outs[10:]
    shared = [d_attn, d_up, hidden, w_down, middle]
    outs = back(prefix_at, qx, dox, kv_all, shared, grads, group, planes, shard, pieces, dims)
    dq, kv_grad, d_attn_keep, d_attn_came, up_came, block_out = outs[:6]
    chain = Chain()
    chain.mark(dq)
    if fused:
        w_down_parts = [*w_down_parts, outs[6]]
        w_gate_grad, w_out_grad = outs[7:]
    else:
        down_part = (dot(hidden, og_keep, TN) + dot(hidden_came, og_came, TN)).astype(BF16)
        w_down_grad = ZSum(down_part, 1, shard, planes, z_at).finish(chain)
        gate_part = dot(h_two_keep, d_gate, TN) + dot(h_two_came, x_swap(d_gate), TN)
        w_gate_grad = ZSum(gate_part.astype(BF16), 0, shard, planes, z_at).finish(chain)
        out_part = dot(heads_b, d_attn_keep, TN) + dot(heads_came, d_attn_came, TN)
        w_out_grad = ZSum(out_part.astype(BF16), 1, shard, planes, z_at).finish(chain)

    up_grads = [h_two_keep, h_two_came, d_up, up_came] if fused else None
    outs = front(
        *chain(dq),
        kv_grad,
        q_raw,
        k_raw,
        q_gain_row,
        k_gain_row,
        cos,
        sin,
        h_one,
        (w_query, key_weight, value_weight),
        tokens,
        d_attn,
        norm_attn_row,
        0.5 * norm_mlp_part,
        up_grads,
        dp_size,
        shard,
    )
    tokens_grad, gains, dq_b, dq_came, dkv_b, dkv_came, h_one_keep, h_one_came = outs[:8]
    if fused:
        w_up_grad, w_query_grad, w_kv_grad = outs[8:]
    else:
        chain.mark(tokens_grad)

        def by_rows(left, left_came, right, right_came):
            part = dot(left, right, TN) + dot(left_came, right_came, TN)
            return ZSum(part.astype(BF16), 0, shard, planes, z_at).finish(chain)

        w_up_grad = by_rows(h_two_keep, h_two_came, d_up, up_came)
        w_query_grad = by_rows(h_one_keep, h_one_came, dq_b, dq_came)
        w_kv_grad = by_rows(h_one_keep, h_one_came, dkv_b, dkv_came)
    kv_width = kv_heads * width
    if fused:
        arrays = [w_gate_grad, w_out_grad, *w_down_parts, w_up_grad, w_query_grad, w_kv_grad, tokens_grad]
        n = 2 + len(w_down_parts)
        results = [[(0, 0)], [(1, 0)], [(i, 0) for i in range(2, n)]]
        results += [[(n, 0)], [(n + 1, 0)], [(n + 2, 0)], [(n + 2, kv_width)], [(n + 3, 0)]]
        units = w_gate.shape[1]
        columns = w_query.shape[1]
        shapes = [(shard, units), (columns, shard), (units, shard), (shard, units), (shard, columns)]
        shapes += [(shard, kv_width)] * 2 + [(rows, model)]
        outs = widen(block_out, arrays, results, shapes, gains[-1], shard, width)
        block_out, w_gate_grad, w_out_grad, w_down_grad, w_up_grad, w_query_grad = outs[:6]
        w_key_grad, w_value_grad, tokens_grad = outs[6:9]
        norm_attn_grad, norm_mlp_grad, query_gain_grad, key_gain_grad = (v[0] for v in outs[9:])
    else:
        w_key_grad, w_value_grad = w_kv_grad[:, :kv_width], w_kv_grad[:, kv_width:]
        tokens_grad = tokens_grad.astype(F32)
        gains = gains[-1, 0]
        norm_attn_grad = lax.dynamic_slice_in_dim(gains, device * shard, shard, 0)
        norm_mlp_grad = lax.dynamic_slice_in_dim(gains, model + device * shard, shard, 0)
        query_gain_grad, key_gain_grad = gains[2 * model : 2 * model + width], gains[2 * model + width :]
    return (
        block_out,
        tokens_grad,
        norm_attn_grad,
        w_query_grad,
        w_key_grad,
        w_value_grad,
        query_gain_grad,
        key_gain_grad,
        w_out_grad,
        norm_mlp_grad,
        w_gate_grad,
        w_up_grad,
        w_down_grad,
    )


def solution(mesh):
    placed = (
        P("dp", None),
        P(),
        P(None, "tensor"),
        P(None, "tensor"),
        P(None, "tensor"),
        P(),
        P(),
        P("tensor", None),
        P(),
        P(None, "tensor"),
        P(None, "tensor"),
        P("tensor", None),
        P("dp", None),
        P(),
    )
    return jax.shard_map(
        functools.partial(shards, mesh.shape["dp"], mesh.shape["tensor"]),
        mesh=mesh,
        in_specs=placed,
        out_specs=(
            P("dp", None),
            P("dp", None),
            P("dp"),
            P("dp", "tensor"),
            P("dp", "tensor"),
            P("dp", "tensor"),
            P(),
            P(),
            P("tensor", "dp"),
            P("dp"),
            P("dp", "tensor"),
            P("dp", "tensor"),
            P("tensor", "dp"),
        ),
        check_vma=False,
    )
```

```python
import functools
import math

import jax
import jax.numpy as jnp
import numpy as np
from jax import lax
from jax.experimental import pallas as pl
from jax.experimental.pallas import tpu as pltpu
from jax.sharding import PartitionSpec as P

F32 = jnp.float32
BF16 = jnp.bfloat16
EPS = 1e-06
ROPE_BASE = 1000000.0
MAX_PREFIX = 2048
VMEM_LIMIT = 56 * 2**20
BACK_VMEM_LIMIT = 60 * 2**20

COST = pl.CostEstimate(flops=1000, bytes_accessed=1000, transcendentals=0)

NN = (((1,), (0,)), ((), ()))
NT = (((1,), (1,)), ((), ()))
TN = (((0,), (0,)), ((), ()))


def dot(left, right, dims=NN):
    return lax.dot_general(left, right, dims, preferred_element_type=F32)


def vmem(count):
    return [pl.BlockSpec(memory_space=pltpu.VMEM)] * count


def params():
    return pltpu.CompilerParams(vmem_limit_bytes=VMEM_LIMIT)


def greet(peers):
    barrier = pltpu.get_barrier_semaphore()
    count = 0
    for peer, there in peers:

        def signal(peer=peer):
            pl.semaphore_signal(barrier, 1, device_id=peer, device_id_type=pl.DeviceIdType.MESH)

        if there is True:
            signal()
            count = count + 1
        else:
            pl.when(there)(signal)
            count = count + there.astype(jnp.int32)
    pl.semaphore_wait(barrier, count)


def remote(src, dst, send, recv, peer):
    return pltpu.make_async_remote_copy(
        src_ref=src,
        dst_ref=dst,
        send_sem=send,
        recv_sem=recv,
        device_id=peer,
        device_id_type=pl.DeviceIdType.MESH,
    )


class Staged:
    def __init__(self, arrays, buffers, sems, out=False):
        self.copies = []
        for i, (array, buffer) in enumerate(zip(arrays, buffers)):
            ends = (buffer, array) if out else (array, buffer)
            self.copies.append((buffer, pltpu.make_async_copy(*ends, sems.at[i])))

    @staticmethod
    def scratch(shapes):
        return [pltpu.VMEM(s.shape, s.dtype) for s in shapes] + [pltpu.SemaphoreType.DMA((len(shapes),))]

    def start(self, *buffers):
        for buffer, copy in self.copies:
            if not buffers or any(buffer is b for b in buffers):
                copy.start()

    def wait(self, *buffers):
        for buffer, copy in self.copies:
            if not buffers or any(buffer is b for b in buffers):
                copy.wait()


ANYWHERE = pl.BlockSpec(memory_space=pl.ANY)


def table_rows(tables, member, rows):
    at = pl.ds(pl.multiple_of(member * rows, rows), rows)
    return [t.at[at, :] for t in tables]


def tensor_peers():
    t = lax.axis_index("tensor")
    core = t % 2
    y = t // 2
    return core, {"tensor": t + 1 - 2 * core}, {"tensor": t + 2 - 4 * y}


def rows_of(core, half):
    return pl.ds(pl.multiple_of(core * half, half), half)


def cut_into(out, out_rows, ref, ref_rows, side, planes, shard):
    for z in range(planes):
        to = slice(z * shard, (z + 1) * shard)
        if shard % 128 == 0:
            at = pl.ds(pl.multiple_of((2 * z + side) * shard, shard), shard)
            out[out_rows, to] = ref[ref_rows, at]
        else:
            low = ref[ref_rows, 2 * z * shard : (2 * z + 1) * shard]
            high = ref[ref_rows, (2 * z + 1) * shard : (2 * z + 2) * shard]
            out[out_rows, to] = jnp.where(side == 0, low, high)


class Columns:
    def __init__(self, whole, keep, came, scratch, x_at, core, x_peer, core_peer, planes, shard):
        self.whole, self.keep, self.came = whole, keep, came
        self.send_ref, self.recv_ref, self.sems = scratch[0], scratch[1], scratch[2:]
        self.x_at, self.core, self.cut = x_at, core, (planes, shard)
        self.x_peer, self.core_peer = x_peer, core_peer
        self.half = whole.shape[0] // 2

    @staticmethod
    def scratch(half, columns):
        return [pltpu.VMEM((half, columns), BF16)] * 2 + [pltpu.SemaphoreType.DMA] * 4

    def over_x(self):
        return remote(self.send_ref, self.recv_ref, self.sems[0], self.sems[1], self.x_peer)

    def over_core(self):
        there = self.came.at[rows_of(self.core, self.half), :]
        return remote(self.recv_ref, there, self.sems[2], self.sems[3], self.core_peer)

    def start(self):
        mine = rows_of(self.core, self.half)
        cut_into(self.send_ref, slice(None), self.whole, mine, 1 - self.x_at, *self.cut)
        self.over_x().start()

    def store(self):
        cut_into(self.keep, slice(None), self.whole, slice(None), self.x_at, *self.cut)

    def forward(self):
        self.over_x().wait_recv()
        self.over_core().start()
        self.came[rows_of(self.core, self.half), :] = self.recv_ref[...]

    def finish(self):
        self.over_core().wait_recv()
        self.over_x().wait_send()
        self.over_core().wait_send()


class LineSum:
    def __init__(self, scratch, device, plane, planes, paced=False):
        self.paced = paced
        self.stack, self.came = scratch[:2]
        self.sems = scratch[2:]
        self.device, self.plane, self.planes = device, plane, planes

    @staticmethod
    def scratch(planes, shape):
        return [pltpu.VMEM((n,) + shape, BF16) for n in (planes, planes + 1)] + [
            pltpu.SemaphoreType.DMA((planes,))
        ] * 4

    def up(self, j):
        s = self.sems
        peer = {"dp": self.device + 2}
        return remote(self.stack.at[j], self.came.at[j], s[0].at[j], s[1].at[j], peer)

    def down(self, j):
        s = self.sems
        slot = jnp.where(self.plane - 1 == j, self.planes, j)
        peer = {"dp": self.device - 2}
        return remote(self.stack.at[j], self.came.at[slot], s[2].at[j], s[3].at[j], peer)

    def start(self):
        last = self.planes - 1

        @pl.when(self.plane == 0)
        def _():
            for j in range(last, last - 1 if self.paced else 0, -1):
                self.up(j).start()

        @pl.when(self.plane == last)
        def _():
            for j in range(1 if self.paced else last):
                self.down(j).start()

    def advance(self, step):
        plane, last = self.plane, self.planes - 1
        low, high = last - step + plane, step - last + plane
        if self.paced:

            @pl.when(plane == 0)
            def _():
                self.up(last - step + 1).wait_send()
                self.up(last - step).start()

            @pl.when(plane == last)
            def _():
                self.down(step - 1).wait_send()
                self.down(step).start()

        @pl.when((plane >= 1) & (plane <= step))
        def _():
            self.up(low).wait_recv()
            self.stack[low] += self.came[low]
            self.up(low).start()

        @pl.when((plane < last) & (plane >= last - step))
        def _():
            self.down(high).wait_recv()
            self.stack[high] += self.came[high]
            self.down(high).start()

    def finish(self, out):
        plane, planes = self.plane, self.planes

        @pl.when(plane == 0)
        def _():
            self.down(plane).wait_recv()
            out[...] = self.stack[plane] + self.came[planes]

        @pl.when(plane == planes - 1)
        def _():
            self.up(plane).wait_recv()
            out[...] = self.stack[plane] + self.came[plane]

        @pl.when((plane > 0) & (plane < planes - 1))
        def _():
            self.up(plane).wait_recv()
            self.down(plane).wait_recv()
            total = self.stack[plane].astype(F32) + self.came[plane].astype(F32)
            out[...] = (total + self.came[planes].astype(F32)).astype(BF16)

        for j in range(planes):
            ups, downs = plane < j, plane > j
            if self.paced and j > 1:
                ups = ups & (plane > 0)
            if self.paced and j < planes - 2:
                downs = downs & (plane < planes - 1)
            pl.when(ups)(lambda j=j: self.up(j).wait_send())
            pl.when(downs)(lambda j=j: self.down(j).wait_send())

    def fill_rows(self, left, left_came, right, right_came):
        shard = self.stack.shape[1]

        def body(j, carry):
            at = pl.ds(pl.multiple_of(j * shard, shard), shard)
            self.stack[j] = (
                dot(left[:, at], right[...], TN) + dot(left_came[:, at], right_came[...], TN)
            ).astype(BF16)
            return carry

        lax.fori_loop(0, self.planes, body, 0)

    def fill_columns(self, left, left_came, right, right_came):
        shard = self.stack.shape[2]
        tile = 256

        def body(t, carry):
            at = pl.ds(pl.multiple_of(t * tile, tile), tile)
            term = dot(left[:, at], right[...], TN) + dot(left_came[:, at], right_came[...], TN)
            for j in range(self.planes):
                self.stack[j, at, :] = term[:, j * shard : (j + 1) * shard].astype(BF16)
            return carry

        lax.fori_loop(0, left.shape[1] // tile, body, 0)


class TensorSum:
    def __init__(self, scratch, mine, core, core_peer, y_peer):
        self.away, self.core_came, self.both, self.y_came = scratch[:4]
        self.sems = scratch[4:]
        self.mine = mine
        self.core, self.core_peer, self.y_peer = core, core_peer, y_peer
        self.chunks, self.half, self.width = self.away.shape

    @staticmethod
    def scratch(chunks, half, width):
        return [pltpu.VMEM((chunks, half, width), BF16)] * 4 + [
            pltpu.SemaphoreType.DMA((chunks,))
        ] * 4

    def over_core(self, i):
        s = self.sems
        return remote(self.away.at[i], self.core_came.at[i], s[0].at[i], s[1].at[i], self.core_peer)

    def over_y(self, i):
        s = self.sems
        return remote(self.both.at[i], self.y_came.at[i], s[2].at[i], s[3].at[i], self.y_peer)

    def add(self, i, value):
        self.mine[i % 2] = value
        self.away[i] = self.mine[i % 2, rows_of(1 - self.core, self.half), :].astype(BF16)
        self.over_core(i).start()
        if i > 0:
            self.pass_on(i - 1)
        if i == self.chunks - 1:
            self.pass_on(i)

    def pass_on(self, i):
        self.over_core(i).wait_recv()
        mine = self.mine[i % 2, rows_of(self.core, self.half), :]
        self.both[i] = (mine + self.core_came[i].astype(F32)).astype(BF16)
        self.over_y(i).start()

    def total(self, i):
        self.over_y(i).wait_recv()
        return self.both[i].astype(F32) + self.y_came[i].astype(F32)

    def finish(self):
        for i in range(self.chunks):
            self.over_core(i).wait_send()
            self.over_y(i).wait_send()


def roll_half(value):
    return pltpu.roll(value, value.shape[-1] // 2, 1)


def visible(shape, key0, row0, prefix):
    key_pos = key0 + lax.broadcasted_iota(jnp.int32, shape, 1)
    row_pos = row0 + lax.broadcasted_iota(jnp.int32, shape, 0)
    return (key_pos <= row_pos) | (key_pos < prefix)


def attn_fwd_kernel(*refs, group, kv_heads, repeat, width, tile, coef):
    refs = list(refs)

    def take(count):
        out = refs[:count]
        del refs[:count]
        return out

    prefix_ref, gain_ref, q_gain, k_gain = take(4)
    arrays = take(6)
    member = lax.axis_index("dp") % group
    arrays[3:5] = table_rows(arrays[3:5], member, arrays[0].shape[0])
    o_ref, lse_ref, all_out = take(3)
    outs = take(4)
    buffers = take(6)
    inputs = Staged(arrays, buffers, *take(1))
    x_ref, w_k, w_v, cos_ref, sin_ref, w_q = buffers
    out_buffers = take(4)
    h_ref, q_ref, q_raw, k_raw = out_buffers
    outputs = Staged(outs, out_buffers, *take(1), out=True)
    kv_ref, all_ref, all_sems, acc, send_x, recv_x, send_z, recv_z = take(8)
    send_down, send_rest, recv_rest = take(3)
    rows = q_ref.shape[0]
    kv_width = kv_heads * width
    planes = group // 2
    device = lax.axis_index("dp")
    member = device % group
    plane = member // 2
    x_at = member % 2
    x_other = device + 1 - 2 * x_at
    inner = plane < planes - 1
    prefix = prefix_ref[0]
    inputs.start()
    greet([({"dp": x_other}, True), ({"dp": device + 2}, inner), ({"dp": device - 2}, plane > 0)])

    def store(slot):
        return pltpu.make_async_copy(all_ref.at[slot], all_out.at[slot], all_sems.at[slot])

    def source(slot):
        return kv_ref if slot == 0 else all_ref.at[2 * slot]

    split = planes - 1 if planes > 2 else planes
    upper = pl.ds(rows // 2, rows - rows // 2)

    def to_x(slot):
        part = pl.ds(0, rows // 2 if slot == split else rows)
        return pltpu.make_async_remote_copy(
            src_ref=source(slot).at[part, :],
            dst_ref=all_ref.at[2 * slot + 1, part, :],
            send_sem=send_x.at[slot],
            recv_sem=recv_x.at[slot],
            device_id={"dp": x_other},
            device_id_type=pl.DeviceIdType.MESH,
        )

    def to_z(slot):
        return pltpu.make_async_remote_copy(
            src_ref=source(slot - 1),
            dst_ref=all_ref.at[2 * slot],
            send_sem=send_z.at[slot],
            recv_sem=recv_z.at[slot],
            device_id={"dp": device + 2},
            device_id_type=pl.DeviceIdType.MESH,
        )

    def rest_to_z():
        return remote(
            all_ref.at[2 * split - 1, upper, :],
            all_ref.at[2 * split + 1, upper, :],
            send_rest,
            recv_rest,
            {"dp": device + 2},
        )

    def to_first():
        return pltpu.make_async_remote_copy(
            src_ref=kv_ref,
            dst_ref=all_ref.at[2],
            send_sem=send_down,
            recv_sem=recv_z.at[1],
            device_id={"dp": device - 2},
            device_id_type=pl.DeviceIdType.MESH,
        )

    inputs.wait(x_ref, w_k, w_v, cos_ref, sin_ref)
    x = x_ref[...].astype(F32)
    r = lax.rsqrt(jnp.mean(x * x, axis=1, keepdims=True) + EPS)
    h_ref[...] = (x * r * gain_ref[...]).astype(BF16)
    cos, sin = cos_ref[...], sin_ref[...]

    def rotate(u, gain):
        u = u * lax.rsqrt(jnp.mean(u * u, axis=1, keepdims=True) + EPS) * gain[...]
        return (u * cos + roll_half(u) * sin).astype(BF16)

    keys = dot(h_ref[...], w_k[...])
    k_raw[...] = keys
    for at in range(0, kv_width, width):
        kv_ref[:, at : at + width] = rotate(keys[:, at : at + width], k_gain)
    kv_ref[:, kv_width:] = dot(h_ref[...], w_v[...]).astype(BF16)
    ones = jnp.ones((rows, width), BF16)
    row0 = member * rows

    def work(block, other, masked, start=False):
        key0 = other * rows

        def head_pair(h, carry):
            k = block[:, pl.ds(pl.multiple_of(h * width, width), width)]
            v = block[:, pl.ds(pl.multiple_of(kv_width + h * width, width), width)]
            v = jnp.concatenate([v, ones], axis=1)
            for g in range(repeat):
                head = h * repeat + g
                for at in range(0, rows, tile):
                    q = q_ref[at : at + tile, pl.ds(pl.multiple_of(head * width, width), width)]
                    p = jnp.exp2(dot(q, k, NT) * coef)
                    if masked:
                        p = jnp.where(visible(p.shape, key0, row0 + at, prefix), p, 0.0)
                    term = dot(p.astype(BF16), v)
                    if start:
                        acc[head, at : at + tile, :] = term
                    else:
                        acc[head, at : at + tile, :] += term
            return carry

        lax.fori_loop(0, kv_heads, head_pair, 0)

    to_x(0).start()
    if planes > 1:

        @pl.when(inner)
        def _():
            to_z(1).start()

        @pl.when(plane == 1)
        def _():
            to_first().start()

    inputs.wait(w_q)
    queries = dot(h_ref[...], w_q[...])
    q_raw[...] = queries
    for at in range(0, queries.shape[1], width):
        q_ref[:, at : at + width] = rotate(queries[:, at : at + width], q_gain)
    outputs.start()
    all_ref[0] = kv_ref[...]
    store(0).start()
    work(kv_ref, member, True, True)
    to_x(0).wait_recv()
    store(1).start()
    work(all_ref.at[1], member + 1 - 2 * x_at, True)
    for slot in range(1, planes):

        def step(slot=slot):
            to_z(slot).wait_recv()
            if slot < planes - 1:

                @pl.when(inner & (plane >= slot))
                def _():
                    to_z(slot + 1).start()

            to_x(slot).start()
            store(2 * slot).start()
            there = 2 * (plane - slot)
            if slot == 1:

                @pl.when(plane == 0)
                def _():
                    work(all_ref.at[2 * slot], 2 + x_at, True)

                @pl.when(plane > 0)
                def _():
                    work(all_ref.at[2 * slot], there + x_at, False)
            else:
                work(all_ref.at[2 * slot], there + x_at, False)
            to_x(slot).wait_recv()
            if slot == split - 1:

                @pl.when(plane == split - 1)
                def _():
                    rest_to_z().start()

            if slot == split:
                rest_to_z().wait_recv()
            store(2 * slot + 1).start()
            if slot == 1:

                @pl.when(plane == 0)
                def _():
                    work(all_ref.at[2 * slot + 1], 3 - x_at, True)

                @pl.when(plane > 0)
                def _():
                    work(all_ref.at[2 * slot + 1], there + 1 - x_at, False)
            else:
                work(all_ref.at[2 * slot + 1], there + 1 - x_at, False)

        if slot == 1:
            step()
        else:
            pl.when(plane >= slot)(step)

    for head in range(kv_heads * repeat):
        total = acc[head, :, width:]
        o_ref[:, head * width : (head + 1) * width] = (acc[head, :, :width] / total).astype(BF16)
        lse_ref[:, head * width : (head + 1) * width] = jnp.log2(total) * (1.0 / coef)

    outputs.wait()
    if split < planes:
        pl.when(plane == split - 1)(lambda: rest_to_z().wait_send())
    to_x(0).wait_send()
    for slot in range(planes):

        @pl.when((plane >= slot) | (slot <= 1))
        def _(slot=slot):
            store(2 * slot).wait()
            store(2 * slot + 1).wait()

    for slot in range(1, planes):

        @pl.when(inner & (plane >= slot - 1))
        def _(slot=slot):
            to_z(slot).wait_send()

        @pl.when((plane >= slot) | (slot == 1))
        def _(slot=slot):
            to_x(slot).wait_send()

    if planes > 1:

        @pl.when(plane == 1)
        def _():
            to_first().wait_send()


def attn_fwd(prefix, x, gain, w_query, key_weight, value_weight, q_gain, k_gain, cos, sin, group, dims):
    kv_heads, repeat, width = dims
    rows = x.shape[0]
    heads = kv_heads * repeat
    columns = heads * width
    planes = group // 2
    dma = pltpu.SemaphoreType.DMA
    block = (rows, 2 * kv_heads * width)
    staged = [x, key_weight, value_weight, cos, sin, w_query]
    table = jax.ShapeDtypeStruct((rows, width), F32)
    early = [
        jax.ShapeDtypeStruct(x.shape, BF16),
        jax.ShapeDtypeStruct((rows, columns), BF16),
        jax.ShapeDtypeStruct((rows, columns), F32),
        jax.ShapeDtypeStruct((rows, kv_heads * width), F32),
    ]
    return pl.pallas_call(
        functools.partial(
            attn_fwd_kernel,
            group=group,
            kv_heads=kv_heads,
            repeat=repeat,
            width=width,
            tile=min(rows, 256),
            coef=math.log2(math.e) / math.sqrt(width),
        ),
        out_shape=[
            jax.ShapeDtypeStruct((rows, columns), BF16),
            jax.ShapeDtypeStruct((rows, columns), F32),
            jax.ShapeDtypeStruct((group,) + block, BF16),
        ]
        + early,
        in_specs=[smem()] + vmem(3) + [ANYWHERE] * 6,
        out_specs=vmem(2) + [ANYWHERE] * 5,
        scratch_shapes=Staged.scratch([x, key_weight, value_weight, table, table, w_query])
        + Staged.scratch(early)
        + [pltpu.VMEM(block, BF16), pltpu.VMEM((group,) + block, BF16), dma((group,))]
        + [pltpu.VMEM((heads, rows, 2 * width), F32)]
        + [dma((planes,))] * 4
        + [dma] * 3,
        compiler_params=pltpu.CompilerParams(
            vmem_limit_bytes=VMEM_LIMIT, collective_id=0, has_side_effects=True
        ),
        cost_estimate=COST,
        name="attn_fwd",
    )(prefix, gain, q_gain, k_gain, *staged)


def split_three(value):
    high = value.astype(BF16)
    left = value - high.astype(F32)
    mid = left.astype(BF16)
    return high.astype(F32), mid.astype(F32), (left - mid.astype(F32)).astype(BF16).astype(F32)


def back_kernel(
    *refs, group, planes, all_planes, shard, kv_heads, repeat, width, coef, scale, sums
):
    refs = list(refs)

    def take(count):
        out = refs[:count]
        del refs[:count]
        return out

    device = lax.axis_index("dp")
    member = device % group
    plane = member // 2
    last = planes - 1
    prefix_ref, up_ref, w_down_in, middle_in = take(4)
    if sums:
        hid_arrays = take(1)
    count = 12 if sums else 5
    arrays = take(count)
    dq_ref, grad_ref, a_ref, a_came_ref, up_came_ref, block_ref = take(6)
    if sums:
        w_down_ref, w_gate_ref, w_out_ref = take(3)
    if sums:
        hid_buffers = take(1)
        hid_sems = take(1)[0]
    buffers = take(count)
    inputs = Staged(arrays, buffers, *take(1))
    a_all_ref, qx_ref, dox_ref, kv_ref, hid_ref = buffers[:5]
    if sums:
        hid_came_ref = hid_buffers[0]
        og_ref, og_came_ref, gate_ref, h_ref, h_came_ref, heads_ref, heads_came_ref = buffers[5:]
    down_buf, down_sems, mine_ref, middle_buf, middle_sems = take(5)
    block_sems = take(3)
    total_scratch = take(8)
    own_ref, far_ref, xr_ref, zr_ref, first_ref = take(5)
    send_x, recv_x, send_z, recv_z, send_first, recv_first = take(6)
    swap_sems = take(2)
    a_scratch = take(6)
    rows = qx_ref.shape[1]
    kv_width = kv_heads * width
    if sums:
        gate_came_ref, send_gate, recv_gate = take(3)
        left = w_down_ref.shape[0]
        rest = pl.ds(hid_arrays[0].shape[1] - left, left)
        hid_inputs = Staged([h.at[:, rest] for h in hid_arrays], hid_buffers, hid_sems)
        down_sum, out_sum = (LineSum(take(6), device, plane, planes) for _ in range(2))
        piece = gate_came_ref.shape[2]
        pieces = gate_ref.shape[1] // piece
        gate_sums = [LineSum(take(6), device, plane, planes) for _ in range(pieces)]
    x_at = member % 2
    x_other = device + 1 - 2 * x_at
    inner = plane < last
    prefix = prefix_ref[0]

    core, core_peer, y_peer = tensor_peers()
    x_peer = {"dp": x_other}
    total = TensorSum(total_scratch, mine_ref, core, core_peer, y_peer)
    half = total.half
    parts, narrow = total.chunks, total.width

    def load(i):
        at = pl.ds(i * narrow, narrow)
        return pltpu.make_async_copy(w_down_in.at[:, at], down_buf.at[i % 2], down_sems.at[i % 2])

    def middle_load(i):
        at = pl.ds(i * narrow, narrow)
        return pltpu.make_async_copy(middle_in.at[:, at], middle_buf.at[i % 2], middle_sems.at[i % 2])

    def block_at(i):
        return block_ref.at[rows_of(core, half), pl.ds(i * narrow, narrow)]

    def block_store(i):
        return pltpu.make_async_copy(total.both.at[i], block_at(i), block_sems[0].at[i])

    def block_give(i):
        return remote(total.both.at[i], block_at(i), block_sems[1].at[i], block_sems[2].at[i], core_peer)

    def block_add(i):
        load(i).wait()
        total.add(i, dot(hid_ref[...], down_buf[i % 2]))
        if i + 2 < parts:
            load(i + 2).start()

    def block_finish(i):
        middle_load(i).wait()
        value = middle_buf[i % 2] + total.total(i)
        total.over_y(i).wait_send()
        total.both[i] = value.astype(BF16)
        if i + 2 < parts:
            middle_load(i + 2).start()
        block_store(i).start()
        block_give(i).start()

    inputs.start(a_all_ref)
    if sums:
        hid_inputs.start()
        inputs.start(hid_ref, *buffers[5:7])
    inputs.start(*buffers[1:4])
    if sums:
        inputs.start(*buffers[7:])
    else:
        inputs.start(hid_ref)
    for i in range(2):
        load(i).start()
        middle_load(i).start()
    greet(
        [
            (x_peer, True),
            (core_peer, True),
            (y_peer, True),
            ({"dp": device + 2}, inner),
            ({"dp": device - 2}, plane > 0),
        ]
    )

    def copy(src, dst, send, recv, there):
        return remote(src, dst, send, recv, {"dp": there})

    place = (x_at, core, x_peer, core_peer, all_planes, shard)
    d_attn = Columns(a_all_ref, a_ref, a_came_ref, a_scratch, *place)
    up_swap = copy(up_ref, up_came_ref, swap_sems[0], swap_sems[1], x_other)

    def gate_swap(k):
        part = gate_ref.at[:, pl.ds(k * piece, piece)]
        return copy(part, gate_came_ref.at[k], send_gate.at[k], recv_gate.at[k], x_other)

    def gate_start(k):
        gate_swap(k).wait_recv()
        part = gate_ref.at[:, pl.ds(k * piece, piece)]
        gate_sums[k].fill_rows(h_ref, h_came_ref, part, gate_came_ref.at[k])
        gate_sums[k].start()

    lane = lax.broadcasted_iota(jnp.int32, (rows, width), 1)
    minus = jnp.where(lane < 3, -1.0, 0.0).astype(BF16)
    row0 = member * rows

    def work(block, other, masked, out):
        key0 = other * rows

        def head_group(h, carry):
            k_at = pl.ds(pl.multiple_of(h * width, width), width)
            v_at = pl.ds(pl.multiple_of(kv_width + h * width, width), width)
            k = kv_ref[block, :, k_at]
            v = kv_ref[block, :, v_at]
            kx = jnp.concatenate([k, minus], axis=1)
            vx = jnp.concatenate([v, minus], axis=1)
            dk = jnp.zeros((rows, width), F32)
            dv = jnp.zeros((rows, width), F32)
            for g in range(repeat):
                head = h * repeat + g
                qx = qx_ref[head]
                dox = dox_ref[head]
                p = jnp.exp2(dot(qx, kx, NT) * coef)
                if masked:
                    p = jnp.where(visible(p.shape, key0, row0, prefix), p, 0.0)
                ds = (p * dot(dox, vx, NT)).astype(BF16)
                dv += dot(p.astype(BF16), dox[:, :width], TN)
                dk += dot(ds, qx[:, :width], TN)
                dq_ref[:, pl.ds(pl.multiple_of(head * width, width), width)] += dot(ds, k)
            out[:, k_at] = (dk * scale).astype(BF16)
            out[:, v_at] = dv.astype(BF16)
            return carry

        lax.fori_loop(0, kv_heads, head_group, 0)

    def far_swap(slot):
        return copy(far_ref.at[slot], xr_ref.at[slot], send_x.at[slot], recv_x.at[slot], x_other)

    def to_plane(slot):
        return copy(own_ref.at[slot], zr_ref.at[slot], send_z.at[slot], recv_z.at[slot], device - 2)

    def from_first():
        return copy(own_ref.at[1], first_ref, send_first, recv_first, device + 2)

    def attend(slot):
        there = 2 * (plane - slot)
        far, own = there + 1 - x_at, there + x_at

        def both(far, own, masked):
            work(2 * slot + 1, far, masked, far_ref.at[slot])
            far_swap(slot).start()
            work(2 * slot, own, masked, own_ref.at[slot])

        if slot == 0:
            both(far, own, True)
        elif slot == 1:
            pl.when(plane == 0)(lambda: both(3 - x_at, 2 + x_at, True))
            pl.when(plane > 0)(lambda: both(far, own, False))
        else:
            pl.when(plane >= slot)(lambda: both(far, own, False))

    def pass_back(slot):
        def go():
            far_swap(slot).wait_recv()
            own_ref[slot] += xr_ref[slot]
            if slot < last:

                @pl.when(inner & (plane >= slot))
                def _():
                    to_plane(slot + 1).wait_recv()
                    own_ref[slot] += zr_ref[slot + 1]

            if slot == 1:
                pl.when(plane == 0)(lambda: from_first().start())
                pl.when(plane > 0)(lambda: to_plane(slot).start())
            else:
                to_plane(slot).start()

        if slot == 1:
            go()
        else:
            pl.when(plane >= slot)(go)

    dq_ref[...] = jnp.zeros_like(dq_ref)
    inputs.wait(a_all_ref)
    d_attn.start()
    inputs.wait(hid_ref)
    if sums:
        hid_inputs.wait()
        inputs.wait(og_ref, og_came_ref)
        down_sum.fill_columns(hid_ref.at[:, rest], hid_came_ref, og_ref, og_came_ref)
        down_sum.start()
    inputs.wait(*buffers[1:4])
    attend(last)
    d_attn.forward()
    if sums:
        inputs.wait(*buffers[7:])
        gate_swap(0).start()
    d_attn.store()
    pending = list(range(last, 0, -1))
    steps = range(1, last)
    adds = list(range(parts))
    share = -(-parts // last)
    for slot in range(last - 1, -1, -1):
        attend(slot)
        if slot == last - 1:
            if sums:
                d_attn.over_core().wait_recv()
                out_sum.fill_columns(heads_ref, heads_came_ref, a_ref, a_came_ref)
                out_sum.start()
                down_sum.advance(1)
                gate_start(0)
                gate_swap(1).start()
            pass_back(pending.pop(0))
        if slot == last - 2:
            if sums:
                for step in steps[1:]:
                    down_sum.advance(step)
                out_sum.advance(1)
                gate_start(1)
                gate_swap(2).start()
                gate_sums[0].advance(1)
            pass_back(pending.pop(0))
        for i in adds[:share]:
            block_add(i)
        del adds[:share]
    for i in adds:
        block_add(i)
    if sums:
        for step in steps[1:]:
            out_sum.advance(step)
            gate_sums[0].advance(step)
    while pending:
        pass_back(pending.pop(0))
    if sums:
        gate_start(2)
    up_swap.start()
    if sums:
        gate_sums[1].advance(1)
    for i in range(parts // 2):
        block_finish(i)
    if sums:
        for step in steps[1:]:
            gate_sums[1].advance(step)
        gate_sums[2].advance(1)
    for i in range(parts // 2, parts):
        block_finish(i)
    if sums:
        for step in steps[1:]:
            gate_sums[2].advance(step)
    dq_ref[...] = dq_ref[...] * scale

    far_swap(0).wait_recv()
    grad_ref[...] = own_ref[0].astype(F32) + xr_ref[0].astype(F32)
    if last > 0:

        @pl.when(inner)
        def _():
            to_plane(1).wait_recv()
            grad_ref[...] += zr_ref[1].astype(F32)

        @pl.when(plane == 1)
        def _():
            from_first().wait_recv()
            grad_ref[...] += first_ref[...].astype(F32)

    if sums:
        down_sum.finish(w_down_ref)
        out_sum.finish(w_out_ref)
        for k in range(pieces):
            gate_sums[k].finish(w_gate_ref.at[:, pl.ds(k * piece, piece)])
            gate_swap(k).wait_send()
    else:
        d_attn.over_core().wait_recv()
    up_swap.wait_recv()
    up_swap.wait_send()
    for i in range(parts):
        total.over_core(i).wait_send()
        block_store(i).wait()
        block_give(i).wait_recv()
        block_give(i).wait_send()
    d_attn.over_x().wait_send()
    d_attn.over_core().wait_send()
    for slot in range(planes):
        if slot <= 1:
            far_swap(slot).wait_send()
        else:
            pl.when(plane >= slot)(lambda slot=slot: far_swap(slot).wait_send())
        if slot >= 1:
            pl.when(plane >= slot)(lambda slot=slot: to_plane(slot).wait_send())
    if last > 0:
        pl.when(plane == 0)(lambda: from_first().wait_send())


def back(prefix, qx, dox, kv_all, shared, grads, group, all_planes, shard, pieces, dims):
    kv_heads, repeat, width = dims
    rows = qx.shape[1]
    columns = kv_heads * repeat * width
    planes = group // 2
    block = kv_all.shape[1:]
    dma = pltpu.SemaphoreType.DMA
    d_attn, d_up, hidden, w_down, middle = shared
    half, model = middle.shape
    parts = 8
    narrow = model // parts
    units = d_up.shape[1]
    cut_shape = jax.ShapeDtypeStruct((rows, all_planes * shard), BF16)
    out_shape = [jax.ShapeDtypeStruct((rows, columns), F32), jax.ShapeDtypeStruct(block, F32)]
    out_shape += [cut_shape] * 2 + [jax.ShapeDtypeStruct(d_up.shape, BF16)]
    out_shape.append(jax.ShapeDtypeStruct((rows, model), BF16))
    scratch = [pltpu.VMEM((planes,) + block, BF16)] * 4 + [pltpu.VMEM(block, BF16)]
    scratch += [dma((planes,))] * 4 + [dma, dma] + [dma] * 2
    scratch += Columns.scratch(rows // 2, all_planes * shard)
    staged = [d_attn, qx, dox, kv_all, hidden]
    args = [prefix, d_up, w_down, middle]
    first = []
    if grads is not None:
        args += grads[:1]
        staged += grads[1:]
        first = [pltpu.VMEM((rows, units // pieces), BF16), dma((1,))]
    args += staged
    product = [pltpu.VMEM((2, units, narrow), BF16), dma((2,)), pltpu.VMEM((2, rows, narrow), F32)]
    product += [pltpu.VMEM((2, half, narrow), F32), dma((2,))] + [dma((parts,))] * 3
    product += TensorSum.scratch(parts, half, narrow)
    scratch = first + Staged.scratch(staged) + product + scratch
    if grads is not None:
        piece = units // pieces
        shapes = (piece, shard), (shard, units), (columns, shard)
        out_shape += [jax.ShapeDtypeStruct(s, BF16) for s in shapes]
        scratch += [pltpu.VMEM((pieces, rows, piece), BF16)] + [dma((pieces,))] * 2
        for shape in [(piece, shard), (columns, shard)] + [(shard, piece)] * pieces:
            scratch += LineSum.scratch(planes, shape)
    return pl.pallas_call(
        functools.partial(
            back_kernel,
            group=group,
            planes=planes,
            all_planes=all_planes,
            shard=shard,
            kv_heads=kv_heads,
            repeat=repeat,
            width=width,
            coef=math.log2(math.e) / math.sqrt(width),
            scale=1.0 / math.sqrt(width),
            sums=grads is not None,
        ),
        out_shape=out_shape,
        in_specs=[smem()] + [ANYWHERE] * (len(args) - 1),
        out_specs=vmem(4) + [ANYWHERE] * 2 + vmem(len(out_shape) - 6),
        scratch_shapes=scratch,
        compiler_params=pltpu.CompilerParams(
            vmem_limit_bytes=BACK_VMEM_LIMIT, collective_id=1, has_side_effects=True
        ),
        cost_estimate=COST,
        name="back",
    )(*args)


def smem():
    return pl.BlockSpec(memory_space=pltpu.SMEM)


def out_kernel(*refs, planes, shard, blocks):
    refs = list(refs)

    def take(count):
        out = refs[:count]
        del refs[:count]
        return out

    arrays = take(4)
    gain_ref, w_down_ref = take(2)
    middle_ref, h_ref, d_hidden_out, og_keep, og_came, heads_came = take(6)
    buffers = take(4)
    heads_ref, w_ref, og_ref, x_ref = buffers
    inputs = Staged(arrays, buffers, *take(1))
    d_hidden_ref, d_hidden_sem = take(2)
    down_buf, down_sems, whole_ref, h_send, h_recv, heads_send, heads_recv = take(7)
    scratch = refs
    device = lax.axis_index("dp")
    core, core_peer, y_peer = tensor_peers()
    x_at = device % 2
    x_peer = {"dp": device + 1 - 2 * x_at}
    half = middle_ref.shape[0]
    total = TensorSum(scratch[:8], None, core, core_peer, y_peer)
    step = half // blocks
    place = (x_at, core, x_peer, core_peer, planes, shard)
    og = Columns(og_ref, og_keep, og_came, scratch[8:14], *place)
    tiles = down_sems.shape[0]
    tile = down_buf.shape[0] // tiles

    def load(t):
        at = pl.ds(t * tile, tile)
        return pltpu.make_async_copy(w_down_ref.at[at, :], down_buf.at[at, :], down_sems.at[t])

    inputs.start()
    for t in range(tiles):
        load(t).start()
    greet([(x_peer, True), (core_peer, True), (y_peer, True)])
    heads_swap = remote(heads_ref, heads_came, heads_send, heads_recv, x_peer)
    inputs.wait(heads_ref, w_ref)
    heads_swap.start()

    def rows_at(which, b):
        return pl.ds(pl.multiple_of(which * half + b * step, step), step)

    whole_ref[...] = dot(heads_ref[...], w_ref[...])
    for b in range(blocks):
        total.away[b] = whole_ref[rows_at(1 - core, b), :].astype(BF16)
        total.over_core(b).start()
    for b in range(blocks):
        total.over_core(b).wait_recv()
        mine = whole_ref[rows_at(core, b), :] + total.core_came[b].astype(F32)
        total.both[b] = mine.astype(BF16)
        total.over_y(b).start()
    inputs.wait(og_ref)
    og.start()
    og.store()
    for t in range(tiles):
        at = slice(t * tile, (t + 1) * tile)
        load(t).wait()
        d_hidden_ref[:, at] = dot(og_ref[...], down_buf[at, :], NT)
    d_hidden_copy = pltpu.make_async_copy(d_hidden_ref, d_hidden_out, d_hidden_sem)
    d_hidden_copy.start()
    inputs.wait(x_ref)

    def to_core(b):
        rows = h_ref.at[rows_at(core, b), :]
        return remote(rows, rows, h_send.at[b], h_recv.at[b], core_peer)

    for b in range(blocks):
        at = rows_at(core, b)
        v = x_ref[at, :].astype(F32) + total.total(b)
        middle_ref[b * step : (b + 1) * step, :] = v
        r = lax.rsqrt(jnp.mean(v * v, axis=1, keepdims=True) + EPS)
        h_ref[at, :] = (v * r * gain_ref[...]).astype(BF16)
        to_core(b).start()
    og.forward()
    og.finish()
    d_hidden_copy.wait()
    heads_swap.wait_recv()
    heads_swap.wait_send()
    for b in range(blocks):
        to_core(b).wait_recv()
        to_core(b).wait_send()
    total.finish()


def attention_out(heads, w_out, x, gain, out_grad, w_down, planes, shard):
    rows, model = x.shape
    half = rows // 2
    units = w_down.shape[0]
    blocks = 4
    tiles = units // math.gcd(units, 256)
    dma = pltpu.SemaphoreType.DMA
    cut_shape = jax.ShapeDtypeStruct((rows, planes * shard), BF16)
    return pl.pallas_call(
        functools.partial(out_kernel, planes=planes, shard=shard, blocks=blocks),
        out_shape=[
            jax.ShapeDtypeStruct((half, model), F32),
            jax.ShapeDtypeStruct((rows, model), BF16),
            jax.ShapeDtypeStruct((rows, units), F32),
        ]
        + [cut_shape] * 2
        + [jax.ShapeDtypeStruct(heads.shape, BF16)],
        in_specs=[ANYWHERE] * 4 + vmem(1) + [ANYWHERE],
        out_specs=vmem(2) + [ANYWHERE] + vmem(3),
        scratch_shapes=Staged.scratch([heads, w_out, out_grad, x])
        + [pltpu.VMEM((rows, units), F32), dma]
        + [pltpu.VMEM((units, model), BF16), dma((tiles,))]
        + [pltpu.VMEM((rows, model), F32), dma((blocks,)), dma((blocks,)), dma, dma]
        + TensorSum.scratch(blocks, half // blocks, model)
        + Columns.scratch(half, planes * shard),
        compiler_params=pltpu.CompilerParams(
            vmem_limit_bytes=VMEM_LIMIT, collective_id=4, has_side_effects=True
        ),
        cost_estimate=COST,
        name="attention_out",
    )(heads, w_out, out_grad, x, gain, w_down)


def middle_kernel(*refs, planes, shard, heads, width, pieces, blocks, sums):
    refs = list(refs)

    def take(count):
        out = refs[:count]
        del refs[:count]
        return out

    w_gate_ref, w_up_ref, gain_ref = take(3)
    count = 10 if sums else 8
    arrays = take(count)
    outs = take(3)
    hid_came_ref, a_ref, gain_out_ref, qx_ref, dox_ref, h_keep, h_came = take(7)
    if sums:
        down_outs = take(pieces - 1)
    buffers = take(count)
    inputs = Staged(arrays, buffers, *take(1))
    h_ref, d_ref, middle_ref, og_ref, w_out_ref, q_ref, o_ref, lse_ref = buffers[:8]
    if sums:
        og_keep, og_came = buffers[8:]
    out_buffers = take(3)
    hid_ref, gate_ref, up_ref = out_buffers
    outputs = Staged(outs, out_buffers, *take(1), out=True)
    gate_buf, up_buf, load_sems, c_ref, mine_ref = take(5)
    hid_send, hid_recv, a_send, a_recv = take(4)
    sum_scratch, h_scratch = take(8), take(6)
    device = lax.axis_index("dp")
    core, core_peer, y_peer = tensor_peers()
    plane = device // 2
    x_at = device % 2
    x_peer = {"dp": device + 1 - 2 * x_at}
    meets = [(x_peer, True), (core_peer, True), (y_peer, True)]
    h_two = Columns(h_ref, h_keep, h_came, h_scratch, x_at, core, x_peer, core_peer, planes, shard)
    half = middle_ref.shape[0]
    total = TensorSum(sum_scratch, mine_ref, core, core_peer, y_peer)
    chunks, columns = total.chunks, total.width
    units = hid_ref.shape[1]
    piece = units // pieces
    tile = 256
    tiles = units // tile
    if sums:
        downs = [LineSum(take(6), device, plane, planes) for _ in range(pieces - 1)]
        meets += [({"dp": device + 2}, plane < planes - 1), ({"dp": device - 2}, plane > 0)]

    def loads(t):
        at = pl.ds(t * tile, tile)
        return (
            pltpu.make_async_copy(w_gate_ref.at[:, at], gate_buf.at[:, at], load_sems.at[2 * t]),
            pltpu.make_async_copy(w_up_ref.at[:, at], up_buf.at[:, at], load_sems.at[2 * t + 1]),
        )

    inputs.start(h_ref)
    for t in range(tiles):
        for load in loads(t):
            load.start()
        if t == 0:
            inputs.start(d_ref)
    inputs.start(*buffers[2:])
    greet(meets)
    inputs.wait(h_ref)

    def swap(k):
        at = pl.ds(k * piece, piece)
        return remote(hid_ref.at[:, at], hid_came_ref.at[:, at], hid_send.at[k], hid_recv.at[k], x_peer)

    for t in range(tiles):
        for load in loads(t):
            load.wait()
        if t == 0:
            inputs.wait(d_ref)
        at = slice(t * tile, (t + 1) * tile)
        gate = dot(h_ref[...], gate_buf[:, at])
        up = dot(h_ref[...], up_buf[:, at])
        sig = 0.5 * jnp.tanh(0.5 * gate) + 0.5
        silu = gate * sig
        d = d_ref[:, at]
        hid_ref[:, at] = (silu * up).astype(BF16)
        up_ref[:, at] = (d * silu).astype(BF16)
        gate_ref[:, at] = (d * up * (sig * (1.0 + gate * (1.0 - sig)))).astype(BF16)
        if (t + 1) * tile % piece == 0:
            swap((t + 1) * tile // piece - 1).start()

    outputs.start()
    inputs.wait(*buffers[2:])

    def down_start(k):
        if sums:
            at = pl.ds(k * piece, piece)
            swap(k).wait_recv()
            downs[k].fill_columns(hid_ref.at[:, at], hid_came_ref.at[:, at], og_keep, og_came)
            downs[k].start()

    def down_advance(k, step):
        if sums and step <= planes - 2:
            downs[k].advance(step)

    for i in range(chunks):
        at = slice(i * columns, (i + 1) * columns)
        total.add(i, dot(gate_ref[...], gate_buf[at, :], NT) + dot(up_ref[...], up_buf[at, :], NT))
        if i == chunks // 2:
            down_start(0)
    for i in range(chunks):
        if i == chunks // 4:
            down_start(1)
            h_two.start()
        if i == chunks // 2:
            down_advance(0, 1)
        c_ref[:, i * columns : (i + 1) * columns] = total.total(i)
    down_advance(0, 2)

    step = half // blocks

    def to_core(b):
        rows = a_ref.at[pl.ds(pl.multiple_of(core * half + b * step, step), step), :]
        return remote(rows, rows, a_send.at[b], a_recv.at[b], core_peer)

    gain_out_ref[...] = jnp.zeros_like(gain_out_ref)
    for b in range(blocks):
        at = slice(b * step, (b + 1) * step)
        whole_at = pl.ds(pl.multiple_of(core * half + b * step, step), step)
        c = c_ref[at, :]
        v = middle_ref[at, :]
        r = lax.rsqrt(jnp.mean(v * v, axis=1, keepdims=True) + EPS)
        n = v * r
        gain_out_ref[...] += jnp.sum(c * n, axis=0, keepdims=True)
        gc = c * gain_ref[...]
        d = r * (gc - n * jnp.mean(n * gc, axis=1, keepdims=True)) + og_ref[whole_at, :].astype(F32)
        a_ref[whole_at, :] = d.astype(BF16)
        to_core(b).start()

    lane = lax.broadcasted_iota(jnp.int32, (half, width), 1)

    def extra(value):
        a, b, c = split_three(value)
        return jnp.where(lane == 0, a, jnp.where(lane == 1, b, jnp.where(lane == 2, c, 0.0))).astype(BF16)

    def prepare(which):
        at_rows = rows_of(which, half)
        d_heads = dot(a_ref[at_rows, :], w_out_ref[...], NT)
        for head in range(heads):
            at = slice(head * width, (head + 1) * width)
            qx_ref[head, at_rows, :width] = q_ref[at_rows, at]
            qx_ref[head, at_rows, width:] = extra(lse_ref[at_rows, at])
            d = d_heads[:, at].astype(BF16)
            delta = jnp.sum(d.astype(F32) * o_ref[at_rows, at].astype(F32), axis=1, keepdims=True)
            dox_ref[head, at_rows, :width] = d
            dox_ref[head, at_rows, width:] = extra(jnp.broadcast_to(delta, (half, width)))

    down_advance(1, 1)
    h_two.store()
    prepare(core)
    h_two.forward()
    for b in range(blocks):
        to_core(b).wait_recv()
    prepare(1 - core)
    down_advance(1, 2)
    for b in range(blocks):
        to_core(b).wait_send()
    total.finish()
    h_two.finish()
    outputs.wait()
    for k in range(pieces):
        if k == pieces - 1 or not sums:
            swap(k).wait_recv()
        swap(k).wait_send()
    if sums:
        for k in range(pieces - 1):
            for step in range(3, planes - 1):
                downs[k].advance(step)
            downs[k].finish(down_outs[k])


def middle_of(w_gate, w_up, h_two, d_hidden, middle, out_grad, gain, w_out, q, out, lse, cuts, pieces, planes, shard, width):
    half, model = middle.shape
    rows, units = d_hidden.shape
    columns = q.shape[1]
    heads = columns // width
    chunks, blocks = 4, 4
    dma = pltpu.SemaphoreType.DMA
    staged = [h_two, d_hidden, middle, out_grad, w_out, q, out, lse] + ([] if cuts is None else cuts)
    args = [w_gate, w_up, gain, *staged]
    unit_shape = jax.ShapeDtypeStruct((rows, units), BF16)
    out_shape = [unit_shape] * 4 + [
        jax.ShapeDtypeStruct((rows, model), BF16),
        jax.ShapeDtypeStruct((1, model), F32),
    ]
    out_shape += [jax.ShapeDtypeStruct((heads, rows, 2 * width), BF16)] * 2
    out_shape += [jax.ShapeDtypeStruct((rows, planes * shard), BF16)] * 2
    scratch = Staged.scratch(staged) + Staged.scratch([unit_shape] * 3)
    scratch += [pltpu.VMEM((model, units), BF16)] * 2 + [dma((2 * units // 256,))]
    scratch += [pltpu.VMEM((half, model), F32), pltpu.VMEM((2, rows, model // chunks), F32)]
    scratch += [dma((pieces,))] * 2 + [dma((blocks,))] * 2
    scratch += TensorSum.scratch(chunks, half, model // chunks)
    scratch += Columns.scratch(half, planes * shard)
    if cuts is not None:
        out_shape += [jax.ShapeDtypeStruct((units // pieces, shard), BF16)] * (pieces - 1)
        scratch += LineSum.scratch(planes, (units // pieces, shard)) * (pieces - 1)
    return pl.pallas_call(
        functools.partial(
            middle_kernel,
            planes=planes,
            shard=shard,
            heads=heads,
            width=width,
            pieces=pieces,
            blocks=blocks,
            sums=cuts is not None,
        ),
        out_shape=out_shape,
        in_specs=[ANYWHERE] * 2 + vmem(1) + [ANYWHERE] * len(staged),
        out_specs=[ANYWHERE] * 3 + vmem(len(out_shape) - 3),
        scratch_shapes=scratch,
        compiler_params=pltpu.CompilerParams(
            vmem_limit_bytes=BACK_VMEM_LIMIT, collective_id=2, has_side_effects=True
        ),
        cost_estimate=COST,
        name="middle",
    )(*args)


def through_rope(d_ref, raw_ref, gain, cos, sin, out_ref, width, plain):
    columns = d_ref.shape[1]
    total = jnp.zeros((1, width), F32)
    for at in range(0, columns - plain, width):
        d = d_ref[:, at : at + width]
        c = d * cos - roll_half(d) * sin
        v = raw_ref[:, at : at + width]
        r = lax.rsqrt(jnp.mean(v * v, axis=1, keepdims=True) + EPS)
        n = v * r
        total = total + jnp.sum(c * n, axis=0, keepdims=True)
        gc = gain * c
        out_ref[:, at : at + width] = (r * (gc - n * jnp.mean(n * gc, axis=1, keepdims=True))).astype(BF16)
    if plain:
        out_ref[:, columns - plain :] = d_ref[:, columns - plain :].astype(BF16)
    return total


def front_kernel(*refs, dp_size, group, planes, shard, chunks, blocks, sums):
    refs = list(refs)

    def take(count):
        out = refs[:count]
        del refs[:count]
        return out

    q_gain, k_gain, attn_gain, mlp_gain_ref, add_array = take(5)
    count = 15 if sums else 11
    arrays = take(count)
    arrays[2:4] = table_rows(arrays[2:4], lax.axis_index("dp") % group, arrays[0].shape[0])
    x_grad, gains, dq_ref, dq_came, dkv_ref, dkv_came, one_ref, one_came = take(8)
    if sums:
        w_up_out, w_q_out, w_kv_out = take(3)
    buffers = take(count)
    inputs = Staged(arrays, buffers, *take(1))
    dkv_in, k_raw, cos_ref, sin_ref, dq_in, q_raw, one_all = buffers[:7]
    x_ref, w_q, w_k, w_v = buffers[7:11]
    if sums:
        two_ref, two_came, up_ref, up_came = buffers[11:]
    mine, gain_came, c_ref, add_ref, add_sem = take(5)
    swap_sems, one_sems, gain_sems = take(4), take(2), take(2)
    one_sum_scratch, one_scratch = take(8), take(6)
    half = x_ref.shape[0] // 2
    model = x_ref.shape[1]
    width = model // chunks
    head = cos_ref.shape[1]
    kv_width = w_k.shape[1]

    device = lax.axis_index("dp")
    core, core_peer, y_peer = tensor_peers()
    x_at = device % 2
    x_peer = {"dp": device + 1 - 2 * x_at}
    plane = device // 2
    one = Columns(one_all, one_ref, one_came, one_scratch, x_at, core, x_peer, core_peer, planes, shard)
    bits = [1 << i for i in range(dp_size.bit_length() - 1)]
    dp_peers = [{"dp": device + bit - 2 * bit * ((device // bit) % 2)} for bit in bits]
    gain_peers = [core_peer, y_peer] + dp_peers
    meets = [(peer, True) for peer in gain_peers]
    if sums:
        up_sum, q_sum, kv_sum = (LineSum(take(6), device, plane, planes, True) for _ in range(3))
        meets += [({"dp": device + 2}, plane < planes - 1), ({"dp": device - 2}, plane > 0)]

    mine_rows = rows_of(core, half)
    add_load = pltpu.make_async_copy(add_array.at[mine_rows, :], add_ref, add_sem)
    inputs.start(one_all)
    if sums:
        inputs.start(*buffers[11:])
    inputs.start(*buffers[:6])
    inputs.start(*buffers[7:11])
    add_load.start()
    greet(meets)
    inputs.wait(one_all)
    one.start()
    if sums:
        inputs.wait(*buffers[11:])
        up_sum.fill_rows(two_ref, two_came, up_ref, up_came)
        up_sum.start()
    inputs.wait(*buffers[:6])
    cos, sin = cos_ref[...], sin_ref[...]
    k_total = through_rope(dkv_in, k_raw, k_gain[...], cos, sin, dkv_ref, head, kv_width)
    kv_swap = remote(dkv_ref, dkv_came, swap_sems[0], swap_sems[1], x_peer)
    kv_swap.start()
    q_total = through_rope(dq_in, q_raw, q_gain[...], cos, sin, dq_ref, head, 0)
    q_swap = remote(dq_ref, dq_came, swap_sems[2], swap_sems[3], x_peer)
    q_swap.start()
    inputs.wait(*buffers[7:11])

    one_sum = TensorSum(one_sum_scratch, mine, core, core_peer, y_peer)
    x = x_ref[...].astype(F32)
    r = lax.rsqrt(jnp.mean(x * x, axis=1, keepdims=True) + EPS)
    for i in range(chunks):
        at = slice(i * width, (i + 1) * width)
        part = (
            dot(dq_ref[...], w_q[at, :], NT)
            + dot(dkv_ref[:, :kv_width], w_k[at, :], NT)
            + dot(dkv_ref[:, kv_width:], w_v[at, :], NT)
        )
        one_sum.add(i, part)
        gains[0, :, at] = jnp.sum(part * (x_ref[:, at].astype(F32) * r), axis=0, keepdims=True)
    gains[0, :, model : 2 * model] = mlp_gain_ref[...]
    gains[0, :, 2 * model : 2 * model + head] = q_total
    gains[0, :, 2 * model + head :] = k_total
    one.forward()
    one.store()

    def gain_swap(k):
        return remote(
            gains.at[k], gain_came.at[k], gain_sems[0].at[k], gain_sems[1].at[k], gain_peers[k]
        )

    def gain_add(k):
        gain_swap(k).wait_recv()
        gains[k + 1] = gains[k] + gain_came[k]
        if k + 1 < len(gain_peers):
            gain_swap(k + 1).start()

    gain_swap(0).start()

    def advance(line, step):
        if sums and step <= planes - 2:
            line.advance(step)

    gain_add(0)
    if sums:
        advance(up_sum, 1)
        kv_swap.wait_recv()
        one.over_core().wait_recv()
        kv_sum.fill_rows(one_ref, one_came, dkv_ref, dkv_came)
        kv_sum.start()
    gain_add(1)
    if sums:
        q_swap.wait_recv()
        q_sum.fill_rows(one_ref, one_came, dq_ref, dq_came)
        q_sum.start()
        advance(up_sum, 2)
    gain_add(2)

    def give(out, sems):
        rows = out.at[mine_rows, :]
        return remote(rows, rows, sems[0], sems[1], core_peer)

    for i in range(chunks):
        c_ref[:, i * width : (i + 1) * width] = one_sum.total(i)
    add_load.wait()
    step = half // blocks
    for b in range(blocks):
        at = slice(b * step, (b + 1) * step)
        whole_at = pl.ds(pl.multiple_of(core * half + b * step, step), step)
        v = x_ref[whole_at, :].astype(F32)
        v_r = lax.rsqrt(jnp.mean(v * v, axis=1, keepdims=True) + EPS)
        n = v * v_r
        gc = c_ref[at, :] * attn_gain[...]
        d = v_r * (gc - n * jnp.mean(n * gc, axis=1, keepdims=True))
        x_grad[whole_at, :] = (d + add_ref[at, :].astype(F32)).astype(BF16)
    give(x_grad, one_sems).start()
    for k in range(3, len(gain_peers)):
        gain_add(k)
    if sums:
        advance(kv_sum, 1)
        advance(q_sum, 1)
    if sums:
        advance(kv_sum, 2)
        advance(q_sum, 2)
        for line in (up_sum, kv_sum, q_sum):
            for step in range(3, planes - 1):
                advance(line, step)
        up_sum.finish(w_up_out)
        kv_sum.finish(w_kv_out)
        q_sum.finish(w_q_out)
    else:
        kv_swap.wait_recv()
        q_swap.wait_recv()
        one.over_core().wait_recv()
    one.over_x().wait_send()
    one.over_core().wait_send()
    kv_swap.wait_send()
    q_swap.wait_send()
    give(x_grad, one_sems).wait_recv()
    give(x_grad, one_sems).wait_send()
    for k in range(len(gain_peers)):
        gain_swap(k).wait_send()
    one_sum.finish()


def front(dq, dkv, q_raw, k_raw, q_gain, k_gain, cos, sin, h_one, weights, x, d_attn, attn_gain, mlp_gain, grads, dp_size, group, shard):
    rows, model = x.shape
    half = rows // 2
    planes = dp_size // 2
    chunks = 4
    width = model // chunks
    stages = dp_size.bit_length() + 1
    dma = pltpu.SemaphoreType.DMA
    gains = (2 * model + 2 * cos.shape[1],)
    staged = [dkv, k_raw, cos, sin, dq, q_raw, h_one, x, *weights]
    if grads is not None:
        staged += grads
    args = [q_gain, k_gain, attn_gain, mlp_gain, d_attn, *staged]
    cut_shape = jax.ShapeDtypeStruct((rows, planes * shard), BF16)
    whole = jax.ShapeDtypeStruct((rows, model), BF16)
    q_shape, kv_shape = jax.ShapeDtypeStruct(dq.shape, BF16), jax.ShapeDtypeStruct(dkv.shape, BF16)
    out_shape = [whole, jax.ShapeDtypeStruct((stages + 1, 1) + gains, F32)]
    out_shape += [q_shape, q_shape, kv_shape, kv_shape, cut_shape, cut_shape]
    table = jax.ShapeDtypeStruct((rows, cos.shape[1]), F32)
    scratch = Staged.scratch(staged[:2] + [table, table] + staged[4:])
    scratch += [pltpu.VMEM((2, rows, width), F32)]
    scratch += [pltpu.VMEM((stages, 1) + gains, F32), pltpu.VMEM((half, model), F32)]
    scratch += [pltpu.VMEM((half, model), BF16), dma]
    scratch += [dma] * 6 + [dma((stages,))] * 2
    scratch += TensorSum.scratch(chunks, half, width)
    scratch += Columns.scratch(half, planes * shard)
    if grads is not None:
        for columns in (grads[2].shape[1], dq.shape[1], dkv.shape[1]):
            out_shape.append(jax.ShapeDtypeStruct((shard, columns), BF16))
            scratch += LineSum.scratch(planes, (shard, columns))
    return pl.pallas_call(
        functools.partial(
            front_kernel,
            dp_size=dp_size,
            group=group,
            planes=planes,
            shard=shard,
            chunks=chunks,
            blocks=4,
            sums=grads is not None,
        ),
        out_shape=out_shape,
        in_specs=vmem(4) + [ANYWHERE] * (len(args) - 4),
        out_specs=vmem(len(out_shape)),
        scratch_shapes=scratch,
        compiler_params=pltpu.CompilerParams(
            vmem_limit_bytes=BACK_VMEM_LIMIT, collective_id=3, has_side_effects=True
        ),
        cost_estimate=COST,
        name="front",
    )(*args)


def widen_kernel(*refs, results, gains):
    refs = list(refs)

    def take(count):
        out = refs[:count]
        del refs[:count]
        return out

    count = 1 + max(i for parts in results for i, _ in parts)
    block_in = take(1)[0]
    arrays = take(count)
    if gains:
        gain_ref = take(1)[0]
    block_out = take(1)[0]
    outs = take(len(results))
    if gains:
        attn_out, mlp_out, q_out, k_out = take(4)
    buffers = take(count)
    inputs = Staged(arrays, buffers, *take(1))
    out_buffers = take(len(results))
    outputs = Staged(outs, out_buffers, *take(1), out=True)
    block, block_sems = take(2)
    block_load = pltpu.make_async_copy(block_in, block, block_sems.at[0])
    block_copy = pltpu.make_async_copy(block, block_out, block_sems.at[1])
    block_load.start()
    inputs.start()
    if gains:
        shard, head = attn_out.shape[1], q_out.shape[1]
        model = (gain_ref.shape[1] - 2 * head) // 2
        at = pl.multiple_of(lax.axis_index("dp") * shard, shard)
        attn_out[...] = gain_ref[:, pl.ds(at, shard)]
        mlp_out[...] = gain_ref[:, pl.ds(pl.multiple_of(model + at, shard), shard)]
        q_out[...] = gain_ref[:, 2 * model : 2 * model + head]
        k_out[...] = gain_ref[:, 2 * model + head :]
    block_load.wait()
    block_copy.start()
    waited = set()
    for parts, out in zip(results, out_buffers):
        row = 0
        for i, column in parts:
            part = buffers[i]
            if i not in waited:
                inputs.wait(part)
                waited.add(i)
            height = part.shape[0]
            out[row : row + height, :] = part[:, column : column + out.shape[1]].astype(F32)
            row += height
        outputs.start(out)
    block_copy.wait()
    outputs.wait()


def widen(block_out, arrays, results, shapes, gains, shard, head):
    out_shape = [jax.ShapeDtypeStruct(block_out.shape, BF16)]
    out_shape += [jax.ShapeDtypeStruct(s, F32) for s in shapes]
    args = [block_out, *arrays]
    rows = [] if gains is None else [(1, shard), (1, shard), (1, head), (1, head)]
    if gains is not None:
        args.append(gains)
    return pl.pallas_call(
        functools.partial(widen_kernel, results=results, gains=gains is not None),
        out_shape=out_shape + [jax.ShapeDtypeStruct(s, F32) for s in rows],
        in_specs=[ANYWHERE] * (1 + len(arrays)) + vmem(0 if gains is None else 1),
        out_specs=[ANYWHERE] * (1 + len(shapes)) + vmem(len(rows)),
        scratch_shapes=Staged.scratch(arrays)
        + Staged.scratch(out_shape[1:])
        + [pltpu.VMEM(block_out.shape, BF16), pltpu.SemaphoreType.DMA((2,))],
        compiler_params=params(),
        cost_estimate=COST,
        name="widen",
    )(*args)


def rope_tables(length, width):
    frequency = ROPE_BASE ** (-2.0 * np.arange(width // 2) / width)
    angles = np.arange(length)[:, None] * frequency[None, :]
    cos, sin = np.cos(angles), np.sin(angles)
    tables = np.concatenate([cos, cos], axis=1), np.concatenate([-sin, sin], axis=1)
    return tuple(jnp.asarray(t.astype(np.float32)) for t in tables)


class Chain:
    def __init__(self):
        self.last = None

    def mark(self, value):
        self.last = value

    def __call__(self, *values):
        if self.last is None:
            return values
        return lax.optimization_barrier((*values, self.last))[:-1]


class ZSum:
    def __init__(self, part, dim, shard, planes, z_at):
        self.part, self.dim, self.shard, self.planes, self.z_at = part, dim, shard, planes, z_at
        self.at = 0
        self.came = None

    def term(self, j):
        j = jnp.clip(j, 0, self.planes - 1)
        return lax.dynamic_slice_in_dim(self.part, j * self.shard, self.shard, self.dim)

    def send(self, up, down):
        last = self.planes - 1
        self.at += 1
        up_pairs = [(2 * z + x, 2 * z + 2 + x) for z in range(last) for x in range(2) if z < self.at]
        down_pairs = [
            (2 * (last - z) + x, 2 * (last - 1 - z) + x)
            for z in range(last)
            for x in range(2)
            if z < self.at
        ]
        self.came = lax.ppermute(up, "dp", up_pairs), lax.ppermute(down, "dp", down_pairs)

    def terms(self):
        planes, z_at, at = self.planes, self.z_at, self.at
        return self.term(planes - 1 - at + z_at), self.term(at + 1 - planes + z_at)

    def start(self):
        self.send(*self.terms())

    def step(self, chain):
        if self.at >= self.planes - 1:
            return
        up, down = chain(*self.came)
        up_term, down_term = self.terms()
        up, down = up + up_term, down + down_term
        chain.mark(up)
        self.send(up, down)

    def finish(self, chain):
        if self.at == 0:
            self.start()
        while self.at < self.planes - 1:
            self.step(chain)
        up, down = chain(*self.came)
        total = self.term(self.z_at).astype(F32) + up.astype(F32) + down.astype(F32)
        chain.mark(total)
        return total


def shards(
    dp_size,
    tensor_size,
    tokens,
    norm_attn,
    w_query,
    key_weight,
    value_weight,
    query_gain,
    key_gain,
    w_out,
    norm_mlp,
    w_gate,
    w_up,
    w_down,
    out_grad,
    prefix_len,
):
    rows, model = tokens.shape
    width = query_gain.shape[0]
    kv_heads = key_weight.shape[1] // width
    repeat = w_query.shape[1] // key_weight.shape[1]
    dims = (kv_heads, repeat, width)
    group = dp_size // prefix_len.shape[0]
    planes = dp_size // 2
    group_planes = group // 2
    half = rows // 2
    shard = model // dp_size
    assert tensor_size == 4 and MAX_PREFIX <= 4 * rows

    device = lax.axis_index("dp")
    x_at = device % 2
    z_at = device // 2
    sequence = device // group
    member = device % group
    plane = member // 2
    prefix = jnp.sum(jnp.where(jnp.arange(prefix_len.shape[0]) == sequence, prefix_len, 0))

    x_pairs = [(d, d ^ 1) for d in range(dp_size)]

    def x_swap(value):
        return lax.ppermute(value, "dp", x_pairs)

    cos, sin = rope_tables(group * rows, width)
    norm_attn_row = norm_attn[None, :]
    norm_mlp_row = norm_mlp[None, :]
    q_gain_row = query_gain[None, :]
    k_gain_row = key_gain[None, :]

    prefix_at = prefix[None].astype(jnp.int32)
    heads_b, lse, kv_all, h_one, q, q_raw, k_raw = attn_fwd(
        prefix_at,
        tokens,
        norm_attn_row,
        w_query,
        key_weight,
        value_weight,
        q_gain_row,
        k_gain_row,
        cos,
        sin,
        group,
        dims,
    )
    fused = planes == group_planes and shard % 128 == 0
    pieces = 3
    middle, h_two, d_hidden, og_keep, og_came, heads_came = attention_out(
        heads_b, w_out, tokens, norm_mlp_row, out_grad, w_down, planes, shard
    )
    outs = middle_of(
        w_gate,
        w_up,
        h_two,
        d_hidden,
        middle,
        out_grad,
        norm_mlp_row,
        w_out,
        q,
        heads_b,
        lse,
        [og_keep, og_came] if fused else None,
        pieces,
        planes,
        shard,
        width,
    )
    hidden, d_gate, d_up, hidden_came, d_attn, norm_mlp_part, qx, dox, h_two_keep, h_two_came = outs[:10]

    grads = None
    if fused:
        grads = [hidden_came, og_keep, og_came, d_gate, h_two_keep, h_two_came]
        grads += [heads_b, heads_came]
        w_down_parts = outs[10:]
    shared = [d_attn, d_up, hidden, w_down, middle]
    outs = back(prefix_at, qx, dox, kv_all, shared, grads, group, planes, shard, pieces, dims)
    dq, kv_grad, d_attn_keep, d_attn_came, up_came, block_out = outs[:6]
    chain = Chain()
    chain.mark(dq)
    if fused:
        w_down_parts = [*w_down_parts, outs[6]]
        w_gate_grad, w_out_grad = outs[7:]
    else:
        down_part = (dot(hidden, og_keep, TN) + dot(hidden_came, og_came, TN)).astype(BF16)
        w_down_grad = ZSum(down_part, 1, shard, planes, z_at).finish(chain)
        gate_part = dot(h_two_keep, d_gate, TN) + dot(h_two_came, x_swap(d_gate), TN)
        w_gate_grad = ZSum(gate_part.astype(BF16), 0, shard, planes, z_at).finish(chain)
        out_part = dot(heads_b, d_attn_keep, TN) + dot(heads_came, d_attn_came, TN)
        w_out_grad = ZSum(out_part.astype(BF16), 1, shard, planes, z_at).finish(chain)

    up_grads = [h_two_keep, h_two_came, d_up, up_came] if fused else None
    outs = front(
        *chain(dq),
        kv_grad,
        q_raw,
        k_raw,
        q_gain_row,
        k_gain_row,
        cos,
        sin,
        h_one,
        (w_query, key_weight, value_weight),
        tokens,
        d_attn,
        norm_attn_row,
        0.5 * norm_mlp_part,
        up_grads,
        dp_size,
        group,
        shard,
    )
    tokens_grad, gains, dq_b, dq_came, dkv_b, dkv_came, h_one_keep, h_one_came = outs[:8]
    if fused:
        w_up_grad, w_query_grad, w_kv_grad = outs[8:]
    else:
        chain.mark(tokens_grad)

        def by_rows(left, left_came, right, right_came):
            part = dot(left, right, TN) + dot(left_came, right_came, TN)
            return ZSum(part.astype(BF16), 0, shard, planes, z_at).finish(chain)

        w_up_grad = by_rows(h_two_keep, h_two_came, d_up, up_came)
        w_query_grad = by_rows(h_one_keep, h_one_came, dq_b, dq_came)
        w_kv_grad = by_rows(h_one_keep, h_one_came, dkv_b, dkv_came)
    kv_width = kv_heads * width
    if fused:
        arrays = [w_gate_grad, w_out_grad, *w_down_parts, w_up_grad, w_query_grad, w_kv_grad, tokens_grad]
        n = 2 + len(w_down_parts)
        results = [[(0, 0)], [(1, 0)], [(i, 0) for i in range(2, n)]]
        results += [[(n, 0)], [(n + 1, 0)], [(n + 2, 0)], [(n + 2, kv_width)], [(n + 3, 0)]]
        units = w_gate.shape[1]
        columns = w_query.shape[1]
        shapes = [(shard, units), (columns, shard), (units, shard), (shard, units), (shard, columns)]
        shapes += [(shard, kv_width)] * 2 + [(rows, model)]
        outs = widen(block_out, arrays, results, shapes, gains[-1], shard, width)
        block_out, w_gate_grad, w_out_grad, w_down_grad, w_up_grad, w_query_grad = outs[:6]
        w_key_grad, w_value_grad, tokens_grad = outs[6:9]
        norm_attn_grad, norm_mlp_grad, query_gain_grad, key_gain_grad = (v[0] for v in outs[9:])
    else:
        w_key_grad, w_value_grad = w_kv_grad[:, :kv_width], w_kv_grad[:, kv_width:]
        tokens_grad = tokens_grad.astype(F32)
        gains = gains[-1, 0]
        norm_attn_grad = lax.dynamic_slice_in_dim(gains, device * shard, shard, 0)
        norm_mlp_grad = lax.dynamic_slice_in_dim(gains, model + device * shard, shard, 0)
        query_gain_grad, key_gain_grad = gains[2 * model : 2 * model + width], gains[2 * model + width :]
    return (
        block_out,
        tokens_grad,
        norm_attn_grad,
        w_query_grad,
        w_key_grad,
        w_value_grad,
        query_gain_grad,
        key_gain_grad,
        w_out_grad,
        norm_mlp_grad,
        w_gate_grad,
        w_up_grad,
        w_down_grad,
    )


def solution(mesh):
    placed = (
        P("dp", None),
        P(),
        P(None, "tensor"),
        P(None, "tensor"),
        P(None, "tensor"),
        P(),
        P(),
        P("tensor", None),
        P(),
        P(None, "tensor"),
        P(None, "tensor"),
        P("tensor", None),
        P("dp", None),
        P(),
    )
    return jax.shard_map(
        functools.partial(shards, mesh.shape["dp"], mesh.shape["tensor"]),
        mesh=mesh,
        in_specs=placed,
        out_specs=(
            P("dp", None),
            P("dp", None),
            P("dp"),
            P("dp", "tensor"),
            P("dp", "tensor"),
            P("dp", "tensor"),
            P(),
            P(),
            P("tensor", "dp"),
            P("dp"),
            P("dp", "tensor"),
            P("dp", "tensor"),
            P("tensor", "dp"),
        ),
        check_vma=False,
    )
```

```python
import functools
import math

import jax
import jax.numpy as jnp
import numpy as np
from jax import lax
from jax.experimental import pallas as pl
from jax.experimental.pallas import tpu as pltpu
from jax.sharding import PartitionSpec as P

F32 = jnp.float32
BF16 = jnp.bfloat16
EPS = 1e-06
ROPE_BASE = 1000000.0
MAX_PREFIX = 2048
VMEM_LIMIT = 56 * 2**20
BACK_VMEM_LIMIT = 60 * 2**20

COST = pl.CostEstimate(flops=1000, bytes_accessed=1000, transcendentals=0)

NN = (((1,), (0,)), ((), ()))
NT = (((1,), (1,)), ((), ()))
TN = (((0,), (0,)), ((), ()))


def dot(left, right, dims=NN):
    return lax.dot_general(left, right, dims, preferred_element_type=F32)


def vmem(count):
    return [pl.BlockSpec(memory_space=pltpu.VMEM)] * count


def params():
    return pltpu.CompilerParams(vmem_limit_bytes=VMEM_LIMIT)


def greet(peers):
    barrier = pltpu.get_barrier_semaphore()
    count = 0
    for peer, there in peers:

        def signal(peer=peer):
            pl.semaphore_signal(barrier, 1, device_id=peer, device_id_type=pl.DeviceIdType.MESH)

        if there is True:
            signal()
            count = count + 1
        else:
            pl.when(there)(signal)
            count = count + there.astype(jnp.int32)
    pl.semaphore_wait(barrier, count)


def remote(src, dst, send, recv, peer):
    return pltpu.make_async_remote_copy(
        src_ref=src,
        dst_ref=dst,
        send_sem=send,
        recv_sem=recv,
        device_id=peer,
        device_id_type=pl.DeviceIdType.MESH,
    )


class Staged:
    def __init__(self, arrays, buffers, sems, out=False):
        self.copies = []
        for i, (array, buffer) in enumerate(zip(arrays, buffers)):
            ends = (buffer, array) if out else (array, buffer)
            self.copies.append((buffer, pltpu.make_async_copy(*ends, sems.at[i])))

    @staticmethod
    def scratch(shapes):
        return [pltpu.VMEM(s.shape, s.dtype) for s in shapes] + [pltpu.SemaphoreType.DMA((len(shapes),))]

    def start(self, *buffers):
        for buffer, copy in self.copies:
            if not buffers or any(buffer is b for b in buffers):
                copy.start()

    def wait(self, *buffers):
        for buffer, copy in self.copies:
            if not buffers or any(buffer is b for b in buffers):
                copy.wait()


ANYWHERE = pl.BlockSpec(memory_space=pl.ANY)


def table_rows(tables, member, rows):
    at = pl.ds(pl.multiple_of(member * rows, rows), rows)
    return [t.at[at, :] for t in tables]


def tensor_peers():
    t = lax.axis_index("tensor")
    core = t % 2
    y = t // 2
    return core, {"tensor": t + 1 - 2 * core}, {"tensor": t + 2 - 4 * y}


def rows_of(core, half):
    return pl.ds(pl.multiple_of(core * half, half), half)


def cut_into(out, out_rows, ref, ref_rows, side, planes, shard):
    for z in range(planes):
        to = slice(z * shard, (z + 1) * shard)
        if shard % 128 == 0:
            at = pl.ds(pl.multiple_of((2 * z + side) * shard, shard), shard)
            out[out_rows, to] = ref[ref_rows, at]
        else:
            low = ref[ref_rows, 2 * z * shard : (2 * z + 1) * shard]
            high = ref[ref_rows, (2 * z + 1) * shard : (2 * z + 2) * shard]
            out[out_rows, to] = jnp.where(side == 0, low, high)


class Columns:
    def __init__(self, whole, keep, came, scratch, x_at, core, x_peer, core_peer, planes, shard):
        self.whole, self.keep, self.came = whole, keep, came
        self.send_ref, self.recv_ref, self.sems = scratch[0], scratch[1], scratch[2:]
        self.x_at, self.core, self.cut = x_at, core, (planes, shard)
        self.x_peer, self.core_peer = x_peer, core_peer
        self.half = whole.shape[0] // 2

    @staticmethod
    def scratch(half, columns):
        return [pltpu.VMEM((half, columns), BF16)] * 2 + [pltpu.SemaphoreType.DMA] * 4

    def over_x(self):
        return remote(self.send_ref, self.recv_ref, self.sems[0], self.sems[1], self.x_peer)

    def over_core(self):
        there = self.came.at[rows_of(self.core, self.half), :]
        return remote(self.recv_ref, there, self.sems[2], self.sems[3], self.core_peer)

    def start(self):
        mine = rows_of(self.core, self.half)
        cut_into(self.send_ref, slice(None), self.whole, mine, 1 - self.x_at, *self.cut)
        self.over_x().start()

    def store(self):
        cut_into(self.keep, slice(None), self.whole, slice(None), self.x_at, *self.cut)

    def forward(self):
        self.over_x().wait_recv()
        self.over_core().start()
        self.came[rows_of(self.core, self.half), :] = self.recv_ref[...]

    def finish(self):
        self.over_core().wait_recv()
        self.over_x().wait_send()
        self.over_core().wait_send()


class LineSum:
    def __init__(self, scratch, device, plane, planes, paced=False):
        self.paced = paced
        self.stack, self.came = scratch[:2]
        self.sems = scratch[2:]
        self.device, self.plane, self.planes = device, plane, planes

    @staticmethod
    def scratch(planes, shape):
        return [pltpu.VMEM((n,) + shape, BF16) for n in (planes, planes + 1)] + [
            pltpu.SemaphoreType.DMA((planes,))
        ] * 4

    def up(self, j):
        s = self.sems
        peer = {"dp": self.device + 2}
        return remote(self.stack.at[j], self.came.at[j], s[0].at[j], s[1].at[j], peer)

    def down(self, j):
        s = self.sems
        slot = jnp.where(self.plane - 1 == j, self.planes, j)
        peer = {"dp": self.device - 2}
        return remote(self.stack.at[j], self.came.at[slot], s[2].at[j], s[3].at[j], peer)

    def start(self):
        last = self.planes - 1

        @pl.when(self.plane == 0)
        def _():
            for j in range(last, last - 1 if self.paced else 0, -1):
                self.up(j).start()

        @pl.when(self.plane == last)
        def _():
            for j in range(1 if self.paced else last):
                self.down(j).start()

    def advance(self, step):
        plane, last = self.plane, self.planes - 1
        low, high = last - step + plane, step - last + plane
        if self.paced:

            @pl.when(plane == 0)
            def _():
                self.up(last - step + 1).wait_send()
                self.up(last - step).start()

            @pl.when(plane == last)
            def _():
                self.down(step - 1).wait_send()
                self.down(step).start()

        @pl.when((plane >= 1) & (plane <= step))
        def _():
            self.up(low).wait_recv()
            self.stack[low] += self.came[low]
            self.up(low).start()

        @pl.when((plane < last) & (plane >= last - step))
        def _():
            self.down(high).wait_recv()
            self.stack[high] += self.came[high]
            self.down(high).start()

    def finish(self, out):
        plane, planes = self.plane, self.planes

        @pl.when(plane == 0)
        def _():
            self.down(plane).wait_recv()
            out[...] = self.stack[plane] + self.came[planes]

        @pl.when(plane == planes - 1)
        def _():
            self.up(plane).wait_recv()
            out[...] = self.stack[plane] + self.came[plane]

        @pl.when((plane > 0) & (plane < planes - 1))
        def _():
            self.up(plane).wait_recv()
            self.down(plane).wait_recv()
            total = self.stack[plane].astype(F32) + self.came[plane].astype(F32)
            out[...] = (total + self.came[planes].astype(F32)).astype(BF16)

        for j in range(planes):
            ups, downs = plane < j, plane > j
            if self.paced and j > 1:
                ups = ups & (plane > 0)
            if self.paced and j < planes - 2:
                downs = downs & (plane < planes - 1)
            pl.when(ups)(lambda j=j: self.up(j).wait_send())
            pl.when(downs)(lambda j=j: self.down(j).wait_send())

    def fill_rows(self, left, left_came, right, right_came):
        shard, planes = self.stack.shape[1], self.planes

        def compute(i):
            j = jnp.where(self.plane * 2 < planes, planes - 1 - i, i) if self.paced else i
            at = pl.ds(pl.multiple_of(j * shard, shard), shard)
            self.stack[j] = (
                dot(left[:, at], right[...], TN) + dot(left_came[:, at], right_came[...], TN)
            ).astype(BF16)

        if self.paced:
            compute(0)
            self.start()

        def body(i, carry):
            compute(i)
            return carry

        lax.fori_loop(1 if self.paced else 0, planes, body, 0)

    def fill_columns(self, left, left_came, right, right_came):
        shard = self.stack.shape[2]
        tile = 256

        def body(t, carry):
            at = pl.ds(pl.multiple_of(t * tile, tile), tile)
            term = dot(left[:, at], right[...], TN) + dot(left_came[:, at], right_came[...], TN)
            for j in range(self.planes):
                self.stack[j, at, :] = term[:, j * shard : (j + 1) * shard].astype(BF16)
            return carry

        lax.fori_loop(0, left.shape[1] // tile, body, 0)


class TensorSum:
    def __init__(self, scratch, mine, core, core_peer, y_peer):
        self.away, self.core_came, self.both, self.y_came = scratch[:4]
        self.sems = scratch[4:]
        self.mine = mine
        self.core, self.core_peer, self.y_peer = core, core_peer, y_peer
        self.chunks, self.half, self.width = self.away.shape

    @staticmethod
    def scratch(chunks, half, width):
        return [pltpu.VMEM((chunks, half, width), BF16)] * 4 + [
            pltpu.SemaphoreType.DMA((chunks,))
        ] * 4

    def over_core(self, i):
        s = self.sems
        return remote(self.away.at[i], self.core_came.at[i], s[0].at[i], s[1].at[i], self.core_peer)

    def over_y(self, i):
        s = self.sems
        return remote(self.both.at[i], self.y_came.at[i], s[2].at[i], s[3].at[i], self.y_peer)

    def add(self, i, value):
        self.mine[i % 2] = value
        self.away[i] = self.mine[i % 2, rows_of(1 - self.core, self.half), :].astype(BF16)
        self.over_core(i).start()
        if i > 0:
            self.pass_on(i - 1)
        if i == self.chunks - 1:
            self.pass_on(i)

    def pass_on(self, i):
        self.over_core(i).wait_recv()
        mine = self.mine[i % 2, rows_of(self.core, self.half), :]
        self.both[i] = (mine + self.core_came[i].astype(F32)).astype(BF16)
        self.over_y(i).start()

    def total(self, i):
        self.over_y(i).wait_recv()
        return self.both[i].astype(F32) + self.y_came[i].astype(F32)

    def finish(self):
        for i in range(self.chunks):
            self.over_core(i).wait_send()
            self.over_y(i).wait_send()


def roll_half(value):
    return pltpu.roll(value, value.shape[-1] // 2, 1)


def visible(shape, key0, row0, prefix):
    key_pos = key0 + lax.broadcasted_iota(jnp.int32, shape, 1)
    row_pos = row0 + lax.broadcasted_iota(jnp.int32, shape, 0)
    return (key_pos <= row_pos) | (key_pos < prefix)


def attn_fwd_kernel(*refs, group, kv_heads, repeat, width, tile, coef):
    refs = list(refs)

    def take(count):
        out = refs[:count]
        del refs[:count]
        return out

    prefix_ref, gain_ref, q_gain, k_gain = take(4)
    arrays = take(6)
    member = lax.axis_index("dp") % group
    arrays[3:5] = table_rows(arrays[3:5], member, arrays[0].shape[0])
    o_ref, lse_ref, all_out = take(3)
    outs = take(4)
    buffers = take(6)
    inputs = Staged(arrays, buffers, *take(1))
    x_ref, w_k, w_v, cos_ref, sin_ref, w_q = buffers
    out_buffers = take(4)
    h_ref, q_ref, q_raw, k_raw = out_buffers
    outputs = Staged(outs, out_buffers, *take(1), out=True)
    kv_ref, all_ref, all_sems, acc, send_x, recv_x, send_z, recv_z = take(8)
    send_down, send_rest, recv_rest = take(3)
    rows = q_ref.shape[0]
    kv_width = kv_heads * width
    planes = group // 2
    device = lax.axis_index("dp")
    member = device % group
    plane = member // 2
    x_at = member % 2
    x_other = device + 1 - 2 * x_at
    inner = plane < planes - 1
    prefix = prefix_ref[0]
    inputs.start()
    greet([({"dp": x_other}, True), ({"dp": device + 2}, inner), ({"dp": device - 2}, plane > 0)])

    def store(slot):
        return pltpu.make_async_copy(all_ref.at[slot], all_out.at[slot], all_sems.at[slot])

    def source(slot):
        return kv_ref if slot == 0 else all_ref.at[2 * slot]

    split = planes - 1 if planes > 2 else planes
    upper = pl.ds(rows // 2, rows - rows // 2)

    def to_x(slot):
        part = pl.ds(0, rows // 2 if slot == split else rows)
        return pltpu.make_async_remote_copy(
            src_ref=source(slot).at[part, :],
            dst_ref=all_ref.at[2 * slot + 1, part, :],
            send_sem=send_x.at[slot],
            recv_sem=recv_x.at[slot],
            device_id={"dp": x_other},
            device_id_type=pl.DeviceIdType.MESH,
        )

    def to_z(slot):
        return pltpu.make_async_remote_copy(
            src_ref=source(slot - 1),
            dst_ref=all_ref.at[2 * slot],
            send_sem=send_z.at[slot],
            recv_sem=recv_z.at[slot],
            device_id={"dp": device + 2},
            device_id_type=pl.DeviceIdType.MESH,
        )

    def rest_to_z():
        return remote(
            all_ref.at[2 * split - 1, upper, :],
            all_ref.at[2 * split + 1, upper, :],
            send_rest,
            recv_rest,
            {"dp": device + 2},
        )

    def to_first():
        return pltpu.make_async_remote_copy(
            src_ref=kv_ref,
            dst_ref=all_ref.at[2],
            send_sem=send_down,
            recv_sem=recv_z.at[1],
            device_id={"dp": device - 2},
            device_id_type=pl.DeviceIdType.MESH,
        )

    inputs.wait(x_ref, w_k, w_v, cos_ref, sin_ref)
    x = x_ref[...].astype(F32)
    r = lax.rsqrt(jnp.mean(x * x, axis=1, keepdims=True) + EPS)
    h_ref[...] = (x * r * gain_ref[...]).astype(BF16)
    cos, sin = cos_ref[...], sin_ref[...]

    def rotate(u, gain):
        u = u * lax.rsqrt(jnp.mean(u * u, axis=1, keepdims=True) + EPS) * gain[...]
        return (u * cos + roll_half(u) * sin).astype(BF16)

    keys = dot(h_ref[...], w_k[...])
    k_raw[...] = keys
    for at in range(0, kv_width, width):
        kv_ref[:, at : at + width] = rotate(keys[:, at : at + width], k_gain)
    kv_ref[:, kv_width:] = dot(h_ref[...], w_v[...]).astype(BF16)
    ones = jnp.ones((rows, width), BF16)
    row0 = member * rows

    def work(block, other, masked, start=False):
        key0 = other * rows

        def head_pair(h, carry):
            k = block[:, pl.ds(pl.multiple_of(h * width, width), width)]
            v = block[:, pl.ds(pl.multiple_of(kv_width + h * width, width), width)]
            v = jnp.concatenate([v, ones], axis=1)
            for g in range(repeat):
                head = h * repeat + g
                for at in range(0, rows, tile):
                    q = q_ref[at : at + tile, pl.ds(pl.multiple_of(head * width, width), width)]
                    p = jnp.exp2(dot(q, k, NT) * coef)
                    if masked:
                        p = jnp.where(visible(p.shape, key0, row0 + at, prefix), p, 0.0)
                    term = dot(p.astype(BF16), v)
                    if start:
                        acc[head, at : at + tile, :] = term
                    else:
                        acc[head, at : at + tile, :] += term
            return carry

        lax.fori_loop(0, kv_heads, head_pair, 0)

    to_x(0).start()
    if planes > 1:

        @pl.when(inner)
        def _():
            to_z(1).start()

        @pl.when(plane == 1)
        def _():
            to_first().start()

    inputs.wait(w_q)
    queries = dot(h_ref[...], w_q[...])
    q_raw[...] = queries
    for at in range(0, queries.shape[1], width):
        q_ref[:, at : at + width] = rotate(queries[:, at : at + width], q_gain)
    outputs.start()
    all_ref[0] = kv_ref[...]
    store(0).start()
    work(kv_ref, member, True, True)
    to_x(0).wait_recv()
    store(1).start()
    work(all_ref.at[1], member + 1 - 2 * x_at, True)
    for slot in range(1, planes):

        def step(slot=slot):
            to_z(slot).wait_recv()
            if slot < planes - 1:

                @pl.when(inner & (plane >= slot))
                def _():
                    to_z(slot + 1).start()

            to_x(slot).start()
            store(2 * slot).start()
            there = 2 * (plane - slot)
            if slot == 1:

                @pl.when(plane == 0)
                def _():
                    work(all_ref.at[2 * slot], 2 + x_at, True)

                @pl.when(plane > 0)
                def _():
                    work(all_ref.at[2 * slot], there + x_at, False)
            else:
                work(all_ref.at[2 * slot], there + x_at, False)
            to_x(slot).wait_recv()
            if slot == split - 1:

                @pl.when(plane == split - 1)
                def _():
                    rest_to_z().start()

            if slot == split:
                rest_to_z().wait_recv()
            store(2 * slot + 1).start()
            if slot == 1:

                @pl.when(plane == 0)
                def _():
                    work(all_ref.at[2 * slot + 1], 3 - x_at, True)

                @pl.when(plane > 0)
                def _():
                    work(all_ref.at[2 * slot + 1], there + 1 - x_at, False)
            else:
                work(all_ref.at[2 * slot + 1], there + 1 - x_at, False)

        if slot == 1:
            step()
        else:
            pl.when(plane >= slot)(step)

    for head in range(kv_heads * repeat):
        total = acc[head, :, width:]
        o_ref[:, head * width : (head + 1) * width] = (acc[head, :, :width] / total).astype(BF16)
        lse_ref[:, head * width : (head + 1) * width] = jnp.log2(total) * (1.0 / coef)

    outputs.wait()
    if split < planes:
        pl.when(plane == split - 1)(lambda: rest_to_z().wait_send())
    to_x(0).wait_send()
    for slot in range(planes):

        @pl.when((plane >= slot) | (slot <= 1))
        def _(slot=slot):
            store(2 * slot).wait()
            store(2 * slot + 1).wait()

    for slot in range(1, planes):

        @pl.when(inner & (plane >= slot - 1))
        def _(slot=slot):
            to_z(slot).wait_send()

        @pl.when((plane >= slot) | (slot == 1))
        def _(slot=slot):
            to_x(slot).wait_send()

    if planes > 1:

        @pl.when(plane == 1)
        def _():
            to_first().wait_send()


def attn_fwd(prefix, x, gain, w_query, key_weight, value_weight, q_gain, k_gain, cos, sin, group, dims):
    kv_heads, repeat, width = dims
    rows = x.shape[0]
    heads = kv_heads * repeat
    columns = heads * width
    planes = group // 2
    dma = pltpu.SemaphoreType.DMA
    block = (rows, 2 * kv_heads * width)
    staged = [x, key_weight, value_weight, cos, sin, w_query]
    table = jax.ShapeDtypeStruct((rows, width), F32)
    early = [
        jax.ShapeDtypeStruct(x.shape, BF16),
        jax.ShapeDtypeStruct((rows, columns), BF16),
        jax.ShapeDtypeStruct((rows, columns), F32),
        jax.ShapeDtypeStruct((rows, kv_heads * width), F32),
    ]
    return pl.pallas_call(
        functools.partial(
            attn_fwd_kernel,
            group=group,
            kv_heads=kv_heads,
            repeat=repeat,
            width=width,
            tile=min(rows, 256),
            coef=math.log2(math.e) / math.sqrt(width),
        ),
        out_shape=[
            jax.ShapeDtypeStruct((rows, columns), BF16),
            jax.ShapeDtypeStruct((rows, columns), F32),
            jax.ShapeDtypeStruct((group,) + block, BF16),
        ]
        + early,
        in_specs=[smem()] + vmem(3) + [ANYWHERE] * 6,
        out_specs=vmem(2) + [ANYWHERE] * 5,
        scratch_shapes=Staged.scratch([x, key_weight, value_weight, table, table, w_query])
        + Staged.scratch(early)
        + [pltpu.VMEM(block, BF16), pltpu.VMEM((group,) + block, BF16), dma((group,))]
        + [pltpu.VMEM((heads, rows, 2 * width), F32)]
        + [dma((planes,))] * 4
        + [dma] * 3,
        compiler_params=pltpu.CompilerParams(
            vmem_limit_bytes=VMEM_LIMIT, collective_id=0, has_side_effects=True
        ),
        cost_estimate=COST,
        name="attn_fwd",
    )(prefix, gain, q_gain, k_gain, *staged)


def split_three(value):
    high = value.astype(BF16)
    left = value - high.astype(F32)
    mid = left.astype(BF16)
    return high.astype(F32), mid.astype(F32), (left - mid.astype(F32)).astype(BF16).astype(F32)


def back_kernel(
    *refs, group, planes, all_planes, shard, kv_heads, repeat, width, coef, scale, sums
):
    refs = list(refs)

    def take(count):
        out = refs[:count]
        del refs[:count]
        return out

    device = lax.axis_index("dp")
    member = device % group
    plane = member // 2
    last = planes - 1
    prefix_ref, up_ref, w_down_in, middle_in = take(4)
    if sums:
        hid_arrays = take(1)
    count = 12 if sums else 5
    arrays = take(count)
    dq_ref, grad_ref, up_came_ref, block_ref = take(4)
    if sums:
        w_down_ref, w_gate_ref, w_out_ref = take(3)
    a_ref, a_came_ref = take(2)
    if sums:
        hid_buffers = take(1)
        hid_sems = take(1)[0]
    buffers = take(count)
    inputs = Staged(arrays, buffers, *take(1))
    a_all_ref, qx_ref, dox_ref, kv_ref, hid_ref = buffers[:5]
    if sums:
        hid_came_ref = hid_buffers[0]
        og_ref, og_came_ref, gate_ref, h_ref, h_came_ref, heads_ref, heads_came_ref = buffers[5:]
    down_buf, down_sems, mine_ref, middle_buf, middle_sems = take(5)
    block_sems = take(3)
    total_scratch = take(8)
    own_ref, far_ref, xr_ref, zr_ref, first_ref = take(5)
    send_x, recv_x, send_z, recv_z, send_first, recv_first = take(6)
    swap_sems = take(2)
    a_scratch = take(6)
    rows = qx_ref.shape[1]
    kv_width = kv_heads * width
    if sums:
        gate_came_ref, send_gate, recv_gate = take(3)
        left = w_down_ref.shape[0]
        rest = pl.ds(hid_arrays[0].shape[1] - left, left)
        hid_inputs = Staged([h.at[:, rest] for h in hid_arrays], hid_buffers, hid_sems)
        down_sum, out_sum = (LineSum(take(6), device, plane, planes) for _ in range(2))
        piece = gate_came_ref.shape[2]
        pieces = gate_ref.shape[1] // piece
        gate_sums = [LineSum(take(6), device, plane, planes) for _ in range(pieces)]
    x_at = member % 2
    x_other = device + 1 - 2 * x_at
    inner = plane < last
    prefix = prefix_ref[0]

    core, core_peer, y_peer = tensor_peers()
    x_peer = {"dp": x_other}
    total = TensorSum(total_scratch, mine_ref, core, core_peer, y_peer)
    half = total.half
    parts, narrow = total.chunks, total.width

    def load(i):
        at = pl.ds(i * narrow, narrow)
        return pltpu.make_async_copy(w_down_in.at[:, at], down_buf.at[i % 2], down_sems.at[i % 2])

    def middle_load(i):
        at = pl.ds(i * narrow, narrow)
        return pltpu.make_async_copy(middle_in.at[:, at], middle_buf.at[i % 2], middle_sems.at[i % 2])

    def block_at(i):
        return block_ref.at[rows_of(core, half), pl.ds(i * narrow, narrow)]

    def block_store(i):
        return pltpu.make_async_copy(total.both.at[i], block_at(i), block_sems[0].at[i])

    def block_give(i):
        return remote(total.both.at[i], block_at(i), block_sems[1].at[i], block_sems[2].at[i], core_peer)

    def block_add(i):
        load(i).wait()
        total.add(i, dot(hid_ref[...], down_buf[i % 2]))
        if i + 2 < parts:
            load(i + 2).start()

    def block_finish(i):
        middle_load(i).wait()
        value = middle_buf[i % 2] + total.total(i)
        total.over_y(i).wait_send()
        total.both[i] = value.astype(BF16)
        if i + 2 < parts:
            middle_load(i + 2).start()
        block_store(i).start()
        block_give(i).start()

    inputs.start(a_all_ref)
    if sums:
        hid_inputs.start()
        inputs.start(hid_ref, *buffers[5:7])
    inputs.start(*buffers[1:4])
    if sums:
        inputs.start(*buffers[7:])
    else:
        inputs.start(hid_ref)
    for i in range(2):
        load(i).start()
        middle_load(i).start()
    greet(
        [
            (x_peer, True),
            (core_peer, True),
            (y_peer, True),
            ({"dp": device + 2}, inner),
            ({"dp": device - 2}, plane > 0),
        ]
    )

    def copy(src, dst, send, recv, there):
        return remote(src, dst, send, recv, {"dp": there})

    place = (x_at, core, x_peer, core_peer, all_planes, shard)
    d_attn = Columns(a_all_ref, a_ref, a_came_ref, a_scratch, *place)
    up_swap = copy(up_ref, up_came_ref, swap_sems[0], swap_sems[1], x_other)

    def gate_swap(k):
        part = gate_ref.at[:, pl.ds(k * piece, piece)]
        return copy(part, gate_came_ref.at[k], send_gate.at[k], recv_gate.at[k], x_other)

    def gate_start(k):
        gate_swap(k).wait_recv()
        part = gate_ref.at[:, pl.ds(k * piece, piece)]
        gate_sums[k].fill_rows(h_ref, h_came_ref, part, gate_came_ref.at[k])
        gate_sums[k].start()

    lane = lax.broadcasted_iota(jnp.int32, (rows, width), 1)
    minus = jnp.where(lane < 3, -1.0, 0.0).astype(BF16)
    row0 = member * rows

    def work(block, other, masked, out):
        key0 = other * rows

        def head_group(h, carry):
            k_at = pl.ds(pl.multiple_of(h * width, width), width)
            v_at = pl.ds(pl.multiple_of(kv_width + h * width, width), width)
            k = kv_ref[block, :, k_at]
            v = kv_ref[block, :, v_at]
            kx = jnp.concatenate([k, minus], axis=1)
            vx = jnp.concatenate([v, minus], axis=1)
            dk = jnp.zeros((rows, width), F32)
            dv = jnp.zeros((rows, width), F32)
            for g in range(repeat):
                head = h * repeat + g
                qx = qx_ref[head]
                dox = dox_ref[head]
                p = jnp.exp2(dot(qx, kx, NT) * coef)
                if masked:
                    p = jnp.where(visible(p.shape, key0, row0, prefix), p, 0.0)
                ds = (p * dot(dox, vx, NT)).astype(BF16)
                dv += dot(p.astype(BF16), dox[:, :width], TN)
                dk += dot(ds, qx[:, :width], TN)
                dq_ref[:, pl.ds(pl.multiple_of(head * width, width), width)] += dot(ds, k)
            out[:, k_at] = (dk * scale).astype(BF16)
            out[:, v_at] = dv.astype(BF16)
            return carry

        lax.fori_loop(0, kv_heads, head_group, 0)

    def far_swap(slot):
        return copy(far_ref.at[slot], xr_ref.at[slot], send_x.at[slot], recv_x.at[slot], x_other)

    def to_plane(slot):
        return copy(own_ref.at[slot], zr_ref.at[slot], send_z.at[slot], recv_z.at[slot], device - 2)

    def from_first():
        return copy(own_ref.at[1], first_ref, send_first, recv_first, device + 2)

    def attend(slot):
        there = 2 * (plane - slot)
        far, own = there + 1 - x_at, there + x_at

        def both(far, own, masked):
            work(2 * slot + 1, far, masked, far_ref.at[slot])
            far_swap(slot).start()
            work(2 * slot, own, masked, own_ref.at[slot])

        if slot == 0:
            both(far, own, True)
        elif slot == 1:
            pl.when(plane == 0)(lambda: both(3 - x_at, 2 + x_at, True))
            pl.when(plane > 0)(lambda: both(far, own, False))
        else:
            pl.when(plane >= slot)(lambda: both(far, own, False))

    def pass_back(slot):
        def go():
            far_swap(slot).wait_recv()
            own_ref[slot] += xr_ref[slot]
            if slot < last:

                @pl.when(inner & (plane >= slot))
                def _():
                    to_plane(slot + 1).wait_recv()
                    own_ref[slot] += zr_ref[slot + 1]

            if slot == 1:
                pl.when(plane == 0)(lambda: from_first().start())
                pl.when(plane > 0)(lambda: to_plane(slot).start())
            else:
                to_plane(slot).start()

        if slot == 1:
            go()
        else:
            pl.when(plane >= slot)(go)

    dq_ref[...] = jnp.zeros_like(dq_ref)
    inputs.wait(a_all_ref)
    d_attn.start()
    inputs.wait(hid_ref)
    if sums:
        hid_inputs.wait()
        inputs.wait(og_ref, og_came_ref)
        down_sum.fill_columns(hid_ref.at[:, rest], hid_came_ref, og_ref, og_came_ref)
        down_sum.start()
    inputs.wait(*buffers[1:4])
    attend(last)
    d_attn.forward()
    if sums:
        inputs.wait(*buffers[7:])
        gate_swap(0).start()
    d_attn.store()
    pending = list(range(last, 0, -1))
    steps = range(1, last)
    adds = list(range(parts))
    share = -(-parts // last)
    for slot in range(last - 1, -1, -1):
        attend(slot)
        if slot == last - 1:
            if sums:
                d_attn.over_core().wait_recv()
                out_sum.fill_columns(heads_ref, heads_came_ref, a_ref, a_came_ref)
                out_sum.start()
                down_sum.advance(1)
                gate_start(0)
                gate_swap(1).start()
            pass_back(pending.pop(0))
        if slot == last - 2:
            if sums:
                for step in steps[1:]:
                    down_sum.advance(step)
                out_sum.advance(1)
                gate_start(1)
                gate_swap(2).start()
                gate_sums[0].advance(1)
            pass_back(pending.pop(0))
        for i in adds[:share]:
            block_add(i)
        del adds[:share]
    for i in adds:
        block_add(i)
    if sums:
        for step in steps[1:]:
            out_sum.advance(step)
            gate_sums[0].advance(step)
    while pending:
        pass_back(pending.pop(0))
    if sums:
        gate_start(2)
    up_swap.start()
    if sums:
        gate_sums[1].advance(1)
    for i in range(parts // 2):
        block_finish(i)
    if sums:
        for step in steps[1:]:
            gate_sums[1].advance(step)
        gate_sums[2].advance(1)
    for i in range(parts // 2, parts):
        block_finish(i)
    if sums:
        for step in steps[1:]:
            gate_sums[2].advance(step)
    dq_ref[...] = dq_ref[...] * scale

    far_swap(0).wait_recv()
    grad_ref[...] = own_ref[0].astype(F32) + xr_ref[0].astype(F32)
    if last > 0:

        @pl.when(inner)
        def _():
            to_plane(1).wait_recv()
            grad_ref[...] += zr_ref[1].astype(F32)

        @pl.when(plane == 1)
        def _():
            from_first().wait_recv()
            grad_ref[...] += first_ref[...].astype(F32)

    if sums:
        down_sum.finish(w_down_ref)
        out_sum.finish(w_out_ref)
        for k in range(pieces):
            gate_sums[k].finish(w_gate_ref.at[:, pl.ds(k * piece, piece)])
            gate_swap(k).wait_send()
    else:
        d_attn.over_core().wait_recv()
    up_swap.wait_recv()
    up_swap.wait_send()
    for i in range(parts):
        total.over_core(i).wait_send()
        block_store(i).wait()
        block_give(i).wait_recv()
        block_give(i).wait_send()
    d_attn.over_x().wait_send()
    d_attn.over_core().wait_send()
    for slot in range(planes):
        if slot <= 1:
            far_swap(slot).wait_send()
        else:
            pl.when(plane >= slot)(lambda slot=slot: far_swap(slot).wait_send())
        if slot >= 1:
            pl.when(plane >= slot)(lambda slot=slot: to_plane(slot).wait_send())
    if last > 0:
        pl.when(plane == 0)(lambda: from_first().wait_send())


def back(prefix, qx, dox, kv_all, shared, grads, group, all_planes, shard, pieces, dims):
    kv_heads, repeat, width = dims
    rows = qx.shape[1]
    columns = kv_heads * repeat * width
    planes = group // 2
    block = kv_all.shape[1:]
    dma = pltpu.SemaphoreType.DMA
    d_attn, d_up, hidden, w_down, middle = shared
    half, model = middle.shape
    parts = 8
    narrow = model // parts
    units = d_up.shape[1]
    cut_shape = jax.ShapeDtypeStruct((rows, all_planes * shard), BF16)
    out_shape = [jax.ShapeDtypeStruct((rows, columns), F32), jax.ShapeDtypeStruct(block, F32)]
    out_shape += [jax.ShapeDtypeStruct(d_up.shape, BF16), jax.ShapeDtypeStruct((rows, model), BF16)]
    scratch = [pltpu.VMEM((planes,) + block, BF16)] * 4 + [pltpu.VMEM(block, BF16)]
    scratch += [dma((planes,))] * 4 + [dma, dma] + [dma] * 2
    scratch += Columns.scratch(rows // 2, all_planes * shard)
    staged = [d_attn, qx, dox, kv_all, hidden]
    args = [prefix, d_up, w_down, middle]
    first = []
    if grads is not None:
        args += grads[:1]
        staged += grads[1:]
        first = [pltpu.VMEM(cut_shape.shape, BF16)] * 2
        first += [pltpu.VMEM((rows, units // pieces), BF16), dma((1,))]
    else:
        out_shape += [cut_shape] * 2
    args += staged
    product = [pltpu.VMEM((2, units, narrow), BF16), dma((2,)), pltpu.VMEM((2, rows, narrow), F32)]
    product += [pltpu.VMEM((2, half, narrow), F32), dma((2,))] + [dma((parts,))] * 3
    product += TensorSum.scratch(parts, half, narrow)
    scratch = first + Staged.scratch(staged) + product + scratch
    if grads is not None:
        piece = units // pieces
        shapes = (piece, shard), (shard, units), (columns, shard)
        out_shape += [jax.ShapeDtypeStruct(s, BF16) for s in shapes]
        scratch += [pltpu.VMEM((pieces, rows, piece), BF16)] + [dma((pieces,))] * 2
        for shape in [(piece, shard), (columns, shard)] + [(shard, piece)] * pieces:
            scratch += LineSum.scratch(planes, shape)
    return pl.pallas_call(
        functools.partial(
            back_kernel,
            group=group,
            planes=planes,
            all_planes=all_planes,
            shard=shard,
            kv_heads=kv_heads,
            repeat=repeat,
            width=width,
            coef=math.log2(math.e) / math.sqrt(width),
            scale=1.0 / math.sqrt(width),
            sums=grads is not None,
        ),
        out_shape=out_shape,
        in_specs=[smem()] + [ANYWHERE] * (len(args) - 1),
        out_specs=vmem(2) + [ANYWHERE] * 2 + vmem(len(out_shape) - 4),
        scratch_shapes=scratch,
        compiler_params=pltpu.CompilerParams(
            vmem_limit_bytes=BACK_VMEM_LIMIT, collective_id=1, has_side_effects=True
        ),
        cost_estimate=COST,
        name="back",
    )(*args)


def smem():
    return pl.BlockSpec(memory_space=pltpu.SMEM)


def out_kernel(*refs, planes, shard, blocks):
    refs = list(refs)

    def take(count):
        out = refs[:count]
        del refs[:count]
        return out

    arrays = take(4)
    gain_ref, w_down_ref = take(2)
    middle_ref, h_ref, d_hidden_out, og_keep, og_came, heads_came = take(6)
    buffers = take(4)
    heads_ref, w_ref, og_ref, x_ref = buffers
    inputs = Staged(arrays, buffers, *take(1))
    d_hidden_ref, d_hidden_sem = take(2)
    down_buf, down_sems, whole_ref, h_send, h_recv, heads_send, heads_recv = take(7)
    scratch = refs
    device = lax.axis_index("dp")
    core, core_peer, y_peer = tensor_peers()
    x_at = device % 2
    x_peer = {"dp": device + 1 - 2 * x_at}
    half = middle_ref.shape[0]
    total = TensorSum(scratch[:8], None, core, core_peer, y_peer)
    step = half // blocks
    place = (x_at, core, x_peer, core_peer, planes, shard)
    og = Columns(og_ref, og_keep, og_came, scratch[8:14], *place)
    tiles = down_sems.shape[0]
    tile = down_buf.shape[0] // tiles

    def load(t):
        at = pl.ds(t * tile, tile)
        return pltpu.make_async_copy(w_down_ref.at[at, :], down_buf.at[at, :], down_sems.at[t])

    inputs.start()
    for t in range(tiles):
        load(t).start()
    greet([(x_peer, True), (core_peer, True), (y_peer, True)])
    heads_swap = remote(heads_ref, heads_came, heads_send, heads_recv, x_peer)
    inputs.wait(heads_ref, w_ref)
    heads_swap.start()

    def rows_at(which, b):
        return pl.ds(pl.multiple_of(which * half + b * step, step), step)

    whole_ref[...] = dot(heads_ref[...], w_ref[...])
    for b in range(blocks):
        total.away[b] = whole_ref[rows_at(1 - core, b), :].astype(BF16)
        total.over_core(b).start()
    for b in range(blocks):
        total.over_core(b).wait_recv()
        mine = whole_ref[rows_at(core, b), :] + total.core_came[b].astype(F32)
        total.both[b] = mine.astype(BF16)
        total.over_y(b).start()
    inputs.wait(og_ref)
    og.start()
    og.store()
    for t in range(tiles):
        at = slice(t * tile, (t + 1) * tile)
        load(t).wait()
        d_hidden_ref[:, at] = dot(og_ref[...], down_buf[at, :], NT)
    d_hidden_copy = pltpu.make_async_copy(d_hidden_ref, d_hidden_out, d_hidden_sem)
    d_hidden_copy.start()
    inputs.wait(x_ref)

    def to_core(b):
        rows = h_ref.at[rows_at(core, b), :]
        return remote(rows, rows, h_send.at[b], h_recv.at[b], core_peer)

    for b in range(blocks):
        at = rows_at(core, b)
        v = x_ref[at, :].astype(F32) + total.total(b)
        middle_ref[b * step : (b + 1) * step, :] = v
        r = lax.rsqrt(jnp.mean(v * v, axis=1, keepdims=True) + EPS)
        h_ref[at, :] = (v * r * gain_ref[...]).astype(BF16)
        to_core(b).start()
    og.forward()
    og.finish()
    d_hidden_copy.wait()
    heads_swap.wait_recv()
    heads_swap.wait_send()
    for b in range(blocks):
        to_core(b).wait_recv()
        to_core(b).wait_send()
    total.finish()


def attention_out(heads, w_out, x, gain, out_grad, w_down, planes, shard):
    rows, model = x.shape
    half = rows // 2
    units = w_down.shape[0]
    blocks = 4
    tiles = units // math.gcd(units, 256)
    dma = pltpu.SemaphoreType.DMA
    cut_shape = jax.ShapeDtypeStruct((rows, planes * shard), BF16)
    return pl.pallas_call(
        functools.partial(out_kernel, planes=planes, shard=shard, blocks=blocks),
        out_shape=[
            jax.ShapeDtypeStruct((half, model), F32),
            jax.ShapeDtypeStruct((rows, model), BF16),
            jax.ShapeDtypeStruct((rows, units), F32),
        ]
        + [cut_shape] * 2
        + [jax.ShapeDtypeStruct(heads.shape, BF16)],
        in_specs=[ANYWHERE] * 4 + vmem(1) + [ANYWHERE],
        out_specs=vmem(2) + [ANYWHERE] + vmem(3),
        scratch_shapes=Staged.scratch([heads, w_out, out_grad, x])
        + [pltpu.VMEM((rows, units), F32), dma]
        + [pltpu.VMEM((units, model), BF16), dma((tiles,))]
        + [pltpu.VMEM((rows, model), F32), dma((blocks,)), dma((blocks,)), dma, dma]
        + TensorSum.scratch(blocks, half // blocks, model)
        + Columns.scratch(half, planes * shard),
        compiler_params=pltpu.CompilerParams(
            vmem_limit_bytes=VMEM_LIMIT, collective_id=4, has_side_effects=True
        ),
        cost_estimate=COST,
        name="attention_out",
    )(heads, w_out, out_grad, x, gain, w_down)


def middle_kernel(*refs, planes, shard, heads, width, pieces, blocks, sums):
    refs = list(refs)

    def take(count):
        out = refs[:count]
        del refs[:count]
        return out

    w_gate_ref, w_up_ref, gain_ref = take(3)
    count = 10 if sums else 8
    arrays = take(count)
    outs = take(3)
    hid_came_ref, a_ref, gain_out_ref, qx_ref, dox_ref, h_keep, h_came = take(7)
    if sums:
        down_outs = take(pieces - 1)
    buffers = take(count)
    inputs = Staged(arrays, buffers, *take(1))
    h_ref, d_ref, middle_ref, og_ref, w_out_ref, q_ref, o_ref, lse_ref = buffers[:8]
    if sums:
        og_keep, og_came = buffers[8:]
    out_buffers = take(3)
    hid_ref, gate_ref, up_ref = out_buffers
    outputs = Staged(outs, out_buffers, *take(1), out=True)
    gate_buf, up_buf, load_sems, c_ref, mine_ref = take(5)
    hid_send, hid_recv, a_send, a_recv = take(4)
    sum_scratch, h_scratch = take(8), take(6)
    device = lax.axis_index("dp")
    core, core_peer, y_peer = tensor_peers()
    plane = device // 2
    x_at = device % 2
    x_peer = {"dp": device + 1 - 2 * x_at}
    meets = [(x_peer, True), (core_peer, True), (y_peer, True)]
    h_two = Columns(h_ref, h_keep, h_came, h_scratch, x_at, core, x_peer, core_peer, planes, shard)
    half = middle_ref.shape[0]
    total = TensorSum(sum_scratch, mine_ref, core, core_peer, y_peer)
    chunks, columns = total.chunks, total.width
    units = hid_ref.shape[1]
    piece = units // pieces
    tile = 256
    tiles = units // tile
    if sums:
        downs = [LineSum(take(6), device, plane, planes) for _ in range(pieces - 1)]
        meets += [({"dp": device + 2}, plane < planes - 1), ({"dp": device - 2}, plane > 0)]

    def loads(t):
        at = pl.ds(t * tile, tile)
        return (
            pltpu.make_async_copy(w_gate_ref.at[:, at], gate_buf.at[:, at], load_sems.at[2 * t]),
            pltpu.make_async_copy(w_up_ref.at[:, at], up_buf.at[:, at], load_sems.at[2 * t + 1]),
        )

    inputs.start(h_ref)
    for t in range(tiles):
        for load in loads(t):
            load.start()
        if t == 0:
            inputs.start(d_ref)
    inputs.start(*buffers[2:])
    greet(meets)
    inputs.wait(h_ref)

    def swap(k):
        at = pl.ds(k * tile, tile)
        return remote(hid_ref.at[:, at], hid_came_ref.at[:, at], hid_send.at[k], hid_recv.at[k], x_peer)

    for t in range(tiles):
        for load in loads(t):
            load.wait()
        if t == 0:
            inputs.wait(d_ref)
        at = slice(t * tile, (t + 1) * tile)
        gate = dot(h_ref[...], gate_buf[:, at])
        up = dot(h_ref[...], up_buf[:, at])
        sig = 0.5 * jnp.tanh(0.5 * gate) + 0.5
        silu = gate * sig
        d = d_ref[:, at]
        hid_ref[:, at] = (silu * up).astype(BF16)
        up_ref[:, at] = (d * silu).astype(BF16)
        gate_ref[:, at] = (d * up * (sig * (1.0 + gate * (1.0 - sig)))).astype(BF16)
        swap(t).start()

    outputs.start()
    inputs.wait(*buffers[2:])

    def down_start(k):
        if sums:
            at = pl.ds(k * piece, piece)
            for t in range(k * piece // tile, (k + 1) * piece // tile):
                swap(t).wait_recv()
            downs[k].fill_columns(hid_ref.at[:, at], hid_came_ref.at[:, at], og_keep, og_came)
            downs[k].start()

    def down_advance(k, step):
        if sums and step <= planes - 2:
            downs[k].advance(step)

    for i in range(chunks):
        at = slice(i * columns, (i + 1) * columns)
        total.add(i, dot(gate_ref[...], gate_buf[at, :], NT) + dot(up_ref[...], up_buf[at, :], NT))
        if i == chunks // 2:
            down_start(0)
    for i in range(chunks):
        if i == chunks // 4:
            down_start(1)
            h_two.start()
        if i == chunks // 2:
            down_advance(0, 1)
        c_ref[:, i * columns : (i + 1) * columns] = total.total(i)
    down_advance(0, 2)

    step = half // blocks

    def to_core(b):
        rows = a_ref.at[pl.ds(pl.multiple_of(core * half + b * step, step), step), :]
        return remote(rows, rows, a_send.at[b], a_recv.at[b], core_peer)

    gain_out_ref[...] = jnp.zeros_like(gain_out_ref)
    for b in range(blocks):
        at = slice(b * step, (b + 1) * step)
        whole_at = pl.ds(pl.multiple_of(core * half + b * step, step), step)
        c = c_ref[at, :]
        v = middle_ref[at, :]
        r = lax.rsqrt(jnp.mean(v * v, axis=1, keepdims=True) + EPS)
        n = v * r
        gain_out_ref[...] += jnp.sum(c * n, axis=0, keepdims=True)
        gc = c * gain_ref[...]
        d = r * (gc - n * jnp.mean(n * gc, axis=1, keepdims=True)) + og_ref[whole_at, :].astype(F32)
        a_ref[whole_at, :] = d.astype(BF16)
        to_core(b).start()

    lane = lax.broadcasted_iota(jnp.int32, (half, width), 1)

    def extra(value):
        a, b, c = split_three(value)
        return jnp.where(lane == 0, a, jnp.where(lane == 1, b, jnp.where(lane == 2, c, 0.0))).astype(BF16)

    def prepare(which):
        at_rows = rows_of(which, half)
        d_heads = dot(a_ref[at_rows, :], w_out_ref[...], NT)
        for head in range(heads):
            at = slice(head * width, (head + 1) * width)
            qx_ref[head, at_rows, :width] = q_ref[at_rows, at]
            qx_ref[head, at_rows, width:] = extra(lse_ref[at_rows, at])
            d = d_heads[:, at].astype(BF16)
            delta = jnp.sum(d.astype(F32) * o_ref[at_rows, at].astype(F32), axis=1, keepdims=True)
            dox_ref[head, at_rows, :width] = d
            dox_ref[head, at_rows, width:] = extra(jnp.broadcast_to(delta, (half, width)))

    down_advance(1, 1)
    h_two.store()
    prepare(core)
    h_two.forward()
    for b in range(blocks):
        to_core(b).wait_recv()
    prepare(1 - core)
    down_advance(1, 2)
    for b in range(blocks):
        to_core(b).wait_send()
    total.finish()
    h_two.finish()
    outputs.wait()
    for t in range(tiles):
        if t >= (pieces - 1) * piece // tile or not sums:
            swap(t).wait_recv()
        swap(t).wait_send()
    if sums:
        for k in range(pieces - 1):
            for step in range(3, planes - 1):
                downs[k].advance(step)
            downs[k].finish(down_outs[k])


def middle_of(w_gate, w_up, h_two, d_hidden, middle, out_grad, gain, w_out, q, out, lse, cuts, pieces, planes, shard, width):
    half, model = middle.shape
    rows, units = d_hidden.shape
    columns = q.shape[1]
    heads = columns // width
    chunks, blocks = 4, 4
    dma = pltpu.SemaphoreType.DMA
    staged = [h_two, d_hidden, middle, out_grad, w_out, q, out, lse] + ([] if cuts is None else cuts)
    args = [w_gate, w_up, gain, *staged]
    unit_shape = jax.ShapeDtypeStruct((rows, units), BF16)
    out_shape = [unit_shape] * 4 + [
        jax.ShapeDtypeStruct((rows, model), BF16),
        jax.ShapeDtypeStruct((1, model), F32),
    ]
    out_shape += [jax.ShapeDtypeStruct((heads, rows, 2 * width), BF16)] * 2
    out_shape += [jax.ShapeDtypeStruct((rows, planes * shard), BF16)] * 2
    scratch = Staged.scratch(staged) + Staged.scratch([unit_shape] * 3)
    scratch += [pltpu.VMEM((model, units), BF16)] * 2 + [dma((2 * units // 256,))]
    scratch += [pltpu.VMEM((half, model), F32), pltpu.VMEM((2, rows, model // chunks), F32)]
    scratch += [dma((units // 256,))] * 2 + [dma((blocks,))] * 2
    scratch += TensorSum.scratch(chunks, half, model // chunks)
    scratch += Columns.scratch(half, planes * shard)
    if cuts is not None:
        out_shape += [jax.ShapeDtypeStruct((units // pieces, shard), BF16)] * (pieces - 1)
        scratch += LineSum.scratch(planes, (units // pieces, shard)) * (pieces - 1)
    return pl.pallas_call(
        functools.partial(
            middle_kernel,
            planes=planes,
            shard=shard,
            heads=heads,
            width=width,
            pieces=pieces,
            blocks=blocks,
            sums=cuts is not None,
        ),
        out_shape=out_shape,
        in_specs=[ANYWHERE] * 2 + vmem(1) + [ANYWHERE] * len(staged),
        out_specs=[ANYWHERE] * 3 + vmem(len(out_shape) - 3),
        scratch_shapes=scratch,
        compiler_params=pltpu.CompilerParams(
            vmem_limit_bytes=BACK_VMEM_LIMIT, collective_id=2, has_side_effects=True
        ),
        cost_estimate=COST,
        name="middle",
    )(*args)


def through_rope(d_ref, raw_ref, gain, cos, sin, out_ref, width, plain):
    columns = d_ref.shape[1]
    total = jnp.zeros((1, width), F32)
    for at in range(0, columns - plain, width):
        d = d_ref[:, at : at + width]
        c = d * cos - roll_half(d) * sin
        v = raw_ref[:, at : at + width]
        r = lax.rsqrt(jnp.mean(v * v, axis=1, keepdims=True) + EPS)
        n = v * r
        total = total + jnp.sum(c * n, axis=0, keepdims=True)
        gc = gain * c
        out_ref[:, at : at + width] = (r * (gc - n * jnp.mean(n * gc, axis=1, keepdims=True))).astype(BF16)
    if plain:
        out_ref[:, columns - plain :] = d_ref[:, columns - plain :].astype(BF16)
    return total


def front_kernel(*refs, dp_size, group, planes, shard, chunks, blocks, sums):
    refs = list(refs)

    def take(count):
        out = refs[:count]
        del refs[:count]
        return out

    q_gain, k_gain, attn_gain, mlp_gain_ref, add_array = take(5)
    count = 15 if sums else 11
    arrays = take(count)
    arrays[2:4] = table_rows(arrays[2:4], lax.axis_index("dp") % group, arrays[0].shape[0])
    x_grad, gains = take(2)
    if sums:
        w_up_out, w_q_out, w_kv_out = take(3)
    dq_ref, dq_came, dkv_ref, dkv_came, one_ref, one_came = take(6)
    buffers = take(count)
    inputs = Staged(arrays, buffers, *take(1))
    dkv_in, k_raw, cos_ref, sin_ref, dq_in, q_raw, one_all = buffers[:7]
    x_ref, w_q, w_k, w_v = buffers[7:11]
    if sums:
        two_ref, two_came, up_ref, up_came = buffers[11:]
    mine, gain_came, c_ref, add_ref, add_sem = take(5)
    swap_sems, one_sems, gain_sems = take(4), take(2), take(2)
    one_sum_scratch, one_scratch = take(8), take(6)
    half = x_ref.shape[0] // 2
    model = x_ref.shape[1]
    width = model // chunks
    head = cos_ref.shape[1]
    kv_width = w_k.shape[1]

    device = lax.axis_index("dp")
    core, core_peer, y_peer = tensor_peers()
    x_at = device % 2
    x_peer = {"dp": device + 1 - 2 * x_at}
    plane = device // 2
    one = Columns(one_all, one_ref, one_came, one_scratch, x_at, core, x_peer, core_peer, planes, shard)
    bits = [1 << i for i in range(dp_size.bit_length() - 1)]
    dp_peers = [{"dp": device + bit - 2 * bit * ((device // bit) % 2)} for bit in bits]
    gain_peers = [core_peer, y_peer] + dp_peers
    meets = [(peer, True) for peer in gain_peers]
    if sums:
        up_sum, q_sum, kv_sum = (LineSum(take(6), device, plane, planes, True) for _ in range(3))
        meets += [({"dp": device + 2}, plane < planes - 1), ({"dp": device - 2}, plane > 0)]

    mine_rows = rows_of(core, half)
    add_load = pltpu.make_async_copy(add_array.at[mine_rows, :], add_ref, add_sem)
    inputs.start(one_all)
    if sums:
        inputs.start(*buffers[11:])
    inputs.start(*buffers[:6])
    inputs.start(*buffers[7:11])
    add_load.start()
    greet(meets)
    inputs.wait(one_all)
    one.start()
    if sums:
        inputs.wait(*buffers[11:])
        up_sum.fill_rows(two_ref, two_came, up_ref, up_came)
    inputs.wait(*buffers[:6])
    cos, sin = cos_ref[...], sin_ref[...]
    k_total = through_rope(dkv_in, k_raw, k_gain[...], cos, sin, dkv_ref, head, kv_width)
    kv_swap = remote(dkv_ref, dkv_came, swap_sems[0], swap_sems[1], x_peer)
    kv_swap.start()
    q_total = through_rope(dq_in, q_raw, q_gain[...], cos, sin, dq_ref, head, 0)
    q_swap = remote(dq_ref, dq_came, swap_sems[2], swap_sems[3], x_peer)
    q_swap.start()
    inputs.wait(*buffers[7:11])

    one_sum = TensorSum(one_sum_scratch, mine, core, core_peer, y_peer)
    x = x_ref[...].astype(F32)
    r = lax.rsqrt(jnp.mean(x * x, axis=1, keepdims=True) + EPS)
    for i in range(chunks):
        at = slice(i * width, (i + 1) * width)
        part = (
            dot(dq_ref[...], w_q[at, :], NT)
            + dot(dkv_ref[:, :kv_width], w_k[at, :], NT)
            + dot(dkv_ref[:, kv_width:], w_v[at, :], NT)
        )
        one_sum.add(i, part)
        gains[0, :, at] = jnp.sum(part * (x_ref[:, at].astype(F32) * r), axis=0, keepdims=True)
    gains[0, :, model : 2 * model] = 0.5 * mlp_gain_ref[...]
    gains[0, :, 2 * model : 2 * model + head] = q_total
    gains[0, :, 2 * model + head :] = k_total
    one.forward()
    one.store()

    def gain_swap(k):
        return remote(
            gains.at[k], gain_came.at[k], gain_sems[0].at[k], gain_sems[1].at[k], gain_peers[k]
        )

    def gain_add(k):
        gain_swap(k).wait_recv()
        gains[k + 1] = gains[k] + gain_came[k]
        if k + 1 < len(gain_peers):
            gain_swap(k + 1).start()

    gain_swap(0).start()

    def advance(line, step):
        if sums and step <= planes - 2:
            line.advance(step)

    gain_add(0)
    if sums:
        advance(up_sum, 1)
        kv_swap.wait_recv()
        one.over_core().wait_recv()
        kv_sum.fill_rows(one_ref, one_came, dkv_ref, dkv_came)
    gain_add(1)
    if sums:
        q_swap.wait_recv()
        q_sum.fill_rows(one_ref, one_came, dq_ref, dq_came)
        advance(up_sum, 2)
    gain_add(2)

    def give(out, sems):
        rows = out.at[mine_rows, :]
        return remote(rows, rows, sems[0], sems[1], core_peer)

    for i in range(chunks):
        c_ref[:, i * width : (i + 1) * width] = one_sum.total(i)
    add_load.wait()
    step = half // blocks
    for b in range(blocks):
        at = slice(b * step, (b + 1) * step)
        whole_at = pl.ds(pl.multiple_of(core * half + b * step, step), step)
        v = x_ref[whole_at, :].astype(F32)
        v_r = lax.rsqrt(jnp.mean(v * v, axis=1, keepdims=True) + EPS)
        n = v * v_r
        gc = c_ref[at, :] * attn_gain[...]
        d = v_r * (gc - n * jnp.mean(n * gc, axis=1, keepdims=True))
        x_grad[whole_at, :] = (d + add_ref[at, :].astype(F32)).astype(BF16)
    give(x_grad, one_sems).start()
    for k in range(3, len(gain_peers)):
        gain_add(k)
    if sums:
        advance(kv_sum, 1)
        advance(q_sum, 1)
    if sums:
        advance(kv_sum, 2)
        advance(q_sum, 2)
        for line in (up_sum, kv_sum, q_sum):
            for step in range(3, planes - 1):
                advance(line, step)
        up_sum.finish(w_up_out)
        kv_sum.finish(w_kv_out)
        q_sum.finish(w_q_out)
    else:
        kv_swap.wait_recv()
        q_swap.wait_recv()
        one.over_core().wait_recv()
    one.over_x().wait_send()
    one.over_core().wait_send()
    kv_swap.wait_send()
    q_swap.wait_send()
    give(x_grad, one_sems).wait_recv()
    give(x_grad, one_sems).wait_send()
    for k in range(len(gain_peers)):
        gain_swap(k).wait_send()
    one_sum.finish()


def front(dq, dkv, q_raw, k_raw, q_gain, k_gain, cos, sin, h_one, weights, x, d_attn, attn_gain, mlp_gain, grads, dp_size, group, shard):
    rows, model = x.shape
    half = rows // 2
    planes = dp_size // 2
    chunks = 4
    width = model // chunks
    stages = dp_size.bit_length() + 1
    dma = pltpu.SemaphoreType.DMA
    gains = (2 * model + 2 * cos.shape[1],)
    staged = [dkv, k_raw, cos, sin, dq, q_raw, h_one, x, *weights]
    if grads is not None:
        staged += grads
    args = [q_gain, k_gain, attn_gain, mlp_gain, d_attn, *staged]
    cut_shape = jax.ShapeDtypeStruct((rows, planes * shard), BF16)
    whole = jax.ShapeDtypeStruct((rows, model), BF16)
    q_shape, kv_shape = jax.ShapeDtypeStruct(dq.shape, BF16), jax.ShapeDtypeStruct(dkv.shape, BF16)
    out_shape = [whole, jax.ShapeDtypeStruct((stages + 1, 1) + gains, F32)]
    kept = [q_shape, q_shape, kv_shape, kv_shape, cut_shape, cut_shape]
    table = jax.ShapeDtypeStruct((rows, cos.shape[1]), F32)
    scratch = Staged.scratch(staged[:2] + [table, table] + staged[4:])
    scratch += [pltpu.VMEM((2, rows, width), F32)]
    scratch += [pltpu.VMEM((stages, 1) + gains, F32), pltpu.VMEM((half, model), F32)]
    scratch += [pltpu.VMEM((half, model), BF16), dma]
    scratch += [dma] * 6 + [dma((stages,))] * 2
    scratch += TensorSum.scratch(chunks, half, width)
    scratch += Columns.scratch(half, planes * shard)
    if grads is None:
        out_shape += kept
    else:
        scratch = [pltpu.VMEM(s.shape, s.dtype) for s in kept] + scratch
        for columns in (grads[2].shape[1], dq.shape[1], dkv.shape[1]):
            out_shape.append(jax.ShapeDtypeStruct((shard, columns), BF16))
            scratch += LineSum.scratch(planes, (shard, columns))
    return pl.pallas_call(
        functools.partial(
            front_kernel,
            dp_size=dp_size,
            group=group,
            planes=planes,
            shard=shard,
            chunks=chunks,
            blocks=4,
            sums=grads is not None,
        ),
        out_shape=out_shape,
        in_specs=vmem(4) + [ANYWHERE] * (len(args) - 4),
        out_specs=vmem(len(out_shape)),
        scratch_shapes=scratch,
        compiler_params=pltpu.CompilerParams(
            vmem_limit_bytes=BACK_VMEM_LIMIT, collective_id=3, has_side_effects=True
        ),
        cost_estimate=COST,
        name="front",
    )(*args)


def widen_kernel(*refs, results, gains):
    refs = list(refs)

    def take(count):
        out = refs[:count]
        del refs[:count]
        return out

    count = 1 + max(i for parts in results for i, _ in parts)
    block_in = take(1)[0]
    arrays = take(count)
    if gains:
        gain_in = take(1)[0]
    block_out = take(1)[0]
    outs = take(len(results))
    if gains:
        attn_out, mlp_out, q_out, k_out = take(4)
    buffers = take(count)
    inputs = Staged(arrays, buffers, *take(1))
    out_buffers = take(len(results))
    outputs = Staged(outs, out_buffers, *take(1), out=True)
    block, block_sems = take(2)
    if gains:
        gain_ref, gain_sem = take(2)
        gain_load = pltpu.make_async_copy(gain_in.at[gain_in.shape[0] - 1], gain_ref, gain_sem)
        gain_load.start()
    block_load = pltpu.make_async_copy(block_in, block, block_sems.at[0])
    block_copy = pltpu.make_async_copy(block, block_out, block_sems.at[1])
    block_load.start()
    inputs.start()
    if gains:
        gain_load.wait()
        shard, head = attn_out.shape[1], q_out.shape[1]
        model = (gain_ref.shape[1] - 2 * head) // 2
        at = pl.multiple_of(lax.axis_index("dp") * shard, shard)
        attn_out[...] = gain_ref[:, pl.ds(at, shard)]
        mlp_out[...] = gain_ref[:, pl.ds(pl.multiple_of(model + at, shard), shard)]
        q_out[...] = gain_ref[:, 2 * model : 2 * model + head]
        k_out[...] = gain_ref[:, 2 * model + head :]
    block_load.wait()
    block_copy.start()
    waited = set()
    for parts, out in zip(results, out_buffers):
        row = 0
        for i, column in parts:
            part = buffers[i]
            if i not in waited:
                inputs.wait(part)
                waited.add(i)
            height = part.shape[0]
            out[row : row + height, :] = part[:, column : column + out.shape[1]].astype(F32)
            row += height
        outputs.start(out)
    block_copy.wait()
    outputs.wait()


def widen(block_out, arrays, results, shapes, gains, shard, head):
    out_shape = [jax.ShapeDtypeStruct(block_out.shape, BF16)]
    out_shape += [jax.ShapeDtypeStruct(s, F32) for s in shapes]
    args = [block_out, *arrays]
    rows = [] if gains is None else [(1, shard), (1, shard), (1, head), (1, head)]
    if gains is not None:
        args.append(gains)
    return pl.pallas_call(
        functools.partial(widen_kernel, results=results, gains=gains is not None),
        out_shape=out_shape + [jax.ShapeDtypeStruct(s, F32) for s in rows],
        in_specs=[ANYWHERE] * len(args),
        out_specs=[ANYWHERE] * (1 + len(shapes)) + vmem(len(rows)),
        scratch_shapes=Staged.scratch(arrays)
        + Staged.scratch(out_shape[1:])
        + [pltpu.VMEM(block_out.shape, BF16), pltpu.SemaphoreType.DMA((2,))]
        + ([] if gains is None else [pltpu.VMEM(gains.shape[1:], F32), pltpu.SemaphoreType.DMA]),
        compiler_params=params(),
        cost_estimate=COST,
        name="widen",
    )(*args)


def rope_tables(length, width):
    frequency = ROPE_BASE ** (-2.0 * np.arange(width // 2) / width)
    angles = np.arange(length)[:, None] * frequency[None, :]
    cos, sin = np.cos(angles), np.sin(angles)
    tables = np.concatenate([cos, cos], axis=1), np.concatenate([-sin, sin], axis=1)
    return tuple(jnp.asarray(t.astype(np.float32)) for t in tables)


class Chain:
    def __init__(self):
        self.last = None

    def mark(self, value):
        self.last = value

    def __call__(self, *values):
        if self.last is None:
            return values
        return lax.optimization_barrier((*values, self.last))[:-1]


class ZSum:
    def __init__(self, part, dim, shard, planes, z_at):
        self.part, self.dim, self.shard, self.planes, self.z_at = part, dim, shard, planes, z_at
        self.at = 0
        self.came = None

    def term(self, j):
        j = jnp.clip(j, 0, self.planes - 1)
        return lax.dynamic_slice_in_dim(self.part, j * self.shard, self.shard, self.dim)

    def send(self, up, down):
        last = self.planes - 1
        self.at += 1
        up_pairs = [(2 * z + x, 2 * z + 2 + x) for z in range(last) for x in range(2) if z < self.at]
        down_pairs = [
            (2 * (last - z) + x, 2 * (last - 1 - z) + x)
            for z in range(last)
            for x in range(2)
            if z < self.at
        ]
        self.came = lax.ppermute(up, "dp", up_pairs), lax.ppermute(down, "dp", down_pairs)

    def terms(self):
        planes, z_at, at = self.planes, self.z_at, self.at
        return self.term(planes - 1 - at + z_at), self.term(at + 1 - planes + z_at)

    def start(self):
        self.send(*self.terms())

    def step(self, chain):
        if self.at >= self.planes - 1:
            return
        up, down = chain(*self.came)
        up_term, down_term = self.terms()
        up, down = up + up_term, down + down_term
        chain.mark(up)
        self.send(up, down)

    def finish(self, chain):
        if self.at == 0:
            self.start()
        while self.at < self.planes - 1:
            self.step(chain)
        up, down = chain(*self.came)
        total = self.term(self.z_at).astype(F32) + up.astype(F32) + down.astype(F32)
        chain.mark(total)
        return total


def shards(
    dp_size,
    tensor_size,
    tokens,
    norm_attn,
    w_query,
    key_weight,
    value_weight,
    query_gain,
    key_gain,
    w_out,
    norm_mlp,
    w_gate,
    w_up,
    w_down,
    out_grad,
    prefix_len,
):
    rows, model = tokens.shape
    width = query_gain.shape[0]
    kv_heads = key_weight.shape[1] // width
    repeat = w_query.shape[1] // key_weight.shape[1]
    dims = (kv_heads, repeat, width)
    group = dp_size // prefix_len.shape[0]
    planes = dp_size // 2
    group_planes = group // 2
    half = rows // 2
    shard = model // dp_size
    assert tensor_size == 4 and MAX_PREFIX <= 4 * rows

    device = lax.axis_index("dp")
    x_at = device % 2
    z_at = device // 2
    sequence = device // group
    member = device % group
    plane = member // 2
    prefix = jnp.sum(jnp.where(jnp.arange(prefix_len.shape[0]) == sequence, prefix_len, 0))

    x_pairs = [(d, d ^ 1) for d in range(dp_size)]

    def x_swap(value):
        return lax.ppermute(value, "dp", x_pairs)

    cos, sin = rope_tables(group * rows, width)
    norm_attn_row = norm_attn[None, :]
    norm_mlp_row = norm_mlp[None, :]
    q_gain_row = query_gain[None, :]
    k_gain_row = key_gain[None, :]

    prefix_at = prefix[None].astype(jnp.int32)
    heads_b, lse, kv_all, h_one, q, q_raw, k_raw = attn_fwd(
        prefix_at,
        tokens,
        norm_attn_row,
        w_query,
        key_weight,
        value_weight,
        q_gain_row,
        k_gain_row,
        cos,
        sin,
        group,
        dims,
    )
    fused = planes == group_planes and shard % 128 == 0
    pieces = 3
    middle, h_two, d_hidden, og_keep, og_came, heads_came = attention_out(
        heads_b, w_out, tokens, norm_mlp_row, out_grad, w_down, planes, shard
    )
    outs = middle_of(
        w_gate,
        w_up,
        h_two,
        d_hidden,
        middle,
        out_grad,
        norm_mlp_row,
        w_out,
        q,
        heads_b,
        lse,
        [og_keep, og_came] if fused else None,
        pieces,
        planes,
        shard,
        width,
    )
    hidden, d_gate, d_up, hidden_came, d_attn, norm_mlp_part, qx, dox, h_two_keep, h_two_came = outs[:10]

    grads = None
    if fused:
        grads = [hidden_came, og_keep, og_came, d_gate, h_two_keep, h_two_came]
        grads += [heads_b, heads_came]
        w_down_parts = outs[10:]
    shared = [d_attn, d_up, hidden, w_down, middle]
    outs = back(prefix_at, qx, dox, kv_all, shared, grads, group, planes, shard, pieces, dims)
    dq, kv_grad, up_came, block_out = outs[:4]
    chain = Chain()
    chain.mark(dq)
    if fused:
        w_down_parts = [*w_down_parts, outs[4]]
        w_gate_grad, w_out_grad = outs[5:]
    else:
        d_attn_keep, d_attn_came = outs[4:]
        down_part = (dot(hidden, og_keep, TN) + dot(hidden_came, og_came, TN)).astype(BF16)
        w_down_grad = ZSum(down_part, 1, shard, planes, z_at).finish(chain)
        gate_part = dot(h_two_keep, d_gate, TN) + dot(h_two_came, x_swap(d_gate), TN)
        w_gate_grad = ZSum(gate_part.astype(BF16), 0, shard, planes, z_at).finish(chain)
        out_part = dot(heads_b, d_attn_keep, TN) + dot(heads_came, d_attn_came, TN)
        w_out_grad = ZSum(out_part.astype(BF16), 1, shard, planes, z_at).finish(chain)

    up_grads = [h_two_keep, h_two_came, d_up, up_came] if fused else None
    outs = front(
        *chain(dq),
        kv_grad,
        q_raw,
        k_raw,
        q_gain_row,
        k_gain_row,
        cos,
        sin,
        h_one,
        (w_query, key_weight, value_weight),
        tokens,
        d_attn,
        norm_attn_row,
        norm_mlp_part,
        up_grads,
        dp_size,
        group,
        shard,
    )
    tokens_grad, gains = outs[:2]
    if fused:
        w_up_grad, w_query_grad, w_kv_grad = outs[2:]
    else:
        dq_b, dq_came, dkv_b, dkv_came, h_one_keep, h_one_came = outs[2:]
        chain.mark(tokens_grad)

        def by_rows(left, left_came, right, right_came):
            part = dot(left, right, TN) + dot(left_came, right_came, TN)
            return ZSum(part.astype(BF16), 0, shard, planes, z_at).finish(chain)

        w_up_grad = by_rows(h_two_keep, h_two_came, d_up, up_came)
        w_query_grad = by_rows(h_one_keep, h_one_came, dq_b, dq_came)
        w_kv_grad = by_rows(h_one_keep, h_one_came, dkv_b, dkv_came)
    kv_width = kv_heads * width
    if fused:
        arrays = [w_gate_grad, w_out_grad, *w_down_parts, w_up_grad, w_query_grad, w_kv_grad, tokens_grad]
        n = 2 + len(w_down_parts)
        results = [[(0, 0)], [(1, 0)], [(i, 0) for i in range(2, n)]]
        results += [[(n, 0)], [(n + 1, 0)], [(n + 2, 0)], [(n + 2, kv_width)], [(n + 3, 0)]]
        units = w_gate.shape[1]
        columns = w_query.shape[1]
        shapes = [(shard, units), (columns, shard), (units, shard), (shard, units), (shard, columns)]
        shapes += [(shard, kv_width)] * 2 + [(rows, model)]
        outs = widen(block_out, arrays, results, shapes, gains, shard, width)
        block_out, w_gate_grad, w_out_grad, w_down_grad, w_up_grad, w_query_grad = outs[:6]
        w_key_grad, w_value_grad, tokens_grad = outs[6:9]
        norm_attn_grad, norm_mlp_grad, query_gain_grad, key_gain_grad = (v[0] for v in outs[9:])
    else:
        w_key_grad, w_value_grad = w_kv_grad[:, :kv_width], w_kv_grad[:, kv_width:]
        tokens_grad = tokens_grad.astype(F32)
        gains = gains[-1, 0]
        norm_attn_grad = lax.dynamic_slice_in_dim(gains, device * shard, shard, 0)
        norm_mlp_grad = lax.dynamic_slice_in_dim(gains, model + device * shard, shard, 0)
        query_gain_grad, key_gain_grad = gains[2 * model : 2 * model + width], gains[2 * model + width :]
    return (
        block_out,
        tokens_grad,
        norm_attn_grad,
        w_query_grad,
        w_key_grad,
        w_value_grad,
        query_gain_grad,
        key_gain_grad,
        w_out_grad,
        norm_mlp_grad,
        w_gate_grad,
        w_up_grad,
        w_down_grad,
    )


def solution(mesh):
    placed = (
        P("dp", None),
        P(),
        P(None, "tensor"),
        P(None, "tensor"),
        P(None, "tensor"),
        P(),
        P(),
        P("tensor", None),
        P(),
        P(None, "tensor"),
        P(None, "tensor"),
        P("tensor", None),
        P("dp", None),
        P(),
    )
    return jax.shard_map(
        functools.partial(shards, mesh.shape["dp"], mesh.shape["tensor"]),
        mesh=mesh,
        in_specs=placed,
        out_specs=(
            P("dp", None),
            P("dp", None),
            P("dp"),
            P("dp", "tensor"),
            P("dp", "tensor"),
            P("dp", "tensor"),
            P(),
            P(),
            P("tensor", "dp"),
            P("dp"),
            P("dp", "tensor"),
            P("dp", "tensor"),
            P("tensor", "dp"),
        ),
        check_vma=False,
    )
```

```python
import functools
import math

import jax
import jax.numpy as jnp
import numpy as np
from jax import lax
from jax.experimental import pallas as pl
from jax.experimental.pallas import tpu as pltpu
from jax.sharding import PartitionSpec as P

F32 = jnp.float32
BF16 = jnp.bfloat16
EPS = 1e-06
ROPE_BASE = 1000000.0
MAX_PREFIX = 2048
VMEM_LIMIT = 56 * 2**20
BACK_VMEM_LIMIT = 60 * 2**20

COST = pl.CostEstimate(flops=1000, bytes_accessed=1000, transcendentals=0)

NN = (((1,), (0,)), ((), ()))
NT = (((1,), (1,)), ((), ()))
TN = (((0,), (0,)), ((), ()))


def dot(left, right, dims=NN):
    return lax.dot_general(left, right, dims, preferred_element_type=F32)


def vmem(count):
    return [pl.BlockSpec(memory_space=pltpu.VMEM)] * count


def params():
    return pltpu.CompilerParams(vmem_limit_bytes=VMEM_LIMIT)


def greet(peers):
    barrier = pltpu.get_barrier_semaphore()
    count = 0
    for peer, there in peers:

        def signal(peer=peer):
            pl.semaphore_signal(barrier, 1, device_id=peer, device_id_type=pl.DeviceIdType.MESH)

        if there is True:
            signal()
            count = count + 1
        else:
            pl.when(there)(signal)
            count = count + there.astype(jnp.int32)
    pl.semaphore_wait(barrier, count)


def remote(src, dst, send, recv, peer):
    return pltpu.make_async_remote_copy(
        src_ref=src,
        dst_ref=dst,
        send_sem=send,
        recv_sem=recv,
        device_id=peer,
        device_id_type=pl.DeviceIdType.MESH,
    )


class Staged:
    def __init__(self, arrays, buffers, sems, out=False):
        self.copies = []
        for i, (array, buffer) in enumerate(zip(arrays, buffers)):
            ends = (buffer, array) if out else (array, buffer)
            self.copies.append((buffer, pltpu.make_async_copy(*ends, sems.at[i])))

    @staticmethod
    def scratch(shapes):
        return [pltpu.VMEM(s.shape, s.dtype) for s in shapes] + [pltpu.SemaphoreType.DMA((len(shapes),))]

    def start(self, *buffers):
        for buffer, copy in self.copies:
            if not buffers or any(buffer is b for b in buffers):
                copy.start()

    def wait(self, *buffers):
        for buffer, copy in self.copies:
            if not buffers or any(buffer is b for b in buffers):
                copy.wait()


ANYWHERE = pl.BlockSpec(memory_space=pl.ANY)


def table_rows(tables, member, rows):
    at = pl.ds(pl.multiple_of(member * rows, rows), rows)
    return [t.at[at, :] for t in tables]


def tensor_peers():
    t = lax.axis_index("tensor")
    core = t % 2
    y = t // 2
    return core, {"tensor": t + 1 - 2 * core}, {"tensor": t + 2 - 4 * y}


def rows_of(core, half):
    return pl.ds(pl.multiple_of(core * half, half), half)


def cut_into(out, out_rows, ref, ref_rows, side, planes, shard):
    for z in range(planes):
        to = slice(z * shard, (z + 1) * shard)
        if shard % 128 == 0:
            at = pl.ds(pl.multiple_of((2 * z + side) * shard, shard), shard)
            out[out_rows, to] = ref[ref_rows, at]
        else:
            low = ref[ref_rows, 2 * z * shard : (2 * z + 1) * shard]
            high = ref[ref_rows, (2 * z + 1) * shard : (2 * z + 2) * shard]
            out[out_rows, to] = jnp.where(side == 0, low, high)


class Columns:
    def __init__(self, whole, keep, came, scratch, x_at, core, x_peer, core_peer, planes, shard):
        self.whole, self.keep, self.came = whole, keep, came
        self.send_ref, self.recv_ref, self.sems = scratch[0], scratch[1], scratch[2:]
        self.x_at, self.core, self.cut = x_at, core, (planes, shard)
        self.x_peer, self.core_peer = x_peer, core_peer
        self.half = whole.shape[0] // 2

    @staticmethod
    def scratch(half, columns):
        return [pltpu.VMEM((half, columns), BF16)] * 2 + [pltpu.SemaphoreType.DMA] * 4

    def over_x(self):
        return remote(self.send_ref, self.recv_ref, self.sems[0], self.sems[1], self.x_peer)

    def over_core(self):
        there = self.came.at[rows_of(self.core, self.half), :]
        return remote(self.recv_ref, there, self.sems[2], self.sems[3], self.core_peer)

    def start(self):
        mine = rows_of(self.core, self.half)
        cut_into(self.send_ref, slice(None), self.whole, mine, 1 - self.x_at, *self.cut)
        self.over_x().start()

    def store(self):
        cut_into(self.keep, slice(None), self.whole, slice(None), self.x_at, *self.cut)

    def forward(self):
        self.over_x().wait_recv()
        self.over_core().start()
        self.came[rows_of(self.core, self.half), :] = self.recv_ref[...]

    def finish(self):
        self.over_core().wait_recv()
        self.over_x().wait_send()
        self.over_core().wait_send()


class LineSum:
    def __init__(self, scratch, device, plane, planes, paced=False):
        self.paced = paced
        self.stack, self.came = scratch[:2]
        self.sems = scratch[2:]
        self.device, self.plane, self.planes = device, plane, planes

    @staticmethod
    def scratch(planes, shape):
        return [pltpu.VMEM((n,) + shape, BF16) for n in (planes, planes + 1)] + [
            pltpu.SemaphoreType.DMA((planes,))
        ] * 4

    def up(self, j):
        s = self.sems
        peer = {"dp": self.device + 2}
        return remote(self.stack.at[j], self.came.at[j], s[0].at[j], s[1].at[j], peer)

    def down(self, j):
        s = self.sems
        slot = jnp.where(self.plane - 1 == j, self.planes, j)
        peer = {"dp": self.device - 2}
        return remote(self.stack.at[j], self.came.at[slot], s[2].at[j], s[3].at[j], peer)

    def start(self):
        last = self.planes - 1

        @pl.when(self.plane == 0)
        def _():
            for j in range(last, last - 1 if self.paced else 0, -1):
                self.up(j).start()

        @pl.when(self.plane == last)
        def _():
            for j in range(1 if self.paced else last):
                self.down(j).start()

    def advance(self, step):
        plane, last = self.plane, self.planes - 1
        low, high = last - step + plane, step - last + plane
        if self.paced:

            @pl.when(plane == 0)
            def _():
                self.up(last - step + 1).wait_send()
                self.up(last - step).start()

            @pl.when(plane == last)
            def _():
                self.down(step - 1).wait_send()
                self.down(step).start()

        @pl.when((plane >= 1) & (plane <= step))
        def _():
            self.up(low).wait_recv()
            self.stack[low] += self.came[low]
            self.up(low).start()

        @pl.when((plane < last) & (plane >= last - step))
        def _():
            self.down(high).wait_recv()
            self.stack[high] += self.came[high]
            self.down(high).start()

    def finish(self, out):
        plane, planes = self.plane, self.planes

        @pl.when(plane == 0)
        def _():
            self.down(plane).wait_recv()
            out[...] = self.stack[plane] + self.came[planes]

        @pl.when(plane == planes - 1)
        def _():
            self.up(plane).wait_recv()
            out[...] = self.stack[plane] + self.came[plane]

        @pl.when((plane > 0) & (plane < planes - 1))
        def _():
            self.up(plane).wait_recv()
            self.down(plane).wait_recv()
            total = self.stack[plane].astype(F32) + self.came[plane].astype(F32)
            out[...] = (total + self.came[planes].astype(F32)).astype(BF16)

        for j in range(planes):
            ups, downs = plane < j, plane > j
            if self.paced and j > 1:
                ups = ups & (plane > 0)
            if self.paced and j < planes - 2:
                downs = downs & (plane < planes - 1)
            pl.when(ups)(lambda j=j: self.up(j).wait_send())
            pl.when(downs)(lambda j=j: self.down(j).wait_send())

    def fill_rows(self, left, left_came, right, right_came):
        shard, planes = self.stack.shape[1], self.planes

        def compute(i):
            j = jnp.where(self.plane * 2 < planes, planes - 1 - i, i) if self.paced else i
            at = pl.ds(pl.multiple_of(j * shard, shard), shard)
            self.stack[j] = (
                dot(left[:, at], right[...], TN) + dot(left_came[:, at], right_came[...], TN)
            ).astype(BF16)

        if self.paced:
            compute(0)
            self.start()

        def body(i, carry):
            compute(i)
            return carry

        lax.fori_loop(1 if self.paced else 0, planes, body, 0)

    def fill_columns(self, left, left_came, right, right_came):
        shard = self.stack.shape[2]
        tile = 256

        def body(t, carry):
            at = pl.ds(pl.multiple_of(t * tile, tile), tile)
            term = dot(left[:, at], right[...], TN) + dot(left_came[:, at], right_came[...], TN)
            for j in range(self.planes):
                self.stack[j, at, :] = term[:, j * shard : (j + 1) * shard].astype(BF16)
            return carry

        lax.fori_loop(0, left.shape[1] // tile, body, 0)


class TensorSum:
    def __init__(self, scratch, mine, core, core_peer, y_peer):
        self.away, self.core_came, self.both, self.y_came = scratch[:4]
        self.sems = scratch[4:]
        self.mine = mine
        self.core, self.core_peer, self.y_peer = core, core_peer, y_peer
        self.chunks, self.half, self.width = self.away.shape

    @staticmethod
    def scratch(chunks, half, width):
        return [pltpu.VMEM((chunks, half, width), BF16)] * 4 + [
            pltpu.SemaphoreType.DMA((chunks,))
        ] * 4

    def over_core(self, i):
        s = self.sems
        return remote(self.away.at[i], self.core_came.at[i], s[0].at[i], s[1].at[i], self.core_peer)

    def over_y(self, i):
        s = self.sems
        return remote(self.both.at[i], self.y_came.at[i], s[2].at[i], s[3].at[i], self.y_peer)

    def add(self, i, value):
        self.mine[i % 2] = value
        self.away[i] = self.mine[i % 2, rows_of(1 - self.core, self.half), :].astype(BF16)
        self.over_core(i).start()
        if i > 0:
            self.pass_on(i - 1)
        if i == self.chunks - 1:
            self.pass_on(i)

    def pass_on(self, i):
        self.over_core(i).wait_recv()
        mine = self.mine[i % 2, rows_of(self.core, self.half), :]
        self.both[i] = (mine + self.core_came[i].astype(F32)).astype(BF16)
        self.over_y(i).start()

    def total(self, i):
        self.over_y(i).wait_recv()
        return self.both[i].astype(F32) + self.y_came[i].astype(F32)

    def finish(self):
        for i in range(self.chunks):
            self.over_core(i).wait_send()
            self.over_y(i).wait_send()


def roll_half(value):
    return pltpu.roll(value, value.shape[-1] // 2, 1)


def visible(shape, key0, row0, prefix):
    key_pos = key0 + lax.broadcasted_iota(jnp.int32, shape, 1)
    row_pos = row0 + lax.broadcasted_iota(jnp.int32, shape, 0)
    return (key_pos <= row_pos) | (key_pos < prefix)


def attn_fwd_kernel(*refs, group, kv_heads, repeat, width, tile, coef):
    refs = list(refs)

    def take(count):
        out = refs[:count]
        del refs[:count]
        return out

    prefix_ref, gain_ref, q_gain, k_gain = take(4)
    arrays = take(6)
    member = lax.axis_index("dp") % group
    arrays[3:5] = table_rows(arrays[3:5], member, arrays[0].shape[0])
    o_ref, lse_ref, all_out = take(3)
    outs = take(4)
    buffers = take(6)
    inputs = Staged(arrays, buffers, *take(1))
    x_ref, w_k, w_v, cos_ref, sin_ref, w_q = buffers
    out_buffers = take(4)
    h_ref, q_ref, q_raw, k_raw = out_buffers
    outputs = Staged(outs, out_buffers, *take(1), out=True)
    kv_ref, all_ref, all_sems, acc, send_x, recv_x, send_z, recv_z = take(8)
    send_down, send_rest, recv_rest = take(3)
    rows = q_ref.shape[0]
    kv_width = kv_heads * width
    planes = group // 2
    device = lax.axis_index("dp")
    member = device % group
    plane = member // 2
    x_at = member % 2
    x_other = device + 1 - 2 * x_at
    inner = plane < planes - 1
    prefix = prefix_ref[0]
    inputs.start()
    greet([({"dp": x_other}, True), ({"dp": device + 2}, inner), ({"dp": device - 2}, plane > 0)])

    def store(slot):
        return pltpu.make_async_copy(all_ref.at[slot], all_out.at[slot], all_sems.at[slot])

    def source(slot):
        return kv_ref if slot == 0 else all_ref.at[2 * slot]

    split = planes - 1 if planes > 2 else planes
    half = rows // 2
    parts = [pl.ds(0, half), pl.ds(half, rows - half)]

    def halves_over_x(slot):
        return range(1 if slot == split else 2)

    def to_x(slot, h):
        at = parts[h]
        to = all_ref.at[2 * slot + 1, at, :]
        i = 2 * slot + h
        return remote(source(slot).at[at, :], to, send_x.at[i], recv_x.at[i], {"dp": x_other})

    def to_z(slot, h):
        at = parts[h]
        to = all_ref.at[2 * slot, at, :]
        i = 2 * slot + h
        return remote(source(slot - 1).at[at, :], to, send_z.at[i], recv_z.at[i], {"dp": device + 2})

    def rest_to_z():
        return remote(
            all_ref.at[2 * split - 1, parts[1], :],
            all_ref.at[2 * split + 1, parts[1], :],
            send_rest,
            recv_rest,
            {"dp": device + 2},
        )

    def to_first(h):
        at = parts[h]
        to = all_ref.at[2, at, :]
        return remote(kv_ref.at[at, :], to, send_down.at[h], recv_z.at[2 + h], {"dp": device - 2})

    inputs.wait(x_ref, w_k, w_v, cos_ref, sin_ref)
    x = x_ref[...].astype(F32)
    r = lax.rsqrt(jnp.mean(x * x, axis=1, keepdims=True) + EPS)
    h_ref[...] = (x * r * gain_ref[...]).astype(BF16)
    cos, sin = cos_ref[...], sin_ref[...]

    def rotate(u, gain):
        u = u * lax.rsqrt(jnp.mean(u * u, axis=1, keepdims=True) + EPS) * gain[...]
        return (u * cos + roll_half(u) * sin).astype(BF16)

    keys = dot(h_ref[...], w_k[...])
    k_raw[...] = keys
    for at in range(0, kv_width, width):
        kv_ref[:, at : at + width] = rotate(keys[:, at : at + width], k_gain)
    kv_ref[:, kv_width:] = dot(h_ref[...], w_v[...]).astype(BF16)
    ones = jnp.ones((rows, width), BF16)
    row0 = member * rows

    def work(block, other, masked, start=False):
        key0 = other * rows

        def head_pair(h, carry):
            k = block[:, pl.ds(pl.multiple_of(h * width, width), width)]
            v = block[:, pl.ds(pl.multiple_of(kv_width + h * width, width), width)]
            v = jnp.concatenate([v, ones], axis=1)
            for g in range(repeat):
                head = h * repeat + g
                for at in range(0, rows, tile):
                    q = q_ref[at : at + tile, pl.ds(pl.multiple_of(head * width, width), width)]
                    p = jnp.exp2(dot(q, k, NT) * coef)
                    if masked:
                        p = jnp.where(visible(p.shape, key0, row0 + at, prefix), p, 0.0)
                    term = dot(p.astype(BF16), v)
                    if start:
                        acc[head, at : at + tile, :] = term
                    else:
                        acc[head, at : at + tile, :] += term
            return carry

        lax.fori_loop(0, kv_heads, head_pair, 0)

    for h in range(2):
        to_x(0, h).start()
        if planes > 1:
            pl.when(inner)(lambda h=h: to_z(1, h).start())
            pl.when(plane == 1)(lambda h=h: to_first(h).start())

    inputs.wait(w_q)
    queries = dot(h_ref[...], w_q[...])
    q_raw[...] = queries
    for at in range(0, queries.shape[1], width):
        q_ref[:, at : at + width] = rotate(queries[:, at : at + width], q_gain)
    outputs.start()
    all_ref[0] = kv_ref[...]
    store(0).start()
    work(kv_ref, member, True, True)

    def receive(slot):
        for h in range(2):
            to_z(slot, h).wait_recv()
            if slot < planes - 1:
                pl.when(inner & (plane >= slot))(lambda h=h: to_z(slot + 1, h).start())
            if h in halves_over_x(slot):
                to_x(slot, h).start()
        store(2 * slot).start()

    def attend(slot, index, there, first):
        if slot == 1:
            pl.when(plane == 0)(lambda: work(all_ref.at[index], first, True))
            pl.when(plane > 0)(lambda: work(all_ref.at[index], there, False))
        else:
            work(all_ref.at[index], there, slot == 0)

    def far(slot):
        for h in halves_over_x(slot):
            to_x(slot, h).wait_recv()
        if slot == split - 1:
            pl.when(plane == split - 1)(lambda: rest_to_z().start())
        if slot == split:
            rest_to_z().wait_recv()
        store(2 * slot + 1).start()
        attend(slot, 2 * slot + 1, 2 * (plane - slot) + 1 - x_at, 3 - x_at)

    if planes > 1:
        receive(1)
    far(0)
    for slot in range(1, planes):

        def step(slot=slot):
            attend(slot, 2 * slot, 2 * (plane - slot) + x_at, 2 + x_at)
            if slot + 1 < planes:
                pl.when(plane >= slot + 1)(lambda: receive(slot + 1))
            far(slot)

        if slot == 1:
            step()
        else:
            pl.when(plane >= slot)(step)

    for head in range(kv_heads * repeat):
        total = acc[head, :, width:]
        o_ref[:, head * width : (head + 1) * width] = (acc[head, :, :width] / total).astype(BF16)
        lse_ref[:, head * width : (head + 1) * width] = jnp.log2(total) * (1.0 / coef)

    outputs.wait()
    if split < planes:
        pl.when(plane == split - 1)(lambda: rest_to_z().wait_send())
    for slot in range(planes):

        @pl.when((plane >= slot) | (slot <= 1))
        def _(slot=slot):
            store(2 * slot).wait()
            store(2 * slot + 1).wait()
            for h in halves_over_x(slot):
                to_x(slot, h).wait_send()

    for slot in range(1, planes):

        @pl.when(inner & (plane >= slot - 1))
        def _(slot=slot):
            for h in range(2):
                to_z(slot, h).wait_send()

    if planes > 1:

        @pl.when(plane == 1)
        def _():
            for h in range(2):
                to_first(h).wait_send()


def attn_fwd(prefix, x, gain, w_query, key_weight, value_weight, q_gain, k_gain, cos, sin, group, dims):
    kv_heads, repeat, width = dims
    rows = x.shape[0]
    heads = kv_heads * repeat
    columns = heads * width
    planes = group // 2
    dma = pltpu.SemaphoreType.DMA
    block = (rows, 2 * kv_heads * width)
    staged = [x, key_weight, value_weight, cos, sin, w_query]
    table = jax.ShapeDtypeStruct((rows, width), F32)
    early = [
        jax.ShapeDtypeStruct(x.shape, BF16),
        jax.ShapeDtypeStruct((rows, columns), BF16),
        jax.ShapeDtypeStruct((rows, columns), F32),
        jax.ShapeDtypeStruct((rows, kv_heads * width), F32),
    ]
    return pl.pallas_call(
        functools.partial(
            attn_fwd_kernel,
            group=group,
            kv_heads=kv_heads,
            repeat=repeat,
            width=width,
            tile=min(rows, 256),
            coef=math.log2(math.e) / math.sqrt(width),
        ),
        out_shape=[
            jax.ShapeDtypeStruct((rows, columns), BF16),
            jax.ShapeDtypeStruct((rows, columns), F32),
            jax.ShapeDtypeStruct((group,) + block, BF16),
        ]
        + early,
        in_specs=[smem()] + vmem(3) + [ANYWHERE] * 6,
        out_specs=vmem(2) + [ANYWHERE] * 5,
        scratch_shapes=Staged.scratch([x, key_weight, value_weight, table, table, w_query])
        + Staged.scratch(early)
        + [pltpu.VMEM(block, BF16), pltpu.VMEM((group,) + block, BF16), dma((group,))]
        + [pltpu.VMEM((heads, rows, 2 * width), F32)]
        + [dma((2 * planes,))] * 4
        + [dma((2,)), dma, dma],
        compiler_params=pltpu.CompilerParams(
            vmem_limit_bytes=VMEM_LIMIT, collective_id=0, has_side_effects=True
        ),
        cost_estimate=COST,
        name="attn_fwd",
    )(prefix, gain, q_gain, k_gain, *staged)


def split_three(value):
    high = value.astype(BF16)
    left = value - high.astype(F32)
    mid = left.astype(BF16)
    return high.astype(F32), mid.astype(F32), (left - mid.astype(F32)).astype(BF16).astype(F32)


def back_kernel(
    *refs, group, planes, all_planes, shard, kv_heads, repeat, width, coef, scale, sums
):
    refs = list(refs)

    def take(count):
        out = refs[:count]
        del refs[:count]
        return out

    device = lax.axis_index("dp")
    member = device % group
    plane = member // 2
    last = planes - 1
    prefix_ref, up_ref, w_down_in, middle_in = take(4)
    if sums:
        hid_arrays = take(1)
    count = 12 if sums else 5
    arrays = take(count)
    dq_ref, grad_ref, up_came_ref, block_ref = take(4)
    if sums:
        w_down_ref, w_gate_ref, w_out_ref = take(3)
    a_ref, a_came_ref = take(2)
    if sums:
        hid_buffers = take(1)
        hid_sems = take(1)[0]
    buffers = take(count)
    inputs = Staged(arrays, buffers, *take(1))
    a_all_ref, qx_ref, dox_ref, kv_ref, hid_ref = buffers[:5]
    if sums:
        hid_came_ref = hid_buffers[0]
        og_ref, og_came_ref, gate_ref, h_ref, h_came_ref, heads_ref, heads_came_ref = buffers[5:]
    down_buf, down_sems, mine_ref, middle_buf, middle_sems = take(5)
    block_sems = take(3)
    total_scratch = take(8)
    own_ref, far_ref, xr_ref, zr_ref, first_ref = take(5)
    send_x, recv_x, send_z, recv_z, send_first, recv_first = take(6)
    swap_sems = take(2)
    a_scratch = take(6)
    rows = qx_ref.shape[1]
    kv_width = kv_heads * width
    if sums:
        gate_came_ref, send_gate, recv_gate = take(3)
        left = w_down_ref.shape[0]
        rest = pl.ds(hid_arrays[0].shape[1] - left, left)
        hid_inputs = Staged([h.at[:, rest] for h in hid_arrays], hid_buffers, hid_sems)
        down_sum, out_sum = (LineSum(take(6), device, plane, planes) for _ in range(2))
        piece = gate_came_ref.shape[2]
        pieces = gate_ref.shape[1] // piece
        gate_sums = [LineSum(take(6), device, plane, planes) for _ in range(pieces)]
    x_at = member % 2
    x_other = device + 1 - 2 * x_at
    inner = plane < last
    prefix = prefix_ref[0]

    core, core_peer, y_peer = tensor_peers()
    x_peer = {"dp": x_other}
    total = TensorSum(total_scratch, mine_ref, core, core_peer, y_peer)
    half = total.half
    parts, narrow = total.chunks, total.width

    def load(i):
        at = pl.ds(i * narrow, narrow)
        return pltpu.make_async_copy(w_down_in.at[:, at], down_buf.at[i % 2], down_sems.at[i % 2])

    def middle_load(i):
        at = pl.ds(i * narrow, narrow)
        return pltpu.make_async_copy(middle_in.at[:, at], middle_buf.at[i % 2], middle_sems.at[i % 2])

    def block_at(i):
        return block_ref.at[rows_of(core, half), pl.ds(i * narrow, narrow)]

    def block_store(i):
        return pltpu.make_async_copy(total.both.at[i], block_at(i), block_sems[0].at[i])

    def block_give(i):
        return remote(total.both.at[i], block_at(i), block_sems[1].at[i], block_sems[2].at[i], core_peer)

    def block_add(i):
        load(i).wait()
        total.add(i, dot(hid_ref[...], down_buf[i % 2]))
        if i + 2 < parts:
            load(i + 2).start()

    def block_finish(i):
        middle_load(i).wait()
        value = middle_buf[i % 2] + total.total(i)
        total.over_y(i).wait_send()
        total.both[i] = value.astype(BF16)
        if i + 2 < parts:
            middle_load(i + 2).start()
        block_store(i).start()
        block_give(i).start()

    inputs.start(a_all_ref)
    if sums:
        hid_inputs.start()
        inputs.start(hid_ref, *buffers[5:7])
    inputs.start(*buffers[1:4])
    if sums:
        inputs.start(*buffers[7:])
    else:
        inputs.start(hid_ref)
    for i in range(2):
        load(i).start()
        middle_load(i).start()
    greet(
        [
            (x_peer, True),
            (core_peer, True),
            (y_peer, True),
            ({"dp": device + 2}, inner),
            ({"dp": device - 2}, plane > 0),
        ]
    )

    def copy(src, dst, send, recv, there):
        return remote(src, dst, send, recv, {"dp": there})

    place = (x_at, core, x_peer, core_peer, all_planes, shard)
    d_attn = Columns(a_all_ref, a_ref, a_came_ref, a_scratch, *place)
    up_swap = copy(up_ref, up_came_ref, swap_sems[0], swap_sems[1], x_other)

    def gate_swap(k):
        part = gate_ref.at[:, pl.ds(k * piece, piece)]
        return copy(part, gate_came_ref.at[k], send_gate.at[k], recv_gate.at[k], x_other)

    def gate_start(k):
        gate_swap(k).wait_recv()
        part = gate_ref.at[:, pl.ds(k * piece, piece)]
        gate_sums[k].fill_rows(h_ref, h_came_ref, part, gate_came_ref.at[k])
        gate_sums[k].start()

    lane = lax.broadcasted_iota(jnp.int32, (rows, width), 1)
    minus = jnp.where(lane < 3, -1.0, 0.0).astype(BF16)
    row0 = member * rows

    def work(block, other, masked, out):
        key0 = other * rows

        def head_group(h, carry):
            k_at = pl.ds(pl.multiple_of(h * width, width), width)
            v_at = pl.ds(pl.multiple_of(kv_width + h * width, width), width)
            k = kv_ref[block, :, k_at]
            v = kv_ref[block, :, v_at]
            kx = jnp.concatenate([k, minus], axis=1)
            vx = jnp.concatenate([v, minus], axis=1)
            dk = jnp.zeros((rows, width), F32)
            dv = jnp.zeros((rows, width), F32)
            for g in range(repeat):
                head = h * repeat + g
                qx = qx_ref[head]
                dox = dox_ref[head]
                p = jnp.exp2(dot(qx, kx, NT) * coef)
                if masked:
                    p = jnp.where(visible(p.shape, key0, row0, prefix), p, 0.0)
                ds = (p * dot(dox, vx, NT)).astype(BF16)
                dv += dot(p.astype(BF16), dox[:, :width], TN)
                dk += dot(ds, qx[:, :width], TN)
                dq_ref[:, pl.ds(pl.multiple_of(head * width, width), width)] += dot(ds, k)
            out[:, k_at] = (dk * scale).astype(BF16)
            out[:, v_at] = dv.astype(BF16)
            return carry

        lax.fori_loop(0, kv_heads, head_group, 0)

    def far_swap(slot):
        return copy(far_ref.at[slot], xr_ref.at[slot], send_x.at[slot], recv_x.at[slot], x_other)

    def to_plane(slot):
        return copy(own_ref.at[slot], zr_ref.at[slot], send_z.at[slot], recv_z.at[slot], device - 2)

    def from_first():
        return copy(own_ref.at[1], first_ref, send_first, recv_first, device + 2)

    def attend(slot):
        there = 2 * (plane - slot)
        far, own = there + 1 - x_at, there + x_at

        def both(far, own, masked):
            work(2 * slot + 1, far, masked, far_ref.at[slot])
            far_swap(slot).start()
            work(2 * slot, own, masked, own_ref.at[slot])

        if slot == 0:
            both(far, own, True)
        elif slot == 1:
            pl.when(plane == 0)(lambda: both(3 - x_at, 2 + x_at, True))
            pl.when(plane > 0)(lambda: both(far, own, False))
        else:
            pl.when(plane >= slot)(lambda: both(far, own, False))

    def pass_back(slot):
        def go():
            far_swap(slot).wait_recv()
            own_ref[slot] += xr_ref[slot]
            if slot < last:

                @pl.when(inner & (plane >= slot))
                def _():
                    to_plane(slot + 1).wait_recv()
                    own_ref[slot] += zr_ref[slot + 1]

            if slot == 1:
                pl.when(plane == 0)(lambda: from_first().start())
                pl.when(plane > 0)(lambda: to_plane(slot).start())
            else:
                to_plane(slot).start()

        if slot == 1:
            go()
        else:
            pl.when(plane >= slot)(go)

    dq_ref[...] = jnp.zeros_like(dq_ref)
    inputs.wait(a_all_ref)
    d_attn.start()
    inputs.wait(hid_ref)
    if sums:
        hid_inputs.wait()
        inputs.wait(og_ref, og_came_ref)
        down_sum.fill_columns(hid_ref.at[:, rest], hid_came_ref, og_ref, og_came_ref)
        down_sum.start()
    inputs.wait(*buffers[1:4])
    attend(last)
    d_attn.forward()
    if sums:
        inputs.wait(*buffers[7:])
        gate_swap(0).start()
    d_attn.store()
    pending = list(range(last, 0, -1))
    steps = range(1, last)
    adds = list(range(parts))
    share = -(-parts // last)
    for slot in range(last - 1, -1, -1):
        attend(slot)
        if slot == last - 1:
            if sums:
                d_attn.over_core().wait_recv()
                out_sum.fill_columns(heads_ref, heads_came_ref, a_ref, a_came_ref)
                out_sum.start()
                down_sum.advance(1)
                gate_start(0)
                gate_swap(1).start()
            pass_back(pending.pop(0))
        if slot == last - 2:
            if sums:
                for step in steps[1:]:
                    down_sum.advance(step)
                out_sum.advance(1)
                gate_start(1)
                gate_swap(2).start()
                gate_sums[0].advance(1)
            pass_back(pending.pop(0))
        for i in adds[:share]:
            block_add(i)
        del adds[:share]
    for i in adds:
        block_add(i)
    if sums:
        for step in steps[1:]:
            out_sum.advance(step)
            gate_sums[0].advance(step)
    while pending:
        pass_back(pending.pop(0))
    if sums:
        gate_start(2)
    up_swap.start()
    if sums:
        gate_sums[1].advance(1)
    for i in range(parts // 2):
        block_finish(i)
    if sums:
        for step in steps[1:]:
            gate_sums[1].advance(step)
        gate_sums[2].advance(1)
    for i in range(parts // 2, parts):
        block_finish(i)
    if sums:
        for step in steps[1:]:
            gate_sums[2].advance(step)
    dq_ref[...] = dq_ref[...] * scale

    far_swap(0).wait_recv()
    grad_ref[...] = own_ref[0].astype(F32) + xr_ref[0].astype(F32)
    if last > 0:

        @pl.when(inner)
        def _():
            to_plane(1).wait_recv()
            grad_ref[...] += zr_ref[1].astype(F32)

        @pl.when(plane == 1)
        def _():
            from_first().wait_recv()
            grad_ref[...] += first_ref[...].astype(F32)

    if sums:
        down_sum.finish(w_down_ref)
        out_sum.finish(w_out_ref)
        for k in range(pieces):
            gate_sums[k].finish(w_gate_ref.at[:, pl.ds(k * piece, piece)])
            gate_swap(k).wait_send()
    else:
        d_attn.over_core().wait_recv()
    up_swap.wait_recv()
    up_swap.wait_send()
    for i in range(parts):
        total.over_core(i).wait_send()
        block_store(i).wait()
        block_give(i).wait_recv()
        block_give(i).wait_send()
    d_attn.over_x().wait_send()
    d_attn.over_core().wait_send()
    for slot in range(planes):
        if slot <= 1:
            far_swap(slot).wait_send()
        else:
            pl.when(plane >= slot)(lambda slot=slot: far_swap(slot).wait_send())
        if slot >= 1:
            pl.when(plane >= slot)(lambda slot=slot: to_plane(slot).wait_send())
    if last > 0:
        pl.when(plane == 0)(lambda: from_first().wait_send())


def back(prefix, qx, dox, kv_all, shared, grads, group, all_planes, shard, pieces, dims):
    kv_heads, repeat, width = dims
    rows = qx.shape[1]
    columns = kv_heads * repeat * width
    planes = group // 2
    block = kv_all.shape[1:]
    dma = pltpu.SemaphoreType.DMA
    d_attn, d_up, hidden, w_down, middle = shared
    half, model = middle.shape
    parts = 8
    narrow = model // parts
    units = d_up.shape[1]
    cut_shape = jax.ShapeDtypeStruct((rows, all_planes * shard), BF16)
    out_shape = [jax.ShapeDtypeStruct((rows, columns), F32), jax.ShapeDtypeStruct(block, F32)]
    out_shape += [jax.ShapeDtypeStruct(d_up.shape, BF16), jax.ShapeDtypeStruct((rows, model), BF16)]
    scratch = [pltpu.VMEM((planes,) + block, BF16)] * 4 + [pltpu.VMEM(block, BF16)]
    scratch += [dma((planes,))] * 4 + [dma, dma] + [dma] * 2
    scratch += Columns.scratch(rows // 2, all_planes * shard)
    staged = [d_attn, qx, dox, kv_all, hidden]
    args = [prefix, d_up, w_down, middle]
    first = []
    if grads is not None:
        args += grads[:1]
        staged += grads[1:]
        first = [pltpu.VMEM(cut_shape.shape, BF16)] * 2
        first += [pltpu.VMEM((rows, units // pieces), BF16), dma((1,))]
    else:
        out_shape += [cut_shape] * 2
    args += staged
    product = [pltpu.VMEM((2, units, narrow), BF16), dma((2,)), pltpu.VMEM((2, rows, narrow), F32)]
    product += [pltpu.VMEM((2, half, narrow), F32), dma((2,))] + [dma((parts,))] * 3
    product += TensorSum.scratch(parts, half, narrow)
    scratch = first + Staged.scratch(staged) + product + scratch
    if grads is not None:
        piece = units // pieces
        shapes = (piece, shard), (shard, units), (columns, shard)
        out_shape += [jax.ShapeDtypeStruct(s, BF16) for s in shapes]
        scratch += [pltpu.VMEM((pieces, rows, piece), BF16)] + [dma((pieces,))] * 2
        for shape in [(piece, shard), (columns, shard)] + [(shard, piece)] * pieces:
            scratch += LineSum.scratch(planes, shape)
    return pl.pallas_call(
        functools.partial(
            back_kernel,
            group=group,
            planes=planes,
            all_planes=all_planes,
            shard=shard,
            kv_heads=kv_heads,
            repeat=repeat,
            width=width,
            coef=math.log2(math.e) / math.sqrt(width),
            scale=1.0 / math.sqrt(width),
            sums=grads is not None,
        ),
        out_shape=out_shape,
        in_specs=[smem()] + [ANYWHERE] * (len(args) - 1),
        out_specs=vmem(2) + [ANYWHERE] * 2 + vmem(len(out_shape) - 4),
        scratch_shapes=scratch,
        compiler_params=pltpu.CompilerParams(
            vmem_limit_bytes=BACK_VMEM_LIMIT, collective_id=1, has_side_effects=True
        ),
        cost_estimate=COST,
        name="back",
    )(*args)


def smem():
    return pl.BlockSpec(memory_space=pltpu.SMEM)


def out_kernel(*refs, planes, shard, blocks):
    refs = list(refs)

    def take(count):
        out = refs[:count]
        del refs[:count]
        return out

    arrays = take(4)
    gain_ref, w_down_ref = take(2)
    middle_ref, h_ref, d_hidden_out, og_keep, og_came, heads_came = take(6)
    buffers = take(4)
    heads_ref, w_ref, og_ref, x_ref = buffers
    inputs = Staged(arrays, buffers, *take(1))
    d_hidden_ref, d_hidden_sem = take(2)
    down_buf, down_sems, whole_ref, h_send, h_recv, heads_send, heads_recv = take(7)
    scratch = refs
    device = lax.axis_index("dp")
    core, core_peer, y_peer = tensor_peers()
    x_at = device % 2
    x_peer = {"dp": device + 1 - 2 * x_at}
    half = middle_ref.shape[0]
    total = TensorSum(scratch[:8], None, core, core_peer, y_peer)
    step = half // blocks
    place = (x_at, core, x_peer, core_peer, planes, shard)
    og = Columns(og_ref, og_keep, og_came, scratch[8:14], *place)
    tiles = down_sems.shape[0]
    tile = down_buf.shape[0] // tiles

    def load(t):
        at = pl.ds(t * tile, tile)
        return pltpu.make_async_copy(w_down_ref.at[at, :], down_buf.at[at, :], down_sems.at[t])

    inputs.start()
    for t in range(tiles):
        load(t).start()
    greet([(x_peer, True), (core_peer, True), (y_peer, True)])
    heads_swap = remote(heads_ref, heads_came, heads_send, heads_recv, x_peer)
    inputs.wait(heads_ref, w_ref)
    heads_swap.start()

    def rows_at(which, b):
        return pl.ds(pl.multiple_of(which * half + b * step, step), step)

    whole_ref[...] = dot(heads_ref[...], w_ref[...])
    for b in range(blocks):
        total.away[b] = whole_ref[rows_at(1 - core, b), :].astype(BF16)
        total.over_core(b).start()
    for b in range(blocks):
        total.over_core(b).wait_recv()
        mine = whole_ref[rows_at(core, b), :] + total.core_came[b].astype(F32)
        total.both[b] = mine.astype(BF16)
        total.over_y(b).start()
    inputs.wait(og_ref)
    og.start()
    og.store()
    for t in range(tiles):
        at = slice(t * tile, (t + 1) * tile)
        load(t).wait()
        d_hidden_ref[:, at] = dot(og_ref[...], down_buf[at, :], NT)
    d_hidden_copy = pltpu.make_async_copy(d_hidden_ref, d_hidden_out, d_hidden_sem)
    d_hidden_copy.start()
    inputs.wait(x_ref)

    def to_core(b):
        rows = h_ref.at[rows_at(core, b), :]
        return remote(rows, rows, h_send.at[b], h_recv.at[b], core_peer)

    for b in range(blocks):
        at = rows_at(core, b)
        v = x_ref[at, :].astype(F32) + total.total(b)
        middle_ref[b * step : (b + 1) * step, :] = v
        r = lax.rsqrt(jnp.mean(v * v, axis=1, keepdims=True) + EPS)
        h_ref[at, :] = (v * r * gain_ref[...]).astype(BF16)
        to_core(b).start()
    og.forward()
    og.finish()
    d_hidden_copy.wait()
    heads_swap.wait_recv()
    heads_swap.wait_send()
    for b in range(blocks):
        to_core(b).wait_recv()
        to_core(b).wait_send()
    total.finish()


def attention_out(heads, w_out, x, gain, out_grad, w_down, planes, shard):
    rows, model = x.shape
    half = rows // 2
    units = w_down.shape[0]
    blocks = 4
    tiles = units // math.gcd(units, 256)
    dma = pltpu.SemaphoreType.DMA
    cut_shape = jax.ShapeDtypeStruct((rows, planes * shard), BF16)
    return pl.pallas_call(
        functools.partial(out_kernel, planes=planes, shard=shard, blocks=blocks),
        out_shape=[
            jax.ShapeDtypeStruct((half, model), F32),
            jax.ShapeDtypeStruct((rows, model), BF16),
            jax.ShapeDtypeStruct((rows, units), F32),
        ]
        + [cut_shape] * 2
        + [jax.ShapeDtypeStruct(heads.shape, BF16)],
        in_specs=[ANYWHERE] * 4 + vmem(1) + [ANYWHERE],
        out_specs=vmem(2) + [ANYWHERE] + vmem(3),
        scratch_shapes=Staged.scratch([heads, w_out, out_grad, x])
        + [pltpu.VMEM((rows, units), F32), dma]
        + [pltpu.VMEM((units, model), BF16), dma((tiles,))]
        + [pltpu.VMEM((rows, model), F32), dma((blocks,)), dma((blocks,)), dma, dma]
        + TensorSum.scratch(blocks, half // blocks, model)
        + Columns.scratch(half, planes * shard),
        compiler_params=pltpu.CompilerParams(
            vmem_limit_bytes=VMEM_LIMIT, collective_id=4, has_side_effects=True
        ),
        cost_estimate=COST,
        name="attention_out",
    )(heads, w_out, out_grad, x, gain, w_down)


def middle_kernel(*refs, planes, shard, heads, width, pieces, blocks, sums):
    refs = list(refs)

    def take(count):
        out = refs[:count]
        del refs[:count]
        return out

    w_gate_ref, w_up_ref, gain_ref = take(3)
    count = 10 if sums else 8
    arrays = take(count)
    outs = take(3)
    hid_came_ref, a_ref, gain_out_ref, qx_ref, dox_ref, h_keep, h_came = take(7)
    if sums:
        down_outs = take(pieces - 1)
    buffers = take(count)
    inputs = Staged(arrays, buffers, *take(1))
    h_ref, d_ref, middle_ref, og_ref, w_out_ref, q_ref, o_ref, lse_ref = buffers[:8]
    if sums:
        og_keep, og_came = buffers[8:]
    out_buffers = take(3)
    hid_ref, gate_ref, up_ref = out_buffers
    outputs = Staged(outs, out_buffers, *take(1), out=True)
    gate_buf, up_buf, load_sems, c_ref, mine_ref = take(5)
    hid_send, hid_recv, a_send, a_recv = take(4)
    sum_scratch, h_scratch = take(8), take(6)
    device = lax.axis_index("dp")
    core, core_peer, y_peer = tensor_peers()
    plane = device // 2
    x_at = device % 2
    x_peer = {"dp": device + 1 - 2 * x_at}
    meets = [(x_peer, True), (core_peer, True), (y_peer, True)]
    h_two = Columns(h_ref, h_keep, h_came, h_scratch, x_at, core, x_peer, core_peer, planes, shard)
    half = middle_ref.shape[0]
    total = TensorSum(sum_scratch, mine_ref, core, core_peer, y_peer)
    chunks, columns = total.chunks, total.width
    units = hid_ref.shape[1]
    piece = units // pieces
    tile = 256
    tiles = units // tile
    if sums:
        downs = [LineSum(take(6), device, plane, planes) for _ in range(pieces - 1)]
        meets += [({"dp": device + 2}, plane < planes - 1), ({"dp": device - 2}, plane > 0)]

    def loads(t):
        at = pl.ds(t * tile, tile)
        return (
            pltpu.make_async_copy(w_gate_ref.at[:, at], gate_buf.at[:, at], load_sems.at[2 * t]),
            pltpu.make_async_copy(w_up_ref.at[:, at], up_buf.at[:, at], load_sems.at[2 * t + 1]),
        )

    inputs.start(h_ref)
    for t in range(tiles):
        for load in loads(t):
            load.start()
        if t == 0:
            inputs.start(d_ref)
    inputs.start(*buffers[2:])
    greet(meets)
    inputs.wait(h_ref)

    def swap(k):
        at = pl.ds(k * tile, tile)
        return remote(hid_ref.at[:, at], hid_came_ref.at[:, at], hid_send.at[k], hid_recv.at[k], x_peer)

    for t in range(tiles):
        for load in loads(t):
            load.wait()
        if t == 0:
            inputs.wait(d_ref)
        at = slice(t * tile, (t + 1) * tile)
        gate = dot(h_ref[...], gate_buf[:, at])
        up = dot(h_ref[...], up_buf[:, at])
        sig = 0.5 * jnp.tanh(0.5 * gate) + 0.5
        silu = gate * sig
        d = d_ref[:, at]
        hid_ref[:, at] = (silu * up).astype(BF16)
        up_ref[:, at] = (d * silu).astype(BF16)
        gate_ref[:, at] = (d * up * (sig * (1.0 + gate * (1.0 - sig)))).astype(BF16)
        swap(t).start()

    outputs.start()
    inputs.wait(*buffers[2:])

    def down_start(k):
        if sums:
            at = pl.ds(k * piece, piece)
            for t in range(k * piece // tile, (k + 1) * piece // tile):
                swap(t).wait_recv()
            downs[k].fill_columns(hid_ref.at[:, at], hid_came_ref.at[:, at], og_keep, og_came)
            downs[k].start()

    def down_advance(k, step):
        if sums and step <= planes - 2:
            downs[k].advance(step)

    for i in range(chunks):
        at = slice(i * columns, (i + 1) * columns)
        total.add(i, dot(gate_ref[...], gate_buf[at, :], NT) + dot(up_ref[...], up_buf[at, :], NT))
        if i == chunks // 2:
            down_start(0)
    for i in range(chunks):
        if i == chunks // 4:
            down_start(1)
            h_two.start()
        if i == chunks // 2:
            down_advance(0, 1)
        c_ref[:, i * columns : (i + 1) * columns] = total.total(i)
    down_advance(0, 2)

    step = half // blocks

    def to_core(b):
        rows = a_ref.at[pl.ds(pl.multiple_of(core * half + b * step, step), step), :]
        return remote(rows, rows, a_send.at[b], a_recv.at[b], core_peer)

    gain_out_ref[...] = jnp.zeros_like(gain_out_ref)
    for b in range(blocks):
        at = slice(b * step, (b + 1) * step)
        whole_at = pl.ds(pl.multiple_of(core * half + b * step, step), step)
        c = c_ref[at, :]
        v = middle_ref[at, :]
        r = lax.rsqrt(jnp.mean(v * v, axis=1, keepdims=True) + EPS)
        n = v * r
        gain_out_ref[...] += jnp.sum(c * n, axis=0, keepdims=True)
        gc = c * gain_ref[...]
        d = r * (gc - n * jnp.mean(n * gc, axis=1, keepdims=True)) + og_ref[whole_at, :].astype(F32)
        a_ref[whole_at, :] = d.astype(BF16)
        to_core(b).start()

    lane = lax.broadcasted_iota(jnp.int32, (half, width), 1)

    def extra(value):
        a, b, c = split_three(value)
        return jnp.where(lane == 0, a, jnp.where(lane == 1, b, jnp.where(lane == 2, c, 0.0))).astype(BF16)

    def prepare(which):
        at_rows = rows_of(which, half)
        d_heads = dot(a_ref[at_rows, :], w_out_ref[...], NT)
        for head in range(heads):
            at = slice(head * width, (head + 1) * width)
            qx_ref[head, at_rows, :width] = q_ref[at_rows, at]
            qx_ref[head, at_rows, width:] = extra(lse_ref[at_rows, at])
            d = d_heads[:, at].astype(BF16)
            delta = jnp.sum(d.astype(F32) * o_ref[at_rows, at].astype(F32), axis=1, keepdims=True)
            dox_ref[head, at_rows, :width] = d
            dox_ref[head, at_rows, width:] = extra(jnp.broadcast_to(delta, (half, width)))

    down_advance(1, 1)
    h_two.store()
    prepare(core)
    h_two.forward()
    for b in range(blocks):
        to_core(b).wait_recv()
    prepare(1 - core)
    down_advance(1, 2)
    for b in range(blocks):
        to_core(b).wait_send()
    total.finish()
    h_two.finish()
    outputs.wait()
    for t in range(tiles):
        if t >= (pieces - 1) * piece // tile or not sums:
            swap(t).wait_recv()
        swap(t).wait_send()
    if sums:
        for k in range(pieces - 1):
            for step in range(3, planes - 1):
                downs[k].advance(step)
            downs[k].finish(down_outs[k])


def middle_of(w_gate, w_up, h_two, d_hidden, middle, out_grad, gain, w_out, q, out, lse, cuts, pieces, planes, shard, width):
    half, model = middle.shape
    rows, units = d_hidden.shape
    columns = q.shape[1]
    heads = columns // width
    chunks, blocks = 4, 4
    dma = pltpu.SemaphoreType.DMA
    staged = [h_two, d_hidden, middle, out_grad, w_out, q, out, lse] + ([] if cuts is None else cuts)
    args = [w_gate, w_up, gain, *staged]
    unit_shape = jax.ShapeDtypeStruct((rows, units), BF16)
    out_shape = [unit_shape] * 4 + [
        jax.ShapeDtypeStruct((rows, model), BF16),
        jax.ShapeDtypeStruct((1, model), F32),
    ]
    out_shape += [jax.ShapeDtypeStruct((heads, rows, 2 * width), BF16)] * 2
    out_shape += [jax.ShapeDtypeStruct((rows, planes * shard), BF16)] * 2
    scratch = Staged.scratch(staged) + Staged.scratch([unit_shape] * 3)
    scratch += [pltpu.VMEM((model, units), BF16)] * 2 + [dma((2 * units // 256,))]
    scratch += [pltpu.VMEM((half, model), F32), pltpu.VMEM((2, rows, model // chunks), F32)]
    scratch += [dma((units // 256,))] * 2 + [dma((blocks,))] * 2
    scratch += TensorSum.scratch(chunks, half, model // chunks)
    scratch += Columns.scratch(half, planes * shard)
    if cuts is not None:
        out_shape += [jax.ShapeDtypeStruct((units // pieces, shard), BF16)] * (pieces - 1)
        scratch += LineSum.scratch(planes, (units // pieces, shard)) * (pieces - 1)
    return pl.pallas_call(
        functools.partial(
            middle_kernel,
            planes=planes,
            shard=shard,
            heads=heads,
            width=width,
            pieces=pieces,
            blocks=blocks,
            sums=cuts is not None,
        ),
        out_shape=out_shape,
        in_specs=[ANYWHERE] * 2 + vmem(1) + [ANYWHERE] * len(staged),
        out_specs=[ANYWHERE] * 3 + vmem(len(out_shape) - 3),
        scratch_shapes=scratch,
        compiler_params=pltpu.CompilerParams(
            vmem_limit_bytes=BACK_VMEM_LIMIT, collective_id=2, has_side_effects=True
        ),
        cost_estimate=COST,
        name="middle",
    )(*args)


def through_rope(d_ref, raw_ref, gain, cos, sin, out_ref, width, plain):
    columns = d_ref.shape[1]
    total = jnp.zeros((1, width), F32)
    for at in range(0, columns - plain, width):
        d = d_ref[:, at : at + width]
        c = d * cos - roll_half(d) * sin
        v = raw_ref[:, at : at + width]
        r = lax.rsqrt(jnp.mean(v * v, axis=1, keepdims=True) + EPS)
        n = v * r
        total = total + jnp.sum(c * n, axis=0, keepdims=True)
        gc = gain * c
        out_ref[:, at : at + width] = (r * (gc - n * jnp.mean(n * gc, axis=1, keepdims=True))).astype(BF16)
    if plain:
        out_ref[:, columns - plain :] = d_ref[:, columns - plain :].astype(BF16)
    return total


def front_kernel(*refs, dp_size, group, planes, shard, chunks, blocks, sums):
    refs = list(refs)

    def take(count):
        out = refs[:count]
        del refs[:count]
        return out

    q_gain, k_gain, attn_gain, mlp_gain_ref, add_array = take(5)
    count = 15 if sums else 11
    arrays = take(count)
    arrays[2:4] = table_rows(arrays[2:4], lax.axis_index("dp") % group, arrays[0].shape[0])
    x_grad, gains = take(2)
    if sums:
        w_up_out, w_q_out, w_kv_out = take(3)
    dq_ref, dq_came, dkv_ref, dkv_came, one_ref, one_came = take(6)
    buffers = take(count)
    inputs = Staged(arrays, buffers, *take(1))
    dkv_in, k_raw, cos_ref, sin_ref, dq_in, q_raw, one_all = buffers[:7]
    x_ref, w_q, w_k, w_v = buffers[7:11]
    if sums:
        two_ref, two_came, up_ref, up_came = buffers[11:]
    mine, gain_came, c_ref, add_ref, add_sem = take(5)
    swap_sems, one_sems, gain_sems = take(4), take(2), take(2)
    one_sum_scratch, one_scratch = take(8), take(6)
    half = x_ref.shape[0] // 2
    model = x_ref.shape[1]
    width = model // chunks
    head = cos_ref.shape[1]
    kv_width = w_k.shape[1]

    device = lax.axis_index("dp")
    core, core_peer, y_peer = tensor_peers()
    x_at = device % 2
    x_peer = {"dp": device + 1 - 2 * x_at}
    plane = device // 2
    one = Columns(one_all, one_ref, one_came, one_scratch, x_at, core, x_peer, core_peer, planes, shard)
    bits = [1 << i for i in range(dp_size.bit_length() - 1)]
    dp_peers = [{"dp": device + bit - 2 * bit * ((device // bit) % 2)} for bit in bits]
    gain_peers = [core_peer, y_peer] + dp_peers
    meets = [(peer, True) for peer in gain_peers]
    if sums:
        up_sum, q_sum, kv_sum = (LineSum(take(6), device, plane, planes, True) for _ in range(3))
        meets += [({"dp": device + 2}, plane < planes - 1), ({"dp": device - 2}, plane > 0)]

    mine_rows = rows_of(core, half)
    add_load = pltpu.make_async_copy(add_array.at[mine_rows, :], add_ref, add_sem)
    inputs.start(one_all)
    if sums:
        inputs.start(*buffers[11:])
    inputs.start(*buffers[:6])
    inputs.start(*buffers[7:11])
    add_load.start()
    greet(meets)
    inputs.wait(one_all)
    one.start()
    if sums:
        inputs.wait(*buffers[11:])
        up_sum.fill_rows(two_ref, two_came, up_ref, up_came)
    inputs.wait(*buffers[:6])
    cos, sin = cos_ref[...], sin_ref[...]
    k_total = through_rope(dkv_in, k_raw, k_gain[...], cos, sin, dkv_ref, head, kv_width)
    kv_swap = remote(dkv_ref, dkv_came, swap_sems[0], swap_sems[1], x_peer)
    kv_swap.start()
    q_total = through_rope(dq_in, q_raw, q_gain[...], cos, sin, dq_ref, head, 0)
    q_swap = remote(dq_ref, dq_came, swap_sems[2], swap_sems[3], x_peer)
    q_swap.start()
    inputs.wait(*buffers[7:11])

    one_sum = TensorSum(one_sum_scratch, mine, core, core_peer, y_peer)
    x = x_ref[...].astype(F32)
    r = lax.rsqrt(jnp.mean(x * x, axis=1, keepdims=True) + EPS)
    for i in range(chunks):
        at = slice(i * width, (i + 1) * width)
        part = (
            dot(dq_ref[...], w_q[at, :], NT)
            + dot(dkv_ref[:, :kv_width], w_k[at, :], NT)
            + dot(dkv_ref[:, kv_width:], w_v[at, :], NT)
        )
        one_sum.add(i, part)
        gains[0, :, at] = jnp.sum(part * (x_ref[:, at].astype(F32) * r), axis=0, keepdims=True)
    gains[0, :, model : 2 * model] = 0.5 * mlp_gain_ref[...]
    gains[0, :, 2 * model : 2 * model + head] = q_total
    gains[0, :, 2 * model + head :] = k_total
    one.forward()
    one.store()

    def gain_swap(k):
        return remote(
            gains.at[k], gain_came.at[k], gain_sems[0].at[k], gain_sems[1].at[k], gain_peers[k]
        )

    def gain_add(k):
        gain_swap(k).wait_recv()
        gains[k + 1] = gains[k] + gain_came[k]
        if k + 1 < len(gain_peers):
            gain_swap(k + 1).start()

    gain_swap(0).start()

    def advance(line, step):
        if sums and step <= planes - 2:
            line.advance(step)

    gain_add(0)
    if sums:
        advance(up_sum, 1)
        kv_swap.wait_recv()
        one.over_core().wait_recv()
        kv_sum.fill_rows(one_ref, one_came, dkv_ref, dkv_came)
    gain_add(1)
    if sums:
        q_swap.wait_recv()
        q_sum.fill_rows(one_ref, one_came, dq_ref, dq_came)
        advance(up_sum, 2)
    gain_add(2)

    def give(out, sems):
        rows = out.at[mine_rows, :]
        return remote(rows, rows, sems[0], sems[1], core_peer)

    for i in range(chunks):
        c_ref[:, i * width : (i + 1) * width] = one_sum.total(i)
    add_load.wait()
    step = half // blocks
    for b in range(blocks):
        at = slice(b * step, (b + 1) * step)
        whole_at = pl.ds(pl.multiple_of(core * half + b * step, step), step)
        v = x_ref[whole_at, :].astype(F32)
        v_r = lax.rsqrt(jnp.mean(v * v, axis=1, keepdims=True) + EPS)
        n = v * v_r
        gc = c_ref[at, :] * attn_gain[...]
        d = v_r * (gc - n * jnp.mean(n * gc, axis=1, keepdims=True))
        x_grad[whole_at, :] = (d + add_ref[at, :].astype(F32)).astype(BF16)
    give(x_grad, one_sems).start()
    for k in range(3, len(gain_peers)):
        gain_add(k)
    if sums:
        advance(kv_sum, 1)
        advance(q_sum, 1)
    if sums:
        advance(kv_sum, 2)
        advance(q_sum, 2)
        for line in (up_sum, kv_sum, q_sum):
            for step in range(3, planes - 1):
                advance(line, step)
        up_sum.finish(w_up_out)
        kv_sum.finish(w_kv_out)
        q_sum.finish(w_q_out)
    else:
        kv_swap.wait_recv()
        q_swap.wait_recv()
        one.over_core().wait_recv()
    one.over_x().wait_send()
    one.over_core().wait_send()
    kv_swap.wait_send()
    q_swap.wait_send()
    give(x_grad, one_sems).wait_recv()
    give(x_grad, one_sems).wait_send()
    for k in range(len(gain_peers)):
        gain_swap(k).wait_send()
    one_sum.finish()


def front(dq, dkv, q_raw, k_raw, q_gain, k_gain, cos, sin, h_one, weights, x, d_attn, attn_gain, mlp_gain, grads, dp_size, group, shard):
    rows, model = x.shape
    half = rows // 2
    planes = dp_size // 2
    chunks = 4
    width = model // chunks
    stages = dp_size.bit_length() + 1
    dma = pltpu.SemaphoreType.DMA
    gains = (2 * model + 2 * cos.shape[1],)
    staged = [dkv, k_raw, cos, sin, dq, q_raw, h_one, x, *weights]
    if grads is not None:
        staged += grads
    args = [q_gain, k_gain, attn_gain, mlp_gain, d_attn, *staged]
    cut_shape = jax.ShapeDtypeStruct((rows, planes * shard), BF16)
    whole = jax.ShapeDtypeStruct((rows, model), BF16)
    q_shape, kv_shape = jax.ShapeDtypeStruct(dq.shape, BF16), jax.ShapeDtypeStruct(dkv.shape, BF16)
    out_shape = [whole, jax.ShapeDtypeStruct((stages + 1, 1) + gains, F32)]
    kept = [q_shape, q_shape, kv_shape, kv_shape, cut_shape, cut_shape]
    table = jax.ShapeDtypeStruct((rows, cos.shape[1]), F32)
    scratch = Staged.scratch(staged[:2] + [table, table] + staged[4:])
    scratch += [pltpu.VMEM((2, rows, width), F32)]
    scratch += [pltpu.VMEM((stages, 1) + gains, F32), pltpu.VMEM((half, model), F32)]
    scratch += [pltpu.VMEM((half, model), BF16), dma]
    scratch += [dma] * 6 + [dma((stages,))] * 2
    scratch += TensorSum.scratch(chunks, half, width)
    scratch += Columns.scratch(half, planes * shard)
    if grads is None:
        out_shape += kept
    else:
        scratch = [pltpu.VMEM(s.shape, s.dtype) for s in kept] + scratch
        for columns in (grads[2].shape[1], dq.shape[1], dkv.shape[1]):
            out_shape.append(jax.ShapeDtypeStruct((shard, columns), BF16))
            scratch += LineSum.scratch(planes, (shard, columns))
    return pl.pallas_call(
        functools.partial(
            front_kernel,
            dp_size=dp_size,
            group=group,
            planes=planes,
            shard=shard,
            chunks=chunks,
            blocks=4,
            sums=grads is not None,
        ),
        out_shape=out_shape,
        in_specs=vmem(4) + [ANYWHERE] * (len(args) - 4),
        out_specs=vmem(len(out_shape)),
        scratch_shapes=scratch,
        compiler_params=pltpu.CompilerParams(
            vmem_limit_bytes=BACK_VMEM_LIMIT, collective_id=3, has_side_effects=True
        ),
        cost_estimate=COST,
        name="front",
    )(*args)


def widen_kernel(*refs, results, gains):
    refs = list(refs)

    def take(count):
        out = refs[:count]
        del refs[:count]
        return out

    count = 1 + max(i for parts in results for i, _ in parts)
    block_in = take(1)[0]
    arrays = take(count)
    if gains:
        gain_in = take(1)[0]
    block_out = take(1)[0]
    outs = take(len(results))
    if gains:
        attn_out, mlp_out, q_out, k_out = take(4)
    buffers = take(count)
    inputs = Staged(arrays, buffers, *take(1))
    out_buffers = take(len(results))
    outputs = Staged(outs, out_buffers, *take(1), out=True)
    block, block_sems = take(2)
    if gains:
        gain_ref, gain_sem = take(2)
        gain_load = pltpu.make_async_copy(gain_in.at[gain_in.shape[0] - 1], gain_ref, gain_sem)
        gain_load.start()
    block_load = pltpu.make_async_copy(block_in, block, block_sems.at[0])
    block_copy = pltpu.make_async_copy(block, block_out, block_sems.at[1])
    block_load.start()
    inputs.start()
    if gains:
        gain_load.wait()
        shard, head = attn_out.shape[1], q_out.shape[1]
        model = (gain_ref.shape[1] - 2 * head) // 2
        at = pl.multiple_of(lax.axis_index("dp") * shard, shard)
        attn_out[...] = gain_ref[:, pl.ds(at, shard)]
        mlp_out[...] = gain_ref[:, pl.ds(pl.multiple_of(model + at, shard), shard)]
        q_out[...] = gain_ref[:, 2 * model : 2 * model + head]
        k_out[...] = gain_ref[:, 2 * model + head :]
    block_load.wait()
    block_copy.start()
    waited = set()
    for parts, out in zip(results, out_buffers):
        row = 0
        for i, column in parts:
            part = buffers[i]
            if i not in waited:
                inputs.wait(part)
                waited.add(i)
            height = part.shape[0]
            out[row : row + height, :] = part[:, column : column + out.shape[1]].astype(F32)
            row += height
        outputs.start(out)
    block_copy.wait()
    outputs.wait()


def widen(block_out, arrays, results, shapes, gains, shard, head):
    out_shape = [jax.ShapeDtypeStruct(block_out.shape, BF16)]
    out_shape += [jax.ShapeDtypeStruct(s, F32) for s in shapes]
    args = [block_out, *arrays]
    rows = [] if gains is None else [(1, shard), (1, shard), (1, head), (1, head)]
    if gains is not None:
        args.append(gains)
    return pl.pallas_call(
        functools.partial(widen_kernel, results=results, gains=gains is not None),
        out_shape=out_shape + [jax.ShapeDtypeStruct(s, F32) for s in rows],
        in_specs=[ANYWHERE] * len(args),
        out_specs=[ANYWHERE] * (1 + len(shapes)) + vmem(len(rows)),
        scratch_shapes=Staged.scratch(arrays)
        + Staged.scratch(out_shape[1:])
        + [pltpu.VMEM(block_out.shape, BF16), pltpu.SemaphoreType.DMA((2,))]
        + ([] if gains is None else [pltpu.VMEM(gains.shape[1:], F32), pltpu.SemaphoreType.DMA]),
        compiler_params=params(),
        cost_estimate=COST,
        name="widen",
    )(*args)


def rope_tables(length, width):
    frequency = ROPE_BASE ** (-2.0 * np.arange(width // 2) / width)
    angles = np.arange(length)[:, None] * frequency[None, :]
    cos, sin = np.cos(angles), np.sin(angles)
    tables = np.concatenate([cos, cos], axis=1), np.concatenate([-sin, sin], axis=1)
    return tuple(jnp.asarray(t.astype(np.float32)) for t in tables)


class Chain:
    def __init__(self):
        self.last = None

    def mark(self, value):
        self.last = value

    def __call__(self, *values):
        if self.last is None:
            return values
        return lax.optimization_barrier((*values, self.last))[:-1]


class ZSum:
    def __init__(self, part, dim, shard, planes, z_at):
        self.part, self.dim, self.shard, self.planes, self.z_at = part, dim, shard, planes, z_at
        self.at = 0
        self.came = None

    def term(self, j):
        j = jnp.clip(j, 0, self.planes - 1)
        return lax.dynamic_slice_in_dim(self.part, j * self.shard, self.shard, self.dim)

    def send(self, up, down):
        last = self.planes - 1
        self.at += 1
        up_pairs = [(2 * z + x, 2 * z + 2 + x) for z in range(last) for x in range(2) if z < self.at]
        down_pairs = [
            (2 * (last - z) + x, 2 * (last - 1 - z) + x)
            for z in range(last)
            for x in range(2)
            if z < self.at
        ]
        self.came = lax.ppermute(up, "dp", up_pairs), lax.ppermute(down, "dp", down_pairs)

    def terms(self):
        planes, z_at, at = self.planes, self.z_at, self.at
        return self.term(planes - 1 - at + z_at), self.term(at + 1 - planes + z_at)

    def start(self):
        self.send(*self.terms())

    def step(self, chain):
        if self.at >= self.planes - 1:
            return
        up, down = chain(*self.came)
        up_term, down_term = self.terms()
        up, down = up + up_term, down + down_term
        chain.mark(up)
        self.send(up, down)

    def finish(self, chain):
        if self.at == 0:
            self.start()
        while self.at < self.planes - 1:
            self.step(chain)
        up, down = chain(*self.came)
        total = self.term(self.z_at).astype(F32) + up.astype(F32) + down.astype(F32)
        chain.mark(total)
        return total


def shards(
    dp_size,
    tensor_size,
    tokens,
    norm_attn,
    w_query,
    key_weight,
    value_weight,
    query_gain,
    key_gain,
    w_out,
    norm_mlp,
    w_gate,
    w_up,
    w_down,
    out_grad,
    prefix_len,
):
    rows, model = tokens.shape
    width = query_gain.shape[0]
    kv_heads = key_weight.shape[1] // width
    repeat = w_query.shape[1] // key_weight.shape[1]
    dims = (kv_heads, repeat, width)
    group = dp_size // prefix_len.shape[0]
    planes = dp_size // 2
    group_planes = group // 2
    half = rows // 2
    shard = model // dp_size
    assert tensor_size == 4 and MAX_PREFIX <= 4 * rows

    device = lax.axis_index("dp")
    x_at = device % 2
    z_at = device // 2
    sequence = device // group
    member = device % group
    plane = member // 2
    prefix = jnp.sum(jnp.where(jnp.arange(prefix_len.shape[0]) == sequence, prefix_len, 0))

    x_pairs = [(d, d ^ 1) for d in range(dp_size)]

    def x_swap(value):
        return lax.ppermute(value, "dp", x_pairs)

    cos, sin = rope_tables(group * rows, width)
    norm_attn_row = norm_attn[None, :]
    norm_mlp_row = norm_mlp[None, :]
    q_gain_row = query_gain[None, :]
    k_gain_row = key_gain[None, :]

    prefix_at = prefix[None].astype(jnp.int32)
    heads_b, lse, kv_all, h_one, q, q_raw, k_raw = attn_fwd(
        prefix_at,
        tokens,
        norm_attn_row,
        w_query,
        key_weight,
        value_weight,
        q_gain_row,
        k_gain_row,
        cos,
        sin,
        group,
        dims,
    )
    fused = planes == group_planes and shard % 128 == 0
    pieces = 3
    middle, h_two, d_hidden, og_keep, og_came, heads_came = attention_out(
        heads_b, w_out, tokens, norm_mlp_row, out_grad, w_down, planes, shard
    )
    outs = middle_of(
        w_gate,
        w_up,
        h_two,
        d_hidden,
        middle,
        out_grad,
        norm_mlp_row,
        w_out,
        q,
        heads_b,
        lse,
        [og_keep, og_came] if fused else None,
        pieces,
        planes,
        shard,
        width,
    )
    hidden, d_gate, d_up, hidden_came, d_attn, norm_mlp_part, qx, dox, h_two_keep, h_two_came = outs[:10]

    grads = None
    if fused:
        grads = [hidden_came, og_keep, og_came, d_gate, h_two_keep, h_two_came]
        grads += [heads_b, heads_came]
        w_down_parts = outs[10:]
    shared = [d_attn, d_up, hidden, w_down, middle]
    outs = back(prefix_at, qx, dox, kv_all, shared, grads, group, planes, shard, pieces, dims)
    dq, kv_grad, up_came, block_out = outs[:4]
    chain = Chain()
    chain.mark(dq)
    if fused:
        w_down_parts = [*w_down_parts, outs[4]]
        w_gate_grad, w_out_grad = outs[5:]
    else:
        d_attn_keep, d_attn_came = outs[4:]
        down_part = (dot(hidden, og_keep, TN) + dot(hidden_came, og_came, TN)).astype(BF16)
        w_down_grad = ZSum(down_part, 1, shard, planes, z_at).finish(chain)
        gate_part = dot(h_two_keep, d_gate, TN) + dot(h_two_came, x_swap(d_gate), TN)
        w_gate_grad = ZSum(gate_part.astype(BF16), 0, shard, planes, z_at).finish(chain)
        out_part = dot(heads_b, d_attn_keep, TN) + dot(heads_came, d_attn_came, TN)
        w_out_grad = ZSum(out_part.astype(BF16), 1, shard, planes, z_at).finish(chain)

    up_grads = [h_two_keep, h_two_came, d_up, up_came] if fused else None
    outs = front(
        *chain(dq),
        kv_grad,
        q_raw,
        k_raw,
        q_gain_row,
        k_gain_row,
        cos,
        sin,
        h_one,
        (w_query, key_weight, value_weight),
        tokens,
        d_attn,
        norm_attn_row,
        norm_mlp_part,
        up_grads,
        dp_size,
        group,
        shard,
    )
    tokens_grad, gains = outs[:2]
    if fused:
        w_up_grad, w_query_grad, w_kv_grad = outs[2:]
    else:
        dq_b, dq_came, dkv_b, dkv_came, h_one_keep, h_one_came = outs[2:]
        chain.mark(tokens_grad)

        def by_rows(left, left_came, right, right_came):
            part = dot(left, right, TN) + dot(left_came, right_came, TN)
            return ZSum(part.astype(BF16), 0, shard, planes, z_at).finish(chain)

        w_up_grad = by_rows(h_two_keep, h_two_came, d_up, up_came)
        w_query_grad = by_rows(h_one_keep, h_one_came, dq_b, dq_came)
        w_kv_grad = by_rows(h_one_keep, h_one_came, dkv_b, dkv_came)
    kv_width = kv_heads * width
    if fused:
        arrays = [w_gate_grad, w_out_grad, *w_down_parts, w_up_grad, w_query_grad, w_kv_grad, tokens_grad]
        n = 2 + len(w_down_parts)
        results = [[(0, 0)], [(1, 0)], [(i, 0) for i in range(2, n)]]
        results += [[(n, 0)], [(n + 1, 0)], [(n + 2, 0)], [(n + 2, kv_width)], [(n + 3, 0)]]
        units = w_gate.shape[1]
        columns = w_query.shape[1]
        shapes = [(shard, units), (columns, shard), (units, shard), (shard, units), (shard, columns)]
        shapes += [(shard, kv_width)] * 2 + [(rows, model)]
        outs = widen(block_out, arrays, results, shapes, gains, shard, width)
        block_out, w_gate_grad, w_out_grad, w_down_grad, w_up_grad, w_query_grad = outs[:6]
        w_key_grad, w_value_grad, tokens_grad = outs[6:9]
        norm_attn_grad, norm_mlp_grad, query_gain_grad, key_gain_grad = (v[0] for v in outs[9:])
    else:
        w_key_grad, w_value_grad = w_kv_grad[:, :kv_width], w_kv_grad[:, kv_width:]
        tokens_grad = tokens_grad.astype(F32)
        gains = gains[-1, 0]
        norm_attn_grad = lax.dynamic_slice_in_dim(gains, device * shard, shard, 0)
        norm_mlp_grad = lax.dynamic_slice_in_dim(gains, model + device * shard, shard, 0)
        query_gain_grad, key_gain_grad = gains[2 * model : 2 * model + width], gains[2 * model + width :]
    return (
        block_out,
        tokens_grad,
        norm_attn_grad,
        w_query_grad,
        w_key_grad,
        w_value_grad,
        query_gain_grad,
        key_gain_grad,
        w_out_grad,
        norm_mlp_grad,
        w_gate_grad,
        w_up_grad,
        w_down_grad,
    )


def solution(mesh):
    placed = (
        P("dp", None),
        P(),
        P(None, "tensor"),
        P(None, "tensor"),
        P(None, "tensor"),
        P(),
        P(),
        P("tensor", None),
        P(),
        P(None, "tensor"),
        P(None, "tensor"),
        P("tensor", None),
        P("dp", None),
        P(),
    )
    return jax.shard_map(
        functools.partial(shards, mesh.shape["dp"], mesh.shape["tensor"]),
        mesh=mesh,
        in_specs=placed,
        out_specs=(
            P("dp", None),
            P("dp", None),
            P("dp"),
            P("dp", "tensor"),
            P("dp", "tensor"),
            P("dp", "tensor"),
            P(),
            P(),
            P("tensor", "dp"),
            P("dp"),
            P("dp", "tensor"),
            P("dp", "tensor"),
            P("tensor", "dp"),
        ),
        check_vma=False,
    )
```

```python
import functools
import math

import jax
import jax.numpy as jnp
import numpy as np
from jax import lax
from jax.experimental import pallas as pl
from jax.experimental.pallas import tpu as pltpu
from jax.sharding import PartitionSpec as P

F32 = jnp.float32
BF16 = jnp.bfloat16
EPS = 1e-06
ROPE_BASE = 1000000.0
MAX_PREFIX = 2048
VMEM_LIMIT = 56 * 2**20
BACK_VMEM_LIMIT = 60 * 2**20

COST = pl.CostEstimate(flops=1000, bytes_accessed=1000, transcendentals=0)

NN = (((1,), (0,)), ((), ()))
NT = (((1,), (1,)), ((), ()))
TN = (((0,), (0,)), ((), ()))


def dot(left, right, dims=NN):
    return lax.dot_general(left, right, dims, preferred_element_type=F32)


def vmem(count):
    return [pl.BlockSpec(memory_space=pltpu.VMEM)] * count


def params():
    return pltpu.CompilerParams(vmem_limit_bytes=VMEM_LIMIT)


def greet(peers):
    barrier = pltpu.get_barrier_semaphore()
    count = 0
    for peer, there in peers:

        def signal(peer=peer):
            pl.semaphore_signal(barrier, 1, device_id=peer, device_id_type=pl.DeviceIdType.MESH)

        if there is True:
            signal()
            count = count + 1
        else:
            pl.when(there)(signal)
            count = count + there.astype(jnp.int32)
    pl.semaphore_wait(barrier, count)


def remote(src, dst, send, recv, peer):
    return pltpu.make_async_remote_copy(
        src_ref=src,
        dst_ref=dst,
        send_sem=send,
        recv_sem=recv,
        device_id=peer,
        device_id_type=pl.DeviceIdType.MESH,
    )


class Staged:
    def __init__(self, arrays, buffers, sems, out=False):
        self.copies = []
        for i, (array, buffer) in enumerate(zip(arrays, buffers)):
            ends = (buffer, array) if out else (array, buffer)
            self.copies.append((buffer, pltpu.make_async_copy(*ends, sems.at[i])))

    @staticmethod
    def scratch(shapes):
        return [pltpu.VMEM(s.shape, s.dtype) for s in shapes] + [pltpu.SemaphoreType.DMA((len(shapes),))]

    def start(self, *buffers):
        for buffer, copy in self.copies:
            if not buffers or any(buffer is b for b in buffers):
                copy.start()

    def wait(self, *buffers):
        for buffer, copy in self.copies:
            if not buffers or any(buffer is b for b in buffers):
                copy.wait()


ANYWHERE = pl.BlockSpec(memory_space=pl.ANY)


def table_rows(tables, member, rows):
    at = pl.ds(pl.multiple_of(member * rows, rows), rows)
    return [t.at[at, :] for t in tables]


def tensor_peers():
    t = lax.axis_index("tensor")
    core = t % 2
    y = t // 2
    return core, {"tensor": t + 1 - 2 * core}, {"tensor": t + 2 - 4 * y}


def rows_of(core, half):
    return pl.ds(pl.multiple_of(core * half, half), half)


def cut_into(out, out_rows, ref, ref_rows, side, planes, shard):
    for z in range(planes):
        to = slice(z * shard, (z + 1) * shard)
        if shard % 128 == 0:
            at = pl.ds(pl.multiple_of((2 * z + side) * shard, shard), shard)
            out[out_rows, to] = ref[ref_rows, at]
        else:
            low = ref[ref_rows, 2 * z * shard : (2 * z + 1) * shard]
            high = ref[ref_rows, (2 * z + 1) * shard : (2 * z + 2) * shard]
            out[out_rows, to] = jnp.where(side == 0, low, high)


class Columns:
    def __init__(self, whole, keep, came, scratch, x_at, core, x_peer, core_peer, planes, shard):
        self.whole, self.keep, self.came = whole, keep, came
        self.send_ref, self.recv_ref, self.sems = scratch[0], scratch[1], scratch[2:]
        self.x_at, self.core, self.cut = x_at, core, (planes, shard)
        self.x_peer, self.core_peer = x_peer, core_peer
        self.half = whole.shape[0] // 2

    @staticmethod
    def scratch(half, columns):
        return [pltpu.VMEM((half, columns), BF16)] * 2 + [pltpu.SemaphoreType.DMA] * 4

    def over_x(self):
        return remote(self.send_ref, self.recv_ref, self.sems[0], self.sems[1], self.x_peer)

    def over_core(self):
        there = self.came.at[rows_of(self.core, self.half), :]
        return remote(self.recv_ref, there, self.sems[2], self.sems[3], self.core_peer)

    def start(self):
        mine = rows_of(self.core, self.half)
        cut_into(self.send_ref, slice(None), self.whole, mine, 1 - self.x_at, *self.cut)
        self.over_x().start()

    def store(self):
        cut_into(self.keep, slice(None), self.whole, slice(None), self.x_at, *self.cut)

    def forward(self):
        self.over_x().wait_recv()
        self.over_core().start()
        self.came[rows_of(self.core, self.half), :] = self.recv_ref[...]

    def finish(self):
        self.over_core().wait_recv()
        self.over_x().wait_send()
        self.over_core().wait_send()


class LineSum:
    def __init__(self, scratch, device, plane, planes, paced=False):
        self.paced = paced
        self.stack, self.came = scratch[:2]
        self.sems = scratch[2:]
        self.device, self.plane, self.planes = device, plane, planes

    @staticmethod
    def scratch(planes, shape):
        return [pltpu.VMEM((n,) + shape, BF16) for n in (planes, planes + 1)] + [
            pltpu.SemaphoreType.DMA((planes,))
        ] * 4

    def up(self, j):
        s = self.sems
        peer = {"dp": self.device + 2}
        return remote(self.stack.at[j], self.came.at[j], s[0].at[j], s[1].at[j], peer)

    def down(self, j):
        s = self.sems
        slot = jnp.where(self.plane - 1 == j, self.planes, j)
        peer = {"dp": self.device - 2}
        return remote(self.stack.at[j], self.came.at[slot], s[2].at[j], s[3].at[j], peer)

    def start(self):
        last = self.planes - 1

        @pl.when(self.plane == 0)
        def _():
            for j in range(last, last - 1 if self.paced else 0, -1):
                self.up(j).start()

        @pl.when(self.plane == last)
        def _():
            for j in range(1 if self.paced else last):
                self.down(j).start()

    def advance(self, step):
        plane, last = self.plane, self.planes - 1
        low, high = last - step + plane, step - last + plane
        if self.paced:

            @pl.when(plane == 0)
            def _():
                self.up(last - step + 1).wait_send()
                self.up(last - step).start()

            @pl.when(plane == last)
            def _():
                self.down(step - 1).wait_send()
                self.down(step).start()

        @pl.when((plane >= 1) & (plane <= step))
        def _():
            self.up(low).wait_recv()
            self.stack[low] += self.came[low]
            self.up(low).start()

        @pl.when((plane < last) & (plane >= last - step))
        def _():
            self.down(high).wait_recv()
            self.stack[high] += self.came[high]
            self.down(high).start()

    def finish(self, out):
        plane, planes = self.plane, self.planes

        @pl.when(plane == 0)
        def _():
            self.down(plane).wait_recv()
            out[...] = self.stack[plane] + self.came[planes]

        @pl.when(plane == planes - 1)
        def _():
            self.up(plane).wait_recv()
            out[...] = self.stack[plane] + self.came[plane]

        @pl.when((plane > 0) & (plane < planes - 1))
        def _():
            self.up(plane).wait_recv()
            self.down(plane).wait_recv()
            total = self.stack[plane].astype(F32) + self.came[plane].astype(F32)
            out[...] = (total + self.came[planes].astype(F32)).astype(BF16)

        for j in range(planes):
            ups, downs = plane < j, plane > j
            if self.paced and j > 1:
                ups = ups & (plane > 0)
            if self.paced and j < planes - 2:
                downs = downs & (plane < planes - 1)
            pl.when(ups)(lambda j=j: self.up(j).wait_send())
            pl.when(downs)(lambda j=j: self.down(j).wait_send())

    def fill_rows(self, left, left_came, right, right_came):
        shard, planes = self.stack.shape[1], self.planes

        def compute(i):
            j = jnp.where(self.plane * 2 < planes, planes - 1 - i, i) if self.paced else i
            at = pl.ds(pl.multiple_of(j * shard, shard), shard)
            self.stack[j] = (
                dot(left[:, at], right[...], TN) + dot(left_came[:, at], right_came[...], TN)
            ).astype(BF16)

        if self.paced:
            compute(0)
            self.start()

        def body(i, carry):
            compute(i)
            return carry

        lax.fori_loop(1 if self.paced else 0, planes, body, 0)

    def fill_columns(self, left, left_came, right, right_came):
        shard = self.stack.shape[2]
        tile = 256

        def body(t, carry):
            at = pl.ds(pl.multiple_of(t * tile, tile), tile)
            term = dot(left[:, at], right[...], TN) + dot(left_came[:, at], right_came[...], TN)
            for j in range(self.planes):
                self.stack[j, at, :] = term[:, j * shard : (j + 1) * shard].astype(BF16)
            return carry

        lax.fori_loop(0, left.shape[1] // tile, body, 0)


class TensorSum:
    def __init__(self, scratch, mine, core, core_peer, y_peer):
        self.away, self.core_came, self.both, self.y_came = scratch[:4]
        self.sems = scratch[4:]
        self.mine = mine
        self.core, self.core_peer, self.y_peer = core, core_peer, y_peer
        self.chunks, self.half, self.width = self.away.shape

    @staticmethod
    def scratch(chunks, half, width):
        return [pltpu.VMEM((chunks, half, width), BF16)] * 4 + [
            pltpu.SemaphoreType.DMA((chunks,))
        ] * 4

    def over_core(self, i):
        s = self.sems
        return remote(self.away.at[i], self.core_came.at[i], s[0].at[i], s[1].at[i], self.core_peer)

    def over_y(self, i):
        s = self.sems
        return remote(self.both.at[i], self.y_came.at[i], s[2].at[i], s[3].at[i], self.y_peer)

    def add(self, i, value):
        self.mine[i % 2] = value
        self.away[i] = self.mine[i % 2, rows_of(1 - self.core, self.half), :].astype(BF16)
        self.over_core(i).start()
        if i > 0:
            self.pass_on(i - 1)
        if i == self.chunks - 1:
            self.pass_on(i)

    def pass_on(self, i):
        self.over_core(i).wait_recv()
        mine = self.mine[i % 2, rows_of(self.core, self.half), :]
        self.both[i] = (mine + self.core_came[i].astype(F32)).astype(BF16)
        self.over_y(i).start()

    def total(self, i):
        self.over_y(i).wait_recv()
        return self.both[i].astype(F32) + self.y_came[i].astype(F32)

    def finish(self):
        for i in range(self.chunks):
            self.over_core(i).wait_send()
            self.over_y(i).wait_send()


def roll_half(value):
    return pltpu.roll(value, value.shape[-1] // 2, 1)


def visible(shape, key0, row0, prefix):
    key_pos = key0 + lax.broadcasted_iota(jnp.int32, shape, 1)
    row_pos = row0 + lax.broadcasted_iota(jnp.int32, shape, 0)
    return (key_pos <= row_pos) | (key_pos < prefix)


def attn_fwd_kernel(*refs, group, kv_heads, repeat, width, tile, coef):
    refs = list(refs)

    def take(count):
        out = refs[:count]
        del refs[:count]
        return out

    prefix_ref, gain_ref, q_gain, k_gain = take(4)
    arrays = take(6)
    member = lax.axis_index("dp") % group
    arrays[3:5] = table_rows(arrays[3:5], member, arrays[0].shape[0])
    o_ref, lse_ref, all_out = take(3)
    outs = take(4)
    buffers = take(6)
    inputs = Staged(arrays, buffers, *take(1))
    x_ref, w_k, w_v, cos_ref, sin_ref, w_q = buffers
    out_buffers = take(4)
    h_ref, q_ref, q_raw, k_raw = out_buffers
    outputs = Staged(outs, out_buffers, *take(1), out=True)
    kv_ref, all_ref, all_sems, acc, send_x, recv_x, send_z, recv_z = take(8)
    send_down, send_rest, recv_rest = take(3)
    rows = q_ref.shape[0]
    kv_width = kv_heads * width
    planes = group // 2
    device = lax.axis_index("dp")
    member = device % group
    plane = member // 2
    x_at = member % 2
    x_other = device + 1 - 2 * x_at
    inner = plane < planes - 1
    prefix = prefix_ref[0]
    inputs.start()
    greet([({"dp": x_other}, True), ({"dp": device + 2}, inner), ({"dp": device - 2}, plane > 0)])

    def store(slot):
        return pltpu.make_async_copy(all_ref.at[slot], all_out.at[slot], all_sems.at[slot])

    def source(slot):
        return kv_ref if slot == 0 else all_ref.at[2 * slot]

    split = planes - 1 if planes > 2 else planes
    half = rows // 2
    parts = [pl.ds(0, half), pl.ds(half, rows - half)]

    def halves_over_x(slot):
        return range(1 if slot == split else 2)

    def to_x(slot, h):
        at = parts[h]
        to = all_ref.at[2 * slot + 1, at, :]
        i = 2 * slot + h
        return remote(source(slot).at[at, :], to, send_x.at[i], recv_x.at[i], {"dp": x_other})

    def to_z(slot, h):
        at = parts[h]
        to = all_ref.at[2 * slot, at, :]
        i = 2 * slot + h
        return remote(source(slot - 1).at[at, :], to, send_z.at[i], recv_z.at[i], {"dp": device + 2})

    def rest_to_z():
        return remote(
            all_ref.at[2 * split - 1, parts[1], :],
            all_ref.at[2 * split + 1, parts[1], :],
            send_rest,
            recv_rest,
            {"dp": device + 2},
        )

    def to_first(h):
        at = parts[h]
        to = all_ref.at[2, at, :]
        return remote(kv_ref.at[at, :], to, send_down.at[h], recv_z.at[2 + h], {"dp": device - 2})

    inputs.wait(x_ref, w_k, w_v, cos_ref, sin_ref)

    def rotate(u, gain, at):
        u = u * lax.rsqrt(jnp.mean(u * u, axis=1, keepdims=True) + EPS) * gain[...]
        return (u * cos_ref[at, :] + roll_half(u) * sin_ref[at, :]).astype(BF16)

    ones = jnp.ones((rows, width), BF16)
    row0 = member * rows

    def work(block, other, masked, start=False):
        key0 = other * rows

        def head_pair(h, carry):
            k = block[:, pl.ds(pl.multiple_of(h * width, width), width)]
            v = block[:, pl.ds(pl.multiple_of(kv_width + h * width, width), width)]
            v = jnp.concatenate([v, ones], axis=1)
            for g in range(repeat):
                head = h * repeat + g
                for at in range(0, rows, tile):
                    q = q_ref[at : at + tile, pl.ds(pl.multiple_of(head * width, width), width)]
                    p = jnp.exp2(dot(q, k, NT) * coef)
                    if masked:
                        p = jnp.where(visible(p.shape, key0, row0 + at, prefix), p, 0.0)
                    term = dot(p.astype(BF16), v)
                    if start:
                        acc[head, at : at + tile, :] = term
                    else:
                        acc[head, at : at + tile, :] += term
            return carry

        lax.fori_loop(0, kv_heads, head_pair, 0)

    for h in range(2):
        at = parts[h]
        x = x_ref[at, :].astype(F32)
        r = lax.rsqrt(jnp.mean(x * x, axis=1, keepdims=True) + EPS)
        h_ref[at, :] = (x * r * gain_ref[...]).astype(BF16)
        keys = dot(h_ref[at, :], w_k[...])
        k_raw[at, :] = keys
        for c in range(0, kv_width, width):
            kv_ref[at, c : c + width] = rotate(keys[:, c : c + width], k_gain, at)
        kv_ref[at, kv_width:] = dot(h_ref[at, :], w_v[...]).astype(BF16)
        to_x(0, h).start()
        if planes > 1:
            pl.when(inner)(lambda h=h: to_z(1, h).start())
            pl.when(plane == 1)(lambda h=h: to_first(h).start())

    inputs.wait(w_q)
    queries = dot(h_ref[...], w_q[...])
    q_raw[...] = queries
    for at in range(0, queries.shape[1], width):
        q_ref[:, at : at + width] = rotate(queries[:, at : at + width], q_gain, slice(None))
    outputs.start()
    all_ref[0] = kv_ref[...]
    store(0).start()
    work(kv_ref, member, True, True)

    def receive(slot):
        for h in range(2):
            to_z(slot, h).wait_recv()
            if slot < planes - 1:
                pl.when(inner & (plane >= slot))(lambda h=h: to_z(slot + 1, h).start())
            if h in halves_over_x(slot):
                to_x(slot, h).start()
        store(2 * slot).start()

    def attend(slot, index, there, first):
        if slot == 1:
            pl.when(plane == 0)(lambda: work(all_ref.at[index], first, True))
            pl.when(plane > 0)(lambda: work(all_ref.at[index], there, False))
        else:
            work(all_ref.at[index], there, slot == 0)

    def far(slot):
        for h in halves_over_x(slot):
            to_x(slot, h).wait_recv()
        if slot == split - 1:
            pl.when(plane == split - 1)(lambda: rest_to_z().start())
        if slot == split:
            rest_to_z().wait_recv()
        store(2 * slot + 1).start()
        attend(slot, 2 * slot + 1, 2 * (plane - slot) + 1 - x_at, 3 - x_at)

    if planes > 1:
        receive(1)
    far(0)
    for slot in range(1, planes):

        def step(slot=slot):
            attend(slot, 2 * slot, 2 * (plane - slot) + x_at, 2 + x_at)
            if slot + 1 < planes:
                pl.when(plane >= slot + 1)(lambda: receive(slot + 1))
            far(slot)

        if slot == 1:
            step()
        else:
            pl.when(plane >= slot)(step)

    for head in range(kv_heads * repeat):
        total = acc[head, :, width:]
        o_ref[:, head * width : (head + 1) * width] = (acc[head, :, :width] / total).astype(BF16)
        lse_ref[:, head * width : (head + 1) * width] = jnp.log2(total) * (1.0 / coef)

    outputs.wait()
    if split < planes:
        pl.when(plane == split - 1)(lambda: rest_to_z().wait_send())
    for slot in range(planes):

        @pl.when((plane >= slot) | (slot <= 1))
        def _(slot=slot):
            store(2 * slot).wait()
            store(2 * slot + 1).wait()
            for h in halves_over_x(slot):
                to_x(slot, h).wait_send()

    for slot in range(1, planes):

        @pl.when(inner & (plane >= slot - 1))
        def _(slot=slot):
            for h in range(2):
                to_z(slot, h).wait_send()

    if planes > 1:

        @pl.when(plane == 1)
        def _():
            for h in range(2):
                to_first(h).wait_send()


def attn_fwd(prefix, x, gain, w_query, key_weight, value_weight, q_gain, k_gain, cos, sin, group, dims):
    kv_heads, repeat, width = dims
    rows = x.shape[0]
    heads = kv_heads * repeat
    columns = heads * width
    planes = group // 2
    dma = pltpu.SemaphoreType.DMA
    block = (rows, 2 * kv_heads * width)
    staged = [x, key_weight, value_weight, cos, sin, w_query]
    table = jax.ShapeDtypeStruct((rows, width), F32)
    early = [
        jax.ShapeDtypeStruct(x.shape, BF16),
        jax.ShapeDtypeStruct((rows, columns), BF16),
        jax.ShapeDtypeStruct((rows, columns), F32),
        jax.ShapeDtypeStruct((rows, kv_heads * width), F32),
    ]
    return pl.pallas_call(
        functools.partial(
            attn_fwd_kernel,
            group=group,
            kv_heads=kv_heads,
            repeat=repeat,
            width=width,
            tile=min(rows, 256),
            coef=math.log2(math.e) / math.sqrt(width),
        ),
        out_shape=[
            jax.ShapeDtypeStruct((rows, columns), BF16),
            jax.ShapeDtypeStruct((rows, columns), F32),
            jax.ShapeDtypeStruct((group,) + block, BF16),
        ]
        + early,
        in_specs=[smem()] + vmem(3) + [ANYWHERE] * 6,
        out_specs=vmem(2) + [ANYWHERE] * 5,
        scratch_shapes=Staged.scratch([x, key_weight, value_weight, table, table, w_query])
        + Staged.scratch(early)
        + [pltpu.VMEM(block, BF16), pltpu.VMEM((group,) + block, BF16), dma((group,))]
        + [pltpu.VMEM((heads, rows, 2 * width), F32)]
        + [dma((2 * planes,))] * 4
        + [dma((2,)), dma, dma],
        compiler_params=pltpu.CompilerParams(
            vmem_limit_bytes=VMEM_LIMIT, collective_id=0, has_side_effects=True
        ),
        cost_estimate=COST,
        name="attn_fwd",
    )(prefix, gain, q_gain, k_gain, *staged)


def split_three(value):
    high = value.astype(BF16)
    left = value - high.astype(F32)
    mid = left.astype(BF16)
    return high.astype(F32), mid.astype(F32), (left - mid.astype(F32)).astype(BF16).astype(F32)


def back_kernel(
    *refs, group, planes, all_planes, shard, kv_heads, repeat, width, coef, scale, sums
):
    refs = list(refs)

    def take(count):
        out = refs[:count]
        del refs[:count]
        return out

    device = lax.axis_index("dp")
    member = device % group
    plane = member // 2
    last = planes - 1
    prefix_ref, up_ref, w_down_in, middle_in = take(4)
    if sums:
        hid_arrays = take(1)
    count = 12 if sums else 5
    arrays = take(count)
    dq_ref, grad_ref, up_came_ref, block_ref = take(4)
    if sums:
        w_down_ref, w_gate_ref, w_out_ref = take(3)
    a_ref, a_came_ref = take(2)
    if sums:
        hid_buffers = take(1)
        hid_sems = take(1)[0]
    buffers = take(count)
    inputs = Staged(arrays, buffers, *take(1))
    a_all_ref, qx_ref, dox_ref, kv_ref, hid_ref = buffers[:5]
    if sums:
        hid_came_ref = hid_buffers[0]
        og_ref, og_came_ref, gate_ref, h_ref, h_came_ref, heads_ref, heads_came_ref = buffers[5:]
    down_buf, down_sems, mine_ref, middle_buf, middle_sems = take(5)
    block_sems = take(3)
    total_scratch = take(8)
    own_ref, far_ref, xr_ref, zr_ref, first_ref = take(5)
    send_x, recv_x, send_z, recv_z, send_first, recv_first = take(6)
    swap_sems = take(2)
    a_scratch = take(6)
    rows = qx_ref.shape[1]
    kv_width = kv_heads * width
    if sums:
        gate_came_ref, send_gate, recv_gate = take(3)
        left = w_down_ref.shape[0]
        rest = pl.ds(hid_arrays[0].shape[1] - left, left)
        hid_inputs = Staged([h.at[:, rest] for h in hid_arrays], hid_buffers, hid_sems)
        down_sum, out_sum = (LineSum(take(6), device, plane, planes) for _ in range(2))
        piece = gate_came_ref.shape[2]
        pieces = gate_ref.shape[1] // piece
        gate_sums = [LineSum(take(6), device, plane, planes) for _ in range(pieces)]
    x_at = member % 2
    x_other = device + 1 - 2 * x_at
    inner = plane < last
    prefix = prefix_ref[0]

    core, core_peer, y_peer = tensor_peers()
    x_peer = {"dp": x_other}
    total = TensorSum(total_scratch, mine_ref, core, core_peer, y_peer)
    half = total.half
    parts, narrow = total.chunks, total.width

    def load(i):
        at = pl.ds(i * narrow, narrow)
        return pltpu.make_async_copy(w_down_in.at[:, at], down_buf.at[i % 2], down_sems.at[i % 2])

    def middle_load(i):
        at = pl.ds(i * narrow, narrow)
        return pltpu.make_async_copy(middle_in.at[:, at], middle_buf.at[i % 2], middle_sems.at[i % 2])

    def block_at(i):
        return block_ref.at[rows_of(core, half), pl.ds(i * narrow, narrow)]

    def block_store(i):
        return pltpu.make_async_copy(total.both.at[i], block_at(i), block_sems[0].at[i])

    def block_give(i):
        return remote(total.both.at[i], block_at(i), block_sems[1].at[i], block_sems[2].at[i], core_peer)

    def block_add(i):
        load(i).wait()
        total.add(i, dot(hid_ref[...], down_buf[i % 2]))
        if i + 2 < parts:
            load(i + 2).start()

    def block_finish(i):
        middle_load(i).wait()
        value = middle_buf[i % 2] + total.total(i)
        total.over_y(i).wait_send()
        total.both[i] = value.astype(BF16)
        if i + 2 < parts:
            middle_load(i + 2).start()
        block_store(i).start()
        block_give(i).start()

    inputs.start(a_all_ref)
    if sums:
        hid_inputs.start()
        inputs.start(hid_ref, *buffers[5:7])
    inputs.start(*buffers[1:4])
    if sums:
        inputs.start(*buffers[7:])
    else:
        inputs.start(hid_ref)
    for i in range(2):
        load(i).start()
        middle_load(i).start()
    greet(
        [
            (x_peer, True),
            (core_peer, True),
            (y_peer, True),
            ({"dp": device + 2}, inner),
            ({"dp": device - 2}, plane > 0),
        ]
    )

    def copy(src, dst, send, recv, there):
        return remote(src, dst, send, recv, {"dp": there})

    place = (x_at, core, x_peer, core_peer, all_planes, shard)
    d_attn = Columns(a_all_ref, a_ref, a_came_ref, a_scratch, *place)
    up_swap = copy(up_ref, up_came_ref, swap_sems[0], swap_sems[1], x_other)

    def gate_swap(k):
        part = gate_ref.at[:, pl.ds(k * piece, piece)]
        return copy(part, gate_came_ref.at[k], send_gate.at[k], recv_gate.at[k], x_other)

    def gate_start(k):
        gate_swap(k).wait_recv()
        part = gate_ref.at[:, pl.ds(k * piece, piece)]
        gate_sums[k].fill_rows(h_ref, h_came_ref, part, gate_came_ref.at[k])
        gate_sums[k].start()

    lane = lax.broadcasted_iota(jnp.int32, (rows, width), 1)
    minus = jnp.where(lane < 3, -1.0, 0.0).astype(BF16)
    row0 = member * rows

    def work(block, other, masked, out):
        key0 = other * rows

        def head_group(h, carry):
            k_at = pl.ds(pl.multiple_of(h * width, width), width)
            v_at = pl.ds(pl.multiple_of(kv_width + h * width, width), width)
            k = kv_ref[block, :, k_at]
            v = kv_ref[block, :, v_at]
            kx = jnp.concatenate([k, minus], axis=1)
            vx = jnp.concatenate([v, minus], axis=1)
            dk = jnp.zeros((rows, width), F32)
            dv = jnp.zeros((rows, width), F32)
            for g in range(repeat):
                head = h * repeat + g
                qx = qx_ref[head]
                dox = dox_ref[head]
                p = jnp.exp2(dot(qx, kx, NT) * coef)
                if masked:
                    p = jnp.where(visible(p.shape, key0, row0, prefix), p, 0.0)
                ds = (p * dot(dox, vx, NT)).astype(BF16)
                dv += dot(p.astype(BF16), dox[:, :width], TN)
                dk += dot(ds, qx[:, :width], TN)
                dq_ref[:, pl.ds(pl.multiple_of(head * width, width), width)] += dot(ds, k)
            out[:, k_at] = (dk * scale).astype(BF16)
            out[:, v_at] = dv.astype(BF16)
            return carry

        lax.fori_loop(0, kv_heads, head_group, 0)

    def far_swap(slot):
        return copy(far_ref.at[slot], xr_ref.at[slot], send_x.at[slot], recv_x.at[slot], x_other)

    def to_plane(slot):
        return copy(own_ref.at[slot], zr_ref.at[slot], send_z.at[slot], recv_z.at[slot], device - 2)

    def from_first():
        return copy(own_ref.at[1], first_ref, send_first, recv_first, device + 2)

    def attend(slot):
        there = 2 * (plane - slot)
        far, own = there + 1 - x_at, there + x_at

        def both(far, own, masked):
            work(2 * slot + 1, far, masked, far_ref.at[slot])
            far_swap(slot).start()
            work(2 * slot, own, masked, own_ref.at[slot])

        if slot == 0:
            both(far, own, True)
        elif slot == 1:
            pl.when(plane == 0)(lambda: both(3 - x_at, 2 + x_at, True))
            pl.when(plane > 0)(lambda: both(far, own, False))
        else:
            pl.when(plane >= slot)(lambda: both(far, own, False))

    def pass_back(slot):
        def go():
            far_swap(slot).wait_recv()
            own_ref[slot] += xr_ref[slot]
            if slot < last:

                @pl.when(inner & (plane >= slot))
                def _():
                    to_plane(slot + 1).wait_recv()
                    own_ref[slot] += zr_ref[slot + 1]

            if slot == 1:
                pl.when(plane == 0)(lambda: from_first().start())
                pl.when(plane > 0)(lambda: to_plane(slot).start())
            else:
                to_plane(slot).start()

        if slot == 1:
            go()
        else:
            pl.when(plane >= slot)(go)

    dq_ref[...] = jnp.zeros_like(dq_ref)
    inputs.wait(a_all_ref)
    d_attn.start()
    inputs.wait(hid_ref)
    if sums:
        hid_inputs.wait()
        inputs.wait(og_ref, og_came_ref)
        down_sum.fill_columns(hid_ref.at[:, rest], hid_came_ref, og_ref, og_came_ref)
        down_sum.start()
    inputs.wait(*buffers[1:4])
    attend(last)
    d_attn.forward()
    if sums:
        inputs.wait(*buffers[7:])
        gate_swap(0).start()
    d_attn.store()
    pending = list(range(last, 0, -1))
    steps = range(1, last)
    adds = list(range(parts))
    share = -(-parts // last)
    for slot in range(last - 1, -1, -1):
        attend(slot)
        if slot == last - 1:
            if sums:
                d_attn.over_core().wait_recv()
                out_sum.fill_columns(heads_ref, heads_came_ref, a_ref, a_came_ref)
                out_sum.start()
                down_sum.advance(1)
                gate_start(0)
                gate_swap(1).start()
            pass_back(pending.pop(0))
        if slot == last - 2:
            if sums:
                for step in steps[1:]:
                    down_sum.advance(step)
                out_sum.advance(1)
                gate_start(1)
                gate_swap(2).start()
                gate_sums[0].advance(1)
            pass_back(pending.pop(0))
        for i in adds[:share]:
            block_add(i)
        del adds[:share]
    for i in adds:
        block_add(i)
    if sums:
        for step in steps[1:]:
            out_sum.advance(step)
            gate_sums[0].advance(step)
    while pending:
        pass_back(pending.pop(0))
    if sums:
        gate_start(2)
    up_swap.start()
    if sums:
        gate_sums[1].advance(1)
    for i in range(parts // 2):
        block_finish(i)
    if sums:
        for step in steps[1:]:
            gate_sums[1].advance(step)
        gate_sums[2].advance(1)
    for i in range(parts // 2, parts):
        block_finish(i)
    if sums:
        for step in steps[1:]:
            gate_sums[2].advance(step)
    dq_ref[...] = dq_ref[...] * scale

    far_swap(0).wait_recv()
    grad_ref[...] = own_ref[0].astype(F32) + xr_ref[0].astype(F32)
    if last > 0:

        @pl.when(inner)
        def _():
            to_plane(1).wait_recv()
            grad_ref[...] += zr_ref[1].astype(F32)

        @pl.when(plane == 1)
        def _():
            from_first().wait_recv()
            grad_ref[...] += first_ref[...].astype(F32)

    if sums:
        down_sum.finish(w_down_ref)
        out_sum.finish(w_out_ref)
        for k in range(pieces):
            gate_sums[k].finish(w_gate_ref.at[:, pl.ds(k * piece, piece)])
            gate_swap(k).wait_send()
    else:
        d_attn.over_core().wait_recv()
    up_swap.wait_recv()
    up_swap.wait_send()
    for i in range(parts):
        total.over_core(i).wait_send()
        block_store(i).wait()
        block_give(i).wait_recv()
        block_give(i).wait_send()
    d_attn.over_x().wait_send()
    d_attn.over_core().wait_send()
    for slot in range(planes):
        if slot <= 1:
            far_swap(slot).wait_send()
        else:
            pl.when(plane >= slot)(lambda slot=slot: far_swap(slot).wait_send())
        if slot >= 1:
            pl.when(plane >= slot)(lambda slot=slot: to_plane(slot).wait_send())
    if last > 0:
        pl.when(plane == 0)(lambda: from_first().wait_send())


def back(prefix, qx, dox, kv_all, shared, grads, group, all_planes, shard, pieces, dims):
    kv_heads, repeat, width = dims
    rows = qx.shape[1]
    columns = kv_heads * repeat * width
    planes = group // 2
    block = kv_all.shape[1:]
    dma = pltpu.SemaphoreType.DMA
    d_attn, d_up, hidden, w_down, middle = shared
    half, model = middle.shape
    parts = 8
    narrow = model // parts
    units = d_up.shape[1]
    cut_shape = jax.ShapeDtypeStruct((rows, all_planes * shard), BF16)
    out_shape = [jax.ShapeDtypeStruct((rows, columns), F32), jax.ShapeDtypeStruct(block, F32)]
    out_shape += [jax.ShapeDtypeStruct(d_up.shape, BF16), jax.ShapeDtypeStruct((rows, model), BF16)]
    scratch = [pltpu.VMEM((planes,) + block, BF16)] * 4 + [pltpu.VMEM(block, BF16)]
    scratch += [dma((planes,))] * 4 + [dma, dma] + [dma] * 2
    scratch += Columns.scratch(rows // 2, all_planes * shard)
    staged = [d_attn, qx, dox, kv_all, hidden]
    args = [prefix, d_up, w_down, middle]
    first = []
    if grads is not None:
        args += grads[:1]
        staged += grads[1:]
        first = [pltpu.VMEM(cut_shape.shape, BF16)] * 2
        first += [pltpu.VMEM((rows, units // pieces), BF16), dma((1,))]
    else:
        out_shape += [cut_shape] * 2
    args += staged
    product = [pltpu.VMEM((2, units, narrow), BF16), dma((2,)), pltpu.VMEM((2, rows, narrow), F32)]
    product += [pltpu.VMEM((2, half, narrow), F32), dma((2,))] + [dma((parts,))] * 3
    product += TensorSum.scratch(parts, half, narrow)
    scratch = first + Staged.scratch(staged) + product + scratch
    if grads is not None:
        piece = units // pieces
        shapes = (piece, shard), (shard, units), (columns, shard)
        out_shape += [jax.ShapeDtypeStruct(s, BF16) for s in shapes]
        scratch += [pltpu.VMEM((pieces, rows, piece), BF16)] + [dma((pieces,))] * 2
        for shape in [(piece, shard), (columns, shard)] + [(shard, piece)] * pieces:
            scratch += LineSum.scratch(planes, shape)
    return pl.pallas_call(
        functools.partial(
            back_kernel,
            group=group,
            planes=planes,
            all_planes=all_planes,
            shard=shard,
            kv_heads=kv_heads,
            repeat=repeat,
            width=width,
            coef=math.log2(math.e) / math.sqrt(width),
            scale=1.0 / math.sqrt(width),
            sums=grads is not None,
        ),
        out_shape=out_shape,
        in_specs=[smem()] + [ANYWHERE] * (len(args) - 1),
        out_specs=vmem(2) + [ANYWHERE] * 2 + vmem(len(out_shape) - 4),
        scratch_shapes=scratch,
        compiler_params=pltpu.CompilerParams(
            vmem_limit_bytes=BACK_VMEM_LIMIT, collective_id=1, has_side_effects=True
        ),
        cost_estimate=COST,
        name="back",
    )(*args)


def smem():
    return pl.BlockSpec(memory_space=pltpu.SMEM)


def out_kernel(*refs, planes, shard, blocks):
    refs = list(refs)

    def take(count):
        out = refs[:count]
        del refs[:count]
        return out

    arrays = take(4)
    gain_ref, w_down_ref = take(2)
    middle_ref, h_ref, d_hidden_out, og_keep, og_came, heads_came = take(6)
    buffers = take(4)
    heads_ref, w_ref, og_ref, x_ref = buffers
    inputs = Staged(arrays, buffers, *take(1))
    d_hidden_ref, d_hidden_sem = take(2)
    down_buf, down_sems, whole_ref, h_send, h_recv, heads_send, heads_recv = take(7)
    scratch = refs
    device = lax.axis_index("dp")
    core, core_peer, y_peer = tensor_peers()
    x_at = device % 2
    x_peer = {"dp": device + 1 - 2 * x_at}
    half = middle_ref.shape[0]
    total = TensorSum(scratch[:8], None, core, core_peer, y_peer)
    step = half // blocks
    place = (x_at, core, x_peer, core_peer, planes, shard)
    og = Columns(og_ref, og_keep, og_came, scratch[8:14], *place)
    tiles = down_sems.shape[0]
    tile = down_buf.shape[0] // tiles

    def load(t):
        at = pl.ds(t * tile, tile)
        return pltpu.make_async_copy(w_down_ref.at[at, :], down_buf.at[at, :], down_sems.at[t])

    inputs.start()
    for t in range(tiles):
        load(t).start()
    greet([(x_peer, True), (core_peer, True), (y_peer, True)])
    heads_swap = remote(heads_ref, heads_came, heads_send, heads_recv, x_peer)
    inputs.wait(heads_ref, w_ref)
    heads_swap.start()

    def rows_at(which, b):
        return pl.ds(pl.multiple_of(which * half + b * step, step), step)

    whole_ref[...] = dot(heads_ref[...], w_ref[...])
    for b in range(blocks):
        total.away[b] = whole_ref[rows_at(1 - core, b), :].astype(BF16)
        total.over_core(b).start()
    for b in range(blocks):
        total.over_core(b).wait_recv()
        mine = whole_ref[rows_at(core, b), :] + total.core_came[b].astype(F32)
        total.both[b] = mine.astype(BF16)
        total.over_y(b).start()
    inputs.wait(og_ref)
    og.start()
    og.store()
    for t in range(tiles):
        at = slice(t * tile, (t + 1) * tile)
        load(t).wait()
        d_hidden_ref[:, at] = dot(og_ref[...], down_buf[at, :], NT)
    d_hidden_copy = pltpu.make_async_copy(d_hidden_ref, d_hidden_out, d_hidden_sem)
    d_hidden_copy.start()
    inputs.wait(x_ref)

    def to_core(b):
        rows = h_ref.at[rows_at(core, b), :]
        return remote(rows, rows, h_send.at[b], h_recv.at[b], core_peer)

    for b in range(blocks):
        at = rows_at(core, b)
        v = x_ref[at, :].astype(F32) + total.total(b)
        middle_ref[b * step : (b + 1) * step, :] = v
        r = lax.rsqrt(jnp.mean(v * v, axis=1, keepdims=True) + EPS)
        h_ref[at, :] = (v * r * gain_ref[...]).astype(BF16)
        to_core(b).start()
    og.forward()
    og.finish()
    d_hidden_copy.wait()
    heads_swap.wait_recv()
    heads_swap.wait_send()
    for b in range(blocks):
        to_core(b).wait_recv()
        to_core(b).wait_send()
    total.finish()


def attention_out(heads, w_out, x, gain, out_grad, w_down, planes, shard):
    rows, model = x.shape
    half = rows // 2
    units = w_down.shape[0]
    blocks = 4
    tiles = units // math.gcd(units, 256)
    dma = pltpu.SemaphoreType.DMA
    cut_shape = jax.ShapeDtypeStruct((rows, planes * shard), BF16)
    return pl.pallas_call(
        functools.partial(out_kernel, planes=planes, shard=shard, blocks=blocks),
        out_shape=[
            jax.ShapeDtypeStruct((half, model), F32),
            jax.ShapeDtypeStruct((rows, model), BF16),
            jax.ShapeDtypeStruct((rows, units), F32),
        ]
        + [cut_shape] * 2
        + [jax.ShapeDtypeStruct(heads.shape, BF16)],
        in_specs=[ANYWHERE] * 4 + vmem(1) + [ANYWHERE],
        out_specs=vmem(2) + [ANYWHERE] + vmem(3),
        scratch_shapes=Staged.scratch([heads, w_out, out_grad, x])
        + [pltpu.VMEM((rows, units), F32), dma]
        + [pltpu.VMEM((units, model), BF16), dma((tiles,))]
        + [pltpu.VMEM((rows, model), F32), dma((blocks,)), dma((blocks,)), dma, dma]
        + TensorSum.scratch(blocks, half // blocks, model)
        + Columns.scratch(half, planes * shard),
        compiler_params=pltpu.CompilerParams(
            vmem_limit_bytes=VMEM_LIMIT, collective_id=4, has_side_effects=True
        ),
        cost_estimate=COST,
        name="attention_out",
    )(heads, w_out, out_grad, x, gain, w_down)


def middle_kernel(*refs, planes, shard, heads, width, pieces, blocks, sums):
    refs = list(refs)

    def take(count):
        out = refs[:count]
        del refs[:count]
        return out

    w_gate_ref, w_up_ref, gain_ref = take(3)
    count = 10 if sums else 8
    arrays = take(count)
    outs = take(3)
    hid_came_ref, a_ref, gain_out_ref, qx_ref, dox_ref, h_keep, h_came = take(7)
    if sums:
        down_outs = take(pieces - 1)
    buffers = take(count)
    inputs = Staged(arrays, buffers, *take(1))
    h_ref, d_ref, middle_ref, og_ref, w_out_ref, q_ref, o_ref, lse_ref = buffers[:8]
    if sums:
        og_keep, og_came = buffers[8:]
    out_buffers = take(3)
    hid_ref, gate_ref, up_ref = out_buffers
    outputs = Staged(outs, out_buffers, *take(1), out=True)
    gate_buf, up_buf, load_sems, c_ref, mine_ref = take(5)
    hid_send, hid_recv, a_send, a_recv = take(4)
    sum_scratch, h_scratch = take(8), take(6)
    device = lax.axis_index("dp")
    core, core_peer, y_peer = tensor_peers()
    plane = device // 2
    x_at = device % 2
    x_peer = {"dp": device + 1 - 2 * x_at}
    meets = [(x_peer, True), (core_peer, True), (y_peer, True)]
    h_two = Columns(h_ref, h_keep, h_came, h_scratch, x_at, core, x_peer, core_peer, planes, shard)
    half = middle_ref.shape[0]
    total = TensorSum(sum_scratch, mine_ref, core, core_peer, y_peer)
    chunks, columns = total.chunks, total.width
    units = hid_ref.shape[1]
    piece = units // pieces
    tile = 256
    tiles = units // tile
    if sums:
        downs = [LineSum(take(6), device, plane, planes) for _ in range(pieces - 1)]
        meets += [({"dp": device + 2}, plane < planes - 1), ({"dp": device - 2}, plane > 0)]

    def loads(t):
        at = pl.ds(t * tile, tile)
        return (
            pltpu.make_async_copy(w_gate_ref.at[:, at], gate_buf.at[:, at], load_sems.at[2 * t]),
            pltpu.make_async_copy(w_up_ref.at[:, at], up_buf.at[:, at], load_sems.at[2 * t + 1]),
        )

    inputs.start(h_ref)
    for t in range(tiles):
        for load in loads(t):
            load.start()
        if t == 0:
            inputs.start(d_ref)
    inputs.start(*buffers[2:])
    greet(meets)
    inputs.wait(h_ref)

    def swap(k):
        at = pl.ds(k * tile, tile)
        return remote(hid_ref.at[:, at], hid_came_ref.at[:, at], hid_send.at[k], hid_recv.at[k], x_peer)

    for t in range(tiles):
        for load in loads(t):
            load.wait()
        if t == 0:
            inputs.wait(d_ref)
        at = slice(t * tile, (t + 1) * tile)
        gate = dot(h_ref[...], gate_buf[:, at])
        up = dot(h_ref[...], up_buf[:, at])
        sig = 0.5 * jnp.tanh(0.5 * gate) + 0.5
        silu = gate * sig
        d = d_ref[:, at]
        hid_ref[:, at] = (silu * up).astype(BF16)
        up_ref[:, at] = (d * silu).astype(BF16)
        gate_ref[:, at] = (d * up * (sig * (1.0 + gate * (1.0 - sig)))).astype(BF16)
        swap(t).start()

    outputs.start()
    inputs.wait(*buffers[2:])

    def down_start(k):
        if sums:
            at = pl.ds(k * piece, piece)
            for t in range(k * piece // tile, (k + 1) * piece // tile):
                swap(t).wait_recv()
            downs[k].fill_columns(hid_ref.at[:, at], hid_came_ref.at[:, at], og_keep, og_came)
            downs[k].start()

    def down_advance(k, step):
        if sums and step <= planes - 2:
            downs[k].advance(step)

    for i in range(chunks):
        at = slice(i * columns, (i + 1) * columns)
        total.add(i, dot(gate_ref[...], gate_buf[at, :], NT) + dot(up_ref[...], up_buf[at, :], NT))
        if i == chunks // 2:
            down_start(0)
    for i in range(chunks):
        if i == chunks // 4:
            down_start(1)
            h_two.start()
        if i == chunks // 2:
            down_advance(0, 1)
        c_ref[:, i * columns : (i + 1) * columns] = total.total(i)
    down_advance(0, 2)

    step = half // blocks

    def to_core(b):
        rows = a_ref.at[pl.ds(pl.multiple_of(core * half + b * step, step), step), :]
        return remote(rows, rows, a_send.at[b], a_recv.at[b], core_peer)

    gain_out_ref[...] = jnp.zeros_like(gain_out_ref)
    for b in range(blocks):
        at = slice(b * step, (b + 1) * step)
        whole_at = pl.ds(pl.multiple_of(core * half + b * step, step), step)
        c = c_ref[at, :]
        v = middle_ref[at, :]
        r = lax.rsqrt(jnp.mean(v * v, axis=1, keepdims=True) + EPS)
        n = v * r
        gain_out_ref[...] += jnp.sum(c * n, axis=0, keepdims=True)
        gc = c * gain_ref[...]
        d = r * (gc - n * jnp.mean(n * gc, axis=1, keepdims=True)) + og_ref[whole_at, :].astype(F32)
        a_ref[whole_at, :] = d.astype(BF16)
        to_core(b).start()

    lane = lax.broadcasted_iota(jnp.int32, (half, width), 1)

    def extra(value):
        a, b, c = split_three(value)
        return jnp.where(lane == 0, a, jnp.where(lane == 1, b, jnp.where(lane == 2, c, 0.0))).astype(BF16)

    def prepare(which):
        at_rows = rows_of(which, half)
        d_heads = dot(a_ref[at_rows, :], w_out_ref[...], NT)
        for head in range(heads):
            at = slice(head * width, (head + 1) * width)
            qx_ref[head, at_rows, :width] = q_ref[at_rows, at]
            qx_ref[head, at_rows, width:] = extra(lse_ref[at_rows, at])
            d = d_heads[:, at].astype(BF16)
            delta = jnp.sum(d.astype(F32) * o_ref[at_rows, at].astype(F32), axis=1, keepdims=True)
            dox_ref[head, at_rows, :width] = d
            dox_ref[head, at_rows, width:] = extra(jnp.broadcast_to(delta, (half, width)))

    down_advance(1, 1)
    h_two.store()
    prepare(core)
    h_two.forward()
    for b in range(blocks):
        to_core(b).wait_recv()
    prepare(1 - core)
    down_advance(1, 2)
    for b in range(blocks):
        to_core(b).wait_send()
    total.finish()
    h_two.finish()
    outputs.wait()
    for t in range(tiles):
        if t >= (pieces - 1) * piece // tile or not sums:
            swap(t).wait_recv()
        swap(t).wait_send()
    if sums:
        for k in range(pieces - 1):
            for step in range(3, planes - 1):
                downs[k].advance(step)
            downs[k].finish(down_outs[k])


def middle_of(w_gate, w_up, h_two, d_hidden, middle, out_grad, gain, w_out, q, out, lse, cuts, pieces, planes, shard, width):
    half, model = middle.shape
    rows, units = d_hidden.shape
    columns = q.shape[1]
    heads = columns // width
    chunks, blocks = 4, 4
    dma = pltpu.SemaphoreType.DMA
    staged = [h_two, d_hidden, middle, out_grad, w_out, q, out, lse] + ([] if cuts is None else cuts)
    args = [w_gate, w_up, gain, *staged]
    unit_shape = jax.ShapeDtypeStruct((rows, units), BF16)
    out_shape = [unit_shape] * 4 + [
        jax.ShapeDtypeStruct((rows, model), BF16),
        jax.ShapeDtypeStruct((1, model), F32),
    ]
    out_shape += [jax.ShapeDtypeStruct((heads, rows, 2 * width), BF16)] * 2
    out_shape += [jax.ShapeDtypeStruct((rows, planes * shard), BF16)] * 2
    scratch = Staged.scratch(staged) + Staged.scratch([unit_shape] * 3)
    scratch += [pltpu.VMEM((model, units), BF16)] * 2 + [dma((2 * units // 256,))]
    scratch += [pltpu.VMEM((half, model), F32), pltpu.VMEM((2, rows, model // chunks), F32)]
    scratch += [dma((units // 256,))] * 2 + [dma((blocks,))] * 2
    scratch += TensorSum.scratch(chunks, half, model // chunks)
    scratch += Columns.scratch(half, planes * shard)
    if cuts is not None:
        out_shape += [jax.ShapeDtypeStruct((units // pieces, shard), BF16)] * (pieces - 1)
        scratch += LineSum.scratch(planes, (units // pieces, shard)) * (pieces - 1)
    return pl.pallas_call(
        functools.partial(
            middle_kernel,
            planes=planes,
            shard=shard,
            heads=heads,
            width=width,
            pieces=pieces,
            blocks=blocks,
            sums=cuts is not None,
        ),
        out_shape=out_shape,
        in_specs=[ANYWHERE] * 2 + vmem(1) + [ANYWHERE] * len(staged),
        out_specs=[ANYWHERE] * 3 + vmem(len(out_shape) - 3),
        scratch_shapes=scratch,
        compiler_params=pltpu.CompilerParams(
            vmem_limit_bytes=BACK_VMEM_LIMIT, collective_id=2, has_side_effects=True
        ),
        cost_estimate=COST,
        name="middle",
    )(*args)


def through_rope(d_ref, raw_ref, gain, cos, sin, out_ref, width, plain):
    columns = d_ref.shape[1]
    total = jnp.zeros((1, width), F32)
    for at in range(0, columns - plain, width):
        d = d_ref[:, at : at + width]
        c = d * cos - roll_half(d) * sin
        v = raw_ref[:, at : at + width]
        r = lax.rsqrt(jnp.mean(v * v, axis=1, keepdims=True) + EPS)
        n = v * r
        total = total + jnp.sum(c * n, axis=0, keepdims=True)
        gc = gain * c
        out_ref[:, at : at + width] = (r * (gc - n * jnp.mean(n * gc, axis=1, keepdims=True))).astype(BF16)
    if plain:
        out_ref[:, columns - plain :] = d_ref[:, columns - plain :].astype(BF16)
    return total


def front_kernel(*refs, dp_size, group, planes, shard, chunks, blocks, sums):
    refs = list(refs)

    def take(count):
        out = refs[:count]
        del refs[:count]
        return out

    q_gain, k_gain, attn_gain, mlp_gain_ref, add_array = take(5)
    count = 15 if sums else 11
    arrays = take(count)
    arrays[2:4] = table_rows(arrays[2:4], lax.axis_index("dp") % group, arrays[0].shape[0])
    x_grad, gains = take(2)
    if sums:
        w_up_out, w_q_out, w_kv_out = take(3)
    dq_ref, dq_came, dkv_ref, dkv_came, one_ref, one_came = take(6)
    buffers = take(count)
    inputs = Staged(arrays, buffers, *take(1))
    dkv_in, k_raw, cos_ref, sin_ref, dq_in, q_raw, one_all = buffers[:7]
    x_ref, w_q, w_k, w_v = buffers[7:11]
    if sums:
        two_ref, two_came, up_ref, up_came = buffers[11:]
    mine, gain_came, c_ref, add_ref, add_sem = take(5)
    swap_sems, one_sems, gain_sems = take(4), take(2), take(2)
    one_sum_scratch, one_scratch = take(8), take(6)
    half = x_ref.shape[0] // 2
    model = x_ref.shape[1]
    width = model // chunks
    head = cos_ref.shape[1]
    kv_width = w_k.shape[1]

    device = lax.axis_index("dp")
    core, core_peer, y_peer = tensor_peers()
    x_at = device % 2
    x_peer = {"dp": device + 1 - 2 * x_at}
    plane = device // 2
    one = Columns(one_all, one_ref, one_came, one_scratch, x_at, core, x_peer, core_peer, planes, shard)
    bits = [1 << i for i in range(dp_size.bit_length() - 1)]
    dp_peers = [{"dp": device + bit - 2 * bit * ((device // bit) % 2)} for bit in bits]
    gain_peers = [core_peer, y_peer] + dp_peers
    meets = [(peer, True) for peer in gain_peers]
    if sums:
        up_sum, q_sum, kv_sum = (LineSum(take(6), device, plane, planes, True) for _ in range(3))
        meets += [({"dp": device + 2}, plane < planes - 1), ({"dp": device - 2}, plane > 0)]

    mine_rows = rows_of(core, half)
    add_load = pltpu.make_async_copy(add_array.at[mine_rows, :], add_ref, add_sem)
    inputs.start(one_all)
    if sums:
        inputs.start(*buffers[11:])
    inputs.start(*buffers[:6])
    inputs.start(*buffers[7:11])
    add_load.start()
    greet(meets)
    inputs.wait(one_all)
    one.start()
    if sums:
        inputs.wait(*buffers[11:])
        up_sum.fill_rows(two_ref, two_came, up_ref, up_came)
    inputs.wait(*buffers[:6])
    cos, sin = cos_ref[...], sin_ref[...]
    k_total = through_rope(dkv_in, k_raw, k_gain[...], cos, sin, dkv_ref, head, kv_width)
    kv_swap = remote(dkv_ref, dkv_came, swap_sems[0], swap_sems[1], x_peer)
    kv_swap.start()
    q_total = through_rope(dq_in, q_raw, q_gain[...], cos, sin, dq_ref, head, 0)
    q_swap = remote(dq_ref, dq_came, swap_sems[2], swap_sems[3], x_peer)
    q_swap.start()
    inputs.wait(*buffers[7:11])

    one_sum = TensorSum(one_sum_scratch, mine, core, core_peer, y_peer)
    x = x_ref[...].astype(F32)
    r = lax.rsqrt(jnp.mean(x * x, axis=1, keepdims=True) + EPS)
    for i in range(chunks):
        at = slice(i * width, (i + 1) * width)
        part = (
            dot(dq_ref[...], w_q[at, :], NT)
            + dot(dkv_ref[:, :kv_width], w_k[at, :], NT)
            + dot(dkv_ref[:, kv_width:], w_v[at, :], NT)
        )
        one_sum.add(i, part)
        gains[0, :, at] = jnp.sum(part * (x_ref[:, at].astype(F32) * r), axis=0, keepdims=True)
    gains[0, :, model : 2 * model] = 0.5 * mlp_gain_ref[...]
    gains[0, :, 2 * model : 2 * model + head] = q_total
    gains[0, :, 2 * model + head :] = k_total
    one.forward()
    one.store()

    def gain_swap(k):
        return remote(
            gains.at[k], gain_came.at[k], gain_sems[0].at[k], gain_sems[1].at[k], gain_peers[k]
        )

    def gain_add(k):
        gain_swap(k).wait_recv()
        gains[k + 1] = gains[k] + gain_came[k]
        if k + 1 < len(gain_peers):
            gain_swap(k + 1).start()

    gain_swap(0).start()

    def advance(line, step):
        if sums and step <= planes - 2:
            line.advance(step)

    gain_add(0)
    if sums:
        advance(up_sum, 1)
        kv_swap.wait_recv()
        one.over_core().wait_recv()
        kv_sum.fill_rows(one_ref, one_came, dkv_ref, dkv_came)
    gain_add(1)
    if sums:
        q_swap.wait_recv()
        q_sum.fill_rows(one_ref, one_came, dq_ref, dq_came)
        advance(up_sum, 2)
    gain_add(2)

    def give(out, sems):
        rows = out.at[mine_rows, :]
        return remote(rows, rows, sems[0], sems[1], core_peer)

    for i in range(chunks):
        c_ref[:, i * width : (i + 1) * width] = one_sum.total(i)
    add_load.wait()
    step = half // blocks
    for b in range(blocks):
        at = slice(b * step, (b + 1) * step)
        whole_at = pl.ds(pl.multiple_of(core * half + b * step, step), step)
        v = x_ref[whole_at, :].astype(F32)
        v_r = lax.rsqrt(jnp.mean(v * v, axis=1, keepdims=True) + EPS)
        n = v * v_r
        gc = c_ref[at, :] * attn_gain[...]
        d = v_r * (gc - n * jnp.mean(n * gc, axis=1, keepdims=True))
        x_grad[whole_at, :] = (d + add_ref[at, :].astype(F32)).astype(BF16)
    give(x_grad, one_sems).start()
    for k in range(3, len(gain_peers)):
        gain_add(k)
    if sums:
        advance(kv_sum, 1)
        advance(q_sum, 1)
    if sums:
        advance(kv_sum, 2)
        advance(q_sum, 2)
        for line in (up_sum, kv_sum, q_sum):
            for step in range(3, planes - 1):
                advance(line, step)
        up_sum.finish(w_up_out)
        kv_sum.finish(w_kv_out)
        q_sum.finish(w_q_out)
    else:
        kv_swap.wait_recv()
        q_swap.wait_recv()
        one.over_core().wait_recv()
    one.over_x().wait_send()
    one.over_core().wait_send()
    kv_swap.wait_send()
    q_swap.wait_send()
    give(x_grad, one_sems).wait_recv()
    give(x_grad, one_sems).wait_send()
    for k in range(len(gain_peers)):
        gain_swap(k).wait_send()
    one_sum.finish()


def front(dq, dkv, q_raw, k_raw, q_gain, k_gain, cos, sin, h_one, weights, x, d_attn, attn_gain, mlp_gain, grads, dp_size, group, shard):
    rows, model = x.shape
    half = rows // 2
    planes = dp_size // 2
    chunks = 4
    width = model // chunks
    stages = dp_size.bit_length() + 1
    dma = pltpu.SemaphoreType.DMA
    gains = (2 * model + 2 * cos.shape[1],)
    staged = [dkv, k_raw, cos, sin, dq, q_raw, h_one, x, *weights]
    if grads is not None:
        staged += grads
    args = [q_gain, k_gain, attn_gain, mlp_gain, d_attn, *staged]
    cut_shape = jax.ShapeDtypeStruct((rows, planes * shard), BF16)
    whole = jax.ShapeDtypeStruct((rows, model), BF16)
    q_shape, kv_shape = jax.ShapeDtypeStruct(dq.shape, BF16), jax.ShapeDtypeStruct(dkv.shape, BF16)
    out_shape = [whole, jax.ShapeDtypeStruct((stages + 1, 1) + gains, F32)]
    kept = [q_shape, q_shape, kv_shape, kv_shape, cut_shape, cut_shape]
    table = jax.ShapeDtypeStruct((rows, cos.shape[1]), F32)
    scratch = Staged.scratch(staged[:2] + [table, table] + staged[4:])
    scratch += [pltpu.VMEM((2, rows, width), F32)]
    scratch += [pltpu.VMEM((stages, 1) + gains, F32), pltpu.VMEM((half, model), F32)]
    scratch += [pltpu.VMEM((half, model), BF16), dma]
    scratch += [dma] * 6 + [dma((stages,))] * 2
    scratch += TensorSum.scratch(chunks, half, width)
    scratch += Columns.scratch(half, planes * shard)
    if grads is None:
        out_shape += kept
    else:
        scratch = [pltpu.VMEM(s.shape, s.dtype) for s in kept] + scratch
        for columns in (grads[2].shape[1], dq.shape[1], dkv.shape[1]):
            out_shape.append(jax.ShapeDtypeStruct((shard, columns), BF16))
            scratch += LineSum.scratch(planes, (shard, columns))
    return pl.pallas_call(
        functools.partial(
            front_kernel,
            dp_size=dp_size,
            group=group,
            planes=planes,
            shard=shard,
            chunks=chunks,
            blocks=4,
            sums=grads is not None,
        ),
        out_shape=out_shape,
        in_specs=vmem(4) + [ANYWHERE] * (len(args) - 4),
        out_specs=vmem(len(out_shape)),
        scratch_shapes=scratch,
        compiler_params=pltpu.CompilerParams(
            vmem_limit_bytes=BACK_VMEM_LIMIT, collective_id=3, has_side_effects=True
        ),
        cost_estimate=COST,
        name="front",
    )(*args)


def widen_kernel(*refs, results, gains):
    refs = list(refs)

    def take(count):
        out = refs[:count]
        del refs[:count]
        return out

    count = 1 + max(i for parts in results for i, _ in parts)
    block_in = take(1)[0]
    arrays = take(count)
    if gains:
        gain_in = take(1)[0]
    block_out = take(1)[0]
    outs = take(len(results))
    if gains:
        attn_out, mlp_out, q_out, k_out = take(4)
    buffers = take(count)
    inputs = Staged(arrays, buffers, *take(1))
    out_buffers = take(len(results))
    outputs = Staged(outs, out_buffers, *take(1), out=True)
    block, block_sems = take(2)
    if gains:
        gain_ref, gain_sem = take(2)
        gain_load = pltpu.make_async_copy(gain_in.at[gain_in.shape[0] - 1], gain_ref, gain_sem)
        gain_load.start()
    block_load = pltpu.make_async_copy(block_in, block, block_sems.at[0])
    block_copy = pltpu.make_async_copy(block, block_out, block_sems.at[1])
    block_load.start()
    inputs.start()
    if gains:
        gain_load.wait()
        shard, head = attn_out.shape[1], q_out.shape[1]
        model = (gain_ref.shape[1] - 2 * head) // 2
        at = pl.multiple_of(lax.axis_index("dp") * shard, shard)
        attn_out[...] = gain_ref[:, pl.ds(at, shard)]
        mlp_out[...] = gain_ref[:, pl.ds(pl.multiple_of(model + at, shard), shard)]
        q_out[...] = gain_ref[:, 2 * model : 2 * model + head]
        k_out[...] = gain_ref[:, 2 * model + head :]
    block_load.wait()
    block_copy.start()
    waited = set()
    for parts, out in zip(results, out_buffers):
        row = 0
        for i, column in parts:
            part = buffers[i]
            if i not in waited:
                inputs.wait(part)
                waited.add(i)
            height = part.shape[0]
            out[row : row + height, :] = part[:, column : column + out.shape[1]].astype(F32)
            row += height
        outputs.start(out)
    block_copy.wait()
    outputs.wait()


def widen(block_out, arrays, results, shapes, gains, shard, head):
    out_shape = [jax.ShapeDtypeStruct(block_out.shape, BF16)]
    out_shape += [jax.ShapeDtypeStruct(s, F32) for s in shapes]
    args = [block_out, *arrays]
    rows = [] if gains is None else [(1, shard), (1, shard), (1, head), (1, head)]
    if gains is not None:
        args.append(gains)
    return pl.pallas_call(
        functools.partial(widen_kernel, results=results, gains=gains is not None),
        out_shape=out_shape + [jax.ShapeDtypeStruct(s, F32) for s in rows],
        in_specs=[ANYWHERE] * len(args),
        out_specs=[ANYWHERE] * (1 + len(shapes)) + vmem(len(rows)),
        scratch_shapes=Staged.scratch(arrays)
        + Staged.scratch(out_shape[1:])
        + [pltpu.VMEM(block_out.shape, BF16), pltpu.SemaphoreType.DMA((2,))]
        + ([] if gains is None else [pltpu.VMEM(gains.shape[1:], F32), pltpu.SemaphoreType.DMA]),
        compiler_params=params(),
        cost_estimate=COST,
        name="widen",
    )(*args)


def rope_tables(length, width):
    frequency = ROPE_BASE ** (-2.0 * np.arange(width // 2) / width)
    angles = np.arange(length)[:, None] * frequency[None, :]
    cos, sin = np.cos(angles), np.sin(angles)
    tables = np.concatenate([cos, cos], axis=1), np.concatenate([-sin, sin], axis=1)
    return tuple(jnp.asarray(t.astype(np.float32)) for t in tables)


class Chain:
    def __init__(self):
        self.last = None

    def mark(self, value):
        self.last = value

    def __call__(self, *values):
        if self.last is None:
            return values
        return lax.optimization_barrier((*values, self.last))[:-1]


class ZSum:
    def __init__(self, part, dim, shard, planes, z_at):
        self.part, self.dim, self.shard, self.planes, self.z_at = part, dim, shard, planes, z_at
        self.at = 0
        self.came = None

    def term(self, j):
        j = jnp.clip(j, 0, self.planes - 1)
        return lax.dynamic_slice_in_dim(self.part, j * self.shard, self.shard, self.dim)

    def send(self, up, down):
        last = self.planes - 1
        self.at += 1
        up_pairs = [(2 * z + x, 2 * z + 2 + x) for z in range(last) for x in range(2) if z < self.at]
        down_pairs = [
            (2 * (last - z) + x, 2 * (last - 1 - z) + x)
            for z in range(last)
            for x in range(2)
            if z < self.at
        ]
        self.came = lax.ppermute(up, "dp", up_pairs), lax.ppermute(down, "dp", down_pairs)

    def terms(self):
        planes, z_at, at = self.planes, self.z_at, self.at
        return self.term(planes - 1 - at + z_at), self.term(at + 1 - planes + z_at)

    def start(self):
        self.send(*self.terms())

    def step(self, chain):
        if self.at >= self.planes - 1:
            return
        up, down = chain(*self.came)
        up_term, down_term = self.terms()
        up, down = up + up_term, down + down_term
        chain.mark(up)
        self.send(up, down)

    def finish(self, chain):
        if self.at == 0:
            self.start()
        while self.at < self.planes - 1:
            self.step(chain)
        up, down = chain(*self.came)
        total = self.term(self.z_at).astype(F32) + up.astype(F32) + down.astype(F32)
        chain.mark(total)
        return total


def shards(
    dp_size,
    tensor_size,
    tokens,
    norm_attn,
    w_query,
    key_weight,
    value_weight,
    query_gain,
    key_gain,
    w_out,
    norm_mlp,
    w_gate,
    w_up,
    w_down,
    out_grad,
    prefix_len,
):
    rows, model = tokens.shape
    width = query_gain.shape[0]
    kv_heads = key_weight.shape[1] // width
    repeat = w_query.shape[1] // key_weight.shape[1]
    dims = (kv_heads, repeat, width)
    group = dp_size // prefix_len.shape[0]
    planes = dp_size // 2
    group_planes = group // 2
    half = rows // 2
    shard = model // dp_size
    assert tensor_size == 4 and MAX_PREFIX <= 4 * rows

    device = lax.axis_index("dp")
    x_at = device % 2
    z_at = device // 2
    sequence = device // group
    member = device % group
    plane = member // 2
    prefix = jnp.sum(jnp.where(jnp.arange(prefix_len.shape[0]) == sequence, prefix_len, 0))

    x_pairs = [(d, d ^ 1) for d in range(dp_size)]

    def x_swap(value):
        return lax.ppermute(value, "dp", x_pairs)

    cos, sin = rope_tables(group * rows, width)
    norm_attn_row = norm_attn[None, :]
    norm_mlp_row = norm_mlp[None, :]
    q_gain_row = query_gain[None, :]
    k_gain_row = key_gain[None, :]

    prefix_at = prefix[None].astype(jnp.int32)
    heads_b, lse, kv_all, h_one, q, q_raw, k_raw = attn_fwd(
        prefix_at,
        tokens,
        norm_attn_row,
        w_query,
        key_weight,
        value_weight,
        q_gain_row,
        k_gain_row,
        cos,
        sin,
        group,
        dims,
    )
    fused = planes == group_planes and shard % 128 == 0
    pieces = 3
    middle, h_two, d_hidden, og_keep, og_came, heads_came = attention_out(
        heads_b, w_out, tokens, norm_mlp_row, out_grad, w_down, planes, shard
    )
    outs = middle_of(
        w_gate,
        w_up,
        h_two,
        d_hidden,
        middle,
        out_grad,
        norm_mlp_row,
        w_out,
        q,
        heads_b,
        lse,
        [og_keep, og_came] if fused else None,
        pieces,
        planes,
        shard,
        width,
    )
    hidden, d_gate, d_up, hidden_came, d_attn, norm_mlp_part, qx, dox, h_two_keep, h_two_came = outs[:10]

    grads = None
    if fused:
        grads = [hidden_came, og_keep, og_came, d_gate, h_two_keep, h_two_came]
        grads += [heads_b, heads_came]
        w_down_parts = outs[10:]
    shared = [d_attn, d_up, hidden, w_down, middle]
    outs = back(prefix_at, qx, dox, kv_all, shared, grads, group, planes, shard, pieces, dims)
    dq, kv_grad, up_came, block_out = outs[:4]
    chain = Chain()
    chain.mark(dq)
    if fused:
        w_down_parts = [*w_down_parts, outs[4]]
        w_gate_grad, w_out_grad = outs[5:]
    else:
        d_attn_keep, d_attn_came = outs[4:]
        down_part = (dot(hidden, og_keep, TN) + dot(hidden_came, og_came, TN)).astype(BF16)
        w_down_grad = ZSum(down_part, 1, shard, planes, z_at).finish(chain)
        gate_part = dot(h_two_keep, d_gate, TN) + dot(h_two_came, x_swap(d_gate), TN)
        w_gate_grad = ZSum(gate_part.astype(BF16), 0, shard, planes, z_at).finish(chain)
        out_part = dot(heads_b, d_attn_keep, TN) + dot(heads_came, d_attn_came, TN)
        w_out_grad = ZSum(out_part.astype(BF16), 1, shard, planes, z_at).finish(chain)

    up_grads = [h_two_keep, h_two_came, d_up, up_came] if fused else None
    outs = front(
        *chain(dq),
        kv_grad,
        q_raw,
        k_raw,
        q_gain_row,
        k_gain_row,
        cos,
        sin,
        h_one,
        (w_query, key_weight, value_weight),
        tokens,
        d_attn,
        norm_attn_row,
        norm_mlp_part,
        up_grads,
        dp_size,
        group,
        shard,
    )
    tokens_grad, gains = outs[:2]
    if fused:
        w_up_grad, w_query_grad, w_kv_grad = outs[2:]
    else:
        dq_b, dq_came, dkv_b, dkv_came, h_one_keep, h_one_came = outs[2:]
        chain.mark(tokens_grad)

        def by_rows(left, left_came, right, right_came):
            part = dot(left, right, TN) + dot(left_came, right_came, TN)
            return ZSum(part.astype(BF16), 0, shard, planes, z_at).finish(chain)

        w_up_grad = by_rows(h_two_keep, h_two_came, d_up, up_came)
        w_query_grad = by_rows(h_one_keep, h_one_came, dq_b, dq_came)
        w_kv_grad = by_rows(h_one_keep, h_one_came, dkv_b, dkv_came)
    kv_width = kv_heads * width
    if fused:
        arrays = [w_gate_grad, w_out_grad, *w_down_parts, w_up_grad, w_query_grad, w_kv_grad, tokens_grad]
        n = 2 + len(w_down_parts)
        results = [[(0, 0)], [(1, 0)], [(i, 0) for i in range(2, n)]]
        results += [[(n, 0)], [(n + 1, 0)], [(n + 2, 0)], [(n + 2, kv_width)], [(n + 3, 0)]]
        units = w_gate.shape[1]
        columns = w_query.shape[1]
        shapes = [(shard, units), (columns, shard), (units, shard), (shard, units), (shard, columns)]
        shapes += [(shard, kv_width)] * 2 + [(rows, model)]
        outs = widen(block_out, arrays, results, shapes, gains, shard, width)
        block_out, w_gate_grad, w_out_grad, w_down_grad, w_up_grad, w_query_grad = outs[:6]
        w_key_grad, w_value_grad, tokens_grad = outs[6:9]
        norm_attn_grad, norm_mlp_grad, query_gain_grad, key_gain_grad = (v[0] for v in outs[9:])
    else:
        w_key_grad, w_value_grad = w_kv_grad[:, :kv_width], w_kv_grad[:, kv_width:]
        tokens_grad = tokens_grad.astype(F32)
        gains = gains[-1, 0]
        norm_attn_grad = lax.dynamic_slice_in_dim(gains, device * shard, shard, 0)
        norm_mlp_grad = lax.dynamic_slice_in_dim(gains, model + device * shard, shard, 0)
        query_gain_grad, key_gain_grad = gains[2 * model : 2 * model + width], gains[2 * model + width :]
    return (
        block_out,
        tokens_grad,
        norm_attn_grad,
        w_query_grad,
        w_key_grad,
        w_value_grad,
        query_gain_grad,
        key_gain_grad,
        w_out_grad,
        norm_mlp_grad,
        w_gate_grad,
        w_up_grad,
        w_down_grad,
    )


def solution(mesh):
    placed = (
        P("dp", None),
        P(),
        P(None, "tensor"),
        P(None, "tensor"),
        P(None, "tensor"),
        P(),
        P(),
        P("tensor", None),
        P(),
        P(None, "tensor"),
        P(None, "tensor"),
        P("tensor", None),
        P("dp", None),
        P(),
    )
    return jax.shard_map(
        functools.partial(shards, mesh.shape["dp"], mesh.shape["tensor"]),
        mesh=mesh,
        in_specs=placed,
        out_specs=(
            P("dp", None),
            P("dp", None),
            P("dp"),
            P("dp", "tensor"),
            P("dp", "tensor"),
            P("dp", "tensor"),
            P(),
            P(),
            P("tensor", "dp"),
            P("dp"),
            P("dp", "tensor"),
            P("dp", "tensor"),
            P("tensor", "dp"),
        ),
        check_vma=False,
    )
```

```python
import functools
import math

import jax
import jax.numpy as jnp
import numpy as np
from jax import lax
from jax.experimental import pallas as pl
from jax.experimental.pallas import tpu as pltpu
from jax.sharding import PartitionSpec as P

F32 = jnp.float32
BF16 = jnp.bfloat16
EPS = 1e-06
ROPE_BASE = 1000000.0
MAX_PREFIX = 2048
VMEM_LIMIT = 56 * 2**20
BACK_VMEM_LIMIT = 60 * 2**20

COST = pl.CostEstimate(flops=1000, bytes_accessed=1000, transcendentals=0)

NN = (((1,), (0,)), ((), ()))
NT = (((1,), (1,)), ((), ()))
TN = (((0,), (0,)), ((), ()))


def dot(left, right, dims=NN):
    return lax.dot_general(left, right, dims, preferred_element_type=F32)


def vmem(count):
    return [pl.BlockSpec(memory_space=pltpu.VMEM)] * count


def params():
    return pltpu.CompilerParams(vmem_limit_bytes=VMEM_LIMIT)


def greet(peers):
    barrier = pltpu.get_barrier_semaphore()
    count = 0
    for peer, there in peers:

        def signal(peer=peer):
            pl.semaphore_signal(barrier, 1, device_id=peer, device_id_type=pl.DeviceIdType.MESH)

        if there is True:
            signal()
            count = count + 1
        else:
            pl.when(there)(signal)
            count = count + there.astype(jnp.int32)
    pl.semaphore_wait(barrier, count)


def remote(src, dst, send, recv, peer):
    return pltpu.make_async_remote_copy(
        src_ref=src,
        dst_ref=dst,
        send_sem=send,
        recv_sem=recv,
        device_id=peer,
        device_id_type=pl.DeviceIdType.MESH,
    )


class Staged:
    def __init__(self, arrays, buffers, sems, out=False):
        self.copies = []
        for i, (array, buffer) in enumerate(zip(arrays, buffers)):
            ends = (buffer, array) if out else (array, buffer)
            self.copies.append((buffer, pltpu.make_async_copy(*ends, sems.at[i])))

    @staticmethod
    def scratch(shapes):
        return [pltpu.VMEM(s.shape, s.dtype) for s in shapes] + [pltpu.SemaphoreType.DMA((len(shapes),))]

    def start(self, *buffers):
        for buffer, copy in self.copies:
            if not buffers or any(buffer is b for b in buffers):
                copy.start()

    def wait(self, *buffers):
        for buffer, copy in self.copies:
            if not buffers or any(buffer is b for b in buffers):
                copy.wait()


ANYWHERE = pl.BlockSpec(memory_space=pl.ANY)


def table_rows(tables, member, rows):
    at = pl.ds(pl.multiple_of(member * rows, rows), rows)
    return [t.at[at, :] for t in tables]


def tensor_peers():
    t = lax.axis_index("tensor")
    core = t % 2
    y = t // 2
    return core, {"tensor": t + 1 - 2 * core}, {"tensor": t + 2 - 4 * y}


def rows_of(core, half):
    return pl.ds(pl.multiple_of(core * half, half), half)


def cut_into(out, out_rows, ref, ref_rows, side, planes, shard):
    for z in range(planes):
        to = slice(z * shard, (z + 1) * shard)
        if shard % 128 == 0:
            at = pl.ds(pl.multiple_of((2 * z + side) * shard, shard), shard)
            out[out_rows, to] = ref[ref_rows, at]
        else:
            low = ref[ref_rows, 2 * z * shard : (2 * z + 1) * shard]
            high = ref[ref_rows, (2 * z + 1) * shard : (2 * z + 2) * shard]
            out[out_rows, to] = jnp.where(side == 0, low, high)


class Columns:
    def __init__(self, whole, keep, came, scratch, x_at, core, x_peer, core_peer, planes, shard):
        self.whole, self.keep, self.came = whole, keep, came
        self.send_ref, self.recv_ref, self.sems = scratch[0], scratch[1], scratch[2:]
        self.x_at, self.core, self.cut = x_at, core, (planes, shard)
        self.x_peer, self.core_peer = x_peer, core_peer
        self.half = whole.shape[0] // 2

    @staticmethod
    def scratch(half, columns):
        return [pltpu.VMEM((half, columns), BF16)] * 2 + [pltpu.SemaphoreType.DMA] * 4

    def over_x(self):
        return remote(self.send_ref, self.recv_ref, self.sems[0], self.sems[1], self.x_peer)

    def over_core(self):
        there = self.came.at[rows_of(self.core, self.half), :]
        return remote(self.recv_ref, there, self.sems[2], self.sems[3], self.core_peer)

    def start(self):
        mine = rows_of(self.core, self.half)
        cut_into(self.send_ref, slice(None), self.whole, mine, 1 - self.x_at, *self.cut)
        self.over_x().start()

    def store(self):
        cut_into(self.keep, slice(None), self.whole, slice(None), self.x_at, *self.cut)

    def forward(self):
        self.over_x().wait_recv()
        self.over_core().start()
        self.came[rows_of(self.core, self.half), :] = self.recv_ref[...]

    def finish(self):
        self.over_core().wait_recv()
        self.over_x().wait_send()
        self.over_core().wait_send()


class LineSum:
    def __init__(self, scratch, device, plane, planes, paced=False):
        self.paced = paced
        self.stack, self.came = scratch[:2]
        self.sems = scratch[2:]
        self.device, self.plane, self.planes = device, plane, planes

    @staticmethod
    def scratch(planes, shape):
        return [pltpu.VMEM((n,) + shape, BF16) for n in (planes, planes + 1)] + [
            pltpu.SemaphoreType.DMA((planes,))
        ] * 4

    def up(self, j):
        s = self.sems
        peer = {"dp": self.device + 2}
        return remote(self.stack.at[j], self.came.at[j], s[0].at[j], s[1].at[j], peer)

    def down(self, j):
        s = self.sems
        slot = jnp.where(self.plane - 1 == j, self.planes, j)
        peer = {"dp": self.device - 2}
        return remote(self.stack.at[j], self.came.at[slot], s[2].at[j], s[3].at[j], peer)

    def start(self):
        last = self.planes - 1

        @pl.when(self.plane == 0)
        def _():
            for j in range(last, last - 1 if self.paced else 0, -1):
                self.up(j).start()

        @pl.when(self.plane == last)
        def _():
            for j in range(1 if self.paced else last):
                self.down(j).start()

    def advance(self, step):
        plane, last = self.plane, self.planes - 1
        low, high = last - step + plane, step - last + plane
        if self.paced:

            @pl.when(plane == 0)
            def _():
                self.up(last - step + 1).wait_send()
                self.up(last - step).start()

            @pl.when(plane == last)
            def _():
                self.down(step - 1).wait_send()
                self.down(step).start()

        @pl.when((plane >= 1) & (plane <= step))
        def _():
            self.up(low).wait_recv()
            self.stack[low] += self.came[low]
            self.up(low).start()

        @pl.when((plane < last) & (plane >= last - step))
        def _():
            self.down(high).wait_recv()
            self.stack[high] += self.came[high]
            self.down(high).start()

    def finish(self, out):
        plane, planes = self.plane, self.planes

        @pl.when(plane == 0)
        def _():
            self.down(plane).wait_recv()
            out[...] = self.stack[plane] + self.came[planes]

        @pl.when(plane == planes - 1)
        def _():
            self.up(plane).wait_recv()
            out[...] = self.stack[plane] + self.came[plane]

        @pl.when((plane > 0) & (plane < planes - 1))
        def _():
            self.up(plane).wait_recv()
            self.down(plane).wait_recv()
            total = self.stack[plane].astype(F32) + self.came[plane].astype(F32)
            out[...] = (total + self.came[planes].astype(F32)).astype(BF16)

        for j in range(planes):
            ups, downs = plane < j, plane > j
            if self.paced and j > 1:
                ups = ups & (plane > 0)
            if self.paced and j < planes - 2:
                downs = downs & (plane < planes - 1)
            pl.when(ups)(lambda j=j: self.up(j).wait_send())
            pl.when(downs)(lambda j=j: self.down(j).wait_send())

    def fill_rows(self, left, left_came, right, right_came):
        shard, planes = self.stack.shape[1], self.planes

        def compute(i):
            j = jnp.where(self.plane * 2 < planes, planes - 1 - i, i) if self.paced else i
            at = pl.ds(pl.multiple_of(j * shard, shard), shard)
            self.stack[j] = (
                dot(left[:, at], right[...], TN) + dot(left_came[:, at], right_came[...], TN)
            ).astype(BF16)

        if self.paced:
            compute(0)
            self.start()

        def body(i, carry):
            compute(i)
            return carry

        lax.fori_loop(1 if self.paced else 0, planes, body, 0)

    def fill_columns(self, left, left_came, right, right_came):
        shard = self.stack.shape[2]
        tile = 256

        def body(t, carry):
            at = pl.ds(pl.multiple_of(t * tile, tile), tile)
            term = dot(left[:, at], right[...], TN) + dot(left_came[:, at], right_came[...], TN)
            for j in range(self.planes):
                self.stack[j, at, :] = term[:, j * shard : (j + 1) * shard].astype(BF16)
            return carry

        lax.fori_loop(0, left.shape[1] // tile, body, 0)


class TensorSum:
    def __init__(self, scratch, mine, core, core_peer, y_peer):
        self.away, self.core_came, self.both, self.y_came = scratch[:4]
        self.sems = scratch[4:]
        self.mine = mine
        self.core, self.core_peer, self.y_peer = core, core_peer, y_peer
        self.chunks, self.half, self.width = self.away.shape

    @staticmethod
    def scratch(chunks, half, width):
        return [pltpu.VMEM((chunks, half, width), BF16)] * 4 + [
            pltpu.SemaphoreType.DMA((chunks,))
        ] * 4

    def over_core(self, i):
        s = self.sems
        return remote(self.away.at[i], self.core_came.at[i], s[0].at[i], s[1].at[i], self.core_peer)

    def over_y(self, i):
        s = self.sems
        return remote(self.both.at[i], self.y_came.at[i], s[2].at[i], s[3].at[i], self.y_peer)

    def add(self, i, value):
        self.mine[i % 2] = value
        self.away[i] = self.mine[i % 2, rows_of(1 - self.core, self.half), :].astype(BF16)
        self.over_core(i).start()
        if i > 0:
            self.pass_on(i - 1)
        if i == self.chunks - 1:
            self.pass_on(i)

    def pass_on(self, i):
        self.over_core(i).wait_recv()
        mine = self.mine[i % 2, rows_of(self.core, self.half), :]
        self.both[i] = (mine + self.core_came[i].astype(F32)).astype(BF16)
        self.over_y(i).start()

    def total(self, i):
        self.over_y(i).wait_recv()
        return self.both[i].astype(F32) + self.y_came[i].astype(F32)

    def finish(self):
        for i in range(self.chunks):
            self.over_core(i).wait_send()
            self.over_y(i).wait_send()


def roll_half(value):
    return pltpu.roll(value, value.shape[-1] // 2, 1)


def visible(shape, key0, row0, prefix):
    key_pos = key0 + lax.broadcasted_iota(jnp.int32, shape, 1)
    row_pos = row0 + lax.broadcasted_iota(jnp.int32, shape, 0)
    return (key_pos <= row_pos) | (key_pos < prefix)


def attn_fwd_kernel(*refs, group, kv_heads, repeat, width, tile, coef):
    refs = list(refs)

    def take(count):
        out = refs[:count]
        del refs[:count]
        return out

    prefix_ref, gain_ref, q_gain, k_gain = take(4)
    arrays = take(6)
    member = lax.axis_index("dp") % group
    arrays[3:5] = table_rows(arrays[3:5], member, arrays[0].shape[0])
    o_ref, lse_ref, all_out = take(3)
    outs = take(4)
    buffers = take(6)
    inputs = Staged(arrays, buffers, *take(1))
    x_ref, w_k, w_v, cos_ref, sin_ref, w_q = buffers
    out_buffers = take(4)
    h_ref, q_ref, q_raw, k_raw = out_buffers
    outputs = Staged(outs, out_buffers, *take(1), out=True)
    kv_ref, all_ref, all_sems, acc, send_x, recv_x, send_z, recv_z = take(8)
    send_down, send_rest, recv_rest = take(3)
    rows = q_ref.shape[0]
    kv_width = kv_heads * width
    planes = group // 2
    device = lax.axis_index("dp")
    member = device % group
    plane = member // 2
    x_at = member % 2
    x_other = device + 1 - 2 * x_at
    inner = plane < planes - 1
    prefix = prefix_ref[0]
    inputs.start()
    greet([({"dp": x_other}, True), ({"dp": device + 2}, inner), ({"dp": device - 2}, plane > 0)])

    def store(slot):
        return pltpu.make_async_copy(all_ref.at[slot], all_out.at[slot], all_sems.at[slot])

    def source(slot):
        return kv_ref if slot == 0 else all_ref.at[2 * slot]

    split = planes - 1 if planes > 2 else planes
    half = rows // 2
    parts = [pl.ds(0, half), pl.ds(half, rows - half)]

    def halves_over_x(slot):
        return range(1 if slot == split else 2)

    def to_x(slot, h):
        at = parts[h]
        to = all_ref.at[2 * slot + 1, at, :]
        i = 2 * slot + h
        return remote(source(slot).at[at, :], to, send_x.at[i], recv_x.at[i], {"dp": x_other})

    def to_z(slot, h):
        at = parts[h]
        to = all_ref.at[2 * slot, at, :]
        i = 2 * slot + h
        return remote(source(slot - 1).at[at, :], to, send_z.at[i], recv_z.at[i], {"dp": device + 2})

    def rest_to_z():
        return remote(
            all_ref.at[2 * split - 1, parts[1], :],
            all_ref.at[2 * split + 1, parts[1], :],
            send_rest,
            recv_rest,
            {"dp": device + 2},
        )

    def to_first(h):
        at = parts[h]
        to = all_ref.at[2, at, :]
        return remote(kv_ref.at[at, :], to, send_down.at[h], recv_z.at[2 + h], {"dp": device - 2})

    inputs.wait(x_ref, w_k, w_v, cos_ref, sin_ref)

    def rotate(u, gain, at):
        u = u * lax.rsqrt(jnp.mean(u * u, axis=1, keepdims=True) + EPS) * gain[...]
        return (u * cos_ref[at, :] + roll_half(u) * sin_ref[at, :]).astype(BF16)

    ones = jnp.ones((rows, width), BF16)
    row0 = member * rows

    def work(block, other, masked, start=False):
        key0 = other * rows

        def head_pair(h, carry):
            k = block[:, pl.ds(pl.multiple_of(h * width, width), width)]
            v = block[:, pl.ds(pl.multiple_of(kv_width + h * width, width), width)]
            v = jnp.concatenate([v, ones], axis=1)
            for g in range(repeat):
                head = h * repeat + g
                for at in range(0, rows, tile):
                    q = q_ref[at : at + tile, pl.ds(pl.multiple_of(head * width, width), width)]
                    p = jnp.exp2(dot(q, k, NT) * coef)
                    if masked:
                        p = jnp.where(visible(p.shape, key0, row0 + at, prefix), p, 0.0)
                    term = dot(p.astype(BF16), v)
                    if start:
                        acc[head, at : at + tile, :] = term
                    else:
                        acc[head, at : at + tile, :] += term
            return carry

        lax.fori_loop(0, kv_heads, head_pair, 0)

    for h in range(2):
        at = parts[h]
        x = x_ref[at, :].astype(F32)
        r = lax.rsqrt(jnp.mean(x * x, axis=1, keepdims=True) + EPS)
        h_ref[at, :] = (x * r * gain_ref[...]).astype(BF16)
        keys = dot(h_ref[at, :], w_k[...])
        k_raw[at, :] = keys
        for c in range(0, kv_width, width):
            kv_ref[at, c : c + width] = rotate(keys[:, c : c + width], k_gain, at)
        kv_ref[at, kv_width:] = dot(h_ref[at, :], w_v[...]).astype(BF16)
        to_x(0, h).start()
        if planes > 1:
            pl.when(inner)(lambda h=h: to_z(1, h).start())
            pl.when(plane == 1)(lambda h=h: to_first(h).start())

    inputs.wait(w_q)
    queries = dot(h_ref[...], w_q[...])
    q_raw[...] = queries
    for at in range(0, queries.shape[1], width):
        q_ref[:, at : at + width] = rotate(queries[:, at : at + width], q_gain, slice(None))
    outputs.start()
    all_ref[0] = kv_ref[...]
    store(0).start()
    work(kv_ref, member, True, True)

    def receive(slot):
        for h in range(2):
            to_z(slot, h).wait_recv()
            if slot < planes - 1:
                pl.when(inner & (plane >= slot))(lambda h=h: to_z(slot + 1, h).start())
            if h in halves_over_x(slot):
                to_x(slot, h).start()
        store(2 * slot).start()

    def attend(slot, index, there, first):
        if slot == 1:
            pl.when(plane == 0)(lambda: work(all_ref.at[index], first, True))
            pl.when(plane > 0)(lambda: work(all_ref.at[index], there, False))
        else:
            work(all_ref.at[index], there, slot == 0)

    def far(slot):
        for h in halves_over_x(slot):
            to_x(slot, h).wait_recv()
        if slot == split - 1:
            pl.when(plane == split - 1)(lambda: rest_to_z().start())
        if slot == split:
            rest_to_z().wait_recv()
        store(2 * slot + 1).start()
        attend(slot, 2 * slot + 1, 2 * (plane - slot) + 1 - x_at, 3 - x_at)

    if planes > 1:
        receive(1)
    far(0)
    for slot in range(1, planes):

        def step(slot=slot):
            attend(slot, 2 * slot, 2 * (plane - slot) + x_at, 2 + x_at)
            if slot + 1 < planes:
                pl.when(plane >= slot + 1)(lambda: receive(slot + 1))
            far(slot)

        if slot == 1:
            step()
        else:
            pl.when(plane >= slot)(step)

    for head in range(kv_heads * repeat):
        total = acc[head, :, width:]
        o_ref[:, head * width : (head + 1) * width] = (acc[head, :, :width] / total).astype(BF16)
        lse_ref[:, head * width : (head + 1) * width] = jnp.log2(total) * (1.0 / coef)

    outputs.wait()
    if split < planes:
        pl.when(plane == split - 1)(lambda: rest_to_z().wait_send())
    for slot in range(planes):

        @pl.when((plane >= slot) | (slot <= 1))
        def _(slot=slot):
            store(2 * slot).wait()
            store(2 * slot + 1).wait()
            for h in halves_over_x(slot):
                to_x(slot, h).wait_send()

    for slot in range(1, planes):

        @pl.when(inner & (plane >= slot - 1))
        def _(slot=slot):
            for h in range(2):
                to_z(slot, h).wait_send()

    if planes > 1:

        @pl.when(plane == 1)
        def _():
            for h in range(2):
                to_first(h).wait_send()


def attn_fwd(prefix, x, gain, w_query, key_weight, value_weight, q_gain, k_gain, cos, sin, group, dims):
    kv_heads, repeat, width = dims
    rows = x.shape[0]
    heads = kv_heads * repeat
    columns = heads * width
    planes = group // 2
    dma = pltpu.SemaphoreType.DMA
    block = (rows, 2 * kv_heads * width)
    staged = [x, key_weight, value_weight, cos, sin, w_query]
    table = jax.ShapeDtypeStruct((rows, width), F32)
    early = [
        jax.ShapeDtypeStruct(x.shape, BF16),
        jax.ShapeDtypeStruct((rows, columns), BF16),
        jax.ShapeDtypeStruct((rows, columns), F32),
        jax.ShapeDtypeStruct((rows, kv_heads * width), F32),
    ]
    return pl.pallas_call(
        functools.partial(
            attn_fwd_kernel,
            group=group,
            kv_heads=kv_heads,
            repeat=repeat,
            width=width,
            tile=min(rows, 256),
            coef=math.log2(math.e) / math.sqrt(width),
        ),
        out_shape=[
            jax.ShapeDtypeStruct((rows, columns), BF16),
            jax.ShapeDtypeStruct((rows, columns), F32),
            jax.ShapeDtypeStruct((group,) + block, BF16),
        ]
        + early,
        in_specs=[smem()] + vmem(3) + [ANYWHERE] * 6,
        out_specs=vmem(2) + [ANYWHERE] * 5,
        scratch_shapes=Staged.scratch([x, key_weight, value_weight, table, table, w_query])
        + Staged.scratch(early)
        + [pltpu.VMEM(block, BF16), pltpu.VMEM((group,) + block, BF16), dma((group,))]
        + [pltpu.VMEM((heads, rows, 2 * width), F32)]
        + [dma((2 * planes,))] * 4
        + [dma((2,)), dma, dma],
        compiler_params=pltpu.CompilerParams(
            vmem_limit_bytes=VMEM_LIMIT, collective_id=0, has_side_effects=True
        ),
        cost_estimate=COST,
        name="attn_fwd",
    )(prefix, gain, q_gain, k_gain, *staged)


def split_three(value):
    high = value.astype(BF16)
    left = value - high.astype(F32)
    mid = left.astype(BF16)
    return high.astype(F32), mid.astype(F32), (left - mid.astype(F32)).astype(BF16).astype(F32)


def back_kernel(
    *refs, group, planes, all_planes, shard, kv_heads, repeat, width, coef, scale, sums
):
    refs = list(refs)

    def take(count):
        out = refs[:count]
        del refs[:count]
        return out

    device = lax.axis_index("dp")
    member = device % group
    plane = member // 2
    last = planes - 1
    prefix_ref, up_ref, w_down_in, middle_in = take(4)
    if sums:
        hid_arrays = take(1)
    count = 12 if sums else 5
    arrays = take(count)
    dq_ref, grad_ref, up_came_ref, block_ref = take(4)
    if sums:
        w_down_ref, w_gate_ref, w_out_ref = take(3)
    a_ref, a_came_ref = take(2)
    if sums:
        hid_buffers = take(1)
        hid_sems = take(1)[0]
    buffers = take(count)
    inputs = Staged(arrays, buffers, *take(1))
    a_all_ref, qx_ref, dox_ref, kv_ref, hid_ref = buffers[:5]
    if sums:
        hid_came_ref = hid_buffers[0]
        og_ref, og_came_ref, gate_ref, h_ref, h_came_ref, heads_ref, heads_came_ref = buffers[5:]
    down_buf, down_sems, mine_ref, middle_buf, middle_sems = take(5)
    block_sems = take(3)
    total_scratch = take(8)
    own_ref, far_ref, xr_ref, zr_ref, first_ref = take(5)
    send_x, recv_x, send_z, recv_z, send_first, recv_first = take(6)
    swap_sems = take(2)
    a_scratch = take(6)
    rows = qx_ref.shape[1]
    kv_width = kv_heads * width
    if sums:
        gate_came_ref, send_gate, recv_gate = take(3)
        left = w_down_ref.shape[0]
        rest = pl.ds(hid_arrays[0].shape[1] - left, left)
        hid_inputs = Staged([h.at[:, rest] for h in hid_arrays], hid_buffers, hid_sems)
        down_sum, out_sum = (LineSum(take(6), device, plane, planes) for _ in range(2))
        piece = gate_came_ref.shape[2]
        pieces = gate_ref.shape[1] // piece
        gate_sums = [LineSum(take(6), device, plane, planes) for _ in range(pieces)]
    x_at = member % 2
    x_other = device + 1 - 2 * x_at
    inner = plane < last
    prefix = prefix_ref[0]

    core, core_peer, y_peer = tensor_peers()
    x_peer = {"dp": x_other}
    total = TensorSum(total_scratch, mine_ref, core, core_peer, y_peer)
    half = total.half
    parts, narrow = total.chunks, total.width

    def load(i):
        at = pl.ds(i * narrow, narrow)
        return pltpu.make_async_copy(w_down_in.at[:, at], down_buf.at[i % 2], down_sems.at[i % 2])

    def middle_load(i):
        at = pl.ds(i * narrow, narrow)
        return pltpu.make_async_copy(middle_in.at[:, at], middle_buf.at[i % 2], middle_sems.at[i % 2])

    def block_at(i):
        return block_ref.at[rows_of(core, half), pl.ds(i * narrow, narrow)]

    def block_store(i):
        return pltpu.make_async_copy(total.both.at[i], block_at(i), block_sems[0].at[i])

    def block_give(i):
        return remote(total.both.at[i], block_at(i), block_sems[1].at[i], block_sems[2].at[i], core_peer)

    def block_add(i):
        load(i).wait()
        total.add(i, dot(hid_ref[...], down_buf[i % 2]))
        if i + 2 < parts:
            load(i + 2).start()

    def block_finish(i):
        middle_load(i).wait()
        value = middle_buf[i % 2] + total.total(i)
        total.over_y(i).wait_send()
        total.both[i] = value.astype(BF16)
        if i + 2 < parts:
            middle_load(i + 2).start()
        block_store(i).start()
        block_give(i).start()

    inputs.start(a_all_ref)
    if sums:
        hid_inputs.start()
        inputs.start(hid_ref, *buffers[5:7])
    inputs.start(*buffers[1:4])
    if sums:
        inputs.start(*buffers[7:])
    else:
        inputs.start(hid_ref)
    for i in range(2):
        load(i).start()
        middle_load(i).start()
    greet(
        [
            (x_peer, True),
            (core_peer, True),
            (y_peer, True),
            ({"dp": device + 2}, inner),
            ({"dp": device - 2}, plane > 0),
        ]
    )

    def copy(src, dst, send, recv, there):
        return remote(src, dst, send, recv, {"dp": there})

    place = (x_at, core, x_peer, core_peer, all_planes, shard)
    d_attn = Columns(a_all_ref, a_ref, a_came_ref, a_scratch, *place)
    up_swap = copy(up_ref, up_came_ref, swap_sems[0], swap_sems[1], x_other)

    def gate_swap(k):
        part = gate_ref.at[:, pl.ds(k * piece, piece)]
        return copy(part, gate_came_ref.at[k], send_gate.at[k], recv_gate.at[k], x_other)

    def gate_start(k):
        gate_swap(k).wait_recv()
        part = gate_ref.at[:, pl.ds(k * piece, piece)]
        gate_sums[k].fill_rows(h_ref, h_came_ref, part, gate_came_ref.at[k])
        gate_sums[k].start()

    lane = lax.broadcasted_iota(jnp.int32, (rows, width), 1)
    minus = jnp.where(lane < 3, -1.0, 0.0).astype(BF16)
    row0 = member * rows

    def work(block, other, masked, out):
        key0 = other * rows

        def head_group(h, carry):
            k_at = pl.ds(pl.multiple_of(h * width, width), width)
            v_at = pl.ds(pl.multiple_of(kv_width + h * width, width), width)
            k = kv_ref[block, :, k_at]
            v = kv_ref[block, :, v_at]
            kx = jnp.concatenate([k, minus], axis=1)
            vx = jnp.concatenate([v, minus], axis=1)
            dk = jnp.zeros((rows, width), F32)
            dv = jnp.zeros((rows, width), F32)
            for g in range(repeat):
                head = h * repeat + g
                qx = qx_ref[head]
                dox = dox_ref[head]
                p = jnp.exp2(dot(qx, kx, NT) * coef)
                if masked:
                    p = jnp.where(visible(p.shape, key0, row0, prefix), p, 0.0)
                ds = (p * dot(dox, vx, NT)).astype(BF16)
                dv += dot(p.astype(BF16), dox[:, :width], TN)
                dk += dot(ds, qx[:, :width], TN)
                dq_ref[:, pl.ds(pl.multiple_of(head * width, width), width)] += dot(ds, k)
            out[:, k_at] = (dk * scale).astype(BF16)
            out[:, v_at] = dv.astype(BF16)
            return carry

        lax.fori_loop(0, kv_heads, head_group, 0)

    def far_swap(slot):
        return copy(far_ref.at[slot], xr_ref.at[slot], send_x.at[slot], recv_x.at[slot], x_other)

    def to_plane(slot):
        return copy(own_ref.at[slot], zr_ref.at[slot], send_z.at[slot], recv_z.at[slot], device - 2)

    def from_first():
        return copy(own_ref.at[1], first_ref, send_first, recv_first, device + 2)

    def attend(slot):
        there = 2 * (plane - slot)
        far, own = there + 1 - x_at, there + x_at

        def both(far, own, masked):
            work(2 * slot + 1, far, masked, far_ref.at[slot])
            far_swap(slot).start()
            work(2 * slot, own, masked, own_ref.at[slot])

        if slot == 0:
            both(far, own, True)
        elif slot == 1:
            pl.when(plane == 0)(lambda: both(3 - x_at, 2 + x_at, True))
            pl.when(plane > 0)(lambda: both(far, own, False))
        else:
            pl.when(plane >= slot)(lambda: both(far, own, False))

    def pass_back(slot):
        def go():
            far_swap(slot).wait_recv()
            own_ref[slot] += xr_ref[slot]
            if slot < last:

                @pl.when(inner & (plane >= slot))
                def _():
                    to_plane(slot + 1).wait_recv()
                    own_ref[slot] += zr_ref[slot + 1]

            if slot == 1:
                pl.when(plane == 0)(lambda: from_first().start())
                pl.when(plane > 0)(lambda: to_plane(slot).start())
            else:
                to_plane(slot).start()

        if slot == 1:
            go()
        else:
            pl.when(plane >= slot)(go)

    dq_ref[...] = jnp.zeros_like(dq_ref)
    inputs.wait(a_all_ref)
    d_attn.start()
    inputs.wait(hid_ref)
    if sums:
        hid_inputs.wait()
        inputs.wait(og_ref, og_came_ref)
        down_sum.fill_columns(hid_ref.at[:, rest], hid_came_ref, og_ref, og_came_ref)
        down_sum.start()
    inputs.wait(*buffers[1:4])
    attend(last)
    d_attn.forward()
    if sums:
        inputs.wait(*buffers[7:])
        gate_swap(0).start()
    d_attn.store()
    pending = list(range(last, 0, -1))
    steps = range(1, last)
    adds = list(range(parts))
    share = -(-parts // last)
    for slot in range(last - 1, -1, -1):
        attend(slot)
        if slot == last - 1:
            if sums:
                d_attn.over_core().wait_recv()
                out_sum.fill_columns(heads_ref, heads_came_ref, a_ref, a_came_ref)
                out_sum.start()
                down_sum.advance(1)
                gate_start(0)
                gate_swap(1).start()
            pass_back(pending.pop(0))
        if slot == last - 2:
            if sums:
                for step in steps[1:]:
                    down_sum.advance(step)
                out_sum.advance(1)
                gate_start(1)
                gate_swap(2).start()
                gate_sums[0].advance(1)
            pass_back(pending.pop(0))
        for i in adds[:share]:
            block_add(i)
        del adds[:share]
    for i in adds:
        block_add(i)
    if sums:
        for step in steps[1:]:
            out_sum.advance(step)
            gate_sums[0].advance(step)
    while pending:
        pass_back(pending.pop(0))
    if sums:
        gate_start(2)
    up_swap.start()
    if sums:
        gate_sums[1].advance(1)
    for i in range(parts // 2):
        block_finish(i)
    if sums:
        for step in steps[1:]:
            gate_sums[1].advance(step)
        gate_sums[2].advance(1)
    for i in range(parts // 2, parts):
        block_finish(i)
    if sums:
        for step in steps[1:]:
            gate_sums[2].advance(step)
    dq_ref[...] = dq_ref[...] * scale

    far_swap(0).wait_recv()
    grad_ref[...] = own_ref[0].astype(F32) + xr_ref[0].astype(F32)
    if last > 0:

        @pl.when(inner)
        def _():
            to_plane(1).wait_recv()
            grad_ref[...] += zr_ref[1].astype(F32)

        @pl.when(plane == 1)
        def _():
            from_first().wait_recv()
            grad_ref[...] += first_ref[...].astype(F32)

    if sums:
        down_sum.finish(w_down_ref)
        out_sum.finish(w_out_ref)
        for k in range(pieces):
            gate_sums[k].finish(w_gate_ref.at[:, pl.ds(k * piece, piece)])
            gate_swap(k).wait_send()
    else:
        d_attn.over_core().wait_recv()
    up_swap.wait_recv()
    up_swap.wait_send()
    for i in range(parts):
        total.over_core(i).wait_send()
        block_store(i).wait()
        block_give(i).wait_recv()
        block_give(i).wait_send()
    d_attn.over_x().wait_send()
    d_attn.over_core().wait_send()
    for slot in range(planes):
        if slot <= 1:
            far_swap(slot).wait_send()
        else:
            pl.when(plane >= slot)(lambda slot=slot: far_swap(slot).wait_send())
        if slot >= 1:
            pl.when(plane >= slot)(lambda slot=slot: to_plane(slot).wait_send())
    if last > 0:
        pl.when(plane == 0)(lambda: from_first().wait_send())


def back(prefix, qx, dox, kv_all, shared, grads, group, all_planes, shard, pieces, dims):
    kv_heads, repeat, width = dims
    rows = qx.shape[1]
    columns = kv_heads * repeat * width
    planes = group // 2
    block = kv_all.shape[1:]
    dma = pltpu.SemaphoreType.DMA
    d_attn, d_up, hidden, w_down, middle = shared
    half, model = middle.shape
    parts = 8
    narrow = model // parts
    units = d_up.shape[1]
    cut_shape = jax.ShapeDtypeStruct((rows, all_planes * shard), BF16)
    out_shape = [jax.ShapeDtypeStruct((rows, columns), F32), jax.ShapeDtypeStruct(block, F32)]
    out_shape += [jax.ShapeDtypeStruct(d_up.shape, BF16), jax.ShapeDtypeStruct((rows, model), BF16)]
    scratch = [pltpu.VMEM((planes,) + block, BF16)] * 4 + [pltpu.VMEM(block, BF16)]
    scratch += [dma((planes,))] * 4 + [dma, dma] + [dma] * 2
    scratch += Columns.scratch(rows // 2, all_planes * shard)
    staged = [d_attn, qx, dox, kv_all, hidden]
    args = [prefix, d_up, w_down, middle]
    first = []
    if grads is not None:
        args += grads[:1]
        staged += grads[1:]
        first = [pltpu.VMEM(cut_shape.shape, BF16)] * 2
        first += [pltpu.VMEM((rows, units // pieces), BF16), dma((1,))]
    else:
        out_shape += [cut_shape] * 2
    args += staged
    product = [pltpu.VMEM((2, units, narrow), BF16), dma((2,)), pltpu.VMEM((2, rows, narrow), F32)]
    product += [pltpu.VMEM((2, half, narrow), F32), dma((2,))] + [dma((parts,))] * 3
    product += TensorSum.scratch(parts, half, narrow)
    scratch = first + Staged.scratch(staged) + product + scratch
    if grads is not None:
        piece = units // pieces
        shapes = (piece, shard), (shard, units), (columns, shard)
        out_shape += [jax.ShapeDtypeStruct(s, BF16) for s in shapes]
        scratch += [pltpu.VMEM((pieces, rows, piece), BF16)] + [dma((pieces,))] * 2
        for shape in [(piece, shard), (columns, shard)] + [(shard, piece)] * pieces:
            scratch += LineSum.scratch(planes, shape)
    return pl.pallas_call(
        functools.partial(
            back_kernel,
            group=group,
            planes=planes,
            all_planes=all_planes,
            shard=shard,
            kv_heads=kv_heads,
            repeat=repeat,
            width=width,
            coef=math.log2(math.e) / math.sqrt(width),
            scale=1.0 / math.sqrt(width),
            sums=grads is not None,
        ),
        out_shape=out_shape,
        in_specs=[smem()] + [ANYWHERE] * (len(args) - 1),
        out_specs=vmem(2) + [ANYWHERE] * 2 + vmem(len(out_shape) - 4),
        scratch_shapes=scratch,
        compiler_params=pltpu.CompilerParams(
            vmem_limit_bytes=BACK_VMEM_LIMIT, collective_id=1, has_side_effects=True
        ),
        cost_estimate=COST,
        name="back",
    )(*args)


def smem():
    return pl.BlockSpec(memory_space=pltpu.SMEM)


def out_kernel(*refs, planes, shard, blocks):
    refs = list(refs)

    def take(count):
        out = refs[:count]
        del refs[:count]
        return out

    arrays = take(4)
    gain_ref, w_down_ref = take(2)
    middle_ref, h_ref, d_hidden_out, og_keep, og_came, heads_came = take(6)
    buffers = take(4)
    heads_ref, w_ref, og_ref, x_ref = buffers
    inputs = Staged(arrays, buffers, *take(1))
    d_hidden_ref, d_hidden_sem = take(2)
    down_buf, down_sems, whole_ref, h_send, h_recv, heads_send, heads_recv = take(7)
    scratch = refs
    device = lax.axis_index("dp")
    core, core_peer, y_peer = tensor_peers()
    x_at = device % 2
    x_peer = {"dp": device + 1 - 2 * x_at}
    half = middle_ref.shape[0]
    total = TensorSum(scratch[:8], None, core, core_peer, y_peer)
    step = half // blocks
    place = (x_at, core, x_peer, core_peer, planes, shard)
    og = Columns(og_ref, og_keep, og_came, scratch[8:14], *place)
    tiles = down_sems.shape[0]
    tile = down_buf.shape[0] // tiles

    def load(t):
        at = pl.ds(t * tile, tile)
        return pltpu.make_async_copy(w_down_ref.at[at, :], down_buf.at[at, :], down_sems.at[t])

    inputs.start()
    for t in range(tiles):
        load(t).start()
    greet([(x_peer, True), (core_peer, True), (y_peer, True)])
    heads_swap = remote(heads_ref, heads_came, heads_send, heads_recv, x_peer)
    inputs.wait(heads_ref, w_ref)
    heads_swap.start()

    def rows_at(which, b):
        return pl.ds(pl.multiple_of(which * half + b * step, step), step)

    whole_ref[...] = dot(heads_ref[...], w_ref[...])
    for b in range(blocks):
        total.away[b] = whole_ref[rows_at(1 - core, b), :].astype(BF16)
        total.over_core(b).start()
    for b in range(blocks):
        total.over_core(b).wait_recv()
        mine = whole_ref[rows_at(core, b), :] + total.core_came[b].astype(F32)
        total.both[b] = mine.astype(BF16)
        total.over_y(b).start()
    inputs.wait(og_ref)
    og.start()
    og.store()
    for t in range(tiles):
        at = slice(t * tile, (t + 1) * tile)
        load(t).wait()
        d_hidden_ref[:, at] = dot(og_ref[...], down_buf[at, :], NT)
    d_hidden_copy = pltpu.make_async_copy(d_hidden_ref, d_hidden_out, d_hidden_sem)
    d_hidden_copy.start()
    inputs.wait(x_ref)

    def to_core(b):
        rows = h_ref.at[rows_at(core, b), :]
        return remote(rows, rows, h_send.at[b], h_recv.at[b], core_peer)

    for b in range(blocks):
        at = rows_at(core, b)
        v = x_ref[at, :].astype(F32) + total.total(b)
        middle_ref[b * step : (b + 1) * step, :] = v
        r = lax.rsqrt(jnp.mean(v * v, axis=1, keepdims=True) + EPS)
        h_ref[at, :] = (v * r * gain_ref[...]).astype(BF16)
        to_core(b).start()
    og.forward()
    og.finish()
    d_hidden_copy.wait()
    heads_swap.wait_recv()
    heads_swap.wait_send()
    for b in range(blocks):
        to_core(b).wait_recv()
        to_core(b).wait_send()
    total.finish()


def attention_out(heads, w_out, x, gain, out_grad, w_down, planes, shard):
    rows, model = x.shape
    half = rows // 2
    units = w_down.shape[0]
    blocks = 4
    tiles = units // math.gcd(units, 256)
    dma = pltpu.SemaphoreType.DMA
    cut_shape = jax.ShapeDtypeStruct((rows, planes * shard), BF16)
    return pl.pallas_call(
        functools.partial(out_kernel, planes=planes, shard=shard, blocks=blocks),
        out_shape=[
            jax.ShapeDtypeStruct((half, model), F32),
            jax.ShapeDtypeStruct((rows, model), BF16),
            jax.ShapeDtypeStruct((rows, units), F32),
        ]
        + [cut_shape] * 2
        + [jax.ShapeDtypeStruct(heads.shape, BF16)],
        in_specs=[ANYWHERE] * 4 + vmem(1) + [ANYWHERE],
        out_specs=vmem(2) + [ANYWHERE] + vmem(3),
        scratch_shapes=Staged.scratch([heads, w_out, out_grad, x])
        + [pltpu.VMEM((rows, units), F32), dma]
        + [pltpu.VMEM((units, model), BF16), dma((tiles,))]
        + [pltpu.VMEM((rows, model), F32), dma((blocks,)), dma((blocks,)), dma, dma]
        + TensorSum.scratch(blocks, half // blocks, model)
        + Columns.scratch(half, planes * shard),
        compiler_params=pltpu.CompilerParams(
            vmem_limit_bytes=VMEM_LIMIT, collective_id=4, has_side_effects=True
        ),
        cost_estimate=COST,
        name="attention_out",
    )(heads, w_out, out_grad, x, gain, w_down)


def middle_kernel(*refs, planes, shard, heads, width, pieces, blocks, sums):
    refs = list(refs)

    def take(count):
        out = refs[:count]
        del refs[:count]
        return out

    w_gate_ref, w_up_ref, gain_ref = take(3)
    count = 10 if sums else 8
    arrays = take(count)
    outs = take(3)
    hid_came_ref, a_ref, gain_out_ref, qx_ref, dox_ref, h_keep, h_came = take(7)
    if sums:
        down_outs = take(pieces - 1)
    buffers = take(count)
    inputs = Staged(arrays, buffers, *take(1))
    h_ref, d_ref, middle_ref, og_ref, w_out_ref, q_ref, o_ref, lse_ref = buffers[:8]
    if sums:
        og_keep, og_came = buffers[8:]
    out_buffers = take(3)
    hid_ref, gate_ref, up_ref = out_buffers
    outputs = Staged(outs, out_buffers, *take(1), out=True)
    gate_buf, up_buf, load_sems, c_ref, mine_ref = take(5)
    hid_send, hid_recv, a_send, a_recv = take(4)
    sum_scratch, h_scratch = take(8), take(6)
    device = lax.axis_index("dp")
    core, core_peer, y_peer = tensor_peers()
    plane = device // 2
    x_at = device % 2
    x_peer = {"dp": device + 1 - 2 * x_at}
    meets = [(x_peer, True), (core_peer, True), (y_peer, True)]
    h_two = Columns(h_ref, h_keep, h_came, h_scratch, x_at, core, x_peer, core_peer, planes, shard)
    half = middle_ref.shape[0]
    total = TensorSum(sum_scratch, mine_ref, core, core_peer, y_peer)
    chunks, columns = total.chunks, total.width
    units = hid_ref.shape[1]
    piece = units // pieces
    tile = 256
    tiles = units // tile
    if sums:
        downs = [LineSum(take(6), device, plane, planes) for _ in range(pieces - 1)]
        meets += [({"dp": device + 2}, plane < planes - 1), ({"dp": device - 2}, plane > 0)]

    def loads(t):
        at = pl.ds(t * tile, tile)
        return (
            pltpu.make_async_copy(w_gate_ref.at[:, at], gate_buf.at[:, at], load_sems.at[2 * t]),
            pltpu.make_async_copy(w_up_ref.at[:, at], up_buf.at[:, at], load_sems.at[2 * t + 1]),
        )

    inputs.start(h_ref)
    for t in range(tiles):
        for load in loads(t):
            load.start()
        if t == 0:
            inputs.start(d_ref)
    inputs.start(*buffers[2:])
    greet(meets)
    inputs.wait(h_ref)

    def swap(k):
        at = pl.ds(k * tile, tile)
        return remote(hid_ref.at[:, at], hid_came_ref.at[:, at], hid_send.at[k], hid_recv.at[k], x_peer)

    for t in range(tiles):
        for load in loads(t):
            load.wait()
        if t == 0:
            inputs.wait(d_ref)
        at = slice(t * tile, (t + 1) * tile)
        gate = dot(h_ref[...], gate_buf[:, at])
        up = dot(h_ref[...], up_buf[:, at])
        sig = 0.5 * jnp.tanh(0.5 * gate) + 0.5
        silu = gate * sig
        d = d_ref[:, at]
        hid_ref[:, at] = (silu * up).astype(BF16)
        up_ref[:, at] = (d * silu).astype(BF16)
        gate_ref[:, at] = (d * up * (sig * (1.0 + gate * (1.0 - sig)))).astype(BF16)
        swap(t).start()

    outputs.start()
    inputs.wait(*buffers[2:])

    def down_start(k):
        if sums:
            at = pl.ds(k * piece, piece)
            for t in range(k * piece // tile, (k + 1) * piece // tile):
                swap(t).wait_recv()
            downs[k].fill_columns(hid_ref.at[:, at], hid_came_ref.at[:, at], og_keep, og_came)
            downs[k].start()

    def down_advance(k, step):
        if sums and step <= planes - 2:
            downs[k].advance(step)

    for i in range(chunks):
        at = slice(i * columns, (i + 1) * columns)
        total.add(i, dot(gate_ref[...], gate_buf[at, :], NT) + dot(up_ref[...], up_buf[at, :], NT))
        if i == chunks // 2:
            down_start(0)
    for i in range(chunks):
        if i == chunks // 4:
            down_start(1)
            h_two.start()
        if i == chunks // 2:
            down_advance(0, 1)
        c_ref[:, i * columns : (i + 1) * columns] = total.total(i)
    down_advance(0, 2)

    step = half // blocks

    def to_core(b):
        rows = a_ref.at[pl.ds(pl.multiple_of(core * half + b * step, step), step), :]
        return remote(rows, rows, a_send.at[b], a_recv.at[b], core_peer)

    gain_out_ref[...] = jnp.zeros_like(gain_out_ref)
    for b in range(blocks):
        at = slice(b * step, (b + 1) * step)
        whole_at = pl.ds(pl.multiple_of(core * half + b * step, step), step)
        c = c_ref[at, :]
        v = middle_ref[at, :]
        r = lax.rsqrt(jnp.mean(v * v, axis=1, keepdims=True) + EPS)
        n = v * r
        gain_out_ref[...] += jnp.sum(c * n, axis=0, keepdims=True)
        gc = c * gain_ref[...]
        d = r * (gc - n * jnp.mean(n * gc, axis=1, keepdims=True)) + og_ref[whole_at, :].astype(F32)
        a_ref[whole_at, :] = d.astype(BF16)
        to_core(b).start()

    lane = lax.broadcasted_iota(jnp.int32, (half, width), 1)

    def extra(value):
        a, b, c = split_three(value)
        return jnp.where(lane == 0, a, jnp.where(lane == 1, b, jnp.where(lane == 2, c, 0.0))).astype(BF16)

    def prepare(which):
        at_rows = rows_of(which, half)
        d_heads = dot(a_ref[at_rows, :], w_out_ref[...], NT)
        for head in range(heads):
            at = slice(head * width, (head + 1) * width)
            qx_ref[head, at_rows, :width] = q_ref[at_rows, at]
            qx_ref[head, at_rows, width:] = extra(lse_ref[at_rows, at])
            d = d_heads[:, at].astype(BF16)
            delta = jnp.sum(d.astype(F32) * o_ref[at_rows, at].astype(F32), axis=1, keepdims=True)
            dox_ref[head, at_rows, :width] = d
            dox_ref[head, at_rows, width:] = extra(jnp.broadcast_to(delta, (half, width)))

    down_advance(1, 1)
    h_two.store()
    prepare(core)
    h_two.forward()
    for b in range(blocks):
        to_core(b).wait_recv()
    prepare(1 - core)
    down_advance(1, 2)
    for b in range(blocks):
        to_core(b).wait_send()
    total.finish()
    h_two.finish()
    outputs.wait()
    for t in range(tiles):
        if t >= (pieces - 1) * piece // tile or not sums:
            swap(t).wait_recv()
        swap(t).wait_send()
    if sums:
        for k in range(pieces - 1):
            for step in range(3, planes - 1):
                downs[k].advance(step)
            downs[k].finish(down_outs[k])


def middle_of(w_gate, w_up, h_two, d_hidden, middle, out_grad, gain, w_out, q, out, lse, cuts, pieces, planes, shard, width):
    half, model = middle.shape
    rows, units = d_hidden.shape
    columns = q.shape[1]
    heads = columns // width
    chunks, blocks = 4, 4
    dma = pltpu.SemaphoreType.DMA
    staged = [h_two, d_hidden, middle, out_grad, w_out, q, out, lse] + ([] if cuts is None else cuts)
    args = [w_gate, w_up, gain, *staged]
    unit_shape = jax.ShapeDtypeStruct((rows, units), BF16)
    out_shape = [unit_shape] * 4 + [
        jax.ShapeDtypeStruct((rows, model), BF16),
        jax.ShapeDtypeStruct((1, model), F32),
    ]
    out_shape += [jax.ShapeDtypeStruct((heads, rows, 2 * width), BF16)] * 2
    out_shape += [jax.ShapeDtypeStruct((rows, planes * shard), BF16)] * 2
    scratch = Staged.scratch(staged) + Staged.scratch([unit_shape] * 3)
    scratch += [pltpu.VMEM((model, units), BF16)] * 2 + [dma((2 * units // 256,))]
    scratch += [pltpu.VMEM((half, model), F32), pltpu.VMEM((2, rows, model // chunks), F32)]
    scratch += [dma((units // 256,))] * 2 + [dma((blocks,))] * 2
    scratch += TensorSum.scratch(chunks, half, model // chunks)
    scratch += Columns.scratch(half, planes * shard)
    if cuts is not None:
        out_shape += [jax.ShapeDtypeStruct((units // pieces, shard), BF16)] * (pieces - 1)
        scratch += LineSum.scratch(planes, (units // pieces, shard)) * (pieces - 1)
    return pl.pallas_call(
        functools.partial(
            middle_kernel,
            planes=planes,
            shard=shard,
            heads=heads,
            width=width,
            pieces=pieces,
            blocks=blocks,
            sums=cuts is not None,
        ),
        out_shape=out_shape,
        in_specs=[ANYWHERE] * 2 + vmem(1) + [ANYWHERE] * len(staged),
        out_specs=[ANYWHERE] * 3 + vmem(len(out_shape) - 3),
        scratch_shapes=scratch,
        compiler_params=pltpu.CompilerParams(
            vmem_limit_bytes=BACK_VMEM_LIMIT, collective_id=2, has_side_effects=True
        ),
        cost_estimate=COST,
        name="middle",
    )(*args)


def through_rope(d_ref, raw_ref, gain, cos, sin, out_ref, width, plain):
    columns = d_ref.shape[1]
    total = jnp.zeros((1, width), F32)
    for at in range(0, columns - plain, width):
        d = d_ref[:, at : at + width]
        c = d * cos - roll_half(d) * sin
        v = raw_ref[:, at : at + width]
        r = lax.rsqrt(jnp.mean(v * v, axis=1, keepdims=True) + EPS)
        n = v * r
        total = total + jnp.sum(c * n, axis=0, keepdims=True)
        gc = gain * c
        out_ref[:, at : at + width] = (r * (gc - n * jnp.mean(n * gc, axis=1, keepdims=True))).astype(BF16)
    if plain:
        out_ref[:, columns - plain :] = d_ref[:, columns - plain :].astype(BF16)
    return total


def front_kernel(*refs, dp_size, group, planes, shard, chunks, blocks, sums):
    refs = list(refs)

    def take(count):
        out = refs[:count]
        del refs[:count]
        return out

    q_gain, k_gain, attn_gain, mlp_gain_ref, add_array = take(5)
    count = 15 if sums else 11
    arrays = take(count)
    arrays[2:4] = table_rows(arrays[2:4], lax.axis_index("dp") % group, arrays[0].shape[0])
    x_grad, gains = take(2)
    if sums:
        w_up_out, w_q_out, w_kv_out = take(3)
    dq_ref, dq_came, dkv_ref, dkv_came, one_ref, one_came = take(6)
    buffers = take(count)
    inputs = Staged(arrays, buffers, *take(1))
    dkv_in, k_raw, cos_ref, sin_ref, dq_in, q_raw, one_all = buffers[:7]
    x_ref, w_q, w_k, w_v = buffers[7:11]
    if sums:
        two_ref, two_came, up_ref, up_came = buffers[11:]
    mine, gain_came, c_ref, add_ref, add_sem = take(5)
    swap_sems, one_sems, gain_sems = take(4), take(2), take(2)
    one_sum_scratch, one_scratch = take(8), take(6)
    half = x_ref.shape[0] // 2
    model = x_ref.shape[1]
    width = model // chunks
    head = cos_ref.shape[1]
    kv_width = w_k.shape[1]

    device = lax.axis_index("dp")
    core, core_peer, y_peer = tensor_peers()
    x_at = device % 2
    x_peer = {"dp": device + 1 - 2 * x_at}
    plane = device // 2
    one = Columns(one_all, one_ref, one_came, one_scratch, x_at, core, x_peer, core_peer, planes, shard)
    bits = [1 << i for i in range(dp_size.bit_length() - 1)]
    dp_peers = [{"dp": device + bit - 2 * bit * ((device // bit) % 2)} for bit in bits]
    gain_peers = [core_peer, y_peer] + dp_peers
    meets = [(peer, True) for peer in gain_peers]
    if sums:
        up_sum, q_sum, kv_sum = (LineSum(take(6), device, plane, planes, True) for _ in range(3))
        meets += [({"dp": device + 2}, plane < planes - 1), ({"dp": device - 2}, plane > 0)]

    mine_rows = rows_of(core, half)
    add_load = pltpu.make_async_copy(add_array.at[mine_rows, :], add_ref, add_sem)
    if sums:
        inputs.start(*buffers[11:])
    inputs.start(one_all)
    inputs.start(*buffers[:6])
    inputs.start(*buffers[7:11])
    add_load.start()
    greet(meets)
    if sums:
        inputs.wait(*buffers[11:])
        up_sum.fill_rows(two_ref, two_came, up_ref, up_came)
    inputs.wait(one_all)
    one.start()
    inputs.wait(*buffers[:6])
    cos, sin = cos_ref[...], sin_ref[...]
    k_total = through_rope(dkv_in, k_raw, k_gain[...], cos, sin, dkv_ref, head, kv_width)
    kv_swap = remote(dkv_ref, dkv_came, swap_sems[0], swap_sems[1], x_peer)
    kv_swap.start()
    q_total = through_rope(dq_in, q_raw, q_gain[...], cos, sin, dq_ref, head, 0)
    q_swap = remote(dq_ref, dq_came, swap_sems[2], swap_sems[3], x_peer)
    q_swap.start()
    inputs.wait(*buffers[7:11])

    one_sum = TensorSum(one_sum_scratch, mine, core, core_peer, y_peer)
    x = x_ref[...].astype(F32)
    r = lax.rsqrt(jnp.mean(x * x, axis=1, keepdims=True) + EPS)
    for i in range(chunks):
        at = slice(i * width, (i + 1) * width)
        part = (
            dot(dq_ref[...], w_q[at, :], NT)
            + dot(dkv_ref[:, :kv_width], w_k[at, :], NT)
            + dot(dkv_ref[:, kv_width:], w_v[at, :], NT)
        )
        one_sum.add(i, part)
        gains[0, :, at] = jnp.sum(part * (x_ref[:, at].astype(F32) * r), axis=0, keepdims=True)
    gains[0, :, model : 2 * model] = 0.5 * mlp_gain_ref[...]
    gains[0, :, 2 * model : 2 * model + head] = q_total
    gains[0, :, 2 * model + head :] = k_total
    one.forward()
    one.store()

    def gain_swap(k):
        return remote(
            gains.at[k], gain_came.at[k], gain_sems[0].at[k], gain_sems[1].at[k], gain_peers[k]
        )

    def gain_add(k):
        gain_swap(k).wait_recv()
        gains[k + 1] = gains[k] + gain_came[k]
        if k + 1 < len(gain_peers):
            gain_swap(k + 1).start()

    gain_swap(0).start()

    def advance(line, step):
        if sums and step <= planes - 2:
            line.advance(step)

    gain_add(0)
    if sums:
        advance(up_sum, 1)
        kv_swap.wait_recv()
        one.over_core().wait_recv()
        kv_sum.fill_rows(one_ref, one_came, dkv_ref, dkv_came)
    gain_add(1)
    if sums:
        q_swap.wait_recv()
        q_sum.fill_rows(one_ref, one_came, dq_ref, dq_came)
        advance(up_sum, 2)
    gain_add(2)

    def give(out, sems):
        rows = out.at[mine_rows, :]
        return remote(rows, rows, sems[0], sems[1], core_peer)

    for i in range(chunks):
        c_ref[:, i * width : (i + 1) * width] = one_sum.total(i)
    add_load.wait()
    step = half // blocks
    for b in range(blocks):
        at = slice(b * step, (b + 1) * step)
        whole_at = pl.ds(pl.multiple_of(core * half + b * step, step), step)
        v = x_ref[whole_at, :].astype(F32)
        v_r = lax.rsqrt(jnp.mean(v * v, axis=1, keepdims=True) + EPS)
        n = v * v_r
        gc = c_ref[at, :] * attn_gain[...]
        d = v_r * (gc - n * jnp.mean(n * gc, axis=1, keepdims=True))
        x_grad[whole_at, :] = (d + add_ref[at, :].astype(F32)).astype(BF16)
    give(x_grad, one_sems).start()
    for k in range(3, len(gain_peers)):
        gain_add(k)
    if sums:
        advance(kv_sum, 1)
        advance(q_sum, 1)
    if sums:
        advance(kv_sum, 2)
        advance(q_sum, 2)
        for line in (up_sum, kv_sum, q_sum):
            for step in range(3, planes - 1):
                advance(line, step)
        up_sum.finish(w_up_out)
        kv_sum.finish(w_kv_out)
        q_sum.finish(w_q_out)
    else:
        kv_swap.wait_recv()
        q_swap.wait_recv()
        one.over_core().wait_recv()
    one.over_x().wait_send()
    one.over_core().wait_send()
    kv_swap.wait_send()
    q_swap.wait_send()
    give(x_grad, one_sems).wait_recv()
    give(x_grad, one_sems).wait_send()
    for k in range(len(gain_peers)):
        gain_swap(k).wait_send()
    one_sum.finish()


def front(dq, dkv, q_raw, k_raw, q_gain, k_gain, cos, sin, h_one, weights, x, d_attn, attn_gain, mlp_gain, grads, dp_size, group, shard):
    rows, model = x.shape
    half = rows // 2
    planes = dp_size // 2
    chunks = 4
    width = model // chunks
    stages = dp_size.bit_length() + 1
    dma = pltpu.SemaphoreType.DMA
    gains = (2 * model + 2 * cos.shape[1],)
    staged = [dkv, k_raw, cos, sin, dq, q_raw, h_one, x, *weights]
    if grads is not None:
        staged += grads
    args = [q_gain, k_gain, attn_gain, mlp_gain, d_attn, *staged]
    cut_shape = jax.ShapeDtypeStruct((rows, planes * shard), BF16)
    whole = jax.ShapeDtypeStruct((rows, model), BF16)
    q_shape, kv_shape = jax.ShapeDtypeStruct(dq.shape, BF16), jax.ShapeDtypeStruct(dkv.shape, BF16)
    out_shape = [whole, jax.ShapeDtypeStruct((stages + 1, 1) + gains, F32)]
    kept = [q_shape, q_shape, kv_shape, kv_shape, cut_shape, cut_shape]
    table = jax.ShapeDtypeStruct((rows, cos.shape[1]), F32)
    scratch = Staged.scratch(staged[:2] + [table, table] + staged[4:])
    scratch += [pltpu.VMEM((2, rows, width), F32)]
    scratch += [pltpu.VMEM((stages, 1) + gains, F32), pltpu.VMEM((half, model), F32)]
    scratch += [pltpu.VMEM((half, model), BF16), dma]
    scratch += [dma] * 6 + [dma((stages,))] * 2
    scratch += TensorSum.scratch(chunks, half, width)
    scratch += Columns.scratch(half, planes * shard)
    if grads is None:
        out_shape += kept
    else:
        scratch = [pltpu.VMEM(s.shape, s.dtype) for s in kept] + scratch
        for columns in (grads[2].shape[1], dq.shape[1], dkv.shape[1]):
            out_shape.append(jax.ShapeDtypeStruct((shard, columns), BF16))
            scratch += LineSum.scratch(planes, (shard, columns))
    return pl.pallas_call(
        functools.partial(
            front_kernel,
            dp_size=dp_size,
            group=group,
            planes=planes,
            shard=shard,
            chunks=chunks,
            blocks=4,
            sums=grads is not None,
        ),
        out_shape=out_shape,
        in_specs=vmem(4) + [ANYWHERE] * (len(args) - 4),
        out_specs=vmem(len(out_shape)),
        scratch_shapes=scratch,
        compiler_params=pltpu.CompilerParams(
            vmem_limit_bytes=BACK_VMEM_LIMIT, collective_id=3, has_side_effects=True
        ),
        cost_estimate=COST,
        name="front",
    )(*args)


def widen_kernel(*refs, results, gains):
    refs = list(refs)

    def take(count):
        out = refs[:count]
        del refs[:count]
        return out

    count = 1 + max(i for parts in results for i, _ in parts)
    block_in = take(1)[0]
    arrays = take(count)
    if gains:
        gain_in = take(1)[0]
    block_out = take(1)[0]
    outs = take(len(results))
    if gains:
        attn_out, mlp_out, q_out, k_out = take(4)
    buffers = take(count)
    inputs = Staged(arrays, buffers, *take(1))
    out_buffers = take(len(results))
    outputs = Staged(outs, out_buffers, *take(1), out=True)
    block, block_sems = take(2)
    if gains:
        gain_ref, gain_sem = take(2)
        gain_load = pltpu.make_async_copy(gain_in.at[gain_in.shape[0] - 1], gain_ref, gain_sem)
        gain_load.start()
    block_load = pltpu.make_async_copy(block_in, block, block_sems.at[0])
    block_copy = pltpu.make_async_copy(block, block_out, block_sems.at[1])
    block_load.start()
    inputs.start()
    if gains:
        gain_load.wait()
        shard, head = attn_out.shape[1], q_out.shape[1]
        model = (gain_ref.shape[1] - 2 * head) // 2
        at = pl.multiple_of(lax.axis_index("dp") * shard, shard)
        attn_out[...] = gain_ref[:, pl.ds(at, shard)]
        mlp_out[...] = gain_ref[:, pl.ds(pl.multiple_of(model + at, shard), shard)]
        q_out[...] = gain_ref[:, 2 * model : 2 * model + head]
        k_out[...] = gain_ref[:, 2 * model + head :]
    block_load.wait()
    block_copy.start()
    waited = set()
    for parts, out in zip(results, out_buffers):
        row = 0
        for i, column in parts:
            part = buffers[i]
            if i not in waited:
                inputs.wait(part)
                waited.add(i)
            height = part.shape[0]
            out[row : row + height, :] = part[:, column : column + out.shape[1]].astype(F32)
            row += height
        outputs.start(out)
    block_copy.wait()
    outputs.wait()


def widen(block_out, arrays, results, shapes, gains, shard, head):
    out_shape = [jax.ShapeDtypeStruct(block_out.shape, BF16)]
    out_shape += [jax.ShapeDtypeStruct(s, F32) for s in shapes]
    args = [block_out, *arrays]
    rows = [] if gains is None else [(1, shard), (1, shard), (1, head), (1, head)]
    if gains is not None:
        args.append(gains)
    return pl.pallas_call(
        functools.partial(widen_kernel, results=results, gains=gains is not None),
        out_shape=out_shape + [jax.ShapeDtypeStruct(s, F32) for s in rows],
        in_specs=[ANYWHERE] * len(args),
        out_specs=[ANYWHERE] * (1 + len(shapes)) + vmem(len(rows)),
        scratch_shapes=Staged.scratch(arrays)
        + Staged.scratch(out_shape[1:])
        + [pltpu.VMEM(block_out.shape, BF16), pltpu.SemaphoreType.DMA((2,))]
        + ([] if gains is None else [pltpu.VMEM(gains.shape[1:], F32), pltpu.SemaphoreType.DMA]),
        compiler_params=params(),
        cost_estimate=COST,
        name="widen",
    )(*args)


def rope_tables(length, width):
    frequency = ROPE_BASE ** (-2.0 * np.arange(width // 2) / width)
    angles = np.arange(length)[:, None] * frequency[None, :]
    cos, sin = np.cos(angles), np.sin(angles)
    tables = np.concatenate([cos, cos], axis=1), np.concatenate([-sin, sin], axis=1)
    return tuple(jnp.asarray(t.astype(np.float32)) for t in tables)


class Chain:
    def __init__(self):
        self.last = None

    def mark(self, value):
        self.last = value

    def __call__(self, *values):
        if self.last is None:
            return values
        return lax.optimization_barrier((*values, self.last))[:-1]


class ZSum:
    def __init__(self, part, dim, shard, planes, z_at):
        self.part, self.dim, self.shard, self.planes, self.z_at = part, dim, shard, planes, z_at
        self.at = 0
        self.came = None

    def term(self, j):
        j = jnp.clip(j, 0, self.planes - 1)
        return lax.dynamic_slice_in_dim(self.part, j * self.shard, self.shard, self.dim)

    def send(self, up, down):
        last = self.planes - 1
        self.at += 1
        up_pairs = [(2 * z + x, 2 * z + 2 + x) for z in range(last) for x in range(2) if z < self.at]
        down_pairs = [
            (2 * (last - z) + x, 2 * (last - 1 - z) + x)
            for z in range(last)
            for x in range(2)
            if z < self.at
        ]
        self.came = lax.ppermute(up, "dp", up_pairs), lax.ppermute(down, "dp", down_pairs)

    def terms(self):
        planes, z_at, at = self.planes, self.z_at, self.at
        return self.term(planes - 1 - at + z_at), self.term(at + 1 - planes + z_at)

    def start(self):
        self.send(*self.terms())

    def step(self, chain):
        if self.at >= self.planes - 1:
            return
        up, down = chain(*self.came)
        up_term, down_term = self.terms()
        up, down = up + up_term, down + down_term
        chain.mark(up)
        self.send(up, down)

    def finish(self, chain):
        if self.at == 0:
            self.start()
        while self.at < self.planes - 1:
            self.step(chain)
        up, down = chain(*self.came)
        total = self.term(self.z_at).astype(F32) + up.astype(F32) + down.astype(F32)
        chain.mark(total)
        return total


def shards(
    dp_size,
    tensor_size,
    tokens,
    norm_attn,
    w_query,
    key_weight,
    value_weight,
    query_gain,
    key_gain,
    w_out,
    norm_mlp,
    w_gate,
    w_up,
    w_down,
    out_grad,
    prefix_len,
):
    rows, model = tokens.shape
    width = query_gain.shape[0]
    kv_heads = key_weight.shape[1] // width
    repeat = w_query.shape[1] // key_weight.shape[1]
    dims = (kv_heads, repeat, width)
    group = dp_size // prefix_len.shape[0]
    planes = dp_size // 2
    group_planes = group // 2
    half = rows // 2
    shard = model // dp_size
    assert tensor_size == 4 and MAX_PREFIX <= 4 * rows

    device = lax.axis_index("dp")
    x_at = device % 2
    z_at = device // 2
    sequence = device // group
    member = device % group
    plane = member // 2
    prefix = jnp.sum(jnp.where(jnp.arange(prefix_len.shape[0]) == sequence, prefix_len, 0))

    x_pairs = [(d, d ^ 1) for d in range(dp_size)]

    def x_swap(value):
        return lax.ppermute(value, "dp", x_pairs)

    cos, sin = rope_tables(group * rows, width)
    norm_attn_row = norm_attn[None, :]
    norm_mlp_row = norm_mlp[None, :]
    q_gain_row = query_gain[None, :]
    k_gain_row = key_gain[None, :]

    prefix_at = prefix[None].astype(jnp.int32)
    heads_b, lse, kv_all, h_one, q, q_raw, k_raw = attn_fwd(
        prefix_at,
        tokens,
        norm_attn_row,
        w_query,
        key_weight,
        value_weight,
        q_gain_row,
        k_gain_row,
        cos,
        sin,
        group,
        dims,
    )
    fused = planes == group_planes and shard % 128 == 0
    pieces = 3
    middle, h_two, d_hidden, og_keep, og_came, heads_came = attention_out(
        heads_b, w_out, tokens, norm_mlp_row, out_grad, w_down, planes, shard
    )
    outs = middle_of(
        w_gate,
        w_up,
        h_two,
        d_hidden,
        middle,
        out_grad,
        norm_mlp_row,
        w_out,
        q,
        heads_b,
        lse,
        [og_keep, og_came] if fused else None,
        pieces,
        planes,
        shard,
        width,
    )
    hidden, d_gate, d_up, hidden_came, d_attn, norm_mlp_part, qx, dox, h_two_keep, h_two_came = outs[:10]

    grads = None
    if fused:
        grads = [hidden_came, og_keep, og_came, d_gate, h_two_keep, h_two_came]
        grads += [heads_b, heads_came]
        w_down_parts = outs[10:]
    shared = [d_attn, d_up, hidden, w_down, middle]
    outs = back(prefix_at, qx, dox, kv_all, shared, grads, group, planes, shard, pieces, dims)
    dq, kv_grad, up_came, block_out = outs[:4]
    chain = Chain()
    chain.mark(dq)
    if fused:
        w_down_parts = [*w_down_parts, outs[4]]
        w_gate_grad, w_out_grad = outs[5:]
    else:
        d_attn_keep, d_attn_came = outs[4:]
        down_part = (dot(hidden, og_keep, TN) + dot(hidden_came, og_came, TN)).astype(BF16)
        w_down_grad = ZSum(down_part, 1, shard, planes, z_at).finish(chain)
        gate_part = dot(h_two_keep, d_gate, TN) + dot(h_two_came, x_swap(d_gate), TN)
        w_gate_grad = ZSum(gate_part.astype(BF16), 0, shard, planes, z_at).finish(chain)
        out_part = dot(heads_b, d_attn_keep, TN) + dot(heads_came, d_attn_came, TN)
        w_out_grad = ZSum(out_part.astype(BF16), 1, shard, planes, z_at).finish(chain)

    up_grads = [h_two_keep, h_two_came, d_up, up_came] if fused else None
    outs = front(
        *chain(dq),
        kv_grad,
        q_raw,
        k_raw,
        q_gain_row,
        k_gain_row,
        cos,
        sin,
        h_one,
        (w_query, key_weight, value_weight),
        tokens,
        d_attn,
        norm_attn_row,
        norm_mlp_part,
        up_grads,
        dp_size,
        group,
        shard,
    )
    tokens_grad, gains = outs[:2]
    if fused:
        w_up_grad, w_query_grad, w_kv_grad = outs[2:]
    else:
        dq_b, dq_came, dkv_b, dkv_came, h_one_keep, h_one_came = outs[2:]
        chain.mark(tokens_grad)

        def by_rows(left, left_came, right, right_came):
            part = dot(left, right, TN) + dot(left_came, right_came, TN)
            return ZSum(part.astype(BF16), 0, shard, planes, z_at).finish(chain)

        w_up_grad = by_rows(h_two_keep, h_two_came, d_up, up_came)
        w_query_grad = by_rows(h_one_keep, h_one_came, dq_b, dq_came)
        w_kv_grad = by_rows(h_one_keep, h_one_came, dkv_b, dkv_came)
    kv_width = kv_heads * width
    if fused:
        arrays = [w_gate_grad, w_out_grad, *w_down_parts, w_up_grad, w_query_grad, w_kv_grad, tokens_grad]
        n = 2 + len(w_down_parts)
        results = [[(0, 0)], [(1, 0)], [(i, 0) for i in range(2, n)]]
        results += [[(n, 0)], [(n + 1, 0)], [(n + 2, 0)], [(n + 2, kv_width)], [(n + 3, 0)]]
        units = w_gate.shape[1]
        columns = w_query.shape[1]
        shapes = [(shard, units), (columns, shard), (units, shard), (shard, units), (shard, columns)]
        shapes += [(shard, kv_width)] * 2 + [(rows, model)]
        outs = widen(block_out, arrays, results, shapes, gains, shard, width)
        block_out, w_gate_grad, w_out_grad, w_down_grad, w_up_grad, w_query_grad = outs[:6]
        w_key_grad, w_value_grad, tokens_grad = outs[6:9]
        norm_attn_grad, norm_mlp_grad, query_gain_grad, key_gain_grad = (v[0] for v in outs[9:])
    else:
        w_key_grad, w_value_grad = w_kv_grad[:, :kv_width], w_kv_grad[:, kv_width:]
        tokens_grad = tokens_grad.astype(F32)
        gains = gains[-1, 0]
        norm_attn_grad = lax.dynamic_slice_in_dim(gains, device * shard, shard, 0)
        norm_mlp_grad = lax.dynamic_slice_in_dim(gains, model + device * shard, shard, 0)
        query_gain_grad, key_gain_grad = gains[2 * model : 2 * model + width], gains[2 * model + width :]
    return (
        block_out,
        tokens_grad,
        norm_attn_grad,
        w_query_grad,
        w_key_grad,
        w_value_grad,
        query_gain_grad,
        key_gain_grad,
        w_out_grad,
        norm_mlp_grad,
        w_gate_grad,
        w_up_grad,
        w_down_grad,
    )


def solution(mesh):
    placed = (
        P("dp", None),
        P(),
        P(None, "tensor"),
        P(None, "tensor"),
        P(None, "tensor"),
        P(),
        P(),
        P("tensor", None),
        P(),
        P(None, "tensor"),
        P(None, "tensor"),
        P("tensor", None),
        P("dp", None),
        P(),
    )
    return jax.shard_map(
        functools.partial(shards, mesh.shape["dp"], mesh.shape["tensor"]),
        mesh=mesh,
        in_specs=placed,
        out_specs=(
            P("dp", None),
            P("dp", None),
            P("dp"),
            P("dp", "tensor"),
            P("dp", "tensor"),
            P("dp", "tensor"),
            P(),
            P(),
            P("tensor", "dp"),
            P("dp"),
            P("dp", "tensor"),
            P("dp", "tensor"),
            P("tensor", "dp"),
        ),
        check_vma=False,
    )
```
